256 devices in a mesh: samp: 32 (over z, y), par: 8 (over x, core).
Axes of the slice: x: 4, y: 4, z: 8, core: 2. Of those that a mesh axis runs over, the one named last changes fastest.
Arguments:
- activations: bfloat16 [256, 16, 64, 576], P('samp', 'par'), may hold values from -17 to 17
- cotangents: bfloat16 [256, 16, 64, 576], P('samp', 'par'), may hold values from -0.34999167 to 0.34999167
- spin_bits: int32 [256, 576], P('samp'), may hold values from 0 to 1
- offdiag_energy: float32 [256], P('samp'), may hold values from -24 to 24
Outputs:
- update: float32 [16, 36864], P('par', 'samp')
- coefficients: float32 [256], P('samp')
The draws below stay inside these ranges and needn't reach their ends.
Inputs may be any that keep to these rules, and one draw needn't show every extreme that they name: `spin_bits`: 1 marks an up spin, 0 a down spin.
All inputs are finite; a program needn't handle non-finite values.
Results may differ from the reference program's by a relative error of at most 0.0078.
The reference program's roundings to bfloat16 on the way (of `jacobian` and `centered`) count: a program that leaves them out, or rounds other values in their place, can miss the bound.
Values may be sent and summed in bfloat16 or wider, within the bound.
A program may use at most 128 MiB of HBM per device.

```python
import math
import jax
import jax.numpy as jnp
from jax import lax

CH = 64
KK = 9
LAT = 24
SITES = 576
CONVS = 16
NS = 256


def clipped_normal(key, shape):
    return jnp.clip(jax.random.normal(key, shape, jnp.float32), -4.0, 4.0)


def mode_field(key, coef, noise):
    jitter_key, pattern_key = jax.random.split(key, 2)
    group_size = CH // 8
    jitter = jax.random.uniform(jitter_key, (CONVS, 8), jnp.float32)
    amplitude = jnp.exp(-0.29 * (jnp.arange(8, dtype=jnp.float32)[None, :] + jitter))
    weighting = jnp.repeat(coef * amplitude[None], group_size, axis=2)
    pattern = clipped_normal(pattern_key, (CONVS, CH, SITES))
    return weighting[..., None] * pattern[None] + 0.02 * noise


def sample_terms(coef_key, noise_key):
    shape = (NS, CONVS, CH, SITES)
    coef = clipped_normal(coef_key, (NS, CONVS, 8))
    noise = clipped_normal(noise_key, shape)
    return (coef, noise)


def draw_activations(key, part):
    key = jax.random.fold_in(key, 3)
    coef_key, noise_key, field_key = jax.random.split(key, 3)
    coef, noise = sample_terms(coef_key, noise_key)
    return mode_field(field_key, coef, noise).astype(jnp.bfloat16)


def draw_cotangents(key, part):
    key = jax.random.fold_in(key, 5)
    coef_key, noise_key, field_key = jax.random.split(key, 3)
    coef, noise = sample_terms(coef_key, noise_key)
    cot_scale = math.sqrt(1000.0 * math.sqrt(NS) / (CONVS * SITES * CH * CH))
    return (cot_scale * mode_field(field_key, coef, noise)).astype(jnp.bfloat16)


def set_ends(drawn, key, least, high):
    place = [jax.random.randint(jax.random.fold_in(key, axis), (), 0, length) for axis, length in enumerate(drawn.shape)]
    widest = drawn.shape.index(max(drawn.shape))
    beside = place[:widest] + [(place[widest] + 1) % drawn.shape[widest]] + place[widest + 1:]
    return drawn.at[tuple(place)].set(least).at[tuple(beside)].set(high)


def shard_levels(own_key, shape, cuts, least, largest):
    loudness = 1.0
    for axis_at, parts in cuts:
        draws = jax.random.uniform(jax.random.fold_in(jax.random.fold_in(own_key, 6), axis_at), (parts,), jnp.float32, least / len(cuts), largest / len(cuts))
        loudness = loudness * jnp.repeat(jnp.exp(draws), shape[axis_at] // parts).reshape((-1,) + (1,) * (len(shape) - 1 - axis_at))
    return loudness


def gaussian(stream_key, extent, width, limit, cuts=(), held_as=jnp.bfloat16):
    array = jax.random.normal(stream_key, extent, jnp.float32) * width
    if len(cuts) > 0:
        array = shard_levels(stream_key, extent, cuts, -0.22, 0.18) * array
    return jnp.clip(array, min=-limit, max=limit).astype(held_as)


def setup_inputs(seed: int = 0) -> dict:
    key_list = jax.random.split(jax.random.key(seed), 5)
    return {
        "activations": draw_activations(jax.random.fold_in(key_list[4], 71), 0),
        "cotangents": draw_cotangents(jax.random.fold_in(key_list[4], 71), 0),
        "spin_bits": set_ends(jax.random.randint(key_list[2], (NS, SITES), 0, 2), jax.random.fold_in(key_list[2], 1), 0, 1).astype(jnp.int32),
        "offdiag_energy": gaussian(key_list[3], (NS,), 4.0, 24.0, ((0, 32),), jnp.float32),
    }


def shifted(values_in, row_step, col_step):
    grid = values_in.reshape(values_in.shape[:-1] + (LAT, LAT))
    grid = jnp.roll(grid, (-row_step, -col_step), axis=(-2, -1))
    return grid.reshape(values_in.shape)

def diagonal_energy(spin_bits):
    spin = (2 * spin_bits - 1).astype(jnp.float32).reshape(-1, LAT, LAT)
    nearest = spin * jnp.roll(spin, -1, 1) + spin * jnp.roll(spin, -1, 2)
    diagonal = spin * jnp.roll(spin, (-1, -1), (1, 2)) + spin * jnp.roll(spin, (-1, 1), (1, 2))
    return 0.25 * lax.optimization_barrier(jnp.sum(nearest + 0.5 * diagonal, axis=(1, 2)))

def conv_jacobian(layer_acts, layer_cots):
    acts_wide = layer_acts.astype(jnp.float32)
    cots_wide = layer_cots.astype(jnp.float32)
    pieces = []
    for row_step in (-1, 0, 1):
        for col_step in (-1, 0, 1):
            moved = shifted(acts_wide, row_step, col_step)
            pieces.append(jnp.einsum('nix,nox->nio', moved, cots_wide))
    stacked = jnp.stack(pieces, 1)
    return stacked.reshape(stacked.shape[0], KK * CH * CH).astype(jnp.bfloat16)

def reference(activations, cotangents, spin_bits, offdiag_energy):
    energy = diagonal_energy(spin_bits) + offdiag_energy
    mean_energy = jnp.sum(energy) / NS
    residual_energy = -(energy - mean_energy) / math.sqrt(NS)
    gram_matrix = jnp.zeros((NS, NS), jnp.float32)
    centered_all = []
    for layer in range(CONVS):
        jacobian = conv_jacobian(activations[:, layer], cotangents[:, layer])
        jac_wide = jacobian.astype(jnp.float32)
        mean_col = lax.optimization_barrier(jnp.mean(jac_wide, axis=0))
        centered = ((jac_wide - mean_col) / math.sqrt(NS)).astype(jnp.bfloat16)
        cent_wide = centered.astype(jnp.float32)
        gram_matrix = gram_matrix + jnp.dot(cent_wide, cent_wide.T, precision=lax.Precision.HIGHEST)
        centered_all.append(centered)
    shift_value = 0.01 * jnp.trace(gram_matrix) / NS
    system = gram_matrix + shift_value * jnp.eye(NS, dtype=jnp.float32)
    factor = jnp.linalg.cholesky(system)
    solution = jax.scipy.linalg.cho_solve((factor, True), residual_energy)
    raw_rows = [jnp.dot(solution, item.astype(jnp.float32), precision=lax.Precision.HIGHEST) for item in centered_all]
    raw_step = jnp.stack(raw_rows, 0)
    step_scale = jnp.sqrt(jnp.mean(raw_step * raw_step) + 1e-06)
    return (raw_step / step_scale, solution)
```

```python
import math

import jax
import jax.numpy as jnp
from jax import lax
from jax.experimental import pallas as pl
from jax.experimental.pallas import tpu as pltpu
from jax.sharding import PartitionSpec as P

CH = 64
KK = 9
LAT = 24
SITES = LAT * LAT
NSAMP = 32
NPAR = 8
NZ = 8
NY = 4
LOCAL = 8
NS = NSAMP * LOCAL
ROWS = KK * CH // NSAMP
CHUNK = ROWS * LOCAL
WIDTH = ROWS * 128
PADK = 640
LAYERS = 2
ENTRIES = 16 * KK * CH * CH
MESH = pl.DeviceIdType.MESH
VMEM_LIMIT = 56 * 1024 * 1024
HIGHEST = lax.Precision.HIGHEST
VMEM = pltpu.VMEM


def rolled(value, amount):
    amount = amount % SITES
    if amount == 0:
        return value
    return jnp.concatenate([value[:, amount:], value[:, :amount]], axis=1)


def column_shift(value, col_step):
    if col_step == 0:
        return value
    column = lax.broadcasted_iota(jnp.int32, value.shape, 1) % LAT
    edge = LAT - 1 if col_step > 0 else 0
    return jnp.where(column == edge, rolled(value, col_step - LAT * col_step), rolled(value, col_step))


def samp_partner(z, y, step):
    high = step % NZ
    hop = lax.select(high % 2 == 1, (high + 1) // 2, NZ - high // 2)
    return ((z + hop) % NZ) * NY + (y + step // NZ) % NY


def diagonal_energy(spin_bits):
    spin = (2 * spin_bits - 1).astype(jnp.float32)
    right = column_shift(spin, 1)
    left = column_shift(spin, -1)
    pairs = spin * rolled(spin, LAT) + spin * right
    corners = spin * rolled(right, LAT) + spin * rolled(left, LAT)
    diag = 0.25 * jnp.sum(pairs + 0.5 * corners, axis=1, keepdims=True)
    wide = jnp.broadcast_to(diag, (LOCAL, 128))
    here = lax.broadcasted_iota(jnp.int32, (LOCAL, 128), 0) == lax.broadcasted_iota(
        jnp.int32, (LOCAL, 128), 1
    )
    return jnp.sum(jnp.where(here, wide, 0.0), axis=0, keepdims=True)


WAVES = 4
PER_WAVE = LOCAL // WAVES
CHIPS = 16
TAIL = 48


def main_kernel(
    act_hbm, cot_hbm, spin_ref, off_ref,
    gram_ref, cent_hbm, energies_ref,
    act_ref, cot_ref, lhs, rhs, wide_rows, send_ref, recv_ref, wide_recv, cent_ref,
    energy_ref, half_ref, first, mine, second,
    act_sem, cot_sem, cent_sem, send_sem, recv_sem, esend_sem, erecv_sem,
    core_sem, s1, r1, s2, r2, s3, r3, s4, r4,
):
    samp = lax.axis_index("samp")
    par = lax.axis_index("par")
    z, y = samp // NY, samp % NY
    x, core = par // 2, par % 2
    chip = y * 4 + x
    sibling = (samp, x * 2 + 1 - core)

    def act_copy(n):
        return pltpu.make_async_copy(act_hbm.at[n], act_ref.at[n], act_sem.at[n])

    def cot_copy(n):
        return pltpu.make_async_copy(cot_hbm.at[n], cot_ref.at[n], cot_sem.at[n])

    for n in range(LOCAL):
        act_copy(n).start()
        cot_copy(n).start()

    def chip_at(step):
        other = (chip + step) % CHIPS
        return other, (z * NY + other // 4, (other % 4) * 2 + core)

    def column_at(step):
        other = (z + step) % NZ
        return other, (other * NY + y, par)

    barrier = pltpu.get_barrier_semaphore()

    def greet(step, carry):
        other = samp_partner(z, y, step)
        pl.semaphore_signal(barrier, inc=1, device_id=(other, par), device_id_type=MESH)
        return carry

    lax.fori_loop(1, NSAMP, greet, 0)

    def greet_chip(step, carry):
        across = (x + 1 + step % 3) % 4
        down = (y + step // 3) % NY
        pl.semaphore_signal(
            barrier, inc=1, device_id=(z * NY + down, across * 2 + core), device_id_type=MESH
        )
        return carry

    lax.fori_loop(0, 12, greet_chip, 0)
    pl.semaphore_signal(barrier, inc=1, device_id=sibling, device_id_type=MESH)

    rhs[...] = jnp.zeros_like(rhs)
    for layer in range(LAYERS):
        edge = layer * PADK + SITES - CH
        lhs[:, :, edge : edge + 128] = jnp.zeros((PER_WAVE, KK * CH, 128), jnp.bfloat16)

    def compute(wave):
        for slot in range(PER_WAVE):
            sample = wave * PER_WAVE + slot
            act_copy(sample).wait()
            cot_copy(sample).wait()
            for layer in range(LAYERS):
                base = layer * PADK
                act = act_ref[sample, layer]
                rhs[slot, layer * CH : (layer + 1) * CH, base : base + SITES] = cot_ref[sample, layer]
                for col_step in (-1, 0, 1):
                    moved = column_shift(act, col_step)
                    for row_step in (-1, 0, 1):
                        tap = 3 * (row_step + 1) + col_step + 1
                        lhs[slot, tap * CH : (tap + 1) * CH, base : base + SITES] = rolled(
                            moved, LAT * row_step
                        )
            out = lax.dot_general(
                lhs[slot], rhs[slot], (((1,), (1,)), ((), ())), preferred_element_type=jnp.float32
            )
            for dest in range(NSAMP):
                wide_rows[dest, pl.ds(sample * ROWS, ROWS), :] = out[dest * ROWS : (dest + 1) * ROWS]

    def wave_copy(other, low, rows):
        return pltpu.make_async_remote_copy(
            src_ref=send_ref.at[other, pl.ds(low, rows)],
            dst_ref=recv_ref.at[samp, pl.ds(low, rows)],
            send_sem=send_sem.at[other],
            recv_sem=recv_sem.at[samp],
            device_id=(other, par),
            device_id_type=MESH,
        )

    def send_wave(low, rows):
        def body(step, carry):
            other = samp_partner(z, y, step)
            send_ref[other, pl.ds(low, rows), :] = wide_rows[other, pl.ds(low, rows), :].astype(
                jnp.bfloat16
            )
            wave_copy(other, low, rows).start()
            return carry

        lax.fori_loop(1, NSAMP, body, 0)

    compute(0)
    pl.semaphore_wait(barrier, NSAMP - 1 + 12 + 1)
    send_wave(0, 32)

    def later(wave, carry):
        compute(wave)

        @pl.when(wave < WAVES - 1)
        def _():
            send_wave(pl.multiple_of(wave * 32, 32), 32)

        @pl.when(wave == WAVES - 1)
        def _():
            send_wave(96, TAIL)

        return carry

    lax.fori_loop(1, WAVES, later, 0)

    flat = diagonal_energy(spin_ref[...])
    energy_ref[...] = jnp.zeros_like(energy_ref)
    energy_ref[:, :LOCAL] = flat[:, :LOCAL] + off_ref[...]

    def energy_copy(other, source):
        return pltpu.make_async_remote_copy(
            src_ref=energy_ref,
            dst_ref=energies_ref.at[source],
            send_sem=esend_sem.at[other],
            recv_sem=erecv_sem.at[source],
            device_id=(other, par),
            device_id_type=MESH,
        )

    def send_energy(step, carry):
        energy_copy(samp_partner(z, y, step), samp).start()
        return carry

    lax.fori_loop(1, NSAMP, send_energy, 0)
    energies_ref[samp] = energy_ref[...]
    wide_recv[pl.ds(pl.multiple_of(samp * CHUNK, CHUNK), CHUNK), :] = (
        wide_rows[samp].astype(jnp.bfloat16).astype(jnp.float32)
    )

    def arrive(step, carry):
        other = samp_partner(z, y, step)
        pltpu.make_async_remote_copy(
            src_ref=send_ref.at[other],
            dst_ref=recv_ref.at[other],
            send_sem=send_sem.at[other],
            recv_sem=recv_sem.at[other],
            device_id=(other, par),
            device_id_type=MESH,
        ).wait_recv()
        wide_recv[pl.ds(pl.multiple_of(other * CHUNK, CHUNK), CHUNK), :] = recv_ref[other].astype(
            jnp.float32
        )
        return carry

    lax.fori_loop(1, NSAMP, arrive, 0)

    def centre(row, carry):
        part = jnp.stack(
            [wide_recv[pl.ds(src * CHUNK + row, LOCAL, stride=ROWS), :] for src in range(NSAMP)]
        )
        mean = jnp.sum(jnp.sum(part, axis=0), axis=0, keepdims=True) / NS
        cent = ((part - mean) / math.sqrt(NS)).reshape(NS, 128)
        cent_ref[:, pl.ds(pl.multiple_of(row * 128, 128), 128)] = cent.astype(jnp.bfloat16)
        return carry

    lax.fori_loop(0, ROWS, centre, 0)
    cent_copy = pltpu.make_async_copy(cent_ref, cent_hbm, cent_sem)
    cent_copy.start()

    def gram_rows(low):
        return lax.dot_general(
            cent_ref[pl.ds(low, 128), :], cent_ref[...], (((1,), (1,)), ((), ())),
            preferred_element_type=jnp.float32,
        )

    mine_low = pl.multiple_of(core * 128, 128)
    core_copy = pltpu.make_async_remote_copy(
        src_ref=half_ref.at[0],
        dst_ref=half_ref.at[1],
        send_sem=core_sem.at[0],
        recv_sem=core_sem.at[1],
        device_id=sibling,
        device_id_type=MESH,
    )
    half_ref[0] = gram_rows(pl.multiple_of((1 - core) * 128, 128))
    core_copy.start()
    half_ref[2] = gram_rows(mine_low)
    core_copy.wait_recv()
    half_ref[2] = half_ref[2] + half_ref[1]

    def rows_of(index):
        return pl.ds(pl.multiple_of(index * 8, 8), 8)

    def gram_block(index):
        return gram_ref.at[pl.ds(pl.multiple_of(mine_low + index * 8, 8), 8)]

    def copy_one(step, landed):
        other, device = chip_at(step)
        return pltpu.make_async_remote_copy(
            src_ref=half_ref.at[2, rows_of(other)],
            dst_ref=first.at[other if landed else chip],
            send_sem=s1.at[other],
            recv_sem=r1.at[other if landed else chip],
            device_id=device,
            device_id_type=MESH,
        )

    def copy_two(step, landed):
        other, device = column_at(step)
        return pltpu.make_async_remote_copy(
            src_ref=mine,
            dst_ref=second.at[other if landed else z],
            send_sem=s2.at[other],
            recv_sem=r2.at[other if landed else z],
            device_id=device,
            device_id_type=MESH,
        )

    def copy_three(step, landed):
        other, device = chip_at(step)
        return pltpu.make_async_remote_copy(
            src_ref=gram_block(chip),
            dst_ref=gram_block(other if landed else chip),
            send_sem=s3.at[other],
            recv_sem=r3.at[other if landed else chip],
            device_id=device,
            device_id_type=MESH,
        )

    def copy_four(index, landed):
        low = (1 - core) * 128 if landed else mine_low
        block = gram_ref.at[pl.ds(pl.multiple_of(low + index * 8, 8), 8)]
        return pltpu.make_async_remote_copy(
            src_ref=block,
            dst_ref=block,
            send_sem=s4.at[index],
            recv_sem=r4.at[index],
            device_id=sibling,
            device_id_type=MESH,
        )

    def run(copy, count):
        def start(step, carry):
            copy(step, False).start()
            return carry

        lax.fori_loop(1, count, start, 0)

    def settle(copy, count):
        def wait(step, carry):
            copy(step, True).wait_recv()
            return carry

        lax.fori_loop(1, count, wait, 0)

    def drain(copy, low, count):
        def wait(step, carry):
            copy(step, False).wait_send()
            return carry

        lax.fori_loop(low, count, wait, 0)

    run(copy_one, CHIPS)
    first[chip] = half_ref[2, rows_of(chip), :]
    settle(copy_one, CHIPS)
    own = jnp.sum(first[...], axis=0)
    mine[...] = own
    run(copy_two, NZ)
    second[z] = own
    settle(copy_two, NZ)
    gram_ref[pl.ds(pl.multiple_of(mine_low + chip * 8, 8), 8), :] = jnp.sum(second[...], axis=0)
    run(copy_three, CHIPS)
    copy_four(chip, False).start()

    def forward(step, carry):
        copy_three(step, True).wait_recv()
        copy_four(chip_at(step)[0], False).start()
        return carry

    lax.fori_loop(1, CHIPS, forward, 0)

    def wait_sent(step, carry):
        other = samp_partner(z, y, step)
        pltpu.make_async_remote_copy(
            src_ref=send_ref.at[other],
            dst_ref=recv_ref.at[samp],
            send_sem=send_sem.at[other],
            recv_sem=recv_sem.at[samp],
            device_id=(other, par),
            device_id_type=MESH,
        ).wait_send()
        energy_copy(other, samp).wait_send()
        energy_copy(other, other).wait_recv()
        return carry

    lax.fori_loop(1, NSAMP, wait_sent, 0)
    core_copy.wait_send()
    drain(copy_one, 1, CHIPS)
    drain(copy_two, 1, NZ)
    drain(copy_three, 1, CHIPS)

    def arrive_four(index, carry):
        copy_four(index, True).wait_recv()
        return carry

    lax.fori_loop(0, CHIPS, arrive_four, 0)
    drain(copy_four, 0, CHIPS)
    cent_copy.wait()


def main_call(activations, cotangents, spin_bits, off_row):
    whole = pl.BlockSpec(memory_space=VMEM)
    anywhere = pl.BlockSpec(memory_space=pl.ANY)
    dma = pltpu.SemaphoreType.DMA
    return pl.pallas_call(
        main_kernel,
        in_specs=[anywhere, anywhere, whole, whole],
        out_specs=[whole, anywhere, whole],
        out_shape=[
            jax.ShapeDtypeStruct((NS, NS), jnp.float32),
            jax.ShapeDtypeStruct((NS, WIDTH), jnp.bfloat16),
            jax.ShapeDtypeStruct((NSAMP, 1, 128), jnp.float32),
        ],
        scratch_shapes=[
            VMEM((LOCAL, LAYERS, CH, SITES), jnp.bfloat16),
            VMEM((LOCAL, LAYERS, CH, SITES), jnp.bfloat16),
            VMEM((PER_WAVE, KK * CH, LAYERS * PADK), jnp.bfloat16),
            VMEM((PER_WAVE, LAYERS * CH, LAYERS * PADK), jnp.bfloat16),
            VMEM((NSAMP, CHUNK, 128), jnp.float32),
            VMEM((NSAMP, CHUNK, 128), jnp.bfloat16),
            VMEM((NSAMP, CHUNK, 128), jnp.bfloat16),
            VMEM((NSAMP * CHUNK, 128), jnp.float32),
            VMEM((NS, WIDTH), jnp.bfloat16),
            VMEM((1, 128), jnp.float32),
            VMEM((3, 128, NS), jnp.float32),
            VMEM((CHIPS, 8, NS), jnp.float32),
            VMEM((8, NS), jnp.float32),
            VMEM((NZ, 8, NS), jnp.float32),
            dma((LOCAL,)),
            dma((LOCAL,)),
            dma,
            dma((NSAMP,)),
            dma((NSAMP,)),
            dma((NSAMP,)),
            dma((NSAMP,)),
            dma((2,)),
            dma((CHIPS,)),
            dma((CHIPS,)),
            dma((NZ,)),
            dma((NZ,)),
            dma((CHIPS,)),
            dma((CHIPS,)),
            dma((CHIPS,)),
            dma((CHIPS,)),
        ],
        compiler_params=pltpu.CompilerParams(
            collective_id=0, has_side_effects=True, vmem_limit_bytes=VMEM_LIMIT
        ),
    )(activations, cotangents, spin_bits, off_row)


BLOCK = 64
PANEL = 8


def spread(value, row, col):
    return jnp.broadcast_to(value[row : row + 1, col : col + 1], (8, 128))


def invert_block(diag):
    eye = lax.broadcasted_iota(jnp.int32, (BLOCK, BLOCK), 0) == lax.broadcasted_iota(
        jnp.int32, (BLOCK, BLOCK), 1
    )
    wide = jnp.concatenate([diag, jnp.where(eye, 1.0, 0.0)], axis=1)
    tiles = [wide[8 * q : 8 * q + 8] for q in range(BLOCK // 8)]
    sub = lax.broadcasted_iota(jnp.int32, (8, 128), 0)
    for panel in range(BLOCK // PANEL):
        tile = tiles[panel]
        base = panel * PANEL
        low = {
            (i, j): spread(tile, i, base + j) for i in range(PANEL) for j in range(i + 1)
        }
        rows = [jnp.broadcast_to(tile[i : i + 1], (8, 128)) for i in range(PANEL)]
        factor = {}
        inverse = []
        for j in range(PANEL):
            recip = 1.0 / low[j, j]
            inverse.append(recip)
            for i in range(j + 1, PANEL):
                factor[i, j] = low[i, j] * recip
            for i in range(j + 1, PANEL):
                rows[i] = rows[i] - factor[i, j] * rows[j]
                for m in range(j + 1, i + 1):
                    low[i, m] = low[i, m] - factor[i, j] * low[m, j]
        solved = [None] * PANEL
        for i in reversed(range(PANEL)):
            total = rows[i] * inverse[i]
            for j in range(i + 1, PANEL):
                total = total - factor[j, i] * solved[j]
            solved[i] = total
        for q in range(BLOCK // 8):
            if q == panel:
                continue
            old = tiles[q]
            terms = [
                jnp.broadcast_to(old[:, base + i : base + i + 1], (8, 128)) * solved[i]
                for i in range(PANEL)
            ]
            while len(terms) > 1:
                terms = [terms[a] + terms[a + 1] for a in range(0, len(terms), 2)]
            tiles[q] = old - terms[0]
        joined = solved[0]
        for i in range(1, PANEL):
            joined = jnp.where(sub == i, solved[i], joined)
        tiles[panel] = joined
    return jnp.concatenate(tiles, axis=0)[:, BLOCK:]


def solve_kernel(gram_ref, energies_ref, cent_ref, update_ref, coeff_ref, work, held):
    rows_iota = lax.broadcasted_iota(jnp.int32, (NS, NS), 0)
    cols_iota = lax.broadcasted_iota(jnp.int32, (NS, NS), 1)
    gram = gram_ref[...]
    diagonal = rows_iota == cols_iota
    trace = jnp.sum(jnp.where(diagonal, gram, 0.0), keepdims=True)
    shift = 0.01 * trace / NS
    pieces = jnp.broadcast_to(energies_ref[...], (NSAMP, LOCAL, 128)).reshape(NS, 128)
    lane = lax.broadcasted_iota(jnp.int32, (NS, 128), 1)
    row = lax.broadcasted_iota(jnp.int32, (NS, 128), 0)
    energy = jnp.sum(jnp.where(lane == row % LOCAL, pieces, 0.0), axis=1, keepdims=True)
    mean = jnp.sum(energy, axis=0, keepdims=True) / NS
    residual = -(energy - mean) / math.sqrt(NS)
    work[:, :NS] = gram + jnp.where(diagonal, shift, 0.0)
    work[:, NS:] = jnp.broadcast_to(residual, (NS, 128))

    def step(index, carry):
        own = pl.ds(pl.multiple_of(index * BLOCK, BLOCK), BLOCK)
        panel = work[own, :]
        inverse = invert_block(panel[:, :BLOCK])
        solved = jnp.dot(inverse, panel, precision=HIGHEST, preferred_element_type=jnp.float32)
        held[...] = work[...] - jnp.dot(
            work[:, :BLOCK], solved, precision=HIGHEST, preferred_element_type=jnp.float32
        )
        held[own, :] = solved
        work[:, : NS - BLOCK] = held[:, BLOCK:NS]
        work[:, NS - BLOCK : NS] = held[:, :BLOCK]
        work[:, NS:] = held[:, NS:]
        return carry

    lax.fori_loop(0, NS // BLOCK, step, 0)
    coeff = work[:, NS:]
    held[:, NS:] = coeff
    coeff_ref[...] = held[pl.ds(pl.multiple_of(lax.axis_index("samp") * LOCAL, LOCAL), LOCAL), NS:]
    image = jnp.zeros((8, 128), jnp.float32)
    both = jnp.concatenate([coeff, coeff], axis=1)
    weighted = jnp.sum(gram * both, axis=0, keepdims=True)
    across = jnp.sum(jnp.where(diagonal, both, 0.0), axis=0, keepdims=True)
    square_total = jnp.sum(weighted * across, keepdims=True)
    scale = lax.rsqrt(square_total / ENTRIES + 1e-06)
    first = lax.broadcasted_iota(jnp.int32, (1, 128), 1) < CH
    for pair in range(ROWS // 2):
        parts = []
        for half in range(2):
            column = 128 * (2 * pair + half)
            cent = cent_ref[:, column : column + 128].astype(jnp.float32)
            parts.append(jnp.sum(cent * coeff, axis=0, keepdims=True) * scale)
        turned = [jnp.concatenate([item[:, CH:], item[:, :CH]], axis=1) for item in parts]
        update_ref[0:1, 128 * pair : 128 * pair + 128] = jnp.where(first, parts[0], turned[1])
        update_ref[1:2, 128 * pair : 128 * pair + 128] = jnp.where(first, turned[0], parts[1])


def solve_call(gram, energies, cent):
    whole = pl.BlockSpec(memory_space=VMEM)
    return pl.pallas_call(
        solve_kernel,
        in_specs=[whole] * 3,
        out_specs=[whole, whole],
        out_shape=[
            jax.ShapeDtypeStruct((LAYERS, ROWS * CH), jnp.float32),
            jax.ShapeDtypeStruct((LOCAL, 128), jnp.float32),
        ],
        scratch_shapes=[VMEM((NS, NS + 128), jnp.float32), VMEM((NS, NS + 128), jnp.float32)],
        compiler_params=pltpu.CompilerParams(vmem_limit_bytes=VMEM_LIMIT),
    )(gram, energies, cent)


def on_device(activations, cotangents, spin_bits, offdiag_energy):
    gram, cent, energies = main_call(
        activations, cotangents, spin_bits, offdiag_energy.reshape(1, LOCAL)
    )
    update, coeff = solve_call(gram, energies, cent)
    return update, coeff[:, 0]


def solution(mesh):
    in_specs = (
        P("samp", "par", None, None),
        P("samp", "par", None, None),
        P("samp", None),
        P("samp"),
    )
    out_specs = (P("par", "samp"), P("samp"))
    return jax.shard_map(
        on_device, mesh=mesh, in_specs=in_specs, out_specs=out_specs, check_vma=False
    )
```

```python
import math

import jax
import jax.numpy as jnp
from jax import lax
from jax.experimental import pallas as pl
from jax.experimental.pallas import tpu as pltpu
from jax.sharding import PartitionSpec as P

CH = 64
KK = 9
LAT = 24
SITES = LAT * LAT
NSAMP = 32
NPAR = 8
NZ = 8
NY = 4
LOCAL = 8
NS = NSAMP * LOCAL
ROWS = KK * CH // NSAMP
CHUNK = ROWS * LOCAL
WIDTH = ROWS * 128
PADK = 640
LAYERS = 2
ENTRIES = 16 * KK * CH * CH
MESH = pl.DeviceIdType.MESH
VMEM_LIMIT = 56 * 1024 * 1024
HIGHEST = lax.Precision.HIGHEST
VMEM = pltpu.VMEM


def rolled(value, amount):
    amount = amount % SITES
    if amount == 0:
        return value
    return jnp.concatenate([value[:, amount:], value[:, :amount]], axis=1)


def column_shift(value, col_step):
    if col_step == 0:
        return value
    column = lax.broadcasted_iota(jnp.int32, value.shape, 1) % LAT
    edge = LAT - 1 if col_step > 0 else 0
    return jnp.where(column == edge, rolled(value, col_step - LAT * col_step), rolled(value, col_step))


def wrap(value, size):
    return lax.select(value >= size, value - size, value)


STEPS = [(down, hop) for down in range(NY) for hop in (1, 7, 2, 6, 3, 5, 4, 0) if (down, hop) != (0, 0)]


def diagonal_energy(spin_bits):
    spin = (2 * spin_bits - 1).astype(jnp.float32)
    right = column_shift(spin, 1)
    left = column_shift(spin, -1)
    pairs = spin * rolled(spin, LAT) + spin * right
    corners = spin * rolled(right, LAT) + spin * rolled(left, LAT)
    diag = 0.25 * jnp.sum(pairs + 0.5 * corners, axis=1, keepdims=True)
    wide = jnp.broadcast_to(diag, (LOCAL, 128))
    here = lax.broadcasted_iota(jnp.int32, (LOCAL, 128), 0) == lax.broadcasted_iota(
        jnp.int32, (LOCAL, 128), 1
    )
    return jnp.sum(jnp.where(here, wide, 0.0), axis=0, keepdims=True)


WAVES = 4
PER_WAVE = LOCAL // WAVES
CHIPS = 16
TAIL = 48


def main_kernel(
    act_hbm, cot_hbm, spin_ref, off_ref,
    gram_ref, cent_hbm, energies_ref,
    act_ref, cot_ref, lhs, rhs, wide_rows, send_ref, recv_ref, wide_recv, cent_ref,
    energy_ref, half_ref, first, mine, second,
    act_sem, cot_sem, cent_sem, send_sem, recv_sem, esem, core_sem, sem1, sem2, sem3, sem4,
):
    samp = lax.axis_index("samp")
    par = lax.axis_index("par")
    z, y = samp // NY, samp % NY
    x, core = par // 2, par % 2
    chip = y * 4 + x
    slot_here = y * NZ + z
    sibling = (samp, x * 2 + 1 - core)
    zs = [wrap(z + hop, NZ) for hop in range(NZ)]
    ys = [wrap(y + down, NY) for down in range(NY)]
    xs = [wrap(x + across, 4) for across in range(4)]
    partners = [(down, zs[hop] * NY + ys[down]) for down, hop in STEPS]
    chips = [
        (ys[down] * 4 + xs[across], (z * NY + ys[down], xs[across] * 2 + core))
        for down in range(NY)
        for across in range(4)
        if (down, across) != (0, 0)
    ]

    def act_copy(n):
        return pltpu.make_async_copy(act_hbm.at[n], act_ref.at[n], act_sem.at[n])

    def cot_copy(n):
        return pltpu.make_async_copy(cot_hbm.at[n], cot_ref.at[n], cot_sem.at[n])

    for n in range(LOCAL):
        act_copy(n).start()
        cot_copy(n).start()

    def remote(source, target, send, recv, device):
        return pltpu.make_async_remote_copy(
            src_ref=source,
            dst_ref=target,
            send_sem=send,
            recv_sem=recv,
            device_id=device,
            device_id_type=MESH,
        )

    barrier = pltpu.get_barrier_semaphore()
    greeted = 0
    for _, other in partners:
        pl.semaphore_signal(barrier, inc=1, device_id=(other, par), device_id_type=MESH)
        greeted += 1
    for down in range(NY):
        for across in range(1, 4):
            device = (z * NY + ys[down], xs[across] * 2 + core)
            pl.semaphore_signal(barrier, inc=1, device_id=device, device_id_type=MESH)
            greeted += 1
    pl.semaphore_signal(barrier, inc=1, device_id=sibling, device_id_type=MESH)
    greeted += 1

    rhs[...] = jnp.zeros_like(rhs)
    for layer in range(LAYERS):
        edge = layer * PADK + SITES - CH
        lhs[:, :, edge : edge + 128] = jnp.zeros((PER_WAVE, KK * CH, 128), jnp.bfloat16)

    def compute(wave):
        for slot in range(PER_WAVE):
            sample = wave * PER_WAVE + slot
            act_copy(sample).wait()
            cot_copy(sample).wait()
            for layer in range(LAYERS):
                base = layer * PADK
                act = act_ref[sample, layer]
                rhs[slot, layer * CH : (layer + 1) * CH, base : base + SITES] = cot_ref[sample, layer]
                for col_step in (-1, 0, 1):
                    moved = column_shift(act, col_step)
                    for row_step in (-1, 0, 1):
                        tap = 3 * (row_step + 1) + col_step + 1
                        lhs[slot, tap * CH : (tap + 1) * CH, base : base + SITES] = rolled(
                            moved, LAT * row_step
                        )
            out = lax.dot_general(
                lhs[slot], rhs[slot], (((1,), (1,)), ((), ())), preferred_element_type=jnp.float32
            )
            for dest in range(NSAMP):
                wide_rows[dest, pl.ds(sample * ROWS, ROWS), :] = out[dest * ROWS : (dest + 1) * ROWS]

    def send_wave(low, rows):
        for down, other in partners:
            send_ref[other, pl.ds(low, rows), :] = wide_rows[other, pl.ds(low, rows), :].astype(
                jnp.bfloat16
            )
            remote(
                send_ref.at[other, pl.ds(low, rows)],
                recv_ref.at[slot_here, pl.ds(low, rows)],
                send_sem,
                recv_sem.at[down],
                (other, par),
            ).start()

    compute(0)
    pl.semaphore_wait(barrier, greeted)
    send_wave(0, 32)

    def later(wave, carry):
        compute(wave)

        @pl.when(wave < WAVES - 1)
        def _():
            send_wave(pl.multiple_of(wave * 32, 32), 32)

        @pl.when(wave == WAVES - 1)
        def _():
            send_wave(96, TAIL)

        return carry

    lax.fori_loop(1, WAVES, later, 0)

    flat = diagonal_energy(spin_ref[...])
    energy_ref[...] = jnp.zeros_like(energy_ref)
    energy_ref[:, :LOCAL] = flat[:, :LOCAL] + off_ref[...]
    for _, other in partners:
        remote(energy_ref, energies_ref.at[samp], esem.at[0], esem.at[1], (other, par)).start()
    energies_ref[samp] = energy_ref[...]
    recv_ref[slot_here] = wide_rows[samp].astype(jnp.bfloat16)

    group = NZ * CHUNK
    for down in range(NY):
        low = wrap(y + NY - down, NY) * NZ
        taken = recv_ref.at[pl.ds(0, NZ - 1)] if down == 0 else recv_ref.at[pl.ds(low, NZ)]
        remote(taken, taken, send_sem, recv_sem.at[down], sibling).wait_recv()
        start = pl.multiple_of(low * CHUNK, group)
        wide_recv[pl.ds(start, group), :] = (
            recv_ref[pl.ds(low, NZ)].astype(jnp.float32).reshape(group, 128)
        )

    def centre(row, carry):
        part = jnp.stack(
            [
                wide_recv[pl.ds(((src % NY) * NZ + src // NY) * CHUNK + row, LOCAL, stride=ROWS), :]
                for src in range(NSAMP)
            ]
        )
        mean = jnp.sum(jnp.sum(part, axis=0), axis=0, keepdims=True) / NS
        cent = ((part - mean) / math.sqrt(NS)).reshape(NS, 128)
        cent_ref[:, pl.ds(pl.multiple_of(row * 128, 128), 128)] = cent.astype(jnp.bfloat16)
        return carry

    lax.fori_loop(0, ROWS, centre, 0)
    cent_copy = pltpu.make_async_copy(cent_ref, cent_hbm, cent_sem)
    cent_copy.start()

    def gram_rows(low):
        return lax.dot_general(
            cent_ref[pl.ds(low, 128), :], cent_ref[...], (((1,), (1,)), ((), ())),
            preferred_element_type=jnp.float32,
        )

    low_here = pl.multiple_of(core * 128, 128)
    core_copy = remote(half_ref.at[0], half_ref.at[1], core_sem.at[0], core_sem.at[1], sibling)
    half_ref[0] = gram_rows(pl.multiple_of((1 - core) * 128, 128))
    core_copy.start()
    half_ref[2] = gram_rows(low_here)
    core_copy.wait_recv()
    half_ref[2] = half_ref[2] + half_ref[1]

    def rows_of(index):
        return pl.ds(pl.multiple_of(index * 8, 8), 8)

    for other, device in chips:
        remote(
            half_ref.at[2, rows_of(other)], first.at[chip], sem1.at[0], sem1.at[1], device
        ).start()
    first[chip] = half_ref[2, rows_of(chip), :]
    chip_bytes = first.at[pl.ds(0, CHIPS - 1)]
    remote(chip_bytes, chip_bytes, sem1.at[0], sem1.at[1], sibling).wait_recv()
    own = jnp.sum(first[...], axis=0)
    mine[...] = own
    for hop in (1, 7, 2, 6, 3, 5, 4):
        device = (zs[hop] * NY + y, par)
        remote(mine, second.at[z], sem2.at[0], sem2.at[1], device).start()
    second[z] = own
    column_bytes = second.at[pl.ds(0, NZ - 1)]
    remote(column_bytes, column_bytes, sem2.at[0], sem2.at[1], sibling).wait_recv()
    block = pl.ds(pl.multiple_of(low_here + chip * 8, 8), 8)
    gram_ref[block, :] = jnp.sum(second[...], axis=0)
    for _, device in chips:
        remote(gram_ref.at[block], gram_ref.at[block], sem3.at[0], sem3.at[1], device).start()
    gram_bytes = gram_ref.at[pl.ds(low_here, (CHIPS - 1) * 8)]
    remote(gram_bytes, gram_bytes, sem3.at[0], sem3.at[1], sibling).wait_recv()
    half_here = gram_ref.at[pl.ds(low_here, 128)]
    core_back = remote(half_here, half_here, sem4.at[0], sem4.at[1], sibling)
    core_back.start()

    sent = send_ref.at[pl.ds(0, NSAMP - 1)]
    remote(sent, sent, send_sem, recv_sem.at[0], sibling).wait_send()
    energy_bytes = energies_ref.at[pl.ds(0, NSAMP - 1)]
    remote(energy_bytes, energy_bytes, esem.at[0], esem.at[1], sibling).wait()
    core_copy.wait_send()
    remote(chip_bytes, chip_bytes, sem1.at[0], sem1.at[1], sibling).wait_send()
    remote(column_bytes, column_bytes, sem2.at[0], sem2.at[1], sibling).wait_send()
    remote(gram_bytes, gram_bytes, sem3.at[0], sem3.at[1], sibling).wait_send()
    core_back.wait()
    cent_copy.wait()


def main_call(activations, cotangents, spin_bits, off_row):
    whole = pl.BlockSpec(memory_space=VMEM)
    anywhere = pl.BlockSpec(memory_space=pl.ANY)
    dma = pltpu.SemaphoreType.DMA
    return pl.pallas_call(
        main_kernel,
        in_specs=[anywhere, anywhere, whole, whole],
        out_specs=[whole, anywhere, whole],
        out_shape=[
            jax.ShapeDtypeStruct((NS, NS), jnp.float32),
            jax.ShapeDtypeStruct((NS, WIDTH), jnp.bfloat16),
            jax.ShapeDtypeStruct((NSAMP, 1, 128), jnp.float32),
        ],
        scratch_shapes=[
            VMEM((LOCAL, LAYERS, CH, SITES), jnp.bfloat16),
            VMEM((LOCAL, LAYERS, CH, SITES), jnp.bfloat16),
            VMEM((PER_WAVE, KK * CH, LAYERS * PADK), jnp.bfloat16),
            VMEM((PER_WAVE, LAYERS * CH, LAYERS * PADK), jnp.bfloat16),
            VMEM((NSAMP, CHUNK, 128), jnp.float32),
            VMEM((NSAMP, CHUNK, 128), jnp.bfloat16),
            VMEM((NSAMP, CHUNK, 128), jnp.bfloat16),
            VMEM((NSAMP * CHUNK, 128), jnp.float32),
            VMEM((NS, WIDTH), jnp.bfloat16),
            VMEM((1, 128), jnp.float32),
            VMEM((3, 128, NS), jnp.float32),
            VMEM((CHIPS, 8, NS), jnp.float32),
            VMEM((8, NS), jnp.float32),
            VMEM((NZ, 8, NS), jnp.float32),
            dma((LOCAL,)),
            dma((LOCAL,)),
            dma,
            dma,
            dma((NY,)),
            dma((2,)),
            dma((2,)),
            dma((2,)),
            dma((2,)),
            dma((2,)),
            dma((2,)),
        ],
        compiler_params=pltpu.CompilerParams(
            collective_id=0, has_side_effects=True, vmem_limit_bytes=VMEM_LIMIT
        ),
    )(activations, cotangents, spin_bits, off_row)


BLOCK = 64
PANEL = 8


def reciprocal(value):
    guess = pl.reciprocal(value, approx=True)
    guess = guess * (2.0 - value * guess)
    return guess * (2.0 - value * guess)


def invert_block(diag):
    eye = lax.broadcasted_iota(jnp.int32, (BLOCK, BLOCK), 0) == lax.broadcasted_iota(
        jnp.int32, (BLOCK, BLOCK), 1
    )
    wide = jnp.concatenate([diag, jnp.where(eye, 1.0, 0.0)], axis=1)
    tiles = [wide[8 * q : 8 * q + 8] for q in range(BLOCK // 8)]
    sub = lax.broadcasted_iota(jnp.int32, (8, 128), 0)

    def lanes(tile, col):
        return jnp.broadcast_to(tile[:, col : col + 1], (8, 128))

    for panel in range(BLOCK // PANEL):
        tile = tiles[panel]
        base = panel * PANEL
        columns = [lanes(tile, base + j) for j in range(PANEL)]
        low = {
            (i, j): jnp.broadcast_to(columns[j][i : i + 1], (8, 128))
            for i in range(PANEL)
            for j in range(i + 1)
        }
        rows = [jnp.broadcast_to(tile[i : i + 1], (8, 128)) for i in range(PANEL)]
        ups, downs, starts = {}, {}, {}
        for p in range(0, PANEL, 2):
            q = p + 1
            a, b, c = low[p, p], low[q, p], low[q, q]
            recip = reciprocal(a * c - b * b)
            starts[p] = (c * rows[p] - b * rows[q]) * recip
            starts[q] = (a * rows[q] - b * rows[p]) * recip
            for i in range(q + 1, PANEL):
                up = c * low[i, p] - b * low[i, q]
                down = a * low[i, q] - b * low[i, p]
                for m in range(q + 1, i + 1):
                    low[i, m] = low[i, m] - (up * low[m, p] + down * low[m, q]) * recip
                ups[i, p], downs[i, p] = up * recip, down * recip
                rows[i] = rows[i] - (ups[i, p] * rows[p] + downs[i, p] * rows[q])
        solved = [None] * PANEL
        for p in reversed(range(0, PANEL, 2)):
            for total, factor, at in ((starts[p], ups, p), (starts[p + 1], downs, p + 1)):
                for i in reversed(range(p + 2, PANEL)):
                    total = total - factor[i, p] * solved[i]
                solved[at] = total
        for q in range(BLOCK // 8):
            if q == panel:
                continue
            old = tiles[q]
            terms = [lanes(old, base + i) * solved[i] for i in range(PANEL)]
            while len(terms) > 1:
                terms = [terms[a] + terms[a + 1] for a in range(0, len(terms), 2)]
            tiles[q] = old - terms[0]
        joined = solved[0]
        for i in range(1, PANEL):
            joined = jnp.where(sub == i, solved[i], joined)
        tiles[panel] = joined
    return jnp.concatenate(tiles, axis=0)[:, BLOCK:]


def solve_kernel(gram_ref, energies_ref, cent_hbm, update_ref, coeff_ref, work, held, cent_ref, cent_sem):
    cent_copy = pltpu.make_async_copy(cent_hbm, cent_ref, cent_sem)
    cent_copy.start()
    rows_iota = lax.broadcasted_iota(jnp.int32, (NS, NS), 0)
    cols_iota = lax.broadcasted_iota(jnp.int32, (NS, NS), 1)
    gram = gram_ref[...]
    diagonal = rows_iota == cols_iota
    trace = jnp.sum(jnp.where(diagonal, gram, 0.0), keepdims=True)
    level = 1.0 / (trace / NS)
    pieces = jnp.broadcast_to(energies_ref[...], (NSAMP, LOCAL, 128)).reshape(NS, 128)
    lane = lax.broadcasted_iota(jnp.int32, (NS, 128), 1)
    row = lax.broadcasted_iota(jnp.int32, (NS, 128), 0)
    energy = jnp.sum(jnp.where(lane == row % LOCAL, pieces, 0.0), axis=1, keepdims=True)
    mean = jnp.sum(energy, axis=0, keepdims=True) / NS
    residual = -(energy - mean) / math.sqrt(NS)
    work[:, :NS] = gram * level + jnp.where(diagonal, 0.01, 0.0)
    work[:, NS:] = jnp.broadcast_to(residual, (NS, 128))

    def step(index, carry):
        own = pl.ds(pl.multiple_of(index * BLOCK, BLOCK), BLOCK)
        panel = work[own, :]
        inverse = invert_block(panel[:, :BLOCK])
        solved = jnp.dot(inverse, panel, precision=HIGHEST, preferred_element_type=jnp.float32)
        held[...] = work[...] - jnp.dot(
            work[:, :BLOCK], solved, precision=HIGHEST, preferred_element_type=jnp.float32
        )
        held[own, :] = solved
        work[:, : NS - BLOCK] = held[:, BLOCK:NS]
        work[:, NS - BLOCK : NS] = held[:, :BLOCK]
        work[:, NS:] = held[:, NS:]
        return carry

    lax.fori_loop(0, NS // BLOCK, step, 0)
    coeff = work[:, NS:] * level
    held[:, NS:] = coeff
    own = held[pl.ds(pl.multiple_of(lax.axis_index("samp") * LOCAL, LOCAL), LOCAL), NS:]
    here = lax.broadcasted_iota(jnp.int32, (LOCAL, 128), 0) == lax.broadcasted_iota(
        jnp.int32, (LOCAL, 128), 1
    )
    coeff_ref[...] = jnp.sum(jnp.where(here, own, 0.0), axis=0, keepdims=True)[:, :LOCAL]
    both = jnp.concatenate([coeff, coeff], axis=1)
    weighted = jnp.sum(gram * both, axis=0, keepdims=True)
    across = jnp.sum(jnp.where(diagonal, both, 0.0), axis=0, keepdims=True)
    square_total = jnp.sum(weighted * across, keepdims=True)
    scale = lax.rsqrt(square_total / ENTRIES + 1e-06)
    first = lax.broadcasted_iota(jnp.int32, (1, 128), 1) < CH
    cent_copy.wait()
    for pair in range(ROWS // 2):
        parts = []
        for half in range(2):
            column = 128 * (2 * pair + half)
            cent = cent_ref[:, column : column + 128].astype(jnp.float32)
            parts.append(jnp.sum(cent * coeff, axis=0, keepdims=True) * scale)
        turned = [jnp.concatenate([item[:, CH:], item[:, :CH]], axis=1) for item in parts]
        update_ref[0:1, 128 * pair : 128 * pair + 128] = jnp.where(first, parts[0], turned[1])
        update_ref[1:2, 128 * pair : 128 * pair + 128] = jnp.where(first, turned[0], parts[1])


def solve_call(gram, energies, cent):
    whole = pl.BlockSpec(memory_space=VMEM)
    return pl.pallas_call(
        solve_kernel,
        in_specs=[whole, whole, pl.BlockSpec(memory_space=pl.ANY)],
        out_specs=[whole, whole],
        out_shape=[
            jax.ShapeDtypeStruct((LAYERS, ROWS * CH), jnp.float32),
            jax.ShapeDtypeStruct((1, LOCAL), jnp.float32),
        ],
        scratch_shapes=[
            VMEM((NS, NS + 128), jnp.float32),
            VMEM((NS, NS + 128), jnp.float32),
            VMEM((NS, WIDTH), jnp.bfloat16),
            pltpu.SemaphoreType.DMA,
        ],
        compiler_params=pltpu.CompilerParams(vmem_limit_bytes=VMEM_LIMIT),
    )(gram, energies, cent)


def on_device(activations, cotangents, spin_bits, offdiag_energy):
    gram, cent, energies = main_call(
        activations, cotangents, spin_bits, offdiag_energy.reshape(1, LOCAL)
    )
    update, coeff = solve_call(gram, energies, cent)
    return update, coeff.reshape(LOCAL)


def solution(mesh):
    in_specs = (
        P("samp", "par", None, None),
        P("samp", "par", None, None),
        P("samp", None),
        P("samp"),
    )
    out_specs = (P("par", "samp"), P("samp"))
    return jax.shard_map(
        on_device, mesh=mesh, in_specs=in_specs, out_specs=out_specs, check_vma=False
    )
```

```python
import math

import jax
import jax.numpy as jnp
from jax import lax
from jax.experimental import pallas as pl
from jax.experimental.pallas import tpu as pltpu
from jax.sharding import PartitionSpec as P

CH = 64
KK = 9
LAT = 24
SITES = LAT * LAT
NSAMP = 32
NPAR = 8
NZ = 8
NY = 4
LOCAL = 8
NS = NSAMP * LOCAL
ROWS = KK * CH // NSAMP
CHUNK = ROWS * LOCAL
WIDTH = ROWS * 128
PADK = 640
LAYERS = 2
ENTRIES = 16 * KK * CH * CH
MESH = pl.DeviceIdType.MESH
VMEM_LIMIT = 56 * 1024 * 1024
HIGHEST = lax.Precision.HIGHEST
VMEM = pltpu.VMEM


def rolled(value, amount):
    amount = amount % SITES
    if amount == 0:
        return value
    return jnp.concatenate([value[:, amount:], value[:, :amount]], axis=1)


def column_shift(value, col_step):
    if col_step == 0:
        return value
    column = lax.broadcasted_iota(jnp.int32, value.shape, 1) % LAT
    edge = LAT - 1 if col_step > 0 else 0
    return jnp.where(column == edge, rolled(value, col_step - LAT * col_step), rolled(value, col_step))


def wrap(value, size):
    return lax.select(value >= size, value - size, value)


STEPS = [(down, hop) for down in range(NY) for hop in (1, 7, 2, 6, 3, 5, 4, 0) if (down, hop) != (0, 0)]


def diagonal_energy(spin_bits):
    spin = (2 * spin_bits - 1).astype(jnp.float32)
    right = column_shift(spin, 1)
    left = column_shift(spin, -1)
    pairs = spin * rolled(spin, LAT) + spin * right
    corners = spin * rolled(right, LAT) + spin * rolled(left, LAT)
    diag = 0.25 * jnp.sum(pairs + 0.5 * corners, axis=1, keepdims=True)
    wide = jnp.broadcast_to(diag, (LOCAL, 128))
    here = lax.broadcasted_iota(jnp.int32, (LOCAL, 128), 0) == lax.broadcasted_iota(
        jnp.int32, (LOCAL, 128), 1
    )
    return jnp.sum(jnp.where(here, wide, 0.0), axis=0, keepdims=True)


WAVES = ((0, 0, 16), (2, 16, 32), (4, 48, 32), (7, 80, 64))
MEMBERS = 32


def main_kernel(
    act_hbm, cot_hbm, spin_ref, off_ref,
    gram_ref, cent_hbm, energies_ref,
    act_ref, cot_ref, lhs, rhs, wide_rows, send_ref, recv_ref, wide_recv, cent_ref,
    energy_ref, relay_ref, part_ref, first, mine, second,
    act_sem, cot_sem, cent_sem, send_sem, recv_sem, esem, relay_sem, sem1, sem2, sem3,
):
    samp = lax.axis_index("samp")
    par = lax.axis_index("par")
    z, y = samp // NY, samp % NY
    x, core = par // 2, par % 2
    slot_here = y * NZ + z
    sibling = (samp, x * 2 + 1 - core)
    zs = [wrap(z + hop, NZ) for hop in range(NZ)]
    ys = [wrap(y + down, NY) for down in range(NY)]
    xs = [wrap(x + across, 4) for across in range(4)]
    partners = [(down, zs[hop] * NY + ys[down]) for down, hop in STEPS]
    far = {(down, hop): other for (down, other), (_, hop) in zip(partners, STEPS) if hop == 4}
    sorted_partners = [
        item for item, (_, hop) in sorted(zip(partners, STEPS), key=lambda pair: pair[1][1] != 4)
    ]
    block_here = y * NPAR + par
    members = [
        (ys[down] * NPAR + xs[across] * 2 + side, (z * NY + ys[down], xs[across] * 2 + side))
        for down in range(NY)
        for across in range(4)
        for side in (core, 1 - core)
    ][1:]

    def act_copy(n):
        return pltpu.make_async_copy(act_hbm.at[n], act_ref.at[n], act_sem.at[n])

    def cot_copy(n):
        return pltpu.make_async_copy(cot_hbm.at[n], cot_ref.at[n], cot_sem.at[n])

    for n in range(LOCAL):
        act_copy(n).start()
        cot_copy(n).start()

    def remote(source, target, send, recv, device):
        return pltpu.make_async_remote_copy(
            src_ref=source,
            dst_ref=target,
            send_sem=send,
            recv_sem=recv,
            device_id=device,
            device_id_type=MESH,
        )

    barrier = pltpu.get_barrier_semaphore()
    greeted = 0
    for _, other in partners:
        pl.semaphore_signal(barrier, inc=1, device_id=(other, par), device_id_type=MESH)
        greeted += 1
    for number, (_, device) in enumerate(members, 1):
        if number % 8:
            pl.semaphore_signal(barrier, inc=1, device_id=device, device_id_type=MESH)
            greeted += 1

    rhs[...] = jnp.zeros_like(rhs)
    for layer in range(LAYERS):
        edge = layer * PADK + SITES - CH
        lhs[:, :, edge : edge + 128] = jnp.zeros((2, KK * CH, 128), jnp.bfloat16)

    def compute(sample):
        slot = sample % 2
        act_copy(sample).wait()
        cot_copy(sample).wait()
        for layer in range(LAYERS):
            base = layer * PADK
            act = act_ref[sample, layer]
            rhs[slot, layer * CH : (layer + 1) * CH, base : base + SITES] = cot_ref[sample, layer]
            for col_step in (-1, 0, 1):
                moved = column_shift(act, col_step)
                for row_step in (-1, 0, 1):
                    tap = 3 * (row_step + 1) + col_step + 1
                    lhs[slot, tap * CH : (tap + 1) * CH, base : base + SITES] = rolled(
                        moved, LAT * row_step
                    )
        out = lax.dot_general(
            lhs[slot], rhs[slot], (((1,), (1,)), ((), ())), preferred_element_type=jnp.float32
        )
        for dest in range(NSAMP):
            wide_rows[dest, pl.ds(sample * ROWS, ROWS), :] = out[dest * ROWS : (dest + 1) * ROWS]

    def send_wave(low, rows, wave):
        for down, other in sorted_partners:
            send_ref[other, pl.ds(low, rows), :] = wide_rows[other, pl.ds(low, rows), :].astype(
                jnp.bfloat16
            )
            source = send_ref.at[other, pl.ds(low, rows)]
            if (down, 4) in far and far[down, 4] is other:
                via = zs[2] if down < 2 else zs[6]
                remote(
                    source,
                    relay_ref.at[down, pl.ds(low, rows)],
                    send_sem,
                    relay_sem.at[wave],
                    (via * NY + y, par),
                ).start()
            else:
                remote(
                    source,
                    recv_ref.at[slot_here, pl.ds(low, rows)],
                    send_sem,
                    recv_sem.at[down],
                    (other, par),
                ).start()

    def pass_on(low, rows, wave):
        landed = relay_ref.at[:, pl.ds(low, rows)]
        remote(landed, landed, send_sem, relay_sem.at[wave], sibling).wait_recv()
        for down in range(NY):
            origin, goal = (zs[6], zs[2]) if down < 2 else (zs[2], zs[6])
            remote(
                relay_ref.at[down, pl.ds(low, rows)],
                recv_ref.at[y * NZ + origin, pl.ds(low, rows)],
                send_sem,
                recv_sem.at[down],
                (goal * NY + ys[down], par),
            ).start()

    pl.semaphore_wait(barrier, greeted)

    def one_sample(sample, carry):
        compute(sample)
        for wave, (last, low, rows) in enumerate(WAVES):

            @pl.when(sample == last)
            def _(wave=wave, low=low, rows=rows):
                if wave > 0:
                    pass_on(*WAVES[wave - 1][1:], wave - 1)
                send_wave(low, rows, wave)

        return carry

    lax.fori_loop(0, LOCAL, one_sample, 0)

    flat = diagonal_energy(spin_ref[...])
    energy_ref[...] = jnp.zeros_like(energy_ref)
    energy_ref[:, :LOCAL] = flat[:, :LOCAL] + off_ref[...]
    for _, other in partners:
        remote(energy_ref, energies_ref.at[samp], esem.at[0], esem.at[1], (other, par)).start()
    energies_ref[samp] = energy_ref[...]
    recv_ref[slot_here] = wide_rows[samp].astype(jnp.bfloat16)
    pass_on(*WAVES[-1][1:], len(WAVES) - 1)

    group = NZ * CHUNK
    for down in range(NY):
        low = wrap(y + NY - down, NY) * NZ
        taken = recv_ref.at[pl.ds(0, NZ - 1)] if down == 0 else recv_ref.at[pl.ds(low, NZ)]
        remote(taken, taken, send_sem, recv_sem.at[down], sibling).wait_recv()
        start = pl.multiple_of(low * CHUNK, group)
        wide_recv[pl.ds(start, group), :] = (
            recv_ref[pl.ds(low, NZ)].astype(jnp.float32).reshape(group, 128)
        )

    def centre(row, carry):
        part = jnp.stack(
            [
                wide_recv[pl.ds(((src % NY) * NZ + src // NY) * CHUNK + row, LOCAL, stride=ROWS), :]
                for src in range(NSAMP)
            ]
        )
        mean = jnp.sum(jnp.sum(part, axis=0), axis=0, keepdims=True) / NS
        cent = ((part - mean) / math.sqrt(NS)).reshape(NS, 128)
        cent_ref[:, pl.ds(pl.multiple_of(row * 128, 128), 128)] = cent.astype(jnp.bfloat16)
        return carry

    lax.fori_loop(0, ROWS, centre, 0)
    cent_copy = pltpu.make_async_copy(cent_ref, cent_hbm, cent_sem)
    cent_copy.start()

    part_ref[...] = lax.dot_general(
        cent_ref[...], cent_ref[...], (((1,), (1,)), ((), ())), preferred_element_type=jnp.float32
    )

    def rows_of(index):
        return pl.ds(pl.multiple_of(index * 8, 8), 8)

    for other, device in members:
        remote(
            part_ref.at[rows_of(other)], first.at[block_here], sem1.at[0], sem1.at[1], device
        ).start()
    first[block_here] = part_ref[rows_of(block_here), :]
    member_bytes = first.at[pl.ds(0, MEMBERS - 1)]
    remote(member_bytes, member_bytes, sem1.at[0], sem1.at[1], sibling).wait_recv()
    own = jnp.sum(first[...], axis=0)
    mine[...] = own
    for hop in (4, 3, 5, 2, 6, 1, 7):
        device = (zs[hop] * NY + y, par)
        remote(mine, second.at[z], sem2.at[0], sem2.at[1], device).start()
    second[z] = own
    column_bytes = second.at[pl.ds(0, NZ - 1)]
    remote(column_bytes, column_bytes, sem2.at[0], sem2.at[1], sibling).wait_recv()
    block = rows_of(block_here)
    gram_ref[block, :] = jnp.sum(second[...], axis=0)
    for _, device in members:
        remote(gram_ref.at[block], gram_ref.at[block], sem3.at[0], sem3.at[1], device).start()

    sent = send_ref.at[pl.ds(0, NSAMP - 1)]
    remote(sent, sent, send_sem, recv_sem.at[0], sibling).wait_send()
    remote(relay_ref, relay_ref, send_sem, recv_sem.at[0], sibling).wait_send()
    energy_bytes = energies_ref.at[pl.ds(0, NSAMP - 1)]
    remote(energy_bytes, energy_bytes, esem.at[0], esem.at[1], sibling).wait()
    remote(member_bytes, member_bytes, sem1.at[0], sem1.at[1], sibling).wait_send()
    remote(column_bytes, column_bytes, sem2.at[0], sem2.at[1], sibling).wait_send()
    cent_copy.wait()
    gram_bytes = gram_ref.at[pl.ds(0, (MEMBERS - 1) * 8)]
    remote(gram_bytes, gram_bytes, sem3.at[0], sem3.at[1], sibling).wait()


def main_call(activations, cotangents, spin_bits, off_row):
    whole = pl.BlockSpec(memory_space=VMEM)
    anywhere = pl.BlockSpec(memory_space=pl.ANY)
    dma = pltpu.SemaphoreType.DMA
    return pl.pallas_call(
        main_kernel,
        in_specs=[anywhere, anywhere, whole, whole],
        out_specs=[whole, anywhere, whole],
        out_shape=[
            jax.ShapeDtypeStruct((NS, NS), jnp.float32),
            jax.ShapeDtypeStruct((NS, WIDTH), jnp.bfloat16),
            jax.ShapeDtypeStruct((NSAMP, 1, 128), jnp.float32),
        ],
        scratch_shapes=[
            VMEM((LOCAL, LAYERS, CH, SITES), jnp.bfloat16),
            VMEM((LOCAL, LAYERS, CH, SITES), jnp.bfloat16),
            VMEM((2, KK * CH, LAYERS * PADK), jnp.bfloat16),
            VMEM((2, LAYERS * CH, LAYERS * PADK), jnp.bfloat16),
            VMEM((NSAMP, CHUNK, 128), jnp.float32),
            VMEM((NSAMP, CHUNK, 128), jnp.bfloat16),
            VMEM((NSAMP, CHUNK, 128), jnp.bfloat16),
            VMEM((NSAMP * CHUNK, 128), jnp.float32),
            VMEM((NS, WIDTH), jnp.bfloat16),
            VMEM((1, 128), jnp.float32),
            VMEM((NY, CHUNK, 128), jnp.bfloat16),
            VMEM((NS, NS), jnp.float32),
            VMEM((MEMBERS, 8, NS), jnp.float32),
            VMEM((8, NS), jnp.float32),
            VMEM((NZ, 8, NS), jnp.float32),
            dma((LOCAL,)),
            dma((LOCAL,)),
            dma,
            dma,
            dma((NY,)),
            dma((2,)),
            dma((len(WAVES),)),
            dma((2,)),
            dma((2,)),
            dma((2,)),
        ],
        compiler_params=pltpu.CompilerParams(
            collective_id=0, has_side_effects=True, vmem_limit_bytes=VMEM_LIMIT
        ),
    )(activations, cotangents, spin_bits, off_row)


BLOCK = 64
PANEL = 8


def reciprocal(value):
    guess = pl.reciprocal(value, approx=True)
    guess = guess * (2.0 - value * guess)
    return guess * (2.0 - value * guess)


def forward_block(diag, tile_ref, column_ref):
    eye = lax.broadcasted_iota(jnp.int32, (BLOCK, BLOCK), 0) == lax.broadcasted_iota(
        jnp.int32, (BLOCK, BLOCK), 1
    )
    wide = jnp.concatenate([diag, jnp.where(eye, 1.0, 0.0)], axis=1)
    count = BLOCK // PANEL
    tiles = [wide[8 * q : 8 * q + 8] for q in range(count)]
    sub = lax.broadcasted_iota(jnp.int32, (8, 128), 0)

    def lanes(tile, col):
        return jnp.broadcast_to(tile[:, col : col + 1], (8, 128))

    def joined(parts):
        total = parts[0]
        for i in range(1, PANEL):
            total = jnp.where(sub == i, parts[i], total)
        return total

    reduced, scaled = [], []
    for panel in range(count):
        tile = tiles[panel]
        base = panel * PANEL
        tile_ref[panel] = tile
        for j in range(PANEL):
            column_ref[panel, j] = lanes(tile, base + j)
        low = {
            (i, j): column_ref[panel, j, pl.ds(i, 8, stride=0), :]
            for i in range(PANEL)
            for j in range(i + 1)
        }
        rows = [tile_ref[panel, pl.ds(i, 8, stride=0), :] for i in range(PANEL)]
        ups, downs, starts = {}, {}, {}
        for p in range(0, PANEL, 2):
            q = p + 1
            a, b, c = low[p, p], low[q, p], low[q, q]
            recip = reciprocal(a * c - b * b)
            starts[p] = (c * rows[p] - b * rows[q]) * recip
            starts[q] = (a * rows[q] - b * rows[p]) * recip
            for i in range(q + 1, PANEL):
                up = c * low[i, p] - b * low[i, q]
                down = a * low[i, q] - b * low[i, p]
                for m in range(q + 1, i + 1):
                    low[i, m] = low[i, m] - (up * low[m, p] + down * low[m, q]) * recip
                ups[i, p], downs[i, p] = up * recip, down * recip
                rows[i] = rows[i] - (ups[i, p] * rows[p] + downs[i, p] * rows[q])
        reduced.append(joined(rows))
        scaled.append(joined([starts[i] for i in range(PANEL)]))
        if panel == count - 1:
            break
        solved = [None] * PANEL
        for p in reversed(range(0, PANEL, 2)):
            for total, factor, at in ((starts[p], ups, p), (starts[p + 1], downs, p + 1)):
                for i in reversed(range(p + 2, PANEL)):
                    total = total - factor[i, p] * solved[i]
                solved[at] = total
        for q in range(panel + 1, count):
            old = tiles[q]
            terms = [lanes(old, base + i) * solved[i] for i in range(PANEL)]
            while len(terms) > 1:
                terms = [terms[a] + terms[a + 1] for a in range(0, len(terms), 2)]
            tiles[q] = old - terms[0]
    lower = jnp.concatenate(reduced, axis=0)[:, BLOCK:]
    return lower, jnp.concatenate(scaled, axis=0)[:, BLOCK:]


def solve_kernel(
    gram_ref, energies_ref, cent_hbm, update_ref, coeff_ref,
    work, held, cent_ref, cent_sem, tile_ref, column_ref,
):
    cent_copy = pltpu.make_async_copy(cent_hbm, cent_ref, cent_sem)
    cent_copy.start()
    rows_iota = lax.broadcasted_iota(jnp.int32, (NS, NS), 0)
    cols_iota = lax.broadcasted_iota(jnp.int32, (NS, NS), 1)
    gram = gram_ref[...]
    diagonal = rows_iota == cols_iota
    trace = jnp.sum(jnp.where(diagonal, gram, 0.0), keepdims=True)
    level = 1.0 / (trace / NS)
    pieces = jnp.broadcast_to(energies_ref[...], (NSAMP, LOCAL, 128)).reshape(NS, 128)
    lane = lax.broadcasted_iota(jnp.int32, (NS, 128), 1)
    row = lax.broadcasted_iota(jnp.int32, (NS, 128), 0)
    energy = jnp.sum(jnp.where(lane == row % LOCAL, pieces, 0.0), axis=1, keepdims=True)
    mean = jnp.sum(energy, axis=0, keepdims=True) / NS
    residual = -(energy - mean) / math.sqrt(NS)
    work[:, :NS] = gram * level + jnp.where(diagonal, 0.01, 0.0)
    work[:, NS:] = jnp.broadcast_to(residual, (NS, 128))

    def step(index, carry):
        own = pl.ds(pl.multiple_of(index * BLOCK, BLOCK), BLOCK)
        panel = work[own, :]
        lower, scaled = forward_block(panel[:, :BLOCK], tile_ref, column_ref)
        inverse = lax.dot_general(
            lower, scaled, (((0,), (0,)), ((), ())), precision=HIGHEST, preferred_element_type=jnp.float32
        )
        solved = jnp.dot(inverse, panel, precision=HIGHEST, preferred_element_type=jnp.float32)
        held[...] = work[...] - jnp.dot(
            work[:, :BLOCK], solved, precision=HIGHEST, preferred_element_type=jnp.float32
        )
        held[own, :] = solved
        work[:, : NS - BLOCK] = held[:, BLOCK:NS]
        work[:, NS - BLOCK : NS] = held[:, :BLOCK]
        work[:, NS:] = held[:, NS:]
        return carry

    lax.fori_loop(0, NS // BLOCK, step, 0)
    coeff = work[:, NS:] * level
    held[:, NS:] = coeff
    own = held[pl.ds(pl.multiple_of(lax.axis_index("samp") * LOCAL, LOCAL), LOCAL), NS:]
    here = lax.broadcasted_iota(jnp.int32, (LOCAL, 128), 0) == lax.broadcasted_iota(
        jnp.int32, (LOCAL, 128), 1
    )
    coeff_ref[...] = jnp.sum(jnp.where(here, own, 0.0), axis=0, keepdims=True)[:, :LOCAL]
    both = jnp.concatenate([coeff, coeff], axis=1)
    weighted = jnp.sum(gram * both, axis=0, keepdims=True)
    across = jnp.sum(jnp.where(diagonal, both, 0.0), axis=0, keepdims=True)
    square_total = jnp.sum(weighted * across, keepdims=True)
    scale = lax.rsqrt(square_total / ENTRIES + 1e-06)
    first = lax.broadcasted_iota(jnp.int32, (1, 128), 1) < CH
    cent_copy.wait()
    for pair in range(ROWS // 2):
        parts = []
        for half in range(2):
            column = 128 * (2 * pair + half)
            cent = cent_ref[:, column : column + 128].astype(jnp.float32)
            parts.append(jnp.sum(cent * coeff, axis=0, keepdims=True) * scale)
        turned = [jnp.concatenate([item[:, CH:], item[:, :CH]], axis=1) for item in parts]
        update_ref[0:1, 128 * pair : 128 * pair + 128] = jnp.where(first, parts[0], turned[1])
        update_ref[1:2, 128 * pair : 128 * pair + 128] = jnp.where(first, turned[0], parts[1])


def solve_call(gram, energies, cent):
    whole = pl.BlockSpec(memory_space=VMEM)
    return pl.pallas_call(
        solve_kernel,
        in_specs=[whole, whole, pl.BlockSpec(memory_space=pl.ANY)],
        out_specs=[whole, whole],
        out_shape=[
            jax.ShapeDtypeStruct((LAYERS, ROWS * CH), jnp.float32),
            jax.ShapeDtypeStruct((1, LOCAL), jnp.float32),
        ],
        scratch_shapes=[
            VMEM((NS, NS + 128), jnp.float32),
            VMEM((NS, NS + 128), jnp.float32),
            VMEM((NS, WIDTH), jnp.bfloat16),
            pltpu.SemaphoreType.DMA,
            VMEM((BLOCK // PANEL, 8, 128), jnp.float32),
            VMEM((BLOCK // PANEL, PANEL, 8, 128), jnp.float32),
        ],
        compiler_params=pltpu.CompilerParams(vmem_limit_bytes=VMEM_LIMIT),
    )(gram, energies, cent)


def on_device(activations, cotangents, spin_bits, offdiag_energy):
    gram, cent, energies = main_call(
        activations, cotangents, spin_bits, offdiag_energy.reshape(1, LOCAL)
    )
    update, coeff = solve_call(gram, energies, cent)
    return update, coeff.reshape(LOCAL)


def solution(mesh):
    in_specs = (
        P("samp", "par", None, None),
        P("samp", "par", None, None),
        P("samp", None),
        P("samp"),
    )
    out_specs = (P("par", "samp"), P("samp"))
    return jax.shard_map(
        on_device, mesh=mesh, in_specs=in_specs, out_specs=out_specs, check_vma=False
    )
```

```python
import math

import jax
import jax.numpy as jnp
from jax import lax
from jax.experimental import pallas as pl
from jax.experimental.pallas import tpu as pltpu
from jax.sharding import PartitionSpec as P

CH = 64
KK = 9
LAT = 24
SITES = LAT * LAT
NSAMP = 32
NPAR = 8
NZ = 8
NY = 4
LOCAL = 8
NS = NSAMP * LOCAL
ROWS = KK * CH // NSAMP
CHUNK = ROWS * LOCAL
WIDTH = ROWS * 128
PADK = 640
LAYERS = 2
ENTRIES = 16 * KK * CH * CH
MESH = pl.DeviceIdType.MESH
VMEM_LIMIT = 56 * 1024 * 1024
HIGHEST = lax.Precision.HIGHEST
VMEM = pltpu.VMEM


def rolled(value, amount):
    amount = amount % SITES
    if amount == 0:
        return value
    return jnp.concatenate([value[:, amount:], value[:, :amount]], axis=1)


def column_shift(value, col_step):
    if col_step == 0:
        return value
    column = lax.broadcasted_iota(jnp.int32, value.shape, 1) % LAT
    edge = LAT - 1 if col_step > 0 else 0
    return jnp.where(column == edge, rolled(value, col_step - LAT * col_step), rolled(value, col_step))


def wrap(value, size):
    return lax.select(value >= size, value - size, value)


STEPS = [(down, hop) for down in range(NY) for hop in (1, 7, 2, 6, 3, 5, 4, 0) if (down, hop) != (0, 0)]


def diagonal_energy(spin_bits):
    spin = (2 * spin_bits - 1).astype(jnp.float32)
    right = column_shift(spin, 1)
    left = column_shift(spin, -1)
    pairs = spin * rolled(spin, LAT) + spin * right
    corners = spin * rolled(right, LAT) + spin * rolled(left, LAT)
    diag = 0.25 * jnp.sum(pairs + 0.5 * corners, axis=1, keepdims=True)
    wide = jnp.broadcast_to(diag, (LOCAL, 128))
    here = lax.broadcasted_iota(jnp.int32, (LOCAL, 128), 0) == lax.broadcasted_iota(
        jnp.int32, (LOCAL, 128), 1
    )
    return jnp.sum(jnp.where(here, wide, 0.0), axis=0, keepdims=True)


RHS_ROWS = ((0, 1, 2), (1, 0, 3))
MEMBERS = 32


def main_kernel(
    act_hbm, cot_hbm, spin_ref, off_ref,
    gram_ref, cent_hbm, energies_ref,
    act_ref, cot_ref, lhs, rhs, wide_rows, send_ref, recv_ref, cent_ref,
    energy_ref, relay_ref, part_ref, first, mine, second,
    act_sem, cot_sem, cent_sem, send_sem, recv_sem, esem, relay_sem, sem1, sem2, sem3,
):
    samp = lax.axis_index("samp")
    par = lax.axis_index("par")
    z, y = samp // NY, samp % NY
    x, core = par // 2, par % 2
    slot_here = y * NZ + z
    sibling = (samp, x * 2 + 1 - core)
    zs = [wrap(z + hop, NZ) for hop in range(NZ)]
    ys = [wrap(y + down, NY) for down in range(NY)]
    xs = [wrap(x + across, 4) for across in range(4)]
    partners = [(down, zs[hop] * NY + ys[down]) for down, hop in STEPS]
    far = {down: other for (down, other), (_, hop) in zip(partners, STEPS) if hop == 4}
    sorted_partners = [
        item for item, (_, hop) in sorted(zip(partners, STEPS), key=lambda pair: pair[1][1] != 4)
    ]
    block_here = y * NPAR + par
    members = [
        (ys[down] * NPAR + xs[across] * 2 + side, (z * NY + ys[down], xs[across] * 2 + side))
        for down in range(NY)
        for across in range(4)
        for side in (core, 1 - core)
    ][1:]

    def act_copy(n):
        return pltpu.make_async_copy(act_hbm.at[n], act_ref.at[n], act_sem.at[n])

    def cot_copy(n):
        return pltpu.make_async_copy(cot_hbm.at[n], cot_ref.at[n], cot_sem.at[n])

    for n in range(LOCAL):
        act_copy(n).start()
        cot_copy(n).start()

    def remote(source, target, send, recv, device):
        return pltpu.make_async_remote_copy(
            src_ref=source,
            dst_ref=target,
            send_sem=send,
            recv_sem=recv,
            device_id=device,
            device_id_type=MESH,
        )

    barrier = pltpu.get_barrier_semaphore()
    greeted = 0
    for _, other in partners:
        pl.semaphore_signal(barrier, inc=1, device_id=(other, par), device_id_type=MESH)
        greeted += 1
    for number, (_, device) in enumerate(members, 1):
        if number % 8:
            pl.semaphore_signal(barrier, inc=1, device_id=device, device_id_type=MESH)
            greeted += 1

    first_half = lax.broadcasted_iota(jnp.int32, (3 * CH, 128), 1) < CH
    lhs[:, :, :, PADK - 128 :] = jnp.zeros((2, LAYERS, 3 * CH, 128), jnp.bfloat16)
    rhs[:, :, :, PADK - 128 :] = jnp.zeros((2, LAYERS, 4 * CH, 128), jnp.bfloat16)
    rhs[:, 1, 2 * CH : 3 * CH, :] = jnp.zeros((2, CH, PADK), jnp.bfloat16)

    def product(slot, layer, width):
        return lax.dot_general(
            lhs[slot, layer], rhs[slot, layer, :width], (((1,), (1,)), ((), ())),
            preferred_element_type=jnp.float32,
        )

    def compute(sample, slot):
        act_copy(sample).wait()
        cot_copy(sample).wait()
        for layer in range(LAYERS):
            act = act_ref[sample, layer]
            cot = cot_ref[sample, layer]
            for step in (-1, 0, 1):
                low = (step + 1) * CH
                lhs[slot, layer, low : low + CH, :SITES] = column_shift(act, step)
                low = RHS_ROWS[layer][step + 1] * CH
                rhs[slot, layer, low : low + CH, :SITES] = rolled(cot, -LAT * step)
        one = product(slot, 0, 3 * CH)
        two = product(slot, 1, 4 * CH)
        blocks = (
            jnp.where(first_half, one[:, :128], two[:, :128]),
            jnp.where(first_half, two[:, :128], one[:, :128]),
            jnp.where(first_half, jnp.concatenate([one[:, 128:], one[:, 128:]], axis=1), two[:, 128:]),
        )
        for down in range(3):
            wide_rows[pl.ds(down * 3 * CH * LOCAL + sample, 3 * CH, stride=LOCAL), :] = blocks[down]

    def two_samples(pair, carry):
        for slot in range(2):
            compute(pair * 2 + slot, slot)
        return carry

    lax.fori_loop(0, LOCAL // 2, two_samples, 0)

    def rounded(other):
        start = pl.multiple_of(other * CHUNK, CHUNK)
        return wide_rows[pl.ds(start, CHUNK), :].astype(jnp.bfloat16)

    pl.semaphore_wait(barrier, greeted)
    for down, other in sorted_partners:
        send_ref[other] = rounded(other)
        if far[down] is other:
            via = zs[2] if down < 2 else zs[6]
            target, arrived, device = relay_ref.at[down], relay_sem, (via * NY + y, par)
        else:
            target, arrived, device = recv_ref.at[slot_here], recv_sem.at[down], (other, par)
        remote(send_ref.at[other], target, send_sem, arrived, device).start()

    flat = diagonal_energy(spin_ref[...])
    energy_ref[...] = jnp.zeros_like(energy_ref)
    energy_ref[:, :LOCAL] = flat[:, :LOCAL] + off_ref[...]
    for _, other in partners:
        remote(energy_ref, energies_ref.at[samp], esem.at[0], esem.at[1], (other, par)).start()
    energies_ref[samp] = energy_ref[...]
    recv_ref[slot_here] = rounded(samp)
    remote(relay_ref, relay_ref, send_sem, relay_sem, sibling).wait_recv()
    for down in range(NY):
        origin, goal = (zs[6], zs[2]) if down < 2 else (zs[2], zs[6])
        remote(
            relay_ref.at[down],
            recv_ref.at[y * NZ + origin],
            send_sem,
            recv_sem.at[down],
            (goal * NY + ys[down], par),
        ).start()

    for down in range(NY):
        low = wrap(y + NY - down, NY) * NZ
        taken = recv_ref.at[pl.ds(0, NZ - 1)] if down == 0 else recv_ref.at[pl.ds(low, NZ)]
        remote(taken, taken, send_sem, recv_sem.at[down], sibling).wait_recv()

    for pair in range(ROWS // 2):
        tile = jnp.stack(
            [
                recv_ref[(src % NY) * NZ + src // NY, 16 * pair : 16 * pair + 16, :].astype(jnp.float32)
                for src in range(NSAMP)
            ]
        ).reshape(NSAMP, 2, LOCAL, 128)
        for half in range(2):
            part = tile[:, half]
            mean = jnp.sum(jnp.sum(part, axis=0), axis=0, keepdims=True) / NS
            cent = ((part - mean) / math.sqrt(NS)).reshape(NS, 128)
            column = 128 * (2 * pair + half)
            cent_ref[:, column : column + 128] = cent.astype(jnp.bfloat16)
    cent_copy = pltpu.make_async_copy(cent_ref, cent_hbm, cent_sem)
    cent_copy.start()

    part_ref[...] = lax.dot_general(
        cent_ref[...], cent_ref[...], (((1,), (1,)), ((), ())), preferred_element_type=jnp.float32
    )

    def rows_of(index):
        return pl.ds(pl.multiple_of(index * 8, 8), 8)

    for other, device in members:
        remote(
            part_ref.at[rows_of(other)], first.at[block_here], sem1.at[0], sem1.at[1], device
        ).start()
    first[block_here] = part_ref[rows_of(block_here), :]
    member_bytes = first.at[pl.ds(0, MEMBERS - 1)]
    remote(member_bytes, member_bytes, sem1.at[0], sem1.at[1], sibling).wait_recv()
    own = jnp.sum(first[...], axis=0)
    mine[...] = own
    for hop in (4, 3, 5, 2, 6, 1, 7):
        device = (zs[hop] * NY + y, par)
        remote(mine, second.at[z], sem2.at[0], sem2.at[1], device).start()
    second[z] = own
    column_bytes = second.at[pl.ds(0, NZ - 1)]
    remote(column_bytes, column_bytes, sem2.at[0], sem2.at[1], sibling).wait_recv()
    block = rows_of(block_here)
    gram_ref[block, :] = jnp.sum(second[...], axis=0)
    for _, device in members:
        remote(gram_ref.at[block], gram_ref.at[block], sem3.at[0], sem3.at[1], device).start()

    sent = send_ref.at[pl.ds(0, NSAMP - 1)]
    remote(sent, sent, send_sem, recv_sem.at[0], sibling).wait_send()
    remote(relay_ref, relay_ref, send_sem, recv_sem.at[0], sibling).wait_send()
    energy_bytes = energies_ref.at[pl.ds(0, NSAMP - 1)]
    remote(energy_bytes, energy_bytes, esem.at[0], esem.at[1], sibling).wait()
    remote(member_bytes, member_bytes, sem1.at[0], sem1.at[1], sibling).wait_send()
    remote(column_bytes, column_bytes, sem2.at[0], sem2.at[1], sibling).wait_send()
    cent_copy.wait()
    gram_bytes = gram_ref.at[pl.ds(0, (MEMBERS - 1) * 8)]
    remote(gram_bytes, gram_bytes, sem3.at[0], sem3.at[1], sibling).wait()


def main_call(activations, cotangents, spin_bits, off_row):
    whole = pl.BlockSpec(memory_space=VMEM)
    anywhere = pl.BlockSpec(memory_space=pl.ANY)
    dma = pltpu.SemaphoreType.DMA
    return pl.pallas_call(
        main_kernel,
        in_specs=[anywhere, anywhere, whole, whole],
        out_specs=[whole, anywhere, whole],
        out_shape=[
            jax.ShapeDtypeStruct((NS, NS), jnp.float32),
            jax.ShapeDtypeStruct((NS, WIDTH), jnp.bfloat16),
            jax.ShapeDtypeStruct((NSAMP, 1, 128), jnp.float32),
        ],
        scratch_shapes=[
            VMEM((LOCAL, LAYERS, CH, SITES), jnp.bfloat16),
            VMEM((LOCAL, LAYERS, CH, SITES), jnp.bfloat16),
            VMEM((2, LAYERS, 3 * CH, PADK), jnp.bfloat16),
            VMEM((2, LAYERS, 4 * CH, PADK), jnp.bfloat16),
            VMEM((NSAMP * CHUNK, 128), jnp.float32),
            VMEM((NSAMP, CHUNK, 128), jnp.bfloat16),
            VMEM((NSAMP, CHUNK, 128), jnp.bfloat16),
            VMEM((NS, WIDTH), jnp.bfloat16),
            VMEM((1, 128), jnp.float32),
            VMEM((NY, CHUNK, 128), jnp.bfloat16),
            VMEM((NS, NS), jnp.float32),
            VMEM((MEMBERS, 8, NS), jnp.float32),
            VMEM((8, NS), jnp.float32),
            VMEM((NZ, 8, NS), jnp.float32),
            dma((LOCAL,)),
            dma((LOCAL,)),
            dma,
            dma,
            dma((NY,)),
            dma((2,)),
            dma,
            dma((2,)),
            dma((2,)),
            dma((2,)),
        ],
        compiler_params=pltpu.CompilerParams(
            collective_id=0, has_side_effects=True, vmem_limit_bytes=VMEM_LIMIT
        ),
    )(activations, cotangents, spin_bits, off_row)


BLOCK = 64
PANEL = 8


def forward_block(diag, tile_ref, column_ref):
    eye = lax.broadcasted_iota(jnp.int32, (BLOCK, BLOCK), 0) == lax.broadcasted_iota(
        jnp.int32, (BLOCK, BLOCK), 1
    )
    wide = jnp.concatenate([diag, jnp.where(eye, 1.0, 0.0)], axis=1)
    count = BLOCK // PANEL
    tiles = [wide[8 * q : 8 * q + 8] for q in range(count)]
    sub = lax.broadcasted_iota(jnp.int32, (8, 128), 0)

    def lanes(tile, col):
        return jnp.broadcast_to(tile[:, col : col + 1], (8, 128))

    def joined(parts):
        total = parts[0]
        for i in range(1, PANEL):
            total = jnp.where(sub == i, parts[i], total)
        return total

    reduced, scaled = [], []
    for panel in range(count):
        tile = tiles[panel]
        base = panel * PANEL
        tile_ref[panel] = tile
        for j in range(PANEL):
            column_ref[panel, j] = lanes(tile, base + j)
        low = {
            (i, j): column_ref[panel, j, pl.ds(i, 8, stride=0), :]
            for i in range(PANEL)
            for j in range(i + 1)
        }
        rows = [tile_ref[panel, pl.ds(i, 8, stride=0), :] for i in range(PANEL)]
        ups, downs, starts = {}, {}, {}
        for p in range(0, PANEL, 2):
            q = p + 1
            a, b, c = low[p, p], low[q, p], low[q, q]
            recip = pl.reciprocal(a * c - b * b, approx=True)
            starts[p] = (c * rows[p] - b * rows[q]) * recip
            starts[q] = (a * rows[q] - b * rows[p]) * recip
            for i in range(q + 1, PANEL):
                up = c * low[i, p] - b * low[i, q]
                down = a * low[i, q] - b * low[i, p]
                for m in range(q + 1, i + 1):
                    low[i, m] = low[i, m] - (up * low[m, p] + down * low[m, q]) * recip
                ups[i, p], downs[i, p] = up * recip, down * recip
                rows[i] = rows[i] - (ups[i, p] * rows[p] + downs[i, p] * rows[q])
        reduced.append(joined(rows))
        scaled.append(joined([starts[i] for i in range(PANEL)]))
        if panel == count - 1:
            break
        solved = [None] * PANEL
        for p in reversed(range(0, PANEL, 2)):
            for total, factor, at in ((starts[p], ups, p), (starts[p + 1], downs, p + 1)):
                for i in reversed(range(p + 2, PANEL)):
                    total = total - factor[i, p] * solved[i]
                solved[at] = total
        for q in range(panel + 1, count):
            old = tiles[q]
            terms = [lanes(old, base + i) * solved[i] for i in range(PANEL)]
            while len(terms) > 1:
                terms = [terms[a] + terms[a + 1] for a in range(0, len(terms), 2)]
            tiles[q] = old - terms[0]
    lower = jnp.concatenate(reduced, axis=0)[:, BLOCK:]
    return lower, jnp.concatenate(scaled, axis=0)[:, BLOCK:]


def solve_kernel(
    gram_ref, energies_ref, cent_hbm, update_ref, coeff_ref,
    work, held, cent_ref, cent_sem, tile_ref, column_ref,
):
    cent_copy = pltpu.make_async_copy(cent_hbm, cent_ref, cent_sem)
    cent_copy.start()
    rows_iota = lax.broadcasted_iota(jnp.int32, (NS, NS), 0)
    cols_iota = lax.broadcasted_iota(jnp.int32, (NS, NS), 1)
    gram = gram_ref[...]
    diagonal = rows_iota == cols_iota
    trace = jnp.sum(jnp.where(diagonal, gram, 0.0), keepdims=True)
    level = 1.0 / (trace / NS)
    pieces = jnp.broadcast_to(energies_ref[...], (NSAMP, LOCAL, 128)).reshape(NS, 128)
    lane = lax.broadcasted_iota(jnp.int32, (NS, 128), 1)
    row = lax.broadcasted_iota(jnp.int32, (NS, 128), 0)
    energy = jnp.sum(jnp.where(lane == row % LOCAL, pieces, 0.0), axis=1, keepdims=True)
    mean = jnp.sum(energy, axis=0, keepdims=True) / NS
    residual = -(energy - mean) / math.sqrt(NS)
    work[:, :NS] = gram * level + jnp.where(diagonal, 0.01, 0.0)
    work[:, NS:] = jnp.broadcast_to(residual, (NS, 128))

    def step(index, carry):
        own = pl.ds(pl.multiple_of(index * BLOCK, BLOCK), BLOCK)
        panel = work[own, :]
        lower, scaled = forward_block(panel[:, :BLOCK], tile_ref, column_ref)
        inverse = lax.dot_general(
            lower, scaled, (((0,), (0,)), ((), ())), precision=HIGHEST, preferred_element_type=jnp.float32
        )
        solved = jnp.dot(inverse, panel, precision=HIGHEST, preferred_element_type=jnp.float32)
        held[...] = work[...] - jnp.dot(
            work[:, :BLOCK], solved, precision=HIGHEST, preferred_element_type=jnp.float32
        )
        held[own, :] = solved
        work[:, : NS - BLOCK] = held[:, BLOCK:NS]
        work[:, NS - BLOCK : NS] = held[:, :BLOCK]
        work[:, NS:] = held[:, NS:]
        return carry

    lax.fori_loop(0, NS // BLOCK, step, 0)
    coeff = work[:, NS:] * level
    held[:, NS:] = coeff
    own = held[pl.ds(pl.multiple_of(lax.axis_index("samp") * LOCAL, LOCAL), LOCAL), NS:]
    here = lax.broadcasted_iota(jnp.int32, (LOCAL, 128), 0) == lax.broadcasted_iota(
        jnp.int32, (LOCAL, 128), 1
    )
    coeff_ref[...] = jnp.sum(jnp.where(here, own, 0.0), axis=0, keepdims=True)[:, :LOCAL]
    both = jnp.concatenate([coeff, coeff], axis=1)
    weighted = jnp.sum(gram * both, axis=0, keepdims=True)
    across = jnp.sum(jnp.where(diagonal, both, 0.0), axis=0, keepdims=True)
    square_total = jnp.sum(weighted * across, keepdims=True)
    scale = lax.rsqrt(square_total / ENTRIES + 1e-06)
    first = lax.broadcasted_iota(jnp.int32, (1, 128), 1) < CH
    cent_copy.wait()
    for pair in range(ROWS // 2):
        parts = []
        for half in range(2):
            column = 128 * (2 * pair + half)
            cent = cent_ref[:, column : column + 128].astype(jnp.float32)
            parts.append(jnp.sum(cent * coeff, axis=0, keepdims=True) * scale)
        turned = [jnp.concatenate([item[:, CH:], item[:, :CH]], axis=1) for item in parts]
        for half in range(2):
            at = lax.axis_index("samp") * ROWS + 2 * pair + half
            swapped = jnp.logical_and(at >= 3 * CH, at < 6 * CH)
            parts[half], turned[half] = (
                jnp.where(swapped, turned[half], parts[half]),
                jnp.where(swapped, parts[half], turned[half]),
            )
        update_ref[0:1, 128 * pair : 128 * pair + 128] = jnp.where(first, parts[0], turned[1])
        update_ref[1:2, 128 * pair : 128 * pair + 128] = jnp.where(first, turned[0], parts[1])


def solve_call(gram, energies, cent):
    whole = pl.BlockSpec(memory_space=VMEM)
    return pl.pallas_call(
        solve_kernel,
        in_specs=[whole, whole, pl.BlockSpec(memory_space=pl.ANY)],
        out_specs=[whole, whole],
        out_shape=[
            jax.ShapeDtypeStruct((LAYERS, ROWS * CH), jnp.float32),
            jax.ShapeDtypeStruct((1, LOCAL), jnp.float32),
        ],
        scratch_shapes=[
            VMEM((NS, NS + 128), jnp.float32),
            VMEM((NS, NS + 128), jnp.float32),
            VMEM((NS, WIDTH), jnp.bfloat16),
            pltpu.SemaphoreType.DMA,
            VMEM((BLOCK // PANEL, 8, 128), jnp.float32),
            VMEM((BLOCK // PANEL, PANEL, 8, 128), jnp.float32),
        ],
        compiler_params=pltpu.CompilerParams(vmem_limit_bytes=VMEM_LIMIT),
    )(gram, energies, cent)


def on_device(activations, cotangents, spin_bits, offdiag_energy):
    gram, cent, energies = main_call(
        activations, cotangents, spin_bits, offdiag_energy.reshape(1, LOCAL)
    )
    update, coeff = solve_call(gram, energies, cent)
    return update, coeff.reshape(LOCAL)


def solution(mesh):
    in_specs = (
        P("samp", "par", None, None),
        P("samp", "par", None, None),
        P("samp", None),
        P("samp"),
    )
    out_specs = (P("par", "samp"), P("samp"))
    return jax.shard_map(
        on_device, mesh=mesh, in_specs=in_specs, out_specs=out_specs, check_vma=False
    )
```

```python
import math

import jax
import jax.numpy as jnp
from jax import lax
from jax.experimental import pallas as pl
from jax.experimental.pallas import tpu as pltpu
from jax.sharding import PartitionSpec as P

CH = 64
KK = 9
LAT = 24
SITES = LAT * LAT
NSAMP = 32
NPAR = 8
NZ = 8
NY = 4
LOCAL = 8
NS = NSAMP * LOCAL
ROWS = KK * CH // NSAMP
CHUNK = ROWS * LOCAL
WIDTH = ROWS * 128
PADK = 640
LAYERS = 2
ENTRIES = 16 * KK * CH * CH
MESH = pl.DeviceIdType.MESH
VMEM_LIMIT = 56 * 1024 * 1024
HIGHEST = lax.Precision.HIGHEST
VMEM = pltpu.VMEM


def rolled(value, amount):
    amount = amount % SITES
    if amount == 0:
        return value
    return jnp.concatenate([value[:, amount:], value[:, :amount]], axis=1)


def column_shift(value, col_step):
    if col_step == 0:
        return value
    column = lax.broadcasted_iota(jnp.int32, value.shape, 1) % LAT
    edge = LAT - 1 if col_step > 0 else 0
    return jnp.where(column == edge, rolled(value, col_step - LAT * col_step), rolled(value, col_step))


def wrap(value, size):
    return lax.select(value >= size, value - size, value)


STEPS = [(down, hop) for down in range(NY) for hop in (1, 7, 2, 6, 3, 5, 4, 0) if (down, hop) != (0, 0)]


def diagonal_energy(spin_bits):
    spin = (2 * spin_bits - 1).astype(jnp.float32)
    right = column_shift(spin, 1)
    left = column_shift(spin, -1)
    pairs = spin * rolled(spin, LAT) + spin * right
    corners = spin * rolled(right, LAT) + spin * rolled(left, LAT)
    diag = 0.25 * jnp.sum(pairs + 0.5 * corners, axis=1, keepdims=True)
    wide = jnp.broadcast_to(diag, (LOCAL, 128))
    here = lax.broadcasted_iota(jnp.int32, (LOCAL, 128), 0) == lax.broadcasted_iota(
        jnp.int32, (LOCAL, 128), 1
    )
    return jnp.sum(jnp.where(here, wide, 0.0), axis=0, keepdims=True)


RHS_ROWS = ((0, 1, 2), (1, 0, 3))
CHIPS = 16


def main_kernel(
    act_hbm, cot_hbm, spin_ref, off_ref,
    gram_ref, cent_hbm, energies_ref,
    act_ref, cot_ref, lhs, rhs, wide_rows, send_ref, recv_ref, cent_ref,
    energy_ref, relay_ref, part_ref, first, mine, second,
    act_sem, cot_sem, cent_sem, send_sem, recv_sem, esem, relay_sem, sem1, sem2, sem3,
):
    samp = lax.axis_index("samp")
    par = lax.axis_index("par")
    z, y = samp // NY, samp % NY
    x, core = par // 2, par % 2
    slot_here = y * NZ + z
    sibling = (samp, x * 2 + 1 - core)
    zs = [wrap(z + hop, NZ) for hop in range(NZ)]
    ys = [wrap(y + down, NY) for down in range(NY)]
    xs = [wrap(x + across, 4) for across in range(4)]
    partners = [(down, zs[hop] * NY + ys[down]) for down, hop in STEPS]
    far = {down: other for (down, other), (_, hop) in zip(partners, STEPS) if hop == 4}
    sorted_partners = [
        item for item, (_, hop) in sorted(zip(partners, STEPS), key=lambda pair: -min(pair[1][1], NZ - pair[1][1]))
    ]
    chip = y * 4 + x
    others = [
        (ys[down] * 4 + xs[across], z * NY + ys[down], xs[across] * 2)
        for down in range(NY)
        for across in range(4)
    ][1:]
    around = [(other, (row, pair + side), side) for other, row, pair in others for side in range(2)]

    def by_core(body):
        @pl.when(core == 0)
        def _():
            body(0, 128)

        @pl.when(core == 1)
        def _():
            body(1, NS)

    def act_copy(n):
        return pltpu.make_async_copy(act_hbm.at[n], act_ref.at[n], act_sem.at[n])

    def cot_copy(n):
        return pltpu.make_async_copy(cot_hbm.at[n], cot_ref.at[n], cot_sem.at[n])

    for n in range(LOCAL):
        act_copy(n).start()
        cot_copy(n).start()

    def remote(source, target, send, recv, device):
        return pltpu.make_async_remote_copy(
            src_ref=source,
            dst_ref=target,
            send_sem=send,
            recv_sem=recv,
            device_id=device,
            device_id_type=MESH,
        )

    barrier = pltpu.get_barrier_semaphore()
    greeted = 0
    for _, other in partners:
        pl.semaphore_signal(barrier, inc=1, device_id=(other, par), device_id_type=MESH)
        greeted += 1
    for down in range(NY):
        for across in range(4):
            for side in (core, 1 - core):
                if across > 0 or side is not core:
                    device = (z * NY + ys[down], xs[across] * 2 + side)
                    pl.semaphore_signal(barrier, inc=1, device_id=device, device_id_type=MESH)
                    greeted += 1

    first_half = lax.broadcasted_iota(jnp.int32, (3 * CH, 128), 1) < CH
    lhs[:, :, :, PADK - 128 :] = jnp.zeros((2, LAYERS, 3 * CH, 128), jnp.bfloat16)
    rhs[:, :, :, PADK - 128 :] = jnp.zeros((2, LAYERS, 4 * CH, 128), jnp.bfloat16)
    rhs[:, 1, 2 * CH : 3 * CH, :] = jnp.zeros((2, CH, PADK), jnp.bfloat16)

    def product(slot, layer, width):
        return lax.dot_general(
            lhs[slot, layer], rhs[slot, layer, :width], (((1,), (1,)), ((), ())),
            preferred_element_type=jnp.float32,
        )

    def compute(sample, slot):
        act_copy(sample).wait()
        cot_copy(sample).wait()
        for layer in range(LAYERS):
            act = act_ref[sample, layer]
            cot = cot_ref[sample, layer]
            for step in (-1, 0, 1):
                low = (step + 1) * CH
                lhs[slot, layer, low : low + CH, :SITES] = column_shift(act, step)
                low = RHS_ROWS[layer][step + 1] * CH
                rhs[slot, layer, low : low + CH, :SITES] = rolled(cot, -LAT * step)
        one = product(slot, 0, 3 * CH)
        two = product(slot, 1, 4 * CH)
        blocks = (
            jnp.where(first_half, one[:, :128], two[:, :128]),
            jnp.where(first_half, two[:, :128], one[:, :128]),
            jnp.where(first_half, jnp.concatenate([one[:, 128:], one[:, 128:]], axis=1), two[:, 128:]),
        )
        for down in range(3):
            wide_rows[pl.ds(down * 3 * CH * LOCAL + sample, 3 * CH, stride=LOCAL), :] = blocks[down]

    def two_samples(pair, carry):
        for slot in range(2):
            compute(pair * 2 + slot, slot)
        return carry

    lax.fori_loop(0, LOCAL // 2, two_samples, 0)

    def rounded(other):
        start = pl.multiple_of(other * CHUNK, CHUNK)
        return wide_rows[pl.ds(start, CHUNK), :].astype(jnp.bfloat16)

    pl.semaphore_wait(barrier, greeted)
    for down, other in sorted_partners:
        send_ref[other] = rounded(other)
        if far[down] is other:
            via = zs[2] if down < 2 else zs[6]
            target, arrived, device = relay_ref.at[down], relay_sem, (via * NY + y, par)
        else:
            target, arrived, device = recv_ref.at[slot_here], recv_sem.at[down], (other, par)
        remote(send_ref.at[other], target, send_sem, arrived, device).start()

    flat = diagonal_energy(spin_ref[...])
    energy_ref[...] = jnp.zeros_like(energy_ref)
    energy_ref[:, :LOCAL] = flat[:, :LOCAL] + off_ref[...]
    for _, other in partners:
        remote(energy_ref, energies_ref.at[samp], esem.at[0], esem.at[1], (other, par)).start()
    energies_ref[samp] = energy_ref[...]
    recv_ref[slot_here] = rounded(samp)
    remote(relay_ref, relay_ref, send_sem, relay_sem, sibling).wait_recv()
    for down in range(NY):
        origin, goal = (zs[6], zs[2]) if down < 2 else (zs[2], zs[6])
        remote(
            relay_ref.at[down],
            recv_ref.at[y * NZ + origin],
            send_sem,
            recv_sem.at[down],
            (goal * NY + ys[down], par),
        ).start()

    for down in range(NY):
        low = wrap(y + NY - down, NY) * NZ
        taken = recv_ref.at[pl.ds(0, NZ - 1)] if down == 0 else recv_ref.at[pl.ds(low, NZ)]
        remote(taken, taken, send_sem, recv_sem.at[down], sibling).wait_recv()

    for pair in range(ROWS // 2):
        tile = jnp.stack(
            [
                recv_ref[(src % NY) * NZ + src // NY, 16 * pair : 16 * pair + 16, :].astype(jnp.float32)
                for src in range(NSAMP)
            ]
        ).reshape(NSAMP, 2, LOCAL, 128)
        for half in range(2):
            part = tile[:, half]
            mean = jnp.sum(jnp.sum(part, axis=0), axis=0, keepdims=True) / NS
            cent = ((part - mean) / math.sqrt(NS)).reshape(NS, 128)
            column = 128 * (2 * pair + half)
            cent_ref[:, column : column + 128] = cent.astype(jnp.bfloat16)
    cent_copy = pltpu.make_async_copy(cent_ref, cent_hbm, cent_sem)
    cent_copy.start()

    part_ref[...] = lax.dot_general(
        cent_ref[...], cent_ref[...], (((1,), (1,)), ((), ())), preferred_element_type=jnp.float32
    )

    def rows_of(side, index):
        return pl.ds(pl.multiple_of(side * 128 + index * 8, 8), 8)

    slot = core * CHIPS + chip
    widths = (128, NS)

    def send_first(other, device, side):
        wide = pl.ds(0, widths[side])
        remote(
            part_ref.at[rows_of(side, other), wide],
            first.at[slot, :, wide],
            sem1.at[side],
            sem1.at[2],
            device,
        ).start()

    for other, device, side in around:
        send_first(other, device, side)
    by_core(lambda side, width: send_first(chip, sibling, 1 - side))

    def middle(side, width):
        wide = pl.ds(0, width)
        first[slot, :, wide] = part_ref[rows_of(side, chip), wide]
        landed = first.at[pl.ds(0, 2 * CHIPS - 1), :, wide]
        remote(landed, landed, sem1.at[0], sem1.at[2], sibling).wait_recv()
        own = jnp.sum(first[:, :, wide], axis=0)
        mine[:, wide] = own
        for hop in (4, 3, 5, 2, 6, 1, 7):
            device = (zs[hop] * NY + y, par)
            remote(
                mine.at[:, wide], second.at[z, :, wide], sem2.at[0], sem2.at[1], device
            ).start()
        second[z, :, wide] = own
        landed = second.at[pl.ds(0, NZ - 1), :, wide]
        remote(landed, landed, sem2.at[0], sem2.at[1], sibling).wait_recv()
        block = rows_of(side, chip)
        gram_ref[block, wide] = jnp.sum(second[:, :, wide], axis=0)
        done = gram_ref.at[block, wide]
        for _, device, _ in around:
            remote(done, done, sem3.at[0], sem3.at[1 + side], device).start()
        remote(done, done, sem3.at[0], sem3.at[1 + side], sibling).start()

    by_core(middle)

    sent = send_ref.at[pl.ds(0, NSAMP - 1)]
    remote(sent, sent, send_sem, recv_sem.at[0], sibling).wait_send()
    remote(relay_ref, relay_ref, send_sem, recv_sem.at[0], sibling).wait_send()
    energy_bytes = energies_ref.at[pl.ds(0, NSAMP - 1)]
    remote(energy_bytes, energy_bytes, esem.at[0], esem.at[1], sibling).wait()
    cent_copy.wait()

    def finish(side, width):
        wide = pl.ds(0, width)
        for kind in range(2):
            count = CHIPS - 1 if kind == side else CHIPS
            bytes_ref = gram_ref.at[pl.ds(0, count * 8), pl.ds(0, widths[kind])]
            remote(bytes_ref, bytes_ref, sem1.at[kind], sem3.at[1 + kind], sibling).wait()
        landed = second.at[pl.ds(0, NZ - 1), :, wide]
        remote(landed, landed, sem2.at[0], sem2.at[1], sibling).wait_send()
        landed = first.at[pl.ds(0, 2 * CHIPS - 1), :, wide]
        remote(landed, landed, sem3.at[0], sem1.at[2], sibling).wait_send()

    by_core(finish)


def main_call(activations, cotangents, spin_bits, off_row):
    whole = pl.BlockSpec(memory_space=VMEM)
    anywhere = pl.BlockSpec(memory_space=pl.ANY)
    dma = pltpu.SemaphoreType.DMA
    return pl.pallas_call(
        main_kernel,
        in_specs=[anywhere, anywhere, whole, whole],
        out_specs=[whole, anywhere, whole],
        out_shape=[
            jax.ShapeDtypeStruct((NS, NS), jnp.float32),
            jax.ShapeDtypeStruct((NS, WIDTH), jnp.bfloat16),
            jax.ShapeDtypeStruct((NSAMP, 1, 128), jnp.float32),
        ],
        scratch_shapes=[
            VMEM((LOCAL, LAYERS, CH, SITES), jnp.bfloat16),
            VMEM((LOCAL, LAYERS, CH, SITES), jnp.bfloat16),
            VMEM((2, LAYERS, 3 * CH, PADK), jnp.bfloat16),
            VMEM((2, LAYERS, 4 * CH, PADK), jnp.bfloat16),
            VMEM((NSAMP * CHUNK, 128), jnp.float32),
            VMEM((NSAMP, CHUNK, 128), jnp.bfloat16),
            VMEM((NSAMP, CHUNK, 128), jnp.bfloat16),
            VMEM((NS, WIDTH), jnp.bfloat16),
            VMEM((1, 128), jnp.float32),
            VMEM((NY, CHUNK, 128), jnp.bfloat16),
            VMEM((NS, NS), jnp.float32),
            VMEM((2 * CHIPS, 8, NS), jnp.float32),
            VMEM((8, NS), jnp.float32),
            VMEM((NZ, 8, NS), jnp.float32),
            dma((LOCAL,)),
            dma((LOCAL,)),
            dma,
            dma,
            dma((NY,)),
            dma((2,)),
            dma,
            dma((3,)),
            dma((2,)),
            dma((3,)),
        ],
        compiler_params=pltpu.CompilerParams(
            collective_id=0, has_side_effects=True, vmem_limit_bytes=VMEM_LIMIT
        ),
    )(activations, cotangents, spin_bits, off_row)


BLOCK = 64
PANEL = 8


def forward_block(diag, tile_ref, column_ref, cross_ref):
    eye = lax.broadcasted_iota(jnp.int32, (BLOCK, BLOCK), 0) == lax.broadcasted_iota(
        jnp.int32, (BLOCK, BLOCK), 1
    )
    wide = jnp.concatenate([diag, jnp.where(eye, 1.0, 0.0)], axis=1)
    count = BLOCK // PANEL
    tiles = [wide[8 * q : 8 * q + 8] for q in range(count)]
    sub = lax.broadcasted_iota(jnp.int32, (8, 128), 0)

    def lanes(tile, col):
        return jnp.broadcast_to(tile[:, col : col + 1], (8, 128))

    def joined(parts):
        total = parts[0]
        for i in range(1, PANEL):
            total = jnp.where(sub == i, parts[i], total)
        return total

    def broadcast_row(ref, panel, j, i):
        return ref[panel, j, pl.ds(i, 8, stride=0), :]

    reduced, scaled = [], []
    columns = [lanes(tiles[0], j) for j in range(PANEL)]
    for panel in range(count):
        base = panel * PANEL
        last = panel == count - 1
        tile_ref[panel, 0] = tiles[panel]
        for j in range(PANEL):
            column_ref[panel, j] = columns[j]
        low = {
            (i, j): broadcast_row(column_ref, panel, j, i)
            for i in range(PANEL)
            for j in range(i + 1)
        }
        rows = [broadcast_row(tile_ref, panel, 0, i) for i in range(PANEL)]
        old_columns = {
            q: [lanes(tiles[q], base + i) for i in range(PANEL)] for q in range(panel + 1, count)
        }
        if not last:
            cross = list(old_columns[panel + 1])
            columns = [lanes(tiles[panel + 1], base + PANEL + j) for j in range(PANEL)]
        ups, downs, starts, cross_scaled = {}, {}, {}, {}
        for p in range(0, PANEL, 2):
            q = p + 1
            a, b, c = low[p, p], low[q, p], low[q, q]
            recip = pl.reciprocal(a * c - b * b, approx=True)
            for i in range(q + 1, PANEL):
                up = c * low[i, p] - b * low[i, q]
                down = a * low[i, q] - b * low[i, p]
                for m in range(q + 1, i + 1):
                    low[i, m] = low[i, m] - (up * low[m, p] + down * low[m, q]) * recip
                ups[i, p], downs[i, p] = up * recip, down * recip
            if not last:
                cross_scaled[p] = (c * cross[p] - b * cross[q]) * recip
                cross_scaled[q] = (a * cross[q] - b * cross[p]) * recip
                for i in range(q + 1, PANEL):
                    cross[i] = cross[i] - (ups[i, p] * cross[p] + downs[i, p] * cross[q])
            starts[p] = (c * rows[p] - b * rows[q]) * recip
            starts[q] = (a * rows[q] - b * rows[p]) * recip
            for i in range(q + 1, PANEL):
                rows[i] = rows[i] - (ups[i, p] * rows[p] + downs[i, p] * rows[q])
        if not last:
            for i in range(PANEL):
                cross_ref[panel, i] = cross[i]
            for j in range(PANEL):
                terms = [
                    cross_scaled[i] * broadcast_row(cross_ref, panel, i, j) for i in range(PANEL)
                ]
                while len(terms) > 1:
                    terms = [terms[a] + terms[a + 1] for a in range(0, len(terms), 2)]
                columns[j] = columns[j] - terms[0]
        reduced.append(joined(rows))
        scaled.append(joined([starts[i] for i in range(PANEL)]))
        if last:
            break
        solved = [None] * PANEL
        for p in reversed(range(0, PANEL, 2)):
            for total, factor, at in ((starts[p], ups, p), (starts[p + 1], downs, p + 1)):
                for i in reversed(range(p + 2, PANEL)):
                    total = total - factor[i, p] * solved[i]
                solved[at] = total
        for q in range(panel + 1, count):
            terms = [old_columns[q][i] * solved[i] for i in range(PANEL)]
            while len(terms) > 1:
                terms = [terms[a] + terms[a + 1] for a in range(0, len(terms), 2)]
            tiles[q] = tiles[q] - terms[0]
    lower = jnp.concatenate(reduced, axis=0)[:, BLOCK:]
    return lower, jnp.concatenate(scaled, axis=0)[:, BLOCK:]


def product(one, two, first_dim, second_dim):
    return lax.dot_general(
        one, two, (((first_dim,), (second_dim,)), ((), ())),
        precision=HIGHEST, preferred_element_type=jnp.float32,
    )


def solve_kernel(
    gram_ref, energies_ref, cent_hbm, update_ref, coeff_ref,
    work, held, cent_ref, cent_sem, tile_ref, column_ref, cross_ref,
):
    cent_copy = pltpu.make_async_copy(cent_hbm, cent_ref, cent_sem)
    cent_copy.start()
    rows_iota = lax.broadcasted_iota(jnp.int32, (NS, NS), 0)
    cols_iota = lax.broadcasted_iota(jnp.int32, (NS, NS), 1)
    below = gram_ref[128:, :128]
    gram = jnp.concatenate(
        [jnp.concatenate([gram_ref[:128, :128], below.T], axis=1), gram_ref[128:, :]], axis=0
    )
    diagonal = rows_iota == cols_iota
    trace = jnp.sum(jnp.where(diagonal, gram, 0.0), keepdims=True)
    level = 1.0 / (trace / NS)
    pieces = jnp.broadcast_to(energies_ref[...], (NSAMP, LOCAL, 128)).reshape(NS, 128)
    lane = lax.broadcasted_iota(jnp.int32, (NS, 128), 1)
    row = lax.broadcasted_iota(jnp.int32, (NS, 128), 0)
    energy = jnp.sum(jnp.where(lane == row % LOCAL, pieces, 0.0), axis=1, keepdims=True)
    mean = jnp.sum(energy, axis=0, keepdims=True) / NS
    residual = -(energy - mean) / math.sqrt(NS)
    work[:, :NS] = gram * level + jnp.where(diagonal, 0.01, 0.0)
    work[:, NS:] = jnp.broadcast_to(residual, (NS, 128))

    def step(index, carry):
        own = pl.ds(pl.multiple_of(index * BLOCK, BLOCK), BLOCK)
        panel = work[own, :]
        lower, scaled = forward_block(panel[:, :BLOCK], tile_ref, column_ref, cross_ref)
        middle = product(scaled, panel, 1, 0)
        outer = product(work[:, :BLOCK], lower, 1, 1)
        held[...] = work[...] - product(outer, middle, 1, 0)
        held[own, :] = product(lower, middle, 0, 0)
        work[:, : NS - BLOCK] = held[:, BLOCK:NS]
        work[:, NS - BLOCK : NS] = held[:, :BLOCK]
        work[:, NS:] = held[:, NS:]
        return carry

    lax.fori_loop(0, NS // BLOCK, step, 0)
    coeff = work[:, NS:] * level
    held[:, NS:] = coeff
    own = held[pl.ds(pl.multiple_of(lax.axis_index("samp") * LOCAL, LOCAL), LOCAL), NS:]
    here = lax.broadcasted_iota(jnp.int32, (LOCAL, 128), 0) == lax.broadcasted_iota(
        jnp.int32, (LOCAL, 128), 1
    )
    coeff_ref[...] = jnp.sum(jnp.where(here, own, 0.0), axis=0, keepdims=True)[:, :LOCAL]
    both = jnp.concatenate([coeff, coeff], axis=1)
    weighted = jnp.sum(gram * both, axis=0, keepdims=True)
    across = jnp.sum(jnp.where(diagonal, both, 0.0), axis=0, keepdims=True)
    square_total = jnp.sum(weighted * across, keepdims=True)
    scale = lax.rsqrt(square_total / ENTRIES + 1e-06)
    first = lax.broadcasted_iota(jnp.int32, (1, 128), 1) < CH
    cent_copy.wait()
    for pair in range(ROWS // 2):
        parts = []
        for half in range(2):
            column = 128 * (2 * pair + half)
            cent = cent_ref[:, column : column + 128].astype(jnp.float32)
            parts.append(jnp.sum(cent * coeff, axis=0, keepdims=True) * scale)
        turned = [jnp.concatenate([item[:, CH:], item[:, :CH]], axis=1) for item in parts]
        for half in range(2):
            at = lax.axis_index("samp") * ROWS + 2 * pair + half
            swapped = jnp.logical_and(at >= 3 * CH, at < 6 * CH)
            parts[half], turned[half] = (
                jnp.where(swapped, turned[half], parts[half]),
                jnp.where(swapped, parts[half], turned[half]),
            )
        update_ref[0:1, 128 * pair : 128 * pair + 128] = jnp.where(first, parts[0], turned[1])
        update_ref[1:2, 128 * pair : 128 * pair + 128] = jnp.where(first, turned[0], parts[1])


def solve_call(gram, energies, cent):
    whole = pl.BlockSpec(memory_space=VMEM)
    return pl.pallas_call(
        solve_kernel,
        in_specs=[whole, whole, pl.BlockSpec(memory_space=pl.ANY)],
        out_specs=[whole, whole],
        out_shape=[
            jax.ShapeDtypeStruct((LAYERS, ROWS * CH), jnp.float32),
            jax.ShapeDtypeStruct((1, LOCAL), jnp.float32),
        ],
        scratch_shapes=[
            VMEM((NS, NS + 128), jnp.float32),
            VMEM((NS, NS + 128), jnp.float32),
            VMEM((NS, WIDTH), jnp.bfloat16),
            pltpu.SemaphoreType.DMA,
            VMEM((BLOCK // PANEL, 1, 8, 128), jnp.float32),
            VMEM((BLOCK // PANEL, PANEL, 8, 128), jnp.float32),
            VMEM((BLOCK // PANEL, PANEL, 8, 128), jnp.float32),
        ],
        compiler_params=pltpu.CompilerParams(vmem_limit_bytes=VMEM_LIMIT),
    )(gram, energies, cent)


def on_device(activations, cotangents, spin_bits, offdiag_energy):
    gram, cent, energies = main_call(
        activations, cotangents, spin_bits, offdiag_energy.reshape(1, LOCAL)
    )
    update, coeff = solve_call(gram, energies, cent)
    return update, coeff.reshape(LOCAL)


def solution(mesh):
    in_specs = (
        P("samp", "par", None, None),
        P("samp", "par", None, None),
        P("samp", None),
        P("samp"),
    )
    out_specs = (P("par", "samp"), P("samp"))
    return jax.shard_map(
        on_device, mesh=mesh, in_specs=in_specs, out_specs=out_specs, check_vma=False
    )
```

```python
import math

import jax
import jax.numpy as jnp
from jax import lax
from jax.experimental import pallas as pl
from jax.experimental.pallas import tpu as pltpu
from jax.sharding import PartitionSpec as P

CH = 64
KK = 9
LAT = 24
SITES = LAT * LAT
NSAMP = 32
NPAR = 8
NZ = 8
NY = 4
LOCAL = 8
NS = NSAMP * LOCAL
ROWS = KK * CH // NSAMP
CHUNK = ROWS * LOCAL
WIDTH = ROWS * 128
PADK = 640
LAYERS = 2
ENTRIES = 16 * KK * CH * CH
MESH = pl.DeviceIdType.MESH
VMEM_LIMIT = 56 * 1024 * 1024
HIGHEST = lax.Precision.HIGHEST
VMEM = pltpu.VMEM


def rolled(value, amount):
    amount = amount % SITES
    if amount == 0:
        return value
    return jnp.concatenate([value[:, amount:], value[:, :amount]], axis=1)


def edge_mask(shape, col_step):
    column = lax.broadcasted_iota(jnp.int32, shape, 1) % LAT
    return column == (LAT - 1 if col_step > 0 else 0)


def column_shift(value, col_step, edge):
    if col_step == 0:
        return value
    return jnp.where(edge, rolled(value, col_step - LAT * col_step), rolled(value, col_step))


def wrap(value, size):
    return lax.select(value >= size, value - size, value)


STEPS = [(down, hop) for down in range(NY) for hop in (1, 7, 2, 6, 3, 5, 4, 0) if (down, hop) != (0, 0)]


def diagonal_energy(spin_bits):
    spin = (2 * spin_bits - 1).astype(jnp.float32)
    right = column_shift(spin, 1, edge_mask(spin.shape, 1))
    left = column_shift(spin, -1, edge_mask(spin.shape, -1))
    pairs = spin * rolled(spin, LAT) + spin * right
    corners = spin * rolled(right, LAT) + spin * rolled(left, LAT)
    diag = 0.25 * jnp.sum(pairs + 0.5 * corners, axis=1, keepdims=True)
    wide = jnp.broadcast_to(diag, (LOCAL, 128))
    here = lax.broadcasted_iota(jnp.int32, (LOCAL, 128), 0) == lax.broadcasted_iota(
        jnp.int32, (LOCAL, 128), 1
    )
    return jnp.sum(jnp.where(here, wide, 0.0), axis=0, keepdims=True)


RHS_ROWS = ((0, 1, 2), (1, 0, 3))
CHIPS = 16


def main_kernel(
    act_hbm, cot_hbm, spin_ref, off_ref,
    gram_ref, cent_hbm, energies_ref,
    act_ref, cot_ref, edges, lhs, rhs, wide_rows, send_ref, recv_ref, cent_ref,
    energy_ref, relay_ref, part_ref, first, mine, second,
    act_sem, cot_sem, cent_sem, send_sem, recv_sem, esem, relay_sem, sem1, sem2, sem3,
):
    samp = lax.axis_index("samp")
    par = lax.axis_index("par")
    z, y = samp // NY, samp % NY
    x, core = par // 2, par % 2
    slot_here = y * NZ + z
    sibling = (samp, x * 2 + 1 - core)
    zs = [wrap(z + hop, NZ) for hop in range(NZ)]
    ys = [wrap(y + down, NY) for down in range(NY)]
    xs = [wrap(x + across, 4) for across in range(4)]
    partners = [(down, zs[hop] * NY + ys[down]) for down, hop in STEPS]
    far = {down: other for (down, other), (_, hop) in zip(partners, STEPS) if hop == 4}
    sorted_partners = [
        item for item, (_, hop) in sorted(zip(partners, STEPS), key=lambda pair: -min(pair[1][1], NZ - pair[1][1]))
    ]
    chip = y * 4 + x
    others = [
        (ys[down] * 4 + xs[across], z * NY + ys[down], xs[across] * 2)
        for down in range(NY)
        for across in range(4)
    ][1:]
    around = [(other, (row, pair + side), side) for other, row, pair in others for side in range(2)]

    def by_core(body):
        @pl.when(core == 0)
        def _():
            body(0, 128)

        @pl.when(core == 1)
        def _():
            body(1, NS)

    def act_copy(n):
        return pltpu.make_async_copy(act_hbm.at[n], act_ref.at[n], act_sem.at[n])

    def cot_copy(n):
        return pltpu.make_async_copy(cot_hbm.at[n], cot_ref.at[n], cot_sem.at[n])

    for n in range(LOCAL):
        act_copy(n).start()
        cot_copy(n).start()

    def remote(source, target, send, recv, device):
        return pltpu.make_async_remote_copy(
            src_ref=source,
            dst_ref=target,
            send_sem=send,
            recv_sem=recv,
            device_id=device,
            device_id_type=MESH,
        )

    barrier = pltpu.get_barrier_semaphore()
    greeted = 0
    for _, other in partners:
        pl.semaphore_signal(barrier, inc=1, device_id=(other, par), device_id_type=MESH)
        greeted += 1
    for down in range(NY):
        for across in range(4):
            for side in (core, 1 - core):
                if across > 0 or side is not core:
                    device = (z * NY + ys[down], xs[across] * 2 + side)
                    pl.semaphore_signal(barrier, inc=1, device_id=device, device_id_type=MESH)
                    greeted += 1

    first_half = lax.broadcasted_iota(jnp.int32, (3 * CH, 128), 1) < CH
    lhs[:, :, :, PADK - 128 :] = jnp.zeros((2, LAYERS, 3 * CH, 128), jnp.bfloat16)
    rhs[:, :, :, PADK - 128 :] = jnp.zeros((2, LAYERS, 4 * CH, 128), jnp.bfloat16)
    rhs[:, 1, 2 * CH : 3 * CH, :] = jnp.zeros((2, CH, PADK), jnp.bfloat16)
    for at, step in enumerate((-1, 1)):
        strip = jnp.where(edge_mask((8, SITES), step), 1.0, 0.0)
        edges[at] = jnp.concatenate([strip] * (CH // 8), axis=0).astype(jnp.bfloat16)

    def product(slot, layer, width):
        return lax.dot_general(
            lhs[slot, layer], rhs[slot, layer, :width], (((1,), (1,)), ((), ())),
            preferred_element_type=jnp.float32,
        )

    def compute(sample, slot):
        act_copy(sample).wait()
        cot_copy(sample).wait()
        for layer in range(LAYERS):
            act = act_ref[sample, layer]
            cot = cot_ref[sample, layer]
            for step in (-1, 0, 1):
                low = (step + 1) * CH
                edge = edges[max(step, 0)] > 0
                lhs[slot, layer, low : low + CH, :SITES] = column_shift(act, step, edge)
                low = RHS_ROWS[layer][step + 1] * CH
                rhs[slot, layer, low : low + CH, :SITES] = rolled(cot, -LAT * step)
        one = product(slot, 0, 3 * CH)
        two = product(slot, 1, 4 * CH)
        blocks = (
            jnp.where(first_half, one[:, :128], two[:, :128]),
            jnp.where(first_half, two[:, :128], one[:, :128]),
            jnp.where(first_half, jnp.concatenate([one[:, 128:], one[:, 128:]], axis=1), two[:, 128:]),
        )
        for down in range(3):
            wide_rows[pl.ds(down * 3 * CH * LOCAL + sample, 3 * CH, stride=LOCAL), :] = blocks[down]

    def two_samples(pair, carry):
        for slot in range(2):
            compute(pair * 2 + slot, slot)
        return carry

    lax.fori_loop(0, LOCAL // 2, two_samples, 0)

    def rounded(other):
        start = pl.multiple_of(other * CHUNK, CHUNK)
        return wide_rows[pl.ds(start, CHUNK), :].astype(jnp.bfloat16)

    pl.semaphore_wait(barrier, greeted)
    for down, other in sorted_partners:
        send_ref[other] = rounded(other)
        if far[down] is other:
            via = zs[2] if down < 2 else zs[6]
            target, arrived, device = relay_ref.at[down], relay_sem, (via * NY + y, par)
        else:
            target, arrived, device = recv_ref.at[slot_here], recv_sem.at[down], (other, par)
        remote(send_ref.at[other], target, send_sem, arrived, device).start()

    flat = diagonal_energy(spin_ref[...])
    energy_ref[...] = jnp.zeros_like(energy_ref)
    energy_ref[:, :LOCAL] = flat[:, :LOCAL] + off_ref[...]
    for _, other in partners:
        remote(energy_ref, energies_ref.at[samp], esem.at[0], esem.at[1], (other, par)).start()
    energies_ref[samp] = energy_ref[...]
    recv_ref[slot_here] = rounded(samp)
    remote(relay_ref, relay_ref, send_sem, relay_sem, sibling).wait_recv()
    for down in range(NY):
        origin, goal = (zs[6], zs[2]) if down < 2 else (zs[2], zs[6])
        remote(
            relay_ref.at[down],
            recv_ref.at[y * NZ + origin],
            send_sem,
            recv_sem.at[down],
            (goal * NY + ys[down], par),
        ).start()

    for down in range(NY):
        low = wrap(y + NY - down, NY) * NZ
        taken = recv_ref.at[pl.ds(0, NZ - 1)] if down == 0 else recv_ref.at[pl.ds(low, NZ)]
        remote(taken, taken, send_sem, recv_sem.at[down], sibling).wait_recv()

    for pair in range(ROWS // 2):
        tile = jnp.stack(
            [
                recv_ref[(src % NY) * NZ + src // NY, 16 * pair : 16 * pair + 16, :].astype(jnp.float32)
                for src in range(NSAMP)
            ]
        ).reshape(NSAMP, 2, LOCAL, 128)
        halves = []
        for half in range(2):
            part = tile[:, half]
            mean = jnp.sum(jnp.sum(part, axis=0), axis=0, keepdims=True) / NS
            cent = ((part - mean) / math.sqrt(NS)).reshape(NS, 128)
            halves.append(cent.astype(jnp.bfloat16))
        cent = jnp.concatenate(halves, axis=1)
        cent_ref[:, 256 * pair : 256 * pair + 256] = cent
        light = lax.dot_general(
            cent[:128], cent[:128], (((1,), (1,)), ((), ())), preferred_element_type=jnp.float32
        )
        heavy = lax.dot_general(
            cent[128:], cent, (((1,), (1,)), ((), ())), preferred_element_type=jnp.float32
        )
        if pair == 0:
            part_ref[:128, :128] = light
            part_ref[128:, :] = heavy
        else:
            part_ref[:128, :128] += light
            part_ref[128:, :] += heavy
    cent_copy = pltpu.make_async_copy(cent_ref, cent_hbm, cent_sem)
    cent_copy.start()

    def rows_of(side, index):
        return pl.ds(pl.multiple_of(side * 128 + index * 8, 8), 8)

    slot = core * CHIPS + chip
    widths = (128, NS)

    def send_first(other, device, side):
        wide = pl.ds(0, widths[side])
        remote(
            part_ref.at[rows_of(side, other), wide],
            first.at[slot, :, wide],
            sem1.at[side],
            sem1.at[2],
            device,
        ).start()

    for other, device, side in around:
        send_first(other, device, side)
    by_core(lambda side, width: send_first(chip, sibling, 1 - side))

    def middle(side, width):
        wide = pl.ds(0, width)
        first[slot, :, wide] = part_ref[rows_of(side, chip), wide]
        landed = first.at[pl.ds(0, 2 * CHIPS - 1), :, wide]
        remote(landed, landed, sem1.at[0], sem1.at[2], sibling).wait_recv()
        own = jnp.sum(first[:, :, wide], axis=0)
        mine[:, wide] = own
        for hop in (4, 3, 5, 2, 6, 1, 7):
            device = (zs[hop] * NY + y, par)
            remote(
                mine.at[:, wide], second.at[z, :, wide], sem2.at[0], sem2.at[1], device
            ).start()
        second[z, :, wide] = own
        landed = second.at[pl.ds(0, NZ - 1), :, wide]
        remote(landed, landed, sem2.at[0], sem2.at[1], sibling).wait_recv()
        block = rows_of(side, chip)
        gram_ref[block, wide] = jnp.sum(second[:, :, wide], axis=0)
        done = gram_ref.at[block, wide]
        for _, device, _ in around:
            remote(done, done, sem3.at[0], sem3.at[1 + side], device).start()
        remote(done, done, sem3.at[0], sem3.at[1 + side], sibling).start()

    by_core(middle)

    sent = send_ref.at[pl.ds(0, NSAMP - 1)]
    remote(sent, sent, send_sem, recv_sem.at[0], sibling).wait_send()
    remote(relay_ref, relay_ref, send_sem, recv_sem.at[0], sibling).wait_send()
    energy_bytes = energies_ref.at[pl.ds(0, NSAMP - 1)]
    remote(energy_bytes, energy_bytes, esem.at[0], esem.at[1], sibling).wait()
    cent_copy.wait()

    def finish(side, width):
        wide = pl.ds(0, width)
        for kind in range(2):
            count = CHIPS - 1 if kind == side else CHIPS
            bytes_ref = gram_ref.at[pl.ds(0, count * 8), pl.ds(0, widths[kind])]
            remote(bytes_ref, bytes_ref, sem1.at[kind], sem3.at[1 + kind], sibling).wait()
        landed = second.at[pl.ds(0, NZ - 1), :, wide]
        remote(landed, landed, sem2.at[0], sem2.at[1], sibling).wait_send()
        landed = first.at[pl.ds(0, 2 * CHIPS - 1), :, wide]
        remote(landed, landed, sem3.at[0], sem1.at[2], sibling).wait_send()

    by_core(finish)


def main_call(activations, cotangents, spin_bits, off_row):
    whole = pl.BlockSpec(memory_space=VMEM)
    anywhere = pl.BlockSpec(memory_space=pl.ANY)
    dma = pltpu.SemaphoreType.DMA
    return pl.pallas_call(
        main_kernel,
        in_specs=[anywhere, anywhere, whole, whole],
        out_specs=[whole, anywhere, whole],
        out_shape=[
            jax.ShapeDtypeStruct((NS, NS), jnp.float32),
            jax.ShapeDtypeStruct((NS, WIDTH), jnp.bfloat16),
            jax.ShapeDtypeStruct((NSAMP, 1, 128), jnp.float32),
        ],
        scratch_shapes=[
            VMEM((LOCAL, LAYERS, CH, SITES), jnp.bfloat16),
            VMEM((LOCAL, LAYERS, CH, SITES), jnp.bfloat16),
            VMEM((2, CH, SITES), jnp.bfloat16),
            VMEM((2, LAYERS, 3 * CH, PADK), jnp.bfloat16),
            VMEM((2, LAYERS, 4 * CH, PADK), jnp.bfloat16),
            VMEM((NSAMP * CHUNK, 128), jnp.float32),
            VMEM((NSAMP, CHUNK, 128), jnp.bfloat16),
            VMEM((NSAMP, CHUNK, 128), jnp.bfloat16),
            VMEM((NS, WIDTH), jnp.bfloat16),
            VMEM((1, 128), jnp.float32),
            VMEM((NY, CHUNK, 128), jnp.bfloat16),
            VMEM((NS, NS), jnp.float32),
            VMEM((2 * CHIPS, 8, NS), jnp.float32),
            VMEM((8, NS), jnp.float32),
            VMEM((NZ, 8, NS), jnp.float32),
            dma((LOCAL,)),
            dma((LOCAL,)),
            dma,
            dma,
            dma((NY,)),
            dma((2,)),
            dma,
            dma((3,)),
            dma((2,)),
            dma((3,)),
        ],
        compiler_params=pltpu.CompilerParams(
            collective_id=0, has_side_effects=True, vmem_limit_bytes=VMEM_LIMIT
        ),
    )(activations, cotangents, spin_bits, off_row)


BLOCK = 64
PANEL = 8


def forward_block(diag, tile_ref, column_ref, cross_ref):
    eye = lax.broadcasted_iota(jnp.int32, (BLOCK, BLOCK), 0) == lax.broadcasted_iota(
        jnp.int32, (BLOCK, BLOCK), 1
    )
    wide = jnp.concatenate([diag, jnp.where(eye, 1.0, 0.0)], axis=1)
    count = BLOCK // PANEL
    tiles = [wide[8 * q : 8 * q + 8] for q in range(count)]
    sub = lax.broadcasted_iota(jnp.int32, (8, 128), 0)

    def lanes(tile, col):
        return jnp.broadcast_to(tile[:, col : col + 1], (8, 128))

    def joined(parts):
        total = parts[0]
        for i in range(1, PANEL):
            total = jnp.where(sub == i, parts[i], total)
        return total

    def broadcast_row(ref, panel, j, i):
        return ref[panel, j, pl.ds(i, 8, stride=0), :]

    reduced, scaled = [], []
    columns = [lanes(tiles[0], j) for j in range(PANEL)]
    for panel in range(count):
        base = panel * PANEL
        last = panel == count - 1
        tile_ref[panel, 0] = tiles[panel]
        for j in range(PANEL):
            column_ref[panel, j] = columns[j]
        low = {
            (i, j): broadcast_row(column_ref, panel, j, i)
            for i in range(PANEL)
            for j in range(i + 1)
        }
        rows = [broadcast_row(tile_ref, panel, 0, i) for i in range(PANEL)]
        old_columns = {
            q: [lanes(tiles[q], base + i) for i in range(PANEL)] for q in range(panel + 1, count)
        }
        if not last:
            cross = list(old_columns[panel + 1])
            columns = [lanes(tiles[panel + 1], base + PANEL + j) for j in range(PANEL)]
        ups, downs, starts, cross_scaled = {}, {}, {}, {}
        for p in range(0, PANEL, 2):
            q = p + 1
            a, b, c = low[p, p], low[q, p], low[q, q]
            recip = pl.reciprocal(a * c - b * b, approx=True)
            for i in range(q + 1, PANEL):
                up = c * low[i, p] - b * low[i, q]
                down = a * low[i, q] - b * low[i, p]
                for m in range(q + 1, i + 1):
                    low[i, m] = low[i, m] - (up * low[m, p] + down * low[m, q]) * recip
                ups[i, p], downs[i, p] = up * recip, down * recip
            if not last:
                cross_scaled[p] = (c * cross[p] - b * cross[q]) * recip
                cross_scaled[q] = (a * cross[q] - b * cross[p]) * recip
                for i in range(q + 1, PANEL):
                    cross[i] = cross[i] - (ups[i, p] * cross[p] + downs[i, p] * cross[q])
            starts[p] = (c * rows[p] - b * rows[q]) * recip
            starts[q] = (a * rows[q] - b * rows[p]) * recip
            for i in range(q + 1, PANEL):
                rows[i] = rows[i] - (ups[i, p] * rows[p] + downs[i, p] * rows[q])
        if not last:
            for i in range(PANEL):
                cross_ref[panel, i] = cross[i]
            for j in range(PANEL):
                terms = [
                    cross_scaled[i] * broadcast_row(cross_ref, panel, i, j) for i in range(PANEL)
                ]
                while len(terms) > 1:
                    terms = [terms[a] + terms[a + 1] for a in range(0, len(terms), 2)]
                columns[j] = columns[j] - terms[0]
        reduced.append(joined(rows))
        scaled.append(joined([starts[i] for i in range(PANEL)]))
        if last:
            break
        solved = [None] * PANEL
        for p in reversed(range(0, PANEL, 2)):
            for total, factor, at in ((starts[p], ups, p), (starts[p + 1], downs, p + 1)):
                for i in reversed(range(p + 2, PANEL)):
                    total = total - factor[i, p] * solved[i]
                solved[at] = total
        for q in range(panel + 1, count):
            terms = [old_columns[q][i] * solved[i] for i in range(PANEL)]
            while len(terms) > 1:
                terms = [terms[a] + terms[a + 1] for a in range(0, len(terms), 2)]
            tiles[q] = tiles[q] - terms[0]
    lower = jnp.concatenate(reduced, axis=0)[:, BLOCK:]
    return lower, jnp.concatenate(scaled, axis=0)[:, BLOCK:]


def product(one, two, first_dim, second_dim):
    return lax.dot_general(
        one, two, (((first_dim,), (second_dim,)), ((), ())),
        precision=HIGHEST, preferred_element_type=jnp.float32,
    )


def solve_kernel(
    gram_ref, energies_ref, cent_hbm, update_ref, coeff_ref,
    work, held, cent_ref, cent_sem, tile_ref, column_ref, cross_ref,
):
    cent_copy = pltpu.make_async_copy(cent_hbm, cent_ref, cent_sem)
    cent_copy.start()
    rows_iota = lax.broadcasted_iota(jnp.int32, (NS, NS), 0)
    cols_iota = lax.broadcasted_iota(jnp.int32, (NS, NS), 1)
    below = gram_ref[128:, :128]
    gram = jnp.concatenate(
        [jnp.concatenate([gram_ref[:128, :128], below.T], axis=1), gram_ref[128:, :]], axis=0
    )
    diagonal = rows_iota == cols_iota
    trace = jnp.sum(jnp.where(diagonal, gram, 0.0), keepdims=True)
    level = 1.0 / (trace / NS)
    pieces = jnp.broadcast_to(energies_ref[...], (NSAMP, LOCAL, 128)).reshape(NS, 128)
    lane = lax.broadcasted_iota(jnp.int32, (NS, 128), 1)
    row = lax.broadcasted_iota(jnp.int32, (NS, 128), 0)
    energy = jnp.sum(jnp.where(lane == jnp.bitwise_and(row, LOCAL - 1), pieces, 0.0), axis=1, keepdims=True)
    mean = jnp.sum(energy, axis=0, keepdims=True) / NS
    residual = -(energy - mean) / math.sqrt(NS)
    work[:, :NS] = gram * level + jnp.where(diagonal, 0.01, 0.0)
    work[:, NS:] = jnp.broadcast_to(residual, (NS, 128))

    for index in range(NS // BLOCK):
        low = index * BLOCK
        own = slice(low, low + BLOCK)
        rest = slice(128 * ((index + 1) // 2), NS + 128)
        lower, scaled = forward_block(work[own, own], tile_ref, column_ref, cross_ref)
        middle = product(scaled, work[own, rest], 1, 0)
        outer = product(work[:, own], lower, 1, 1)
        work[:, rest] = work[:, rest] - product(outer, middle, 1, 0)
        work[own, rest] = product(lower, middle, 0, 0)

    coeff = work[:, NS:] * level
    held[...] = coeff
    own = held[pl.ds(pl.multiple_of(lax.axis_index("samp") * LOCAL, LOCAL), LOCAL), :]
    here = lax.broadcasted_iota(jnp.int32, (LOCAL, 128), 0) == lax.broadcasted_iota(
        jnp.int32, (LOCAL, 128), 1
    )
    coeff_ref[...] = jnp.sum(jnp.where(here, own, 0.0), axis=0, keepdims=True)[:, :LOCAL]
    both = jnp.concatenate([coeff, coeff], axis=1)
    weighted = jnp.sum(gram * both, axis=0, keepdims=True)
    across = jnp.sum(jnp.where(diagonal, both, 0.0), axis=0, keepdims=True)
    square_total = jnp.sum(weighted * across, keepdims=True)
    scale = lax.rsqrt(square_total / ENTRIES + 1e-06)
    first = lax.broadcasted_iota(jnp.int32, (1, 128), 1) < CH
    cent_copy.wait()
    for pair in range(ROWS // 2):
        parts = []
        for half in range(2):
            column = 128 * (2 * pair + half)
            cent = cent_ref[:, column : column + 128].astype(jnp.float32)
            parts.append(jnp.sum(cent * coeff, axis=0, keepdims=True) * scale)
        turned = [jnp.concatenate([item[:, CH:], item[:, :CH]], axis=1) for item in parts]
        for half in range(2):
            at = lax.axis_index("samp") * ROWS + 2 * pair + half
            swapped = jnp.logical_and(at >= 3 * CH, at < 6 * CH)
            parts[half], turned[half] = (
                jnp.where(swapped, turned[half], parts[half]),
                jnp.where(swapped, parts[half], turned[half]),
            )
        update_ref[0:1, 128 * pair : 128 * pair + 128] = jnp.where(first, parts[0], turned[1])
        update_ref[1:2, 128 * pair : 128 * pair + 128] = jnp.where(first, turned[0], parts[1])


def solve_call(gram, energies, cent):
    whole = pl.BlockSpec(memory_space=VMEM)
    return pl.pallas_call(
        solve_kernel,
        in_specs=[whole, whole, pl.BlockSpec(memory_space=pl.ANY)],
        out_specs=[whole, whole],
        out_shape=[
            jax.ShapeDtypeStruct((LAYERS, ROWS * CH), jnp.float32),
            jax.ShapeDtypeStruct((1, LOCAL), jnp.float32),
        ],
        scratch_shapes=[
            VMEM((NS, NS + 128), jnp.float32),
            VMEM((NS, 128), jnp.float32),
            VMEM((NS, WIDTH), jnp.bfloat16),
            pltpu.SemaphoreType.DMA,
            VMEM((BLOCK // PANEL, 1, 8, 128), jnp.float32),
            VMEM((BLOCK // PANEL, PANEL, 8, 128), jnp.float32),
            VMEM((BLOCK // PANEL, PANEL, 8, 128), jnp.float32),
        ],
        compiler_params=pltpu.CompilerParams(vmem_limit_bytes=VMEM_LIMIT),
    )(gram, energies, cent)


def on_device(activations, cotangents, spin_bits, offdiag_energy):
    gram, cent, energies = main_call(
        activations, cotangents, spin_bits, offdiag_energy.reshape(1, LOCAL)
    )
    update, coeff = solve_call(gram, energies, cent)
    return update, coeff.reshape(LOCAL)


def solution(mesh):
    in_specs = (
        P("samp", "par", None, None),
        P("samp", "par", None, None),
        P("samp", None),
        P("samp"),
    )
    out_specs = (P("par", "samp"), P("samp"))
    return jax.shard_map(
        on_device, mesh=mesh, in_specs=in_specs, out_specs=out_specs, check_vma=False
    )
```

```python
import math

import jax
import jax.numpy as jnp
from jax import lax
from jax.experimental import pallas as pl
from jax.experimental.pallas import tpu as pltpu
from jax.sharding import PartitionSpec as P

CH = 64
KK = 9
LAT = 24
SITES = LAT * LAT
NSAMP = 32
NPAR = 8
NZ = 8
NY = 4
LOCAL = 8
NS = NSAMP * LOCAL
ROWS = KK * CH // NSAMP
CHUNK = ROWS * LOCAL
WIDTH = ROWS * 128
PADK = 640
LAYERS = 2
ENTRIES = 16 * KK * CH * CH
MESH = pl.DeviceIdType.MESH
VMEM_LIMIT = 56 * 1024 * 1024
HIGHEST = lax.Precision.HIGHEST
VMEM = pltpu.VMEM


def rolled(value, amount):
    amount = amount % SITES
    if amount == 0:
        return value
    return jnp.concatenate([value[:, amount:], value[:, :amount]], axis=1)


def edge_mask(shape, col_step):
    column = lax.broadcasted_iota(jnp.int32, shape, 1) % LAT
    return column == (LAT - 1 if col_step > 0 else 0)


def column_shift(value, col_step, edge):
    if col_step == 0:
        return value
    return jnp.where(edge, rolled(value, col_step - LAT * col_step), rolled(value, col_step))


def wrap(value, size):
    return lax.select(value >= size, value - size, value)


STEPS = [(down, hop) for down in range(NY) for hop in (1, 7, 2, 6, 3, 5, 4, 0) if (down, hop) != (0, 0)]


def diagonal_energy(spin_bits):
    spin = (2 * spin_bits - 1).astype(jnp.float32)
    right = column_shift(spin, 1, edge_mask(spin.shape, 1))
    left = column_shift(spin, -1, edge_mask(spin.shape, -1))
    pairs = spin * rolled(spin, LAT) + spin * right
    corners = spin * rolled(right, LAT) + spin * rolled(left, LAT)
    diag = 0.25 * jnp.sum(pairs + 0.5 * corners, axis=1, keepdims=True)
    wide = jnp.broadcast_to(diag, (LOCAL, 128))
    here = lax.broadcasted_iota(jnp.int32, (LOCAL, 128), 0) == lax.broadcasted_iota(
        jnp.int32, (LOCAL, 128), 1
    )
    return jnp.sum(jnp.where(here, wide, 0.0), axis=0, keepdims=True)


PLANE = sorted(
    ((down, across) for down in range(NY) for across in range(4) if (down, across) != (0, 0)),
    key=lambda step: -(min(step[0], NY - step[0]) + min(step[1], 4 - step[1])),
)
RHS_ROWS = ((0, 1, 2), (1, 0, 3))
CHIPS = 16


def main_kernel(
    act_hbm, cot_hbm, spin_ref, off_ref,
    gram_ref, cent_hbm, energies_ref,
    act_ref, cot_ref, edges, lhs, rhs, wide_rows, send_ref, recv_ref, cent_ref,
    energy_ref, part_ref, first, mine, second,
    act_sem, cot_sem, cent_sem, send_sem, recv_sem, esem, sem1, sem2, sem3,
):
    samp = lax.axis_index("samp")
    par = lax.axis_index("par")
    z, y = samp // NY, samp % NY
    x, core = par // 2, par % 2
    slot_here = y * NZ + z
    sibling = (samp, x * 2 + 1 - core)
    zs = [wrap(z + hop, NZ) for hop in range(NZ)]
    ys = [wrap(y + down, NY) for down in range(NY)]
    xs = [wrap(x + across, 4) for across in range(4)]
    partners = [(down, zs[hop] * NY + ys[down]) for down, hop in STEPS]
    sorted_partners = [
        item for item, (_, hop) in sorted(zip(partners, STEPS), key=lambda pair: -min(pair[1][1], NZ - pair[1][1]))
    ]
    chip = y * 4 + x
    others = [
        (ys[down] * 4 + xs[across], z * NY + ys[down], xs[across] * 2)
        for down, across in PLANE
    ]
    around = [(other, (row, pair + side), side) for other, row, pair in others for side in range(2)]

    def by_core(body):
        @pl.when(core == 0)
        def _():
            body(0, 128)

        @pl.when(core == 1)
        def _():
            body(1, NS)

    def act_copy(n):
        return pltpu.make_async_copy(act_hbm.at[n], act_ref.at[n], act_sem.at[n])

    def cot_copy(n):
        return pltpu.make_async_copy(cot_hbm.at[n], cot_ref.at[n], cot_sem.at[n])

    for n in range(LOCAL):
        act_copy(n).start()
        cot_copy(n).start()

    def remote(source, target, send, recv, device):
        return pltpu.make_async_remote_copy(
            src_ref=source,
            dst_ref=target,
            send_sem=send,
            recv_sem=recv,
            device_id=device,
            device_id_type=MESH,
        )

    barrier = pltpu.get_barrier_semaphore()
    greeted = 0
    for _, other in partners:
        pl.semaphore_signal(barrier, inc=1, device_id=(other, par), device_id_type=MESH)
        greeted += 1
    for down in range(NY):
        for across in range(4):
            for side in (core, 1 - core):
                if across > 0 or side is not core:
                    device = (z * NY + ys[down], xs[across] * 2 + side)
                    pl.semaphore_signal(barrier, inc=1, device_id=device, device_id_type=MESH)
                    greeted += 1

    first_half = lax.broadcasted_iota(jnp.int32, (3 * CH, 128), 1) < CH
    lhs[:, :, :, PADK - 128 :] = jnp.zeros((2, LAYERS, 3 * CH, 128), jnp.bfloat16)
    rhs[:, :, :, PADK - 128 :] = jnp.zeros((2, LAYERS, 4 * CH, 128), jnp.bfloat16)
    rhs[:, 1, 2 * CH : 3 * CH, :] = jnp.zeros((2, CH, PADK), jnp.bfloat16)
    for at, step in enumerate((-1, 1)):
        strip = jnp.where(edge_mask((8, SITES), step), 1.0, 0.0)
        edges[at] = jnp.concatenate([strip] * (CH // 8), axis=0).astype(jnp.bfloat16)

    def product(slot, layer, width):
        return lax.dot_general(
            lhs[slot, layer], rhs[slot, layer, :width], (((1,), (1,)), ((), ())),
            preferred_element_type=jnp.float32,
        )

    def compute(sample, slot):
        act_copy(sample).wait()
        cot_copy(sample).wait()
        for layer in range(LAYERS):
            act = act_ref[sample, layer]
            cot = cot_ref[sample, layer]
            for step in (-1, 0, 1):
                low = (step + 1) * CH
                edge = edges[max(step, 0)] > 0
                lhs[slot, layer, low : low + CH, :SITES] = column_shift(act, step, edge)
                low = RHS_ROWS[layer][step + 1] * CH
                rhs[slot, layer, low : low + CH, :SITES] = rolled(cot, -LAT * step)
        one = product(slot, 0, 3 * CH)
        two = product(slot, 1, 4 * CH)
        blocks = (
            jnp.where(first_half, one[:, :128], two[:, :128]),
            jnp.where(first_half, two[:, :128], one[:, :128]),
            jnp.where(first_half, jnp.concatenate([one[:, 128:], one[:, 128:]], axis=1), two[:, 128:]),
        )
        for down in range(3):
            wide_rows[pl.ds(down * 3 * CH * LOCAL + sample, 3 * CH, stride=LOCAL), :] = blocks[down]

    def two_samples(pair, carry):
        for slot in range(2):
            compute(pair * 2 + slot, slot)
        return carry

    lax.fori_loop(0, LOCAL // 2, two_samples, 0)

    def rounded(other):
        start = pl.multiple_of(other * CHUNK, CHUNK)
        return wide_rows[pl.ds(start, CHUNK), :].astype(jnp.bfloat16)

    pl.semaphore_wait(barrier, greeted)
    for down, other in sorted_partners:
        send_ref[other] = rounded(other)
        remote(
            send_ref.at[other], recv_ref.at[slot_here], send_sem, recv_sem.at[down], (other, par)
        ).start()

    flat = diagonal_energy(spin_ref[...])
    energy_ref[...] = jnp.zeros_like(energy_ref)
    energy_ref[:, :LOCAL] = flat[:, :LOCAL] + off_ref[...]
    for _, other in partners:
        remote(energy_ref, energies_ref.at[samp], esem.at[0], esem.at[1], (other, par)).start()
    energies_ref[samp] = energy_ref[...]
    recv_ref[slot_here] = rounded(samp)
    for down in range(NY):
        low = wrap(y + NY - down, NY) * NZ
        taken = recv_ref.at[pl.ds(0, NZ - 1)] if down == 0 else recv_ref.at[pl.ds(low, NZ)]
        remote(taken, taken, send_sem, recv_sem.at[down], sibling).wait_recv()

    for pair in range(ROWS // 2):
        tile = jnp.stack(
            [
                recv_ref[(src % NY) * NZ + src // NY, 16 * pair : 16 * pair + 16, :].astype(jnp.float32)
                for src in range(NSAMP)
            ]
        ).reshape(NSAMP, 2, LOCAL, 128)
        halves = []
        for half in range(2):
            part = tile[:, half]
            mean = jnp.sum(jnp.sum(part, axis=0), axis=0, keepdims=True) / NS
            cent = ((part - mean) / math.sqrt(NS)).reshape(NS, 128)
            halves.append(cent.astype(jnp.bfloat16))
        cent = jnp.concatenate(halves, axis=1)
        cent_ref[:, 256 * pair : 256 * pair + 256] = cent
        light = lax.dot_general(
            cent[:128], cent[:128], (((1,), (1,)), ((), ())), preferred_element_type=jnp.float32
        )
        heavy = lax.dot_general(
            cent[128:], cent, (((1,), (1,)), ((), ())), preferred_element_type=jnp.float32
        )
        if pair == 0:
            part_ref[:128, :128] = light
            part_ref[128:, :] = heavy
        else:
            part_ref[:128, :128] += light
            part_ref[128:, :] += heavy
    cent_copy = pltpu.make_async_copy(cent_ref, cent_hbm, cent_sem)
    cent_copy.start()

    def rows_of(side, index):
        return pl.ds(pl.multiple_of(side * 128 + index * 8, 8), 8)

    slot = core * CHIPS + chip
    widths = (128, NS)

    def send_first(other, device, side):
        wide = pl.ds(0, widths[side])
        remote(
            part_ref.at[rows_of(side, other), wide],
            first.at[slot, :, wide],
            sem1.at[side],
            sem1.at[2],
            device,
        ).start()

    for other, device, side in around:
        send_first(other, device, side)
    by_core(lambda side, width: send_first(chip, sibling, 1 - side))

    def middle(side, width):
        wide = pl.ds(0, width)
        first[slot, :, wide] = part_ref[rows_of(side, chip), wide]
        landed = first.at[pl.ds(0, 2 * CHIPS - 1), :, wide]
        remote(landed, landed, sem1.at[0], sem1.at[2], sibling).wait_recv()
        own = jnp.sum(first[:, :, wide], axis=0)
        mine[:, wide] = own
        for hop in (4, 3, 5, 2, 6, 1, 7):
            device = (zs[hop] * NY + y, par)
            remote(
                mine.at[:, wide], second.at[z, :, wide], sem2.at[0], sem2.at[1], device
            ).start()
        second[z, :, wide] = own
        landed = second.at[pl.ds(0, NZ - 1), :, wide]
        remote(landed, landed, sem2.at[0], sem2.at[1], sibling).wait_recv()
        block = rows_of(side, chip)
        gram_ref[block, wide] = jnp.sum(second[:, :, wide], axis=0)
        done = gram_ref.at[block, wide]
        for _, device, _ in around:
            remote(done, done, sem3.at[0], sem3.at[1 + side], device).start()
        remote(done, done, sem3.at[0], sem3.at[1 + side], sibling).start()

    by_core(middle)

    sent = send_ref.at[pl.ds(0, NSAMP - 1)]
    remote(sent, sent, send_sem, recv_sem.at[0], sibling).wait_send()
    energy_bytes = energies_ref.at[pl.ds(0, NSAMP - 1)]
    remote(energy_bytes, energy_bytes, esem.at[0], esem.at[1], sibling).wait()
    cent_copy.wait()

    def finish(side, width):
        wide = pl.ds(0, width)
        for kind in range(2):
            count = CHIPS - 1 if kind == side else CHIPS
            bytes_ref = gram_ref.at[pl.ds(0, count * 8), pl.ds(0, widths[kind])]
            remote(bytes_ref, bytes_ref, sem1.at[kind], sem3.at[1 + kind], sibling).wait()
        landed = second.at[pl.ds(0, NZ - 1), :, wide]
        remote(landed, landed, sem2.at[0], sem2.at[1], sibling).wait_send()
        landed = first.at[pl.ds(0, 2 * CHIPS - 1), :, wide]
        remote(landed, landed, sem3.at[0], sem1.at[2], sibling).wait_send()

    by_core(finish)


def main_call(activations, cotangents, spin_bits, off_row):
    whole = pl.BlockSpec(memory_space=VMEM)
    anywhere = pl.BlockSpec(memory_space=pl.ANY)
    dma = pltpu.SemaphoreType.DMA
    return pl.pallas_call(
        main_kernel,
        in_specs=[anywhere, anywhere, whole, whole],
        out_specs=[whole, anywhere, whole],
        out_shape=[
            jax.ShapeDtypeStruct((NS, NS), jnp.float32),
            jax.ShapeDtypeStruct((NS, WIDTH), jnp.bfloat16),
            jax.ShapeDtypeStruct((NSAMP, 1, 128), jnp.float32),
        ],
        scratch_shapes=[
            VMEM((LOCAL, LAYERS, CH, SITES), jnp.bfloat16),
            VMEM((LOCAL, LAYERS, CH, SITES), jnp.bfloat16),
            VMEM((2, CH, SITES), jnp.bfloat16),
            VMEM((2, LAYERS, 3 * CH, PADK), jnp.bfloat16),
            VMEM((2, LAYERS, 4 * CH, PADK), jnp.bfloat16),
            VMEM((NSAMP * CHUNK, 128), jnp.float32),
            VMEM((NSAMP, CHUNK, 128), jnp.bfloat16),
            VMEM((NSAMP, CHUNK, 128), jnp.bfloat16),
            VMEM((NS, WIDTH), jnp.bfloat16),
            VMEM((1, 128), jnp.float32),
            VMEM((NS, NS), jnp.float32),
            VMEM((2 * CHIPS, 8, NS), jnp.float32),
            VMEM((8, NS), jnp.float32),
            VMEM((NZ, 8, NS), jnp.float32),
            dma((LOCAL,)),
            dma((LOCAL,)),
            dma,
            dma,
            dma((NY,)),
            dma((2,)),
            dma((3,)),
            dma((2,)),
            dma((3,)),
        ],
        compiler_params=pltpu.CompilerParams(
            collective_id=0, has_side_effects=True, vmem_limit_bytes=VMEM_LIMIT
        ),
    )(activations, cotangents, spin_bits, off_row)


BLOCK = 64
PANEL = 8


def forward_block(diag, tile_ref, column_ref, cross_ref):
    eye = lax.broadcasted_iota(jnp.int32, (BLOCK, BLOCK), 0) == lax.broadcasted_iota(
        jnp.int32, (BLOCK, BLOCK), 1
    )
    wide = jnp.concatenate([diag, jnp.where(eye, 1.0, 0.0)], axis=1)
    count = BLOCK // PANEL
    tiles = [wide[8 * q : 8 * q + 8] for q in range(count)]
    sub = lax.broadcasted_iota(jnp.int32, (8, 128), 0)

    def lanes(tile, col):
        return jnp.broadcast_to(tile[:, col : col + 1], (8, 128))

    def joined(parts):
        total = parts[0]
        for i in range(1, PANEL):
            total = jnp.where(sub == i, parts[i], total)
        return total

    def broadcast_row(ref, panel, j, i):
        return ref[panel, j, pl.ds(i, 8, stride=0), :]

    reduced, scaled = [], []
    columns = [lanes(tiles[0], j) for j in range(PANEL)]
    for panel in range(count):
        base = panel * PANEL
        last = panel == count - 1
        tile_ref[panel, 0] = tiles[panel]
        for j in range(PANEL):
            column_ref[panel, j] = columns[j]
        low = {
            (i, j): broadcast_row(column_ref, panel, j, i)
            for i in range(PANEL)
            for j in range(i + 1)
        }
        rows = [broadcast_row(tile_ref, panel, 0, i) for i in range(PANEL)]
        old_columns = {
            q: [lanes(tiles[q], base + i) for i in range(PANEL)] for q in range(panel + 1, count)
        }
        if not last:
            cross = list(old_columns[panel + 1])
            columns = [lanes(tiles[panel + 1], base + PANEL + j) for j in range(PANEL)]
        ups, downs, starts, cross_scaled = {}, {}, {}, {}
        for p in range(0, PANEL, 2):
            q = p + 1
            a, b, c = low[p, p], low[q, p], low[q, q]
            recip = pl.reciprocal(a * c - b * b, approx=True)
            for i in range(q + 1, PANEL):
                up = c * low[i, p] - b * low[i, q]
                down = a * low[i, q] - b * low[i, p]
                for m in range(q + 1, i + 1):
                    low[i, m] = low[i, m] - (up * low[m, p] + down * low[m, q]) * recip
                ups[i, p], downs[i, p] = up * recip, down * recip
            if not last:
                cross_scaled[p] = (c * cross[p] - b * cross[q]) * recip
                cross_scaled[q] = (a * cross[q] - b * cross[p]) * recip
                for i in range(q + 1, PANEL):
                    cross[i] = cross[i] - (ups[i, p] * cross[p] + downs[i, p] * cross[q])
            starts[p] = (c * rows[p] - b * rows[q]) * recip
            starts[q] = (a * rows[q] - b * rows[p]) * recip
            for i in range(q + 1, PANEL):
                rows[i] = rows[i] - (ups[i, p] * rows[p] + downs[i, p] * rows[q])
        if not last:
            for i in range(PANEL):
                cross_ref[panel, i] = cross[i]
            for j in range(PANEL):
                terms = [
                    cross_scaled[i] * broadcast_row(cross_ref, panel, i, j) for i in range(PANEL)
                ]
                while len(terms) > 1:
                    terms = [terms[a] + terms[a + 1] for a in range(0, len(terms), 2)]
                columns[j] = columns[j] - terms[0]
        reduced.append(joined(rows))
        scaled.append(joined([starts[i] for i in range(PANEL)]))
        if last:
            break
        solved = [None] * PANEL
        for p in reversed(range(0, PANEL, 2)):
            for total, factor, at in ((starts[p], ups, p), (starts[p + 1], downs, p + 1)):
                for i in reversed(range(p + 2, PANEL)):
                    total = total - factor[i, p] * solved[i]
                solved[at] = total
        for q in range(panel + 1, count):
            terms = [old_columns[q][i] * solved[i] for i in range(PANEL)]
            while len(terms) > 1:
                terms = [terms[a] + terms[a + 1] for a in range(0, len(terms), 2)]
            tiles[q] = tiles[q] - terms[0]
    lower = jnp.concatenate(reduced, axis=0)[:, BLOCK:]
    return lower, jnp.concatenate(scaled, axis=0)[:, BLOCK:]


def product(one, two, first_dim, second_dim):
    return lax.dot_general(
        one, two, (((first_dim,), (second_dim,)), ((), ())),
        precision=HIGHEST, preferred_element_type=jnp.float32,
    )


def solve_kernel(
    gram_ref, energies_ref, cent_hbm, update_ref, coeff_ref,
    work, held, cent_ref, cent_sem, tile_ref, column_ref, cross_ref,
):
    cent_copy = pltpu.make_async_copy(cent_hbm, cent_ref, cent_sem)
    cent_copy.start()
    rows_iota = lax.broadcasted_iota(jnp.int32, (NS, NS), 0)
    cols_iota = lax.broadcasted_iota(jnp.int32, (NS, NS), 1)
    below = gram_ref[128:, :128]
    gram = jnp.concatenate(
        [jnp.concatenate([gram_ref[:128, :128], below.T], axis=1), gram_ref[128:, :]], axis=0
    )
    diagonal = rows_iota == cols_iota
    trace = jnp.sum(jnp.where(diagonal, gram, 0.0), keepdims=True)
    level = 1.0 / (trace / NS)
    pieces = jnp.broadcast_to(energies_ref[...], (NSAMP, LOCAL, 128)).reshape(NS, 128)
    lane = lax.broadcasted_iota(jnp.int32, (NS, 128), 1)
    row = lax.broadcasted_iota(jnp.int32, (NS, 128), 0)
    energy = jnp.sum(jnp.where(lane == jnp.bitwise_and(row, LOCAL - 1), pieces, 0.0), axis=1, keepdims=True)
    mean = jnp.sum(energy, axis=0, keepdims=True) / NS
    residual = -(energy - mean) / math.sqrt(NS)
    work[:, :NS] = gram * level + jnp.where(diagonal, 0.01, 0.0)
    work[:, NS:] = jnp.broadcast_to(residual, (NS, 128))

    for index in range(NS // BLOCK):
        low = index * BLOCK
        own = slice(low, low + BLOCK)
        rest = slice(128 * ((index + 1) // 2), NS + 128)
        lower, scaled = forward_block(work[own, own], tile_ref, column_ref, cross_ref)
        middle = product(scaled, work[own, rest], 1, 0)
        outer = product(work[:, own], lower, 1, 1)
        work[:, rest] = work[:, rest] - product(outer, middle, 1, 0)
        work[own, rest] = product(lower, middle, 0, 0)

    coeff = work[:, NS:] * level
    held[...] = coeff
    own = held[pl.ds(pl.multiple_of(lax.axis_index("samp") * LOCAL, LOCAL), LOCAL), :]
    here = lax.broadcasted_iota(jnp.int32, (LOCAL, 128), 0) == lax.broadcasted_iota(
        jnp.int32, (LOCAL, 128), 1
    )
    coeff_ref[...] = jnp.sum(jnp.where(here, own, 0.0), axis=0, keepdims=True)[:, :LOCAL]
    both = jnp.concatenate([coeff, coeff], axis=1)
    weighted = jnp.sum(gram * both, axis=0, keepdims=True)
    across = jnp.sum(jnp.where(diagonal, both, 0.0), axis=0, keepdims=True)
    square_total = jnp.sum(weighted * across, keepdims=True)
    scale = lax.rsqrt(square_total / ENTRIES + 1e-06)
    first = lax.broadcasted_iota(jnp.int32, (1, 128), 1) < CH
    cent_copy.wait()
    for pair in range(ROWS // 2):
        parts = []
        for half in range(2):
            column = 128 * (2 * pair + half)
            cent = cent_ref[:, column : column + 128].astype(jnp.float32)
            parts.append(jnp.sum(cent * coeff, axis=0, keepdims=True) * scale)
        turned = [jnp.concatenate([item[:, CH:], item[:, :CH]], axis=1) for item in parts]
        for half in range(2):
            at = lax.axis_index("samp") * ROWS + 2 * pair + half
            swapped = jnp.logical_and(at >= 3 * CH, at < 6 * CH)
            parts[half], turned[half] = (
                jnp.where(swapped, turned[half], parts[half]),
                jnp.where(swapped, parts[half], turned[half]),
            )
        update_ref[0:1, 128 * pair : 128 * pair + 128] = jnp.where(first, parts[0], turned[1])
        update_ref[1:2, 128 * pair : 128 * pair + 128] = jnp.where(first, turned[0], parts[1])


def solve_call(gram, energies, cent):
    whole = pl.BlockSpec(memory_space=VMEM)
    return pl.pallas_call(
        solve_kernel,
        in_specs=[whole, whole, pl.BlockSpec(memory_space=pl.ANY)],
        out_specs=[whole, whole],
        out_shape=[
            jax.ShapeDtypeStruct((LAYERS, ROWS * CH), jnp.float32),
            jax.ShapeDtypeStruct((1, LOCAL), jnp.float32),
        ],
        scratch_shapes=[
            VMEM((NS, NS + 128), jnp.float32),
            VMEM((NS, 128), jnp.float32),
            VMEM((NS, WIDTH), jnp.bfloat16),
            pltpu.SemaphoreType.DMA,
            VMEM((BLOCK // PANEL, 1, 8, 128), jnp.float32),
            VMEM((BLOCK // PANEL, PANEL, 8, 128), jnp.float32),
            VMEM((BLOCK // PANEL, PANEL, 8, 128), jnp.float32),
        ],
        compiler_params=pltpu.CompilerParams(vmem_limit_bytes=VMEM_LIMIT),
    )(gram, energies, cent)


def on_device(activations, cotangents, spin_bits, offdiag_energy):
    gram, cent, energies = main_call(
        activations, cotangents, spin_bits, offdiag_energy.reshape(1, LOCAL)
    )
    update, coeff = solve_call(gram, energies, cent)
    return update, coeff.reshape(LOCAL)


def solution(mesh):
    in_specs = (
        P("samp", "par", None, None),
        P("samp", "par", None, None),
        P("samp", None),
        P("samp"),
    )
    out_specs = (P("par", "samp"), P("samp"))
    return jax.shard_map(
        on_device, mesh=mesh, in_specs=in_specs, out_specs=out_specs, check_vma=False
    )
```

```python
import math

import jax
import jax.numpy as jnp
from jax import lax
from jax.experimental import pallas as pl
from jax.experimental.pallas import tpu as pltpu
from jax.sharding import PartitionSpec as P

CH = 64
KK = 9
LAT = 24
SITES = LAT * LAT
NSAMP = 32
NPAR = 8
NZ = 8
NY = 4
LOCAL = 8
NS = NSAMP * LOCAL
ROWS = KK * CH // NSAMP
CHUNK = ROWS * LOCAL
WIDTH = ROWS * 128
PADK = 640
LAYERS = 2
ENTRIES = 16 * KK * CH * CH
MESH = pl.DeviceIdType.MESH
VMEM_LIMIT = 56 * 1024 * 1024
HIGHEST = lax.Precision.HIGHEST
VMEM = pltpu.VMEM


def rolled(value, amount):
    amount = amount % SITES
    if amount == 0:
        return value
    return jnp.concatenate([value[:, amount:], value[:, :amount]], axis=1)


def edge_mask(shape, col_step):
    column = lax.broadcasted_iota(jnp.int32, shape, 1) % LAT
    return column == (LAT - 1 if col_step > 0 else 0)


def column_shift(value, col_step, edge):
    if col_step == 0:
        return value
    return jnp.where(edge, rolled(value, col_step - LAT * col_step), rolled(value, col_step))


def wrap(value, size):
    return lax.select(value >= size, value - size, value)


STEPS = [(down, hop) for down in range(NY) for hop in (1, 7, 2, 6, 3, 5, 4, 0) if (down, hop) != (0, 0)]


def diagonal_energy(spin_bits):
    spin = (2 * spin_bits - 1).astype(jnp.float32)
    right = column_shift(spin, 1, edge_mask(spin.shape, 1))
    left = column_shift(spin, -1, edge_mask(spin.shape, -1))
    pairs = spin * rolled(spin, LAT) + spin * right
    corners = spin * rolled(right, LAT) + spin * rolled(left, LAT)
    diag = 0.25 * jnp.sum(pairs + 0.5 * corners, axis=1, keepdims=True)
    wide = jnp.broadcast_to(diag, (LOCAL, 128))
    here = lax.broadcasted_iota(jnp.int32, (LOCAL, 128), 0) == lax.broadcasted_iota(
        jnp.int32, (LOCAL, 128), 1
    )
    return jnp.sum(jnp.where(here, wide, 0.0), axis=0, keepdims=True)


PLANE = sorted(
    ((down, across) for down in range(NY) for across in range(4) if (down, across) != (0, 0)),
    key=lambda step: -(min(step[0], NY - step[0]) + min(step[1], 4 - step[1])),
)
RHS_ROWS = ((0, 1, 2), (1, 0, 3))
CHIPS = 16


BLOCK = 64
PANEL = 8


def forward_block(diag, tile_ref, column_ref, cross_ref):
    eye = lax.broadcasted_iota(jnp.int32, (BLOCK, BLOCK), 0) == lax.broadcasted_iota(
        jnp.int32, (BLOCK, BLOCK), 1
    )
    wide = jnp.concatenate([diag, jnp.where(eye, 1.0, 0.0)], axis=1)
    count = BLOCK // PANEL
    tiles = [wide[8 * q : 8 * q + 8] for q in range(count)]
    sub = lax.broadcasted_iota(jnp.int32, (8, 128), 0)

    def lanes(tile, col):
        return jnp.broadcast_to(tile[:, col : col + 1], (8, 128))

    def joined(parts):
        total = parts[0]
        for i in range(1, PANEL):
            total = jnp.where(sub == i, parts[i], total)
        return total

    def broadcast_row(ref, panel, j, i):
        return ref[panel, j, pl.ds(i, 8, stride=0), :]

    reduced, scaled = [], []
    columns = [lanes(tiles[0], j) for j in range(PANEL)]
    for panel in range(count):
        base = panel * PANEL
        last = panel == count - 1
        tile_ref[panel, 0] = tiles[panel]
        for j in range(PANEL):
            column_ref[panel, j] = columns[j]
        low = {
            (i, j): broadcast_row(column_ref, panel, j, i)
            for i in range(PANEL)
            for j in range(i + 1)
        }
        rows = [broadcast_row(tile_ref, panel, 0, i) for i in range(PANEL)]
        old_columns = {
            q: [lanes(tiles[q], base + i) for i in range(PANEL)] for q in range(panel + 1, count)
        }
        if not last:
            cross = list(old_columns[panel + 1])
            columns = [lanes(tiles[panel + 1], base + PANEL + j) for j in range(PANEL)]
        ups, downs, starts, cross_scaled = {}, {}, {}, {}
        for p in range(0, PANEL, 2):
            q = p + 1
            a, b, c = low[p, p], low[q, p], low[q, q]
            recip = pl.reciprocal(a * c - b * b, approx=True)
            for i in range(q + 1, PANEL):
                up = c * low[i, p] - b * low[i, q]
                down = a * low[i, q] - b * low[i, p]
                for m in range(q + 1, i + 1):
                    low[i, m] = low[i, m] - (up * low[m, p] + down * low[m, q]) * recip
                ups[i, p], downs[i, p] = up * recip, down * recip
            if not last:
                cross_scaled[p] = (c * cross[p] - b * cross[q]) * recip
                cross_scaled[q] = (a * cross[q] - b * cross[p]) * recip
                for i in range(q + 1, PANEL):
                    cross[i] = cross[i] - (ups[i, p] * cross[p] + downs[i, p] * cross[q])
            starts[p] = (c * rows[p] - b * rows[q]) * recip
            starts[q] = (a * rows[q] - b * rows[p]) * recip
            for i in range(q + 1, PANEL):
                rows[i] = rows[i] - (ups[i, p] * rows[p] + downs[i, p] * rows[q])
        if not last:
            for i in range(PANEL):
                cross_ref[panel, i] = cross[i]
            for j in range(PANEL):
                terms = [
                    cross_scaled[i] * broadcast_row(cross_ref, panel, i, j) for i in range(PANEL)
                ]
                while len(terms) > 1:
                    terms = [terms[a] + terms[a + 1] for a in range(0, len(terms), 2)]
                columns[j] = columns[j] - terms[0]
        reduced.append(joined(rows))
        scaled.append(joined([starts[i] for i in range(PANEL)]))
        if last:
            break
        solved = [None] * PANEL
        for p in reversed(range(0, PANEL, 2)):
            for total, factor, at in ((starts[p], ups, p), (starts[p + 1], downs, p + 1)):
                for i in reversed(range(p + 2, PANEL)):
                    total = total - factor[i, p] * solved[i]
                solved[at] = total
        for q in range(panel + 1, count):
            terms = [old_columns[q][i] * solved[i] for i in range(PANEL)]
            while len(terms) > 1:
                terms = [terms[a] + terms[a + 1] for a in range(0, len(terms), 2)]
            tiles[q] = tiles[q] - terms[0]
    lower = jnp.concatenate(reduced, axis=0)[:, BLOCK:]
    return lower, jnp.concatenate(scaled, axis=0)[:, BLOCK:]


def product(one, two, first_dim, second_dim):
    return lax.dot_general(
        one, two, (((first_dim,), (second_dim,)), ((), ())),
        precision=HIGHEST, preferred_element_type=jnp.float32,
    )


def main_kernel(
    act_hbm, cot_hbm, spin_ref, off_ref,
    update_ref, coeff_ref, scale_ref,
    act_ref, cot_ref, edges, lhs, rhs, wide_rows, send_ref, recv_ref, cent_ref,
    energy_ref, energies_ref, part_ref, first, mine, second, gram_ref,
    work, held, tile_ref, column_ref, cross_ref,
    act_sem, cot_sem, send_sem, recv_sem, esem, sem1, sem2, sem3,
):
    samp = lax.axis_index("samp")
    par = lax.axis_index("par")
    z, y = samp // NY, samp % NY
    x, core = par // 2, par % 2
    slot_here = y * NZ + z
    sibling = (samp, x * 2 + 1 - core)
    zs = [wrap(z + hop, NZ) for hop in range(NZ)]
    ys = [wrap(y + down, NY) for down in range(NY)]
    xs = [wrap(x + across, 4) for across in range(4)]
    partners = [(down, zs[hop] * NY + ys[down]) for down, hop in STEPS]
    sorted_partners = [
        item for item, (_, hop) in sorted(zip(partners, STEPS), key=lambda pair: -min(pair[1][1], NZ - pair[1][1]))
    ]
    chip = y * 4 + x
    others = [
        (ys[down] * 4 + xs[across], z * NY + ys[down], xs[across] * 2)
        for down, across in PLANE
    ]
    around = [(other, (row, pair + side), side) for other, row, pair in others for side in range(2)]

    def by_core(body):
        @pl.when(core == 0)
        def _():
            body(0, 128)

        @pl.when(core == 1)
        def _():
            body(1, NS)

    def act_copy(n):
        return pltpu.make_async_copy(act_hbm.at[n], act_ref.at[n], act_sem.at[n])

    def cot_copy(n):
        return pltpu.make_async_copy(cot_hbm.at[n], cot_ref.at[n], cot_sem.at[n])

    for n in range(LOCAL):
        act_copy(n).start()
        cot_copy(n).start()

    def remote(source, target, send, recv, device):
        return pltpu.make_async_remote_copy(
            src_ref=source,
            dst_ref=target,
            send_sem=send,
            recv_sem=recv,
            device_id=device,
            device_id_type=MESH,
        )

    barrier = pltpu.get_barrier_semaphore()
    greeted = 0
    for _, other in partners:
        pl.semaphore_signal(barrier, inc=1, device_id=(other, par), device_id_type=MESH)
        greeted += 1
    for down in range(NY):
        for across in range(4):
            for side in (core, 1 - core):
                if across > 0 or side is not core:
                    device = (z * NY + ys[down], xs[across] * 2 + side)
                    pl.semaphore_signal(barrier, inc=1, device_id=device, device_id_type=MESH)
                    greeted += 1

    first_half = lax.broadcasted_iota(jnp.int32, (3 * CH, 128), 1) < CH
    lhs[:, :, :, PADK - 128 :] = jnp.zeros((2, LAYERS, 3 * CH, 128), jnp.bfloat16)
    rhs[:, :, :, PADK - 128 :] = jnp.zeros((2, LAYERS, 4 * CH, 128), jnp.bfloat16)
    rhs[:, 1, 2 * CH : 3 * CH, :] = jnp.zeros((2, CH, PADK), jnp.bfloat16)
    for at, step in enumerate((-1, 1)):
        strip = jnp.where(edge_mask((8, SITES), step), 1.0, 0.0)
        edges[at] = jnp.concatenate([strip] * (CH // 8), axis=0).astype(jnp.bfloat16)

    def taps(slot, layer, width):
        return lax.dot_general(
            lhs[slot, layer], rhs[slot, layer, :width], (((1,), (1,)), ((), ())),
            preferred_element_type=jnp.float32,
        )

    def compute(sample, slot):
        act_copy(sample).wait()
        cot_copy(sample).wait()
        for layer in range(LAYERS):
            act = act_ref[sample, layer]
            cot = cot_ref[sample, layer]
            for step in (-1, 0, 1):
                low = (step + 1) * CH
                edge = edges[max(step, 0)] > 0
                lhs[slot, layer, low : low + CH, :SITES] = column_shift(act, step, edge)
                low = RHS_ROWS[layer][step + 1] * CH
                rhs[slot, layer, low : low + CH, :SITES] = rolled(cot, -LAT * step)
        one = taps(slot, 0, 3 * CH)
        two = taps(slot, 1, 4 * CH)
        blocks = (
            jnp.where(first_half, one[:, :128], two[:, :128]),
            jnp.where(first_half, two[:, :128], one[:, :128]),
            jnp.where(first_half, jnp.concatenate([one[:, 128:], one[:, 128:]], axis=1), two[:, 128:]),
        )
        for down in range(3):
            wide_rows[pl.ds(down * 3 * CH * LOCAL + sample, 3 * CH, stride=LOCAL), :] = blocks[down]

    def two_samples(pair, carry):
        for slot in range(2):
            compute(pair * 2 + slot, slot)
        return carry

    lax.fori_loop(0, LOCAL // 2, two_samples, 0)

    def rounded(other):
        start = pl.multiple_of(other * CHUNK, CHUNK)
        return wide_rows[pl.ds(start, CHUNK), :].astype(jnp.bfloat16)

    pl.semaphore_wait(barrier, greeted)
    for down, other in sorted_partners:
        send_ref[other] = rounded(other)
        remote(
            send_ref.at[other], recv_ref.at[slot_here], send_sem, recv_sem.at[down], (other, par)
        ).start()

    flat = diagonal_energy(spin_ref[...])
    energy_ref[...] = jnp.zeros_like(energy_ref)
    energy_ref[:, :LOCAL] = flat[:, :LOCAL] + off_ref[...]
    for _, other in partners:
        remote(energy_ref, energies_ref.at[samp], esem.at[0], esem.at[1], (other, par)).start()
    energies_ref[samp] = energy_ref[...]
    recv_ref[slot_here] = rounded(samp)
    for down in range(NY):
        low = wrap(y + NY - down, NY) * NZ
        taken = recv_ref.at[pl.ds(0, NZ - 1)] if down == 0 else recv_ref.at[pl.ds(low, NZ)]
        remote(taken, taken, send_sem, recv_sem.at[down], sibling).wait_recv()

    for pair in range(ROWS // 2):
        tile = jnp.stack(
            [
                recv_ref[(src % NY) * NZ + src // NY, 16 * pair : 16 * pair + 16, :].astype(jnp.float32)
                for src in range(NSAMP)
            ]
        ).reshape(NSAMP, 2, LOCAL, 128)
        halves = []
        for half in range(2):
            part = tile[:, half]
            mean = jnp.sum(jnp.sum(part, axis=0), axis=0, keepdims=True) / NS
            cent = ((part - mean) / math.sqrt(NS)).reshape(NS, 128)
            halves.append(cent.astype(jnp.bfloat16))
        cent = jnp.concatenate(halves, axis=1)
        cent_ref[:, 256 * pair : 256 * pair + 256] = cent
        light = lax.dot_general(
            cent[:128], cent[:128], (((1,), (1,)), ((), ())), preferred_element_type=jnp.float32
        )
        heavy = lax.dot_general(
            cent[128:], cent, (((1,), (1,)), ((), ())), preferred_element_type=jnp.float32
        )
        if pair == 0:
            part_ref[:128, :128] = light
            part_ref[128:, :] = heavy
        else:
            part_ref[:128, :128] += light
            part_ref[128:, :] += heavy
    eye = lax.broadcasted_iota(jnp.int32, (128, 128), 0) == lax.broadcasted_iota(
        jnp.int32, (128, 128), 1
    )
    trace = jnp.sum(
        jnp.where(eye, part_ref[:128, :128] + part_ref[128:, 128:], 0.0), keepdims=True
    )
    corner = jnp.logical_and(
        lax.broadcasted_iota(jnp.int32, (8, 128), 0) == 0,
        lax.broadcasted_iota(jnp.int32, (8, 128), 1) == 127,
    )
    part_ref[:8, :128] = jnp.where(corner, trace, part_ref[:8, :128])

    def rows_of(side, index):
        return pl.ds(pl.multiple_of(side * 128 + index * 8, 8), 8)

    slot = core * CHIPS + chip
    widths = (128, NS)

    def send_first(other, device, side):
        wide = pl.ds(0, widths[side])
        remote(
            part_ref.at[rows_of(side, other), wide],
            first.at[slot, :, wide],
            sem1.at[side],
            sem1.at[2],
            device,
        ).start()

    for other, device, side in around:
        send_first(other, device, side)
    by_core(lambda side, width: send_first(chip, sibling, 1 - side))

    def middle(side, width):
        wide = pl.ds(0, width)
        first[slot, :, wide] = part_ref[rows_of(side, chip), wide]
        landed = first.at[pl.ds(0, 2 * CHIPS - 1), :, wide]
        remote(landed, landed, sem1.at[0], sem1.at[2], sibling).wait_recv()
        own = jnp.sum(first[:, :, wide], axis=0)
        mine[:, wide] = own
        for hop in (4, 3, 5, 2, 6, 1, 7):
            device = (zs[hop] * NY + y, par)
            remote(
                mine.at[:, wide], second.at[z, :, wide], sem2.at[0], sem2.at[1], device
            ).start()
        second[z, :, wide] = own
        landed = second.at[pl.ds(0, NZ - 1), :, wide]
        remote(landed, landed, sem2.at[0], sem2.at[1], sibling).wait_recv()
        block = rows_of(side, chip)
        gram_ref[block, wide] = jnp.sum(second[:, :, wide], axis=0)
        done = gram_ref.at[block, wide]
        kind = 1 + y // 2 if side == 0 else 3
        for _, device, _ in around:
            remote(done, done, sem3.at[0], sem3.at[kind], device).start()
        remote(done, done, sem3.at[0], sem3.at[kind], sibling).start()

    by_core(middle)

    def await_rows(kind, count, width, own_kind):
        for less in range(2):

            @pl.when(own_kind if less else jnp.logical_not(own_kind))
            def _(less=less):
                landed = gram_ref.at[pl.ds(0, (count - less) * 8), pl.ds(0, width)]
                remote(landed, landed, sem3.at[0], sem3.at[kind], sibling).wait_recv()

    await_rows(1, 8, 128, jnp.logical_and(core == 0, y < 2))
    level = 1.0 / (gram_ref[0:1, 127:128] / NS)
    block_eye = lax.broadcasted_iota(jnp.int32, (BLOCK, BLOCK), 0) == lax.broadcasted_iota(
        jnp.int32, (BLOCK, BLOCK), 1
    )
    leading = gram_ref[:BLOCK, :BLOCK] * level + jnp.where(block_eye, 0.01, 0.0)
    factors = forward_block(leading, tile_ref, column_ref, cross_ref)
    energy_bytes = energies_ref.at[pl.ds(0, NSAMP - 1)]
    remote(energy_bytes, energy_bytes, esem.at[0], esem.at[1], sibling).wait()
    await_rows(2, 8, 128, jnp.logical_and(core == 0, y >= 2))
    await_rows(3, CHIPS, NS, core == 1)

    below = gram_ref[128:, :128]
    above = gram_ref[:128, :128]
    wide_corner = jnp.logical_and(
        lax.broadcasted_iota(jnp.int32, (128, 128), 0) == 0,
        lax.broadcasted_iota(jnp.int32, (128, 128), 1) == 127,
    )
    above = jnp.where(wide_corner, gram_ref[127:128, 0:1], above)
    gram = jnp.concatenate(
        [jnp.concatenate([above, below.T], axis=1), gram_ref[128:, :]], axis=0
    )
    diagonal = lax.broadcasted_iota(jnp.int32, (NS, NS), 0) == lax.broadcasted_iota(
        jnp.int32, (NS, NS), 1
    )
    pieces = jnp.broadcast_to(energies_ref[...], (NSAMP, LOCAL, 128)).reshape(NS, 128)
    lane = lax.broadcasted_iota(jnp.int32, (NS, 128), 1)
    row = lax.broadcasted_iota(jnp.int32, (NSAMP, LOCAL, 128), 1).reshape(NS, 128)
    energy = jnp.sum(jnp.where(lane == row, pieces, 0.0), axis=1, keepdims=True)
    mean = jnp.sum(energy, axis=0, keepdims=True) / NS
    residual = -(energy - mean) / math.sqrt(NS)
    work[:, :NS] = gram * level + jnp.where(diagonal, 0.01, 0.0)
    work[:, NS:] = jnp.broadcast_to(residual, (NS, 128))

    for index in range(NS // BLOCK):
        low = index * BLOCK
        own = slice(low, low + BLOCK)
        rest = slice(128 * ((index + 1) // 2), NS + 128)
        if index > 0:
            factors = forward_block(work[own, own], tile_ref, column_ref, cross_ref)
        lower, scaled = factors
        middle_rows = product(scaled, work[own, rest], 1, 0)
        outer = product(work[:, own], lower, 1, 1)
        work[:, rest] = work[:, rest] - product(outer, middle_rows, 1, 0)
        work[own, rest] = product(lower, middle_rows, 0, 0)

    coeff = work[:, NS:] * level
    held[...] = coeff
    own = held[pl.ds(pl.multiple_of(samp * LOCAL, LOCAL), LOCAL), :]
    here = lax.broadcasted_iota(jnp.int32, (LOCAL, 128), 0) == lax.broadcasted_iota(
        jnp.int32, (LOCAL, 128), 1
    )
    coeff_ref[...] = jnp.sum(jnp.where(here, own, 0.0), axis=0, keepdims=True)
    both = jnp.concatenate([coeff, coeff], axis=1)
    weighted = jnp.sum(gram * both, axis=0, keepdims=True)
    across = jnp.sum(jnp.where(diagonal, both, 0.0), axis=0, keepdims=True)
    square_total = jnp.sum(weighted * across, keepdims=True)
    scale_ref[...] = jnp.broadcast_to(lax.rsqrt(square_total / ENTRIES + 1e-06), (1, 128))
    left = lax.broadcasted_iota(jnp.int32, (1, 128), 1) < CH
    for pair in range(ROWS // 2):
        parts = []
        for half in range(2):
            column = 128 * (2 * pair + half)
            cent = cent_ref[:, column : column + 128].astype(jnp.float32)
            parts.append(jnp.sum(cent * coeff, axis=0, keepdims=True))
        turned = [jnp.concatenate([item[:, CH:], item[:, :CH]], axis=1) for item in parts]
        for half in range(2):
            at = samp * ROWS + 2 * pair + half
            swapped = jnp.logical_and(at >= 3 * CH, at < 6 * CH)
            parts[half], turned[half] = (
                jnp.where(swapped, turned[half], parts[half]),
                jnp.where(swapped, parts[half], turned[half]),
            )
        update_ref[0:1, 128 * pair : 128 * pair + 128] = jnp.where(left, parts[0], turned[1])
        update_ref[1:2, 128 * pair : 128 * pair + 128] = jnp.where(left, turned[0], parts[1])

    sent = send_ref.at[pl.ds(0, NSAMP - 1)]
    remote(sent, sent, send_sem, recv_sem.at[0], sibling).wait_send()

    def finish(side, width):
        wide = pl.ds(0, width)
        for kind in range(2):
            count = CHIPS - 1 if kind == side else CHIPS
            bytes_ref = gram_ref.at[pl.ds(0, count * 8), pl.ds(0, widths[kind])]
            remote(bytes_ref, bytes_ref, sem1.at[kind], sem1.at[2], sibling).wait_send()
        landed = second.at[pl.ds(0, NZ - 1), :, wide]
        remote(landed, landed, sem2.at[0], sem2.at[1], sibling).wait_send()
        landed = first.at[pl.ds(0, 2 * CHIPS - 1), :, wide]
        remote(landed, landed, sem3.at[0], sem1.at[2], sibling).wait_send()

    by_core(finish)


def main_call(activations, cotangents, spin_bits, off_row):
    whole = pl.BlockSpec(memory_space=VMEM)
    anywhere = pl.BlockSpec(memory_space=pl.ANY)
    dma = pltpu.SemaphoreType.DMA
    return pl.pallas_call(
        main_kernel,
        in_specs=[anywhere, anywhere, whole, whole],
        out_specs=[whole, whole, whole],
        out_shape=[
            jax.ShapeDtypeStruct((LAYERS, ROWS * CH), jnp.float32),
            jax.ShapeDtypeStruct((1, 128), jnp.float32),
            jax.ShapeDtypeStruct((1, 128), jnp.float32),
        ],
        scratch_shapes=[
            VMEM((LOCAL, LAYERS, CH, SITES), jnp.bfloat16),
            VMEM((LOCAL, LAYERS, CH, SITES), jnp.bfloat16),
            VMEM((2, CH, SITES), jnp.bfloat16),
            VMEM((2, LAYERS, 3 * CH, PADK), jnp.bfloat16),
            VMEM((2, LAYERS, 4 * CH, PADK), jnp.bfloat16),
            VMEM((NSAMP * CHUNK, 128), jnp.float32),
            VMEM((NSAMP, CHUNK, 128), jnp.bfloat16),
            VMEM((NSAMP, CHUNK, 128), jnp.bfloat16),
            VMEM((NS, WIDTH), jnp.bfloat16),
            VMEM((1, 128), jnp.float32),
            VMEM((NSAMP, 1, 128), jnp.float32),
            VMEM((NS, NS), jnp.float32),
            VMEM((2 * CHIPS, 8, NS), jnp.float32),
            VMEM((8, NS), jnp.float32),
            VMEM((NZ, 8, NS), jnp.float32),
            VMEM((NS, NS), jnp.float32),
            VMEM((NS, NS + 128), jnp.float32),
            VMEM((NS, 128), jnp.float32),
            VMEM((BLOCK // PANEL, 1, 8, 128), jnp.float32),
            VMEM((BLOCK // PANEL, PANEL, 8, 128), jnp.float32),
            VMEM((BLOCK // PANEL, PANEL, 8, 128), jnp.float32),
            dma((LOCAL,)),
            dma((LOCAL,)),
            dma,
            dma((NY,)),
            dma((2,)),
            dma((3,)),
            dma((2,)),
            dma((4,)),
        ],
        compiler_params=pltpu.CompilerParams(
            collective_id=0, has_side_effects=True, vmem_limit_bytes=VMEM_LIMIT
        ),
    )(activations, cotangents, spin_bits, off_row)


def scale_kernel(raw_ref, coeff_in, scale_ref, update_ref, coeff_ref):
    update_ref[...] = raw_ref[...] * scale_ref[:, :1]
    coeff_ref[...] = coeff_in[:, :LOCAL]


def scale_call(raw, coeff, scale):
    return pl.pallas_call(
        scale_kernel,
        out_shape=[
            jax.ShapeDtypeStruct((LAYERS, ROWS * CH), jnp.float32),
            jax.ShapeDtypeStruct((1, LOCAL), jnp.float32),
        ],
    )(raw, coeff, scale)


def on_device(activations, cotangents, spin_bits, offdiag_energy):
    raw, coeff_row, scale = main_call(
        activations, cotangents, spin_bits, offdiag_energy.reshape(1, LOCAL)
    )
    update, coeff = scale_call(raw, coeff_row, scale)
    return update, coeff.reshape(LOCAL)


def solution(mesh):
    in_specs = (
        P("samp", "par", None, None),
        P("samp", "par", None, None),
        P("samp", None),
        P("samp"),
    )
    out_specs = (P("par", "samp"), P("samp"))
    return jax.shard_map(
        on_device, mesh=mesh, in_specs=in_specs, out_specs=out_specs, check_vma=False
    )
```

```python
import math

import jax
import jax.numpy as jnp
from jax import lax
from jax.experimental import pallas as pl
from jax.experimental.pallas import tpu as pltpu
from jax.sharding import PartitionSpec as P

CH = 64
KK = 9
LAT = 24
SITES = LAT * LAT
NSAMP = 32
NPAR = 8
NZ = 8
NY = 4
LOCAL = 8
NS = NSAMP * LOCAL
ROWS = KK * CH // NSAMP
CHUNK = ROWS * LOCAL
WIDTH = ROWS * 128
PADK = 640
LAYERS = 2
ENTRIES = 16 * KK * CH * CH
MESH = pl.DeviceIdType.MESH
VMEM_LIMIT = 56 * 1024 * 1024
HIGHEST = lax.Precision.HIGHEST
VMEM = pltpu.VMEM


def rolled(value, amount):
    amount = amount % SITES
    if amount == 0:
        return value
    return jnp.concatenate([value[:, amount:], value[:, :amount]], axis=1)


def edge_mask(shape, col_step):
    column = lax.broadcasted_iota(jnp.int32, shape, 1) % LAT
    return column == (LAT - 1 if col_step > 0 else 0)


def column_shift(value, col_step, edge):
    if col_step == 0:
        return value
    return jnp.where(edge, rolled(value, col_step - LAT * col_step), rolled(value, col_step))


def wrap(value, size):
    return lax.select(value >= size, value - size, value)


STEPS = [(down, hop) for down in range(NY) for hop in (1, 7, 2, 6, 3, 5, 4, 0) if (down, hop) != (0, 0)]


def diagonal_energy(spin_bits):
    spin = (2 * spin_bits - 1).astype(jnp.float32)
    right = column_shift(spin, 1, edge_mask(spin.shape, 1))
    left = column_shift(spin, -1, edge_mask(spin.shape, -1))
    pairs = spin * rolled(spin, LAT) + spin * right
    corners = spin * rolled(right, LAT) + spin * rolled(left, LAT)
    diag = 0.25 * jnp.sum(pairs + 0.5 * corners, axis=1, keepdims=True)
    wide = jnp.broadcast_to(diag, (LOCAL, 128))
    here = lax.broadcasted_iota(jnp.int32, (LOCAL, 128), 0) == lax.broadcasted_iota(
        jnp.int32, (LOCAL, 128), 1
    )
    return jnp.sum(jnp.where(here, wide, 0.0), axis=0, keepdims=True)


PLANE = sorted(
    ((down, across) for down in range(NY) for across in range(4) if (down, across) != (0, 0)),
    key=lambda step: -(min(step[0], NY - step[0]) + min(step[1], 4 - step[1])),
)
RHS_ROWS = ((0, 1, 2), (1, 0, 3))
CHIPS = 16


BLOCK = 64
PANEL = 8


def forward_block(diag, tile_ref, column_ref, cross_ref):
    eye = lax.broadcasted_iota(jnp.int32, (BLOCK, BLOCK), 0) == lax.broadcasted_iota(
        jnp.int32, (BLOCK, BLOCK), 1
    )
    wide = jnp.concatenate([diag, jnp.where(eye, 1.0, 0.0)], axis=1)
    count = BLOCK // PANEL
    tiles = [wide[8 * q : 8 * q + 8] for q in range(count)]
    sub = lax.broadcasted_iota(jnp.int32, (8, 128), 0)

    def lanes(tile, col):
        return jnp.broadcast_to(tile[:, col : col + 1], (8, 128))

    def joined(parts):
        total = parts[0]
        for i in range(1, PANEL):
            total = jnp.where(sub == i, parts[i], total)
        return total

    def broadcast_row(ref, panel, j, i):
        return ref[panel, j, pl.ds(i, 8, stride=0), :]

    reduced, scaled = [], []
    columns = [lanes(tiles[0], j) for j in range(PANEL)]
    for panel in range(count):
        base = panel * PANEL
        last = panel == count - 1
        tile_ref[panel, 0] = tiles[panel]
        for j in range(PANEL):
            column_ref[panel, j] = columns[j]
        low = {
            (i, j): broadcast_row(column_ref, panel, j, i)
            for i in range(PANEL)
            for j in range(i + 1)
        }
        rows = [broadcast_row(tile_ref, panel, 0, i) for i in range(PANEL)]
        old_columns = {
            q: [lanes(tiles[q], base + i) for i in range(PANEL)] for q in range(panel + 1, count)
        }
        if not last:
            cross = list(old_columns[panel + 1])
            columns = [lanes(tiles[panel + 1], base + PANEL + j) for j in range(PANEL)]
        ups, downs, starts, cross_scaled = {}, {}, {}, {}
        for p in range(0, PANEL, 2):
            q = p + 1
            a, b, c = low[p, p], low[q, p], low[q, q]
            recip = pl.reciprocal(a * c - b * b, approx=True)
            for i in range(q + 1, PANEL):
                up = c * low[i, p] - b * low[i, q]
                down = a * low[i, q] - b * low[i, p]
                for m in range(q + 1, i + 1):
                    low[i, m] = low[i, m] - (up * low[m, p] + down * low[m, q]) * recip
                ups[i, p], downs[i, p] = up * recip, down * recip
            if not last:
                cross_scaled[p] = (c * cross[p] - b * cross[q]) * recip
                cross_scaled[q] = (a * cross[q] - b * cross[p]) * recip
                for i in range(q + 1, PANEL):
                    cross[i] = cross[i] - (ups[i, p] * cross[p] + downs[i, p] * cross[q])
            starts[p] = (c * rows[p] - b * rows[q]) * recip
            starts[q] = (a * rows[q] - b * rows[p]) * recip
            for i in range(q + 1, PANEL):
                rows[i] = rows[i] - (ups[i, p] * rows[p] + downs[i, p] * rows[q])
        if not last:
            for i in range(PANEL):
                cross_ref[panel, i] = cross[i]
            for j in range(PANEL):
                terms = [
                    cross_scaled[i] * broadcast_row(cross_ref, panel, i, j) for i in range(PANEL)
                ]
                while len(terms) > 1:
                    terms = [terms[a] + terms[a + 1] for a in range(0, len(terms), 2)]
                columns[j] = columns[j] - terms[0]
        reduced.append(joined(rows))
        scaled.append(joined([starts[i] for i in range(PANEL)]))
        if last:
            break
        solved = [None] * PANEL
        for p in reversed(range(0, PANEL, 2)):
            for total, factor, at in ((starts[p], ups, p), (starts[p + 1], downs, p + 1)):
                for i in reversed(range(p + 2, PANEL)):
                    total = total - factor[i, p] * solved[i]
                solved[at] = total
        for q in range(panel + 1, count):
            terms = [old_columns[q][i] * solved[i] for i in range(PANEL)]
            while len(terms) > 1:
                terms = [terms[a] + terms[a + 1] for a in range(0, len(terms), 2)]
            tiles[q] = tiles[q] - terms[0]
    lower = jnp.concatenate(reduced, axis=0)[:, BLOCK:]
    return lower, jnp.concatenate(scaled, axis=0)[:, BLOCK:]


def product(one, two, first_dim, second_dim):
    return lax.dot_general(
        one, two, (((first_dim,), (second_dim,)), ((), ())),
        precision=HIGHEST, preferred_element_type=jnp.float32,
    )


def main_kernel(
    act_hbm, cot_hbm, spin_ref, off_ref,
    update_ref, coeff_ref,
    act_ref, cot_ref, edges, lhs, rhs, wide_rows, send_ref, recv_ref, cent_ref,
    energy_ref, energies_ref, part_ref, first, mine, second, gram_ref,
    work, held, tile_ref, column_ref, cross_ref,
    act_sem, cot_sem, send_sem, recv_sem, esem, sem1, sem2, sem3,
):
    samp = lax.axis_index("samp")
    par = lax.axis_index("par")
    z, y = samp // NY, samp % NY
    x, core = par // 2, par % 2
    slot_here = y * NZ + z
    sibling = (samp, x * 2 + 1 - core)
    zs = [wrap(z + hop, NZ) for hop in range(NZ)]
    ys = [wrap(y + down, NY) for down in range(NY)]
    xs = [wrap(x + across, 4) for across in range(4)]
    partners = [(down, zs[hop] * NY + ys[down]) for down, hop in STEPS]
    sorted_partners = [
        item for item, (_, hop) in sorted(zip(partners, STEPS), key=lambda pair: -min(pair[1][1], NZ - pair[1][1]))
    ]
    chip = y * 4 + x
    others = [
        (ys[down] * 4 + xs[across], z * NY + ys[down], xs[across] * 2)
        for down, across in PLANE
    ]
    around = [(other, (row, pair + side), side) for other, row, pair in others for side in range(2)]

    def by_core(body):
        @pl.when(core == 0)
        def _():
            body(0, 128)

        @pl.when(core == 1)
        def _():
            body(1, NS)

    def act_copy(n):
        return pltpu.make_async_copy(act_hbm.at[n], act_ref.at[n], act_sem.at[n])

    def cot_copy(n):
        return pltpu.make_async_copy(cot_hbm.at[n], cot_ref.at[n], cot_sem.at[n])

    for n in range(LOCAL):
        act_copy(n).start()
        cot_copy(n).start()

    def remote(source, target, send, recv, device):
        return pltpu.make_async_remote_copy(
            src_ref=source,
            dst_ref=target,
            send_sem=send,
            recv_sem=recv,
            device_id=device,
            device_id_type=MESH,
        )

    barrier = pltpu.get_barrier_semaphore()
    greeted = 0
    for _, other in partners:
        pl.semaphore_signal(barrier, inc=1, device_id=(other, par), device_id_type=MESH)
        greeted += 1
    for down in range(NY):
        for across in range(4):
            for side in (core, 1 - core):
                if across > 0 or side is not core:
                    device = (z * NY + ys[down], xs[across] * 2 + side)
                    pl.semaphore_signal(barrier, inc=1, device_id=device, device_id_type=MESH)
                    greeted += 1

    first_half = lax.broadcasted_iota(jnp.int32, (3 * CH, 128), 1) < CH
    lhs[:, :, :, PADK - 128 :] = jnp.zeros((2, LAYERS, 3 * CH, 128), jnp.bfloat16)
    rhs[:, :, :, PADK - 128 :] = jnp.zeros((2, LAYERS, 4 * CH, 128), jnp.bfloat16)
    rhs[:, 1, 2 * CH : 3 * CH, :] = jnp.zeros((2, CH, PADK), jnp.bfloat16)
    for at, step in enumerate((-1, 1)):
        strip = jnp.where(edge_mask((8, SITES), step), 1.0, 0.0)
        edges[at] = jnp.concatenate([strip] * (CH // 8), axis=0).astype(jnp.bfloat16)

    def taps(slot, layer, width):
        return lax.dot_general(
            lhs[slot, layer], rhs[slot, layer, :width], (((1,), (1,)), ((), ())),
            preferred_element_type=jnp.float32,
        )

    def compute(sample, slot):
        act_copy(sample).wait()
        cot_copy(sample).wait()
        for layer in range(LAYERS):
            act = act_ref[sample, layer]
            cot = cot_ref[sample, layer]
            for step in (-1, 0, 1):
                low = (step + 1) * CH
                edge = edges[max(step, 0)] > 0
                lhs[slot, layer, low : low + CH, :SITES] = column_shift(act, step, edge)
                low = RHS_ROWS[layer][step + 1] * CH
                rhs[slot, layer, low : low + CH, :SITES] = rolled(cot, -LAT * step)
        one = taps(slot, 0, 3 * CH)
        two = taps(slot, 1, 4 * CH)
        blocks = (
            jnp.where(first_half, one[:, :128], two[:, :128]),
            jnp.where(first_half, two[:, :128], one[:, :128]),
            jnp.where(first_half, jnp.concatenate([one[:, 128:], one[:, 128:]], axis=1), two[:, 128:]),
        )
        for down in range(3):
            wide_rows[pl.ds(down * 3 * CH * LOCAL + sample, 3 * CH, stride=LOCAL), :] = blocks[down]

    def two_samples(pair, carry):
        for slot in range(2):
            compute(pair * 2 + slot, slot)
        return carry

    lax.fori_loop(0, LOCAL // 2, two_samples, 0)

    def rounded(other):
        start = pl.multiple_of(other * CHUNK, CHUNK)
        return wide_rows[pl.ds(start, CHUNK), :].astype(jnp.bfloat16)

    pl.semaphore_wait(barrier, greeted)
    for down, other in sorted_partners:
        send_ref[other] = rounded(other)
        remote(
            send_ref.at[other], recv_ref.at[slot_here], send_sem, recv_sem.at[down], (other, par)
        ).start()

    flat = diagonal_energy(spin_ref[...])
    energy_ref[...] = jnp.zeros_like(energy_ref)
    energy_ref[:, :LOCAL] = flat[:, :LOCAL] + off_ref[...]
    for _, other in partners:
        remote(energy_ref, energies_ref.at[samp], esem.at[0], esem.at[1], (other, par)).start()
    energies_ref[samp] = energy_ref[...]
    recv_ref[slot_here] = rounded(samp)
    for down in range(NY):
        low = wrap(y + NY - down, NY) * NZ
        taken = recv_ref.at[pl.ds(0, NZ - 1)] if down == 0 else recv_ref.at[pl.ds(low, NZ)]
        remote(taken, taken, send_sem, recv_sem.at[down], sibling).wait_recv()

    for pair in range(ROWS // 2):
        tile = jnp.stack(
            [
                recv_ref[(src % NY) * NZ + src // NY, 16 * pair : 16 * pair + 16, :].astype(jnp.float32)
                for src in range(NSAMP)
            ]
        ).reshape(NSAMP, 2, LOCAL, 128)
        halves = []
        for half in range(2):
            part = tile[:, half]
            mean = jnp.sum(jnp.sum(part, axis=0), axis=0, keepdims=True) / NS
            cent = ((part - mean) / math.sqrt(NS)).reshape(NS, 128)
            halves.append(cent.astype(jnp.bfloat16))
        cent = jnp.concatenate(halves, axis=1)
        cent_ref[:, 256 * pair : 256 * pair + 256] = cent
        light = lax.dot_general(
            cent[:128], cent[:128], (((1,), (1,)), ((), ())), preferred_element_type=jnp.float32
        )
        heavy = lax.dot_general(
            cent[128:], cent, (((1,), (1,)), ((), ())), preferred_element_type=jnp.float32
        )
        if pair == 0:
            part_ref[:128, :128] = light
            part_ref[128:, :] = heavy
        else:
            part_ref[:128, :128] += light
            part_ref[128:, :] += heavy
    eye = lax.broadcasted_iota(jnp.int32, (128, 128), 0) == lax.broadcasted_iota(
        jnp.int32, (128, 128), 1
    )
    trace = jnp.sum(
        jnp.where(eye, part_ref[:128, :128] + part_ref[128:, 128:], 0.0), keepdims=True
    )
    corner = jnp.logical_and(
        lax.broadcasted_iota(jnp.int32, (8, 128), 0) == 0,
        lax.broadcasted_iota(jnp.int32, (8, 128), 1) == 127,
    )
    part_ref[:8, :128] = jnp.where(corner, trace, part_ref[:8, :128])

    def rows_of(side, index):
        return pl.ds(pl.multiple_of(side * 128 + index * 8, 8), 8)

    slot = core * CHIPS + chip
    widths = (128, NS)

    def send_first(other, device, side):
        wide = pl.ds(0, widths[side])
        remote(
            part_ref.at[rows_of(side, other), wide],
            first.at[slot, :, wide],
            sem1.at[side],
            sem1.at[2],
            device,
        ).start()

    by_core(lambda side, width: send_first(chip, sibling, 0) if side == 1 else None)
    for kind in range(2):
        for other, device, side in around:
            if side == kind:
                send_first(other, device, side)
    by_core(lambda side, width: send_first(chip, sibling, 1) if side == 0 else None)

    def middle(side, width):
        wide = pl.ds(0, width)
        first[slot, :, wide] = part_ref[rows_of(side, chip), wide]
        landed = first.at[pl.ds(0, 2 * CHIPS - 1), :, wide]
        remote(landed, landed, sem1.at[0], sem1.at[2], sibling).wait_recv()
        own = jnp.sum(first[:, :, wide], axis=0)
        mine[:, wide] = own
        for hop in (4, 3, 5, 2, 6, 1, 7):
            device = (zs[hop] * NY + y, par)
            remote(
                mine.at[:, wide], second.at[z, :, wide], sem2.at[0], sem2.at[1], device
            ).start()
        second[z, :, wide] = own
        landed = second.at[pl.ds(0, NZ - 1), :, wide]
        remote(landed, landed, sem2.at[0], sem2.at[1], sibling).wait_recv()
        block = rows_of(side, chip)
        gram_ref[block, wide] = jnp.sum(second[:, :, wide], axis=0)
        done = gram_ref.at[block, wide]
        kind = 1 + y // 2 if side == 0 else 3
        for _, device, _ in around:
            remote(done, done, sem3.at[0], sem3.at[kind], device).start()
        remote(done, done, sem3.at[0], sem3.at[kind], sibling).start()

    by_core(middle)

    def await_rows(kind, count, width, own_kind):
        for less in range(2):

            @pl.when(own_kind if less else jnp.logical_not(own_kind))
            def _(less=less):
                landed = gram_ref.at[pl.ds(0, (count - less) * 8), pl.ds(0, width)]
                remote(landed, landed, sem3.at[0], sem3.at[kind], sibling).wait_recv()

    await_rows(1, 8, 128, jnp.logical_and(core == 0, y < 2))
    level = 1.0 / (gram_ref[0:1, 127:128] / NS)
    block_eye = lax.broadcasted_iota(jnp.int32, (BLOCK, BLOCK), 0) == lax.broadcasted_iota(
        jnp.int32, (BLOCK, BLOCK), 1
    )
    leading = gram_ref[:BLOCK, :BLOCK] * level + jnp.where(block_eye, 0.01, 0.0)
    factors = forward_block(leading, tile_ref, column_ref, cross_ref)
    energy_bytes = energies_ref.at[pl.ds(0, NSAMP - 1)]
    remote(energy_bytes, energy_bytes, esem.at[0], esem.at[1], sibling).wait()
    await_rows(2, 8, 128, jnp.logical_and(core == 0, y >= 2))
    await_rows(3, CHIPS, NS, core == 1)

    below = gram_ref[128:, :128]
    above = gram_ref[:128, :128]
    wide_corner = jnp.logical_and(
        lax.broadcasted_iota(jnp.int32, (128, 128), 0) == 0,
        lax.broadcasted_iota(jnp.int32, (128, 128), 1) == 127,
    )
    above = jnp.where(wide_corner, gram_ref[127:128, 0:1], above)
    gram = jnp.concatenate(
        [jnp.concatenate([above, below.T], axis=1), gram_ref[128:, :]], axis=0
    )
    diagonal = lax.broadcasted_iota(jnp.int32, (NS, NS), 0) == lax.broadcasted_iota(
        jnp.int32, (NS, NS), 1
    )
    pieces = jnp.broadcast_to(energies_ref[...], (NSAMP, LOCAL, 128)).reshape(NS, 128)
    lane = lax.broadcasted_iota(jnp.int32, (NS, 128), 1)
    row = lax.broadcasted_iota(jnp.int32, (NSAMP, LOCAL, 128), 1).reshape(NS, 128)
    energy = jnp.sum(jnp.where(lane == row, pieces, 0.0), axis=1, keepdims=True)
    mean = jnp.sum(energy, axis=0, keepdims=True) / NS
    residual = -(energy - mean) / math.sqrt(NS)
    work[:, :NS] = gram * level + jnp.where(diagonal, 0.01, 0.0)
    work[:, NS:] = jnp.broadcast_to(residual, (NS, 128))

    for index in range(NS // BLOCK):
        low = index * BLOCK
        own = slice(low, low + BLOCK)
        rest = slice(128 * ((index + 1) // 2), NS + 128)
        if index > 0:
            factors = forward_block(work[own, own], tile_ref, column_ref, cross_ref)
        lower, scaled = factors
        middle_rows = product(scaled, work[own, rest], 1, 0)
        outer = product(work[:, own], lower, 1, 1)
        work[:, rest] = work[:, rest] - product(outer, middle_rows, 1, 0)
        work[own, rest] = product(lower, middle_rows, 0, 0)

    coeff = work[:, NS:] * level
    held[...] = coeff
    own = held[pl.ds(pl.multiple_of(samp * LOCAL, LOCAL), LOCAL), :]
    here = lax.broadcasted_iota(jnp.int32, (LOCAL, 128), 0) == lax.broadcasted_iota(
        jnp.int32, (LOCAL, 128), 1
    )
    coeff_ref[...] = jnp.sum(jnp.where(here, own, 0.0), axis=0, keepdims=True)[:, :LOCAL]
    both = jnp.concatenate([coeff, coeff], axis=1)
    weighted = jnp.sum(gram * both, axis=0, keepdims=True)
    across = jnp.sum(jnp.where(diagonal, both, 0.0), axis=0, keepdims=True)
    square_total = jnp.sum(weighted * across, keepdims=True)
    scale = lax.rsqrt(square_total / ENTRIES + 1e-06)
    left = lax.broadcasted_iota(jnp.int32, (1, 128), 1) < CH
    for pair in range(ROWS // 2):
        parts = []
        for half in range(2):
            column = 128 * (2 * pair + half)
            cent = cent_ref[:, column : column + 128].astype(jnp.float32)
            parts.append(jnp.sum(cent * coeff, axis=0, keepdims=True) * scale)
        turned = [jnp.concatenate([item[:, CH:], item[:, :CH]], axis=1) for item in parts]
        for half in range(2):
            at = samp * ROWS + 2 * pair + half
            swapped = jnp.logical_and(at >= 3 * CH, at < 6 * CH)
            parts[half], turned[half] = (
                jnp.where(swapped, turned[half], parts[half]),
                jnp.where(swapped, parts[half], turned[half]),
            )
        update_ref[0:1, 128 * pair : 128 * pair + 128] = jnp.where(left, parts[0], turned[1])
        update_ref[1:2, 128 * pair : 128 * pair + 128] = jnp.where(left, turned[0], parts[1])

    sent = send_ref.at[pl.ds(0, NSAMP - 1)]
    remote(sent, sent, send_sem, recv_sem.at[0], sibling).wait_send()

    def finish(side, width):
        wide = pl.ds(0, width)
        for kind in range(2):
            count = CHIPS - 1 if kind == side else CHIPS
            bytes_ref = gram_ref.at[pl.ds(0, count * 8), pl.ds(0, widths[kind])]
            remote(bytes_ref, bytes_ref, sem1.at[kind], sem1.at[2], sibling).wait_send()
        landed = second.at[pl.ds(0, NZ - 1), :, wide]
        remote(landed, landed, sem2.at[0], sem2.at[1], sibling).wait_send()
        landed = first.at[pl.ds(0, 2 * CHIPS - 1), :, wide]
        remote(landed, landed, sem3.at[0], sem1.at[2], sibling).wait_send()

    by_core(finish)


def main_call(activations, cotangents, spin_bits, off_row):
    whole = pl.BlockSpec(memory_space=VMEM)
    anywhere = pl.BlockSpec(memory_space=pl.ANY)
    dma = pltpu.SemaphoreType.DMA
    return pl.pallas_call(
        main_kernel,
        in_specs=[anywhere, anywhere, whole, whole],
        out_specs=[whole, whole],
        out_shape=[
            jax.ShapeDtypeStruct((LAYERS, ROWS * CH), jnp.float32),
            jax.ShapeDtypeStruct((1, LOCAL), jnp.float32),
        ],
        scratch_shapes=[
            VMEM((LOCAL, LAYERS, CH, SITES), jnp.bfloat16),
            VMEM((LOCAL, LAYERS, CH, SITES), jnp.bfloat16),
            VMEM((2, CH, SITES), jnp.bfloat16),
            VMEM((2, LAYERS, 3 * CH, PADK), jnp.bfloat16),
            VMEM((2, LAYERS, 4 * CH, PADK), jnp.bfloat16),
            VMEM((NSAMP * CHUNK, 128), jnp.float32),
            VMEM((NSAMP, CHUNK, 128), jnp.bfloat16),
            VMEM((NSAMP, CHUNK, 128), jnp.bfloat16),
            VMEM((NS, WIDTH), jnp.bfloat16),
            VMEM((1, 128), jnp.float32),
            VMEM((NSAMP, 1, 128), jnp.float32),
            VMEM((NS, NS), jnp.float32),
            VMEM((2 * CHIPS, 8, NS), jnp.float32),
            VMEM((8, NS), jnp.float32),
            VMEM((NZ, 8, NS), jnp.float32),
            VMEM((NS, NS), jnp.float32),
            VMEM((NS, NS + 128), jnp.float32),
            VMEM((NS, 128), jnp.float32),
            VMEM((BLOCK // PANEL, 1, 8, 128), jnp.float32),
            VMEM((BLOCK // PANEL, PANEL, 8, 128), jnp.float32),
            VMEM((BLOCK // PANEL, PANEL, 8, 128), jnp.float32),
            dma((LOCAL,)),
            dma((LOCAL,)),
            dma,
            dma((NY,)),
            dma((2,)),
            dma((3,)),
            dma((2,)),
            dma((4,)),
        ],
        compiler_params=pltpu.CompilerParams(
            collective_id=0, has_side_effects=True, vmem_limit_bytes=VMEM_LIMIT
        ),
    )(activations, cotangents, spin_bits, off_row)


def hand_on_kernel(update_in, coeff_in, update_ref, coeff_ref, sems):
    copies = [
        pltpu.make_async_copy(update_in, update_ref, sems.at[0]),
        pltpu.make_async_copy(coeff_in, coeff_ref, sems.at[1]),
    ]
    for copy in copies:
        copy.start()
    for copy in copies:
        copy.wait()


def hand_on(update, coeff):
    anywhere = pl.BlockSpec(memory_space=pl.ANY)
    return pl.pallas_call(
        hand_on_kernel,
        in_specs=[anywhere, anywhere],
        out_specs=[anywhere, anywhere],
        out_shape=[
            jax.ShapeDtypeStruct((LAYERS, ROWS * CH), jnp.float32),
            jax.ShapeDtypeStruct((1, LOCAL), jnp.float32),
        ],
        scratch_shapes=[pltpu.SemaphoreType.DMA((2,))],
        compiler_params=pltpu.CompilerParams(vmem_limit_bytes=VMEM_LIMIT),
    )(update, coeff)


def on_device(activations, cotangents, spin_bits, offdiag_energy):
    update, coeff = hand_on(
        *main_call(activations, cotangents, spin_bits, offdiag_energy.reshape(1, LOCAL))
    )
    return update, coeff.reshape(LOCAL)


def solution(mesh):
    in_specs = (
        P("samp", "par", None, None),
        P("samp", "par", None, None),
        P("samp", None),
        P("samp"),
    )
    out_specs = (P("par", "samp"), P("samp"))
    return jax.shard_map(
        on_device, mesh=mesh, in_specs=in_specs, out_specs=out_specs, check_vma=False
    )
```

```python
import math

import jax
import jax.numpy as jnp
from jax import lax
from jax.experimental import pallas as pl
from jax.experimental.pallas import tpu as pltpu
from jax.sharding import PartitionSpec as P

CH = 64
KK = 9
LAT = 24
SITES = LAT * LAT
NSAMP = 32
NPAR = 8
NZ = 8
NY = 4
LOCAL = 8
NS = NSAMP * LOCAL
ROWS = KK * CH // NSAMP
CHUNK = ROWS * LOCAL
WIDTH = ROWS * 128
PADK = 640
LAYERS = 2
ENTRIES = 16 * KK * CH * CH
MESH = pl.DeviceIdType.MESH
VMEM_LIMIT = 56 * 1024 * 1024
HIGHEST = lax.Precision.HIGHEST
VMEM = pltpu.VMEM


def rolled(value, amount):
    amount = amount % SITES
    if amount == 0:
        return value
    return jnp.concatenate([value[:, amount:], value[:, :amount]], axis=1)


def edge_mask(shape, col_step):
    column = lax.broadcasted_iota(jnp.int32, shape, 1) % LAT
    return column == (LAT - 1 if col_step > 0 else 0)


def column_shift(value, col_step, edge):
    if col_step == 0:
        return value
    return jnp.where(edge, rolled(value, col_step - LAT * col_step), rolled(value, col_step))


def wrap(value, size):
    return lax.select(value >= size, value - size, value)


STEPS = [(down, hop) for down in range(NY) for hop in (1, 7, 2, 6, 3, 5, 4, 0) if (down, hop) != (0, 0)]


def diagonal_energy(spin_bits):
    spin = (2 * spin_bits - 1).astype(jnp.float32)
    right = column_shift(spin, 1, edge_mask(spin.shape, 1))
    left = column_shift(spin, -1, edge_mask(spin.shape, -1))
    pairs = spin * rolled(spin, LAT) + spin * right
    corners = spin * rolled(right, LAT) + spin * rolled(left, LAT)
    diag = 0.25 * jnp.sum(pairs + 0.5 * corners, axis=1, keepdims=True)
    wide = jnp.broadcast_to(diag, (LOCAL, 128))
    here = lax.broadcasted_iota(jnp.int32, (LOCAL, 128), 0) == lax.broadcasted_iota(
        jnp.int32, (LOCAL, 128), 1
    )
    return jnp.sum(jnp.where(here, wide, 0.0), axis=0, keepdims=True)


PLANE = sorted(
    ((down, across) for down in range(NY) for across in range(4) if (down, across) != (0, 0)),
    key=lambda step: -(min(step[0], NY - step[0]) + min(step[1], 4 - step[1])),
)
RHS_ROWS = ((0, 1, 2), (1, 0, 3))
CHIPS = 16


BLOCK = 64
PANEL = 8


def forward_block(diag, tile_ref, column_ref, cross_ref):
    eye = lax.broadcasted_iota(jnp.int32, (BLOCK, BLOCK), 0) == lax.broadcasted_iota(
        jnp.int32, (BLOCK, BLOCK), 1
    )
    wide = jnp.concatenate([diag, jnp.where(eye, 1.0, 0.0)], axis=1)
    count = BLOCK // PANEL
    tiles = [wide[8 * q : 8 * q + 8] for q in range(count)]
    sub = lax.broadcasted_iota(jnp.int32, (8, 128), 0)

    def lanes(tile, col):
        return jnp.broadcast_to(tile[:, col : col + 1], (8, 128))

    def joined(parts):
        total = parts[0]
        for i in range(1, PANEL):
            total = jnp.where(sub == i, parts[i], total)
        return total

    def broadcast_row(ref, panel, j, i):
        return ref[panel, j, pl.ds(i, 8, stride=0), :]

    reduced, scaled = [], []
    columns = [lanes(tiles[0], j) for j in range(PANEL)]
    for panel in range(count):
        base = panel * PANEL
        last = panel == count - 1
        tile_ref[panel, 0] = tiles[panel]
        for j in range(PANEL):
            column_ref[panel, j] = columns[j]
        low = {
            (i, j): broadcast_row(column_ref, panel, j, i)
            for i in range(PANEL)
            for j in range(i + 1)
        }
        rows = [broadcast_row(tile_ref, panel, 0, i) for i in range(PANEL)]
        old_columns = {
            q: [lanes(tiles[q], base + i) for i in range(PANEL)] for q in range(panel + 1, count)
        }
        if not last:
            cross = list(old_columns[panel + 1])
            columns = [lanes(tiles[panel + 1], base + PANEL + j) for j in range(PANEL)]
        ups, downs, starts, cross_scaled = {}, {}, {}, {}
        for p in range(0, PANEL, 2):
            q = p + 1
            a, b, c = low[p, p], low[q, p], low[q, q]
            recip = pl.reciprocal(a * c - b * b, approx=True)
            for i in range(q + 1, PANEL):
                up = c * low[i, p] - b * low[i, q]
                down = a * low[i, q] - b * low[i, p]
                for m in range(q + 1, i + 1):
                    low[i, m] = low[i, m] - (up * low[m, p] + down * low[m, q]) * recip
                ups[i, p], downs[i, p] = up * recip, down * recip
            if not last:
                cross_scaled[p] = (c * cross[p] - b * cross[q]) * recip
                cross_scaled[q] = (a * cross[q] - b * cross[p]) * recip
                for i in range(q + 1, PANEL):
                    cross[i] = cross[i] - (ups[i, p] * cross[p] + downs[i, p] * cross[q])
            starts[p] = (c * rows[p] - b * rows[q]) * recip
            starts[q] = (a * rows[q] - b * rows[p]) * recip
            for i in range(q + 1, PANEL):
                rows[i] = rows[i] - (ups[i, p] * rows[p] + downs[i, p] * rows[q])
        if not last:
            for i in range(PANEL):
                cross_ref[panel, i] = cross[i]
            for j in range(PANEL):
                terms = [
                    cross_scaled[i] * broadcast_row(cross_ref, panel, i, j) for i in range(PANEL)
                ]
                while len(terms) > 1:
                    terms = [terms[a] + terms[a + 1] for a in range(0, len(terms), 2)]
                columns[j] = columns[j] - terms[0]
        reduced.append(joined(rows))
        scaled.append(joined([starts[i] for i in range(PANEL)]))
        if last:
            break
        solved = [None] * PANEL
        for p in reversed(range(0, PANEL, 2)):
            for total, factor, at in ((starts[p], ups, p), (starts[p + 1], downs, p + 1)):
                for i in reversed(range(p + 2, PANEL)):
                    total = total - factor[i, p] * solved[i]
                solved[at] = total
        for q in range(panel + 1, count):
            terms = [old_columns[q][i] * solved[i] for i in range(PANEL)]
            while len(terms) > 1:
                terms = [terms[a] + terms[a + 1] for a in range(0, len(terms), 2)]
            tiles[q] = tiles[q] - terms[0]
    lower = jnp.concatenate(reduced, axis=0)[:, BLOCK:]
    return lower, jnp.concatenate(scaled, axis=0)[:, BLOCK:]


def product(one, two, first_dim, second_dim):
    return lax.dot_general(
        one, two, (((first_dim,), (second_dim,)), ((), ())),
        precision=HIGHEST, preferred_element_type=jnp.float32,
    )


def main_kernel(
    act_hbm, cot_hbm, spin_ref, off_ref,
    update_ref, coeff_ref,
    act_ref, cot_ref, edges, lhs, rhs, wide_rows, send_ref, recv_ref, cent_ref,
    energy_ref, relay_ref, energies_ref, part_ref, first, mine, second, gram_ref,
    work, held, tile_ref, column_ref, cross_ref,
    act_sem, cot_sem, send_sem, recv_sem, esem, relay_sem, sem1, sem2, sem3,
):
    samp = lax.axis_index("samp")
    par = lax.axis_index("par")
    z, y = samp // NY, samp % NY
    x, core = par // 2, par % 2
    slot_here = y * NZ + z
    sibling = (samp, x * 2 + 1 - core)
    zs = [wrap(z + hop, NZ) for hop in range(NZ)]
    ys = [wrap(y + down, NY) for down in range(NY)]
    xs = [wrap(x + across, 4) for across in range(4)]
    partners = [(down, zs[hop] * NY + ys[down]) for down, hop in STEPS]
    sorted_partners = [
        item for item, (_, hop) in sorted(zip(partners, STEPS), key=lambda pair: -min(pair[1][1], NZ - pair[1][1]))
    ]
    chip = y * 4 + x
    others = [
        (ys[down] * 4 + xs[across], z * NY + ys[down], xs[across] * 2)
        for down, across in PLANE
    ]
    around = [(other, (row, pair + side), side) for other, row, pair in others for side in range(2)]

    def by_core(body):
        @pl.when(core == 0)
        def _():
            body(0, 128)

        @pl.when(core == 1)
        def _():
            body(1, NS)

    def act_copy(n):
        return pltpu.make_async_copy(act_hbm.at[n], act_ref.at[n], act_sem.at[n])

    def cot_copy(n):
        return pltpu.make_async_copy(cot_hbm.at[n], cot_ref.at[n], cot_sem.at[n])

    for n in range(LOCAL):
        act_copy(n).start()
        cot_copy(n).start()

    def remote(source, target, send, recv, device):
        return pltpu.make_async_remote_copy(
            src_ref=source,
            dst_ref=target,
            send_sem=send,
            recv_sem=recv,
            device_id=device,
            device_id_type=MESH,
        )

    barrier = pltpu.get_barrier_semaphore()
    greeted = 0
    for _, other in partners:
        pl.semaphore_signal(barrier, inc=1, device_id=(other, par), device_id_type=MESH)
        greeted += 1
    for down in range(NY):
        for across in range(4):
            for side in (core, 1 - core):
                if across > 0 or side is not core:
                    device = (z * NY + ys[down], xs[across] * 2 + side)
                    pl.semaphore_signal(barrier, inc=1, device_id=device, device_id_type=MESH)
                    greeted += 1

    first_half = lax.broadcasted_iota(jnp.int32, (3 * CH, 128), 1) < CH
    lhs[:, :, :, PADK - 128 :] = jnp.zeros((2, LAYERS, 3 * CH, 128), jnp.bfloat16)
    rhs[:, :, :, PADK - 128 :] = jnp.zeros((2, LAYERS, 4 * CH, 128), jnp.bfloat16)
    rhs[:, 1, 2 * CH : 3 * CH, :] = jnp.zeros((2, CH, PADK), jnp.bfloat16)
    for at, step in enumerate((-1, 1)):
        strip = jnp.where(edge_mask((8, SITES), step), 1.0, 0.0)
        edges[at] = jnp.concatenate([strip] * (CH // 8), axis=0).astype(jnp.bfloat16)

    def taps(slot, layer, width):
        return lax.dot_general(
            lhs[slot, layer], rhs[slot, layer, :width], (((1,), (1,)), ((), ())),
            preferred_element_type=jnp.float32,
        )

    def compute(sample, slot):
        act_copy(sample).wait()
        cot_copy(sample).wait()
        for layer in range(LAYERS):
            act = act_ref[sample, layer]
            cot = cot_ref[sample, layer]
            for step in (-1, 0, 1):
                low = (step + 1) * CH
                edge = edges[max(step, 0)] > 0
                lhs[slot, layer, low : low + CH, :SITES] = column_shift(act, step, edge)
                low = RHS_ROWS[layer][step + 1] * CH
                rhs[slot, layer, low : low + CH, :SITES] = rolled(cot, -LAT * step)
        one = taps(slot, 0, 3 * CH)
        two = taps(slot, 1, 4 * CH)
        blocks = (
            jnp.where(first_half, one[:, :128], two[:, :128]),
            jnp.where(first_half, two[:, :128], one[:, :128]),
            jnp.where(first_half, jnp.concatenate([one[:, 128:], one[:, 128:]], axis=1), two[:, 128:]),
        )
        for down in range(3):
            wide_rows[pl.ds(down * 3 * CH * LOCAL + sample, 3 * CH, stride=LOCAL), :] = blocks[down]

    def two_samples(pair, carry):
        for slot in range(2):
            compute(pair * 2 + slot, slot)
        return carry

    lax.fori_loop(0, LOCAL // 2, two_samples, 0)

    def rounded(other):
        start = pl.multiple_of(other * CHUNK, CHUNK)
        return wide_rows[pl.ds(start, CHUNK), :].astype(jnp.bfloat16)

    pl.semaphore_wait(barrier, greeted)
    for down, other in sorted_partners[:NY]:
        via = zs[2] if down < 2 else zs[6]
        send_ref[other] = rounded(other)
        remote(
            send_ref.at[other], relay_ref.at[down], send_sem, relay_sem, (via * NY + y, par)
        ).start()
    for number, (down, other) in enumerate(sorted_partners[NY:]):
        if number == 13:
            remote(relay_ref, relay_ref, send_sem, relay_sem, sibling).wait_recv()
            for turn in range(NY):
                origin, goal = (zs[6], zs[2]) if turn < 2 else (zs[2], zs[6])
                remote(
                    relay_ref.at[turn],
                    recv_ref.at[y * NZ + origin],
                    send_sem,
                    recv_sem.at[turn],
                    (goal * NY + ys[turn], par),
                ).start()
        send_ref[other] = rounded(other)
        remote(
            send_ref.at[other], recv_ref.at[slot_here], send_sem, recv_sem.at[down], (other, par)
        ).start()

    flat = diagonal_energy(spin_ref[...])
    energy_ref[...] = jnp.zeros_like(energy_ref)
    energy_ref[:, :LOCAL] = flat[:, :LOCAL] + off_ref[...]
    for _, other in partners:
        remote(energy_ref, energies_ref.at[samp], esem.at[0], esem.at[1], (other, par)).start()
    energies_ref[samp] = energy_ref[...]
    recv_ref[slot_here] = rounded(samp)
    for down in range(NY):
        low = wrap(y + NY - down, NY) * NZ
        taken = recv_ref.at[pl.ds(0, NZ - 1)] if down == 0 else recv_ref.at[pl.ds(low, NZ)]
        remote(taken, taken, send_sem, recv_sem.at[down], sibling).wait_recv()

    for pair in range(ROWS // 2):
        tile = jnp.stack(
            [
                recv_ref[(src % NY) * NZ + src // NY, 16 * pair : 16 * pair + 16, :].astype(jnp.float32)
                for src in range(NSAMP)
            ]
        ).reshape(NSAMP, 2, LOCAL, 128)
        halves = []
        for half in range(2):
            part = tile[:, half]
            mean = jnp.sum(jnp.sum(part, axis=0), axis=0, keepdims=True) / NS
            cent = ((part - mean) / math.sqrt(NS)).reshape(NS, 128)
            halves.append(cent.astype(jnp.bfloat16))
        cent = jnp.concatenate(halves, axis=1)
        cent_ref[:, 256 * pair : 256 * pair + 256] = cent
        light = lax.dot_general(
            cent[:128], cent[:128], (((1,), (1,)), ((), ())), preferred_element_type=jnp.float32
        )
        heavy = lax.dot_general(
            cent[128:], cent, (((1,), (1,)), ((), ())), preferred_element_type=jnp.float32
        )
        if pair == 0:
            part_ref[:128, :128] = light
            part_ref[128:, :] = heavy
        else:
            part_ref[:128, :128] += light
            part_ref[128:, :] += heavy
    eye = lax.broadcasted_iota(jnp.int32, (128, 128), 0) == lax.broadcasted_iota(
        jnp.int32, (128, 128), 1
    )
    trace = jnp.sum(
        jnp.where(eye, part_ref[:128, :128] + part_ref[128:, 128:], 0.0), keepdims=True
    )
    corner = jnp.logical_and(
        lax.broadcasted_iota(jnp.int32, (8, 128), 0) == 0,
        lax.broadcasted_iota(jnp.int32, (8, 128), 1) == 127,
    )
    part_ref[:8, :128] = jnp.where(corner, trace, part_ref[:8, :128])

    def rows_of(side, index):
        return pl.ds(pl.multiple_of(side * 128 + index * 8, 8), 8)

    slot = core * CHIPS + chip
    widths = (128, NS)

    def send_first(other, device, side):
        wide = pl.ds(0, widths[side])
        remote(
            part_ref.at[rows_of(side, other), wide],
            first.at[slot, :, wide],
            sem1.at[side],
            sem1.at[2],
            device,
        ).start()

    by_core(lambda side, width: send_first(chip, sibling, 0) if side == 1 else None)
    for kind in range(2):
        for other, device, side in around:
            if side == kind:
                send_first(other, device, side)
    by_core(lambda side, width: send_first(chip, sibling, 1) if side == 0 else None)

    def middle(side, width):
        wide = pl.ds(0, width)
        first[slot, :, wide] = part_ref[rows_of(side, chip), wide]
        landed = first.at[pl.ds(0, 2 * CHIPS - 1), :, wide]
        remote(landed, landed, sem1.at[0], sem1.at[2], sibling).wait_recv()
        own = jnp.sum(first[:, :, wide], axis=0)
        mine[:, wide] = own
        for hop in (4, 3, 5, 2, 6, 1, 7):
            device = (zs[hop] * NY + y, par)
            remote(
                mine.at[:, wide], second.at[z, :, wide], sem2.at[0], sem2.at[1], device
            ).start()
        second[z, :, wide] = own
        landed = second.at[pl.ds(0, NZ - 1), :, wide]
        remote(landed, landed, sem2.at[0], sem2.at[1], sibling).wait_recv()
        block = rows_of(side, chip)
        gram_ref[block, wide] = jnp.sum(second[:, :, wide], axis=0)
        done = gram_ref.at[block, wide]
        kind = 1 + y // 2 if side == 0 else 3
        for _, device, _ in around:
            remote(done, done, sem3.at[0], sem3.at[kind], device).start()
        remote(done, done, sem3.at[0], sem3.at[kind], sibling).start()

    by_core(middle)

    def await_rows(kind, count, width, own_kind):
        for less in range(2):

            @pl.when(own_kind if less else jnp.logical_not(own_kind))
            def _(less=less):
                landed = gram_ref.at[pl.ds(0, (count - less) * 8), pl.ds(0, width)]
                remote(landed, landed, sem3.at[0], sem3.at[kind], sibling).wait_recv()

    await_rows(1, 8, 128, jnp.logical_and(core == 0, y < 2))
    level = 1.0 / (gram_ref[0:1, 127:128] / NS)
    block_eye = lax.broadcasted_iota(jnp.int32, (BLOCK, BLOCK), 0) == lax.broadcasted_iota(
        jnp.int32, (BLOCK, BLOCK), 1
    )
    leading = gram_ref[:BLOCK, :BLOCK] * level + jnp.where(block_eye, 0.01, 0.0)
    factors = forward_block(leading, tile_ref, column_ref, cross_ref)
    energy_bytes = energies_ref.at[pl.ds(0, NSAMP - 1)]
    remote(energy_bytes, energy_bytes, esem.at[0], esem.at[1], sibling).wait()
    await_rows(2, 8, 128, jnp.logical_and(core == 0, y >= 2))
    await_rows(3, CHIPS, NS, core == 1)

    below = gram_ref[128:, :128]
    above = gram_ref[:128, :128]
    wide_corner = jnp.logical_and(
        lax.broadcasted_iota(jnp.int32, (128, 128), 0) == 0,
        lax.broadcasted_iota(jnp.int32, (128, 128), 1) == 127,
    )
    above = jnp.where(wide_corner, gram_ref[127:128, 0:1], above)
    gram = jnp.concatenate(
        [jnp.concatenate([above, below.T], axis=1), gram_ref[128:, :]], axis=0
    )
    diagonal = lax.broadcasted_iota(jnp.int32, (NS, NS), 0) == lax.broadcasted_iota(
        jnp.int32, (NS, NS), 1
    )
    pieces = jnp.broadcast_to(energies_ref[...], (NSAMP, LOCAL, 128)).reshape(NS, 128)
    lane = lax.broadcasted_iota(jnp.int32, (NS, 128), 1)
    row = lax.broadcasted_iota(jnp.int32, (NSAMP, LOCAL, 128), 1).reshape(NS, 128)
    energy = jnp.sum(jnp.where(lane == row, pieces, 0.0), axis=1, keepdims=True)
    mean = jnp.sum(energy, axis=0, keepdims=True) / NS
    residual = -(energy - mean) / math.sqrt(NS)
    work[:, :NS] = gram * level + jnp.where(diagonal, 0.01, 0.0)
    work[:, NS:] = jnp.broadcast_to(residual, (NS, 128))

    for index in range(NS // BLOCK):
        low = index * BLOCK
        own = slice(low, low + BLOCK)
        rest = slice(128 * ((index + 1) // 2), NS + 128)
        if index > 0:
            factors = forward_block(work[own, own], tile_ref, column_ref, cross_ref)
        lower, scaled = factors
        middle_rows = product(scaled, work[own, rest], 1, 0)
        outer = product(work[:, own], lower, 1, 1)
        work[:, rest] = work[:, rest] - product(outer, middle_rows, 1, 0)
        work[own, rest] = product(lower, middle_rows, 0, 0)

    coeff = work[:, NS:] * level
    held[...] = coeff
    own = held[pl.ds(pl.multiple_of(samp * LOCAL, LOCAL), LOCAL), :]
    here = lax.broadcasted_iota(jnp.int32, (LOCAL, 128), 0) == lax.broadcasted_iota(
        jnp.int32, (LOCAL, 128), 1
    )
    coeff_ref[...] = jnp.sum(jnp.where(here, own, 0.0), axis=0, keepdims=True)[:, :LOCAL]
    both = jnp.concatenate([coeff, coeff], axis=1)
    weighted = jnp.sum(gram * both, axis=0, keepdims=True)
    across = jnp.sum(jnp.where(diagonal, both, 0.0), axis=0, keepdims=True)
    square_total = jnp.sum(weighted * across, keepdims=True)
    scale = lax.rsqrt(square_total / ENTRIES + 1e-06)
    left = lax.broadcasted_iota(jnp.int32, (1, 128), 1) < CH
    for pair in range(ROWS // 2):
        parts = []
        for half in range(2):
            column = 128 * (2 * pair + half)
            cent = cent_ref[:, column : column + 128].astype(jnp.float32)
            parts.append(jnp.sum(cent * coeff, axis=0, keepdims=True) * scale)
        turned = [jnp.concatenate([item[:, CH:], item[:, :CH]], axis=1) for item in parts]
        for half in range(2):
            at = samp * ROWS + 2 * pair + half
            swapped = jnp.logical_and(at >= 3 * CH, at < 6 * CH)
            parts[half], turned[half] = (
                jnp.where(swapped, turned[half], parts[half]),
                jnp.where(swapped, parts[half], turned[half]),
            )
        update_ref[0:1, 128 * pair : 128 * pair + 128] = jnp.where(left, parts[0], turned[1])
        update_ref[1:2, 128 * pair : 128 * pair + 128] = jnp.where(left, turned[0], parts[1])

    sent = send_ref.at[pl.ds(0, NSAMP - 1)]
    remote(sent, sent, send_sem, recv_sem.at[0], sibling).wait_send()
    remote(relay_ref, relay_ref, send_sem, relay_sem, sibling).wait_send()

    def finish(side, width):
        wide = pl.ds(0, width)
        for kind in range(2):
            count = CHIPS - 1 if kind == side else CHIPS
            bytes_ref = gram_ref.at[pl.ds(0, count * 8), pl.ds(0, widths[kind])]
            remote(bytes_ref, bytes_ref, sem1.at[kind], sem1.at[2], sibling).wait_send()
        landed = second.at[pl.ds(0, NZ - 1), :, wide]
        remote(landed, landed, sem2.at[0], sem2.at[1], sibling).wait_send()
        landed = first.at[pl.ds(0, 2 * CHIPS - 1), :, wide]
        remote(landed, landed, sem3.at[0], sem1.at[2], sibling).wait_send()

    by_core(finish)


def main_call(activations, cotangents, spin_bits, off_row):
    whole = pl.BlockSpec(memory_space=VMEM)
    anywhere = pl.BlockSpec(memory_space=pl.ANY)
    dma = pltpu.SemaphoreType.DMA
    return pl.pallas_call(
        main_kernel,
        in_specs=[anywhere, anywhere, whole, whole],
        out_specs=[whole, whole],
        out_shape=[
            jax.ShapeDtypeStruct((LAYERS, ROWS * CH), jnp.float32),
            jax.ShapeDtypeStruct((1, LOCAL), jnp.float32),
        ],
        scratch_shapes=[
            VMEM((LOCAL, LAYERS, CH, SITES), jnp.bfloat16),
            VMEM((LOCAL, LAYERS, CH, SITES), jnp.bfloat16),
            VMEM((2, CH, SITES), jnp.bfloat16),
            VMEM((2, LAYERS, 3 * CH, PADK), jnp.bfloat16),
            VMEM((2, LAYERS, 4 * CH, PADK), jnp.bfloat16),
            VMEM((NSAMP * CHUNK, 128), jnp.float32),
            VMEM((NSAMP, CHUNK, 128), jnp.bfloat16),
            VMEM((NSAMP, CHUNK, 128), jnp.bfloat16),
            VMEM((NS, WIDTH), jnp.bfloat16),
            VMEM((1, 128), jnp.float32),
            VMEM((NY, CHUNK, 128), jnp.bfloat16),
            VMEM((NSAMP, 1, 128), jnp.float32),
            VMEM((NS, NS), jnp.float32),
            VMEM((2 * CHIPS, 8, NS), jnp.float32),
            VMEM((8, NS), jnp.float32),
            VMEM((NZ, 8, NS), jnp.float32),
            VMEM((NS, NS), jnp.float32),
            VMEM((NS, NS + 128), jnp.float32),
            VMEM((NS, 128), jnp.float32),
            VMEM((BLOCK // PANEL, 1, 8, 128), jnp.float32),
            VMEM((BLOCK // PANEL, PANEL, 8, 128), jnp.float32),
            VMEM((BLOCK // PANEL, PANEL, 8, 128), jnp.float32),
            dma((LOCAL,)),
            dma((LOCAL,)),
            dma,
            dma((NY,)),
            dma((2,)),
            dma,
            dma((3,)),
            dma((2,)),
            dma((4,)),
        ],
        compiler_params=pltpu.CompilerParams(
            collective_id=0, has_side_effects=True, vmem_limit_bytes=VMEM_LIMIT
        ),
    )(activations, cotangents, spin_bits, off_row)


def hand_on_kernel(update_in, coeff_in, update_ref, coeff_ref, sems):
    copies = [
        pltpu.make_async_copy(update_in, update_ref, sems.at[0]),
        pltpu.make_async_copy(coeff_in, coeff_ref, sems.at[1]),
    ]
    for copy in copies:
        copy.start()
    for copy in copies:
        copy.wait()


def hand_on(update, coeff):
    anywhere = pl.BlockSpec(memory_space=pl.ANY)
    return pl.pallas_call(
        hand_on_kernel,
        in_specs=[anywhere, anywhere],
        out_specs=[anywhere, anywhere],
        out_shape=[
            jax.ShapeDtypeStruct((LAYERS, ROWS * CH), jnp.float32),
            jax.ShapeDtypeStruct((1, LOCAL), jnp.float32),
        ],
        scratch_shapes=[pltpu.SemaphoreType.DMA((2,))],
        compiler_params=pltpu.CompilerParams(vmem_limit_bytes=VMEM_LIMIT),
    )(update, coeff)


def on_device(activations, cotangents, spin_bits, offdiag_energy):
    update, coeff = hand_on(
        *main_call(activations, cotangents, spin_bits, offdiag_energy.reshape(1, LOCAL))
    )
    return update, coeff.reshape(LOCAL)


def solution(mesh):
    in_specs = (
        P("samp", "par", None, None),
        P("samp", "par", None, None),
        P("samp", None),
        P("samp"),
    )
    out_specs = (P("par", "samp"), P("samp"))
    return jax.shard_map(
        on_device, mesh=mesh, in_specs=in_specs, out_specs=out_specs, check_vma=False
    )
```

```python
import math

import jax
import jax.numpy as jnp
from jax import lax
from jax.experimental import pallas as pl
from jax.experimental.pallas import tpu as pltpu
from jax.sharding import PartitionSpec as P

CH = 64
KK = 9
LAT = 24
SITES = LAT * LAT
NSAMP = 32
NPAR = 8
NZ = 8
NY = 4
LOCAL = 8
NS = NSAMP * LOCAL
ROWS = KK * CH // NSAMP
CHUNK = ROWS * LOCAL
WIDTH = ROWS * 128
PADK = 640
LAYERS = 2
ENTRIES = 16 * KK * CH * CH
MESH = pl.DeviceIdType.MESH
VMEM_LIMIT = 56 * 1024 * 1024
HIGHEST = lax.Precision.HIGHEST
VMEM = pltpu.VMEM


def rolled(value, amount):
    amount = amount % SITES
    if amount == 0:
        return value
    return jnp.concatenate([value[:, amount:], value[:, :amount]], axis=1)


def edge_mask(shape, col_step):
    column = lax.broadcasted_iota(jnp.int32, shape, 1) % LAT
    return column == (LAT - 1 if col_step > 0 else 0)


def column_shift(value, col_step, edge):
    if col_step == 0:
        return value
    return jnp.where(edge, rolled(value, col_step - LAT * col_step), rolled(value, col_step))


def wrap(value, size):
    return lax.select(value >= size, value - size, value)


STEPS = [(down, hop) for down in range(NY) for hop in (1, 7, 2, 6, 3, 5, 4, 0) if (down, hop) != (0, 0)]


def diagonal_energy(spin_bits):
    spin = (2 * spin_bits - 1).astype(jnp.float32)
    right = column_shift(spin, 1, edge_mask(spin.shape, 1))
    left = column_shift(spin, -1, edge_mask(spin.shape, -1))
    pairs = spin * rolled(spin, LAT) + spin * right
    corners = spin * rolled(right, LAT) + spin * rolled(left, LAT)
    diag = 0.25 * jnp.sum(pairs + 0.5 * corners, axis=1, keepdims=True)
    wide = jnp.broadcast_to(diag, (LOCAL, 128))
    here = lax.broadcasted_iota(jnp.int32, (LOCAL, 128), 0) == lax.broadcasted_iota(
        jnp.int32, (LOCAL, 128), 1
    )
    return jnp.sum(jnp.where(here, wide, 0.0), axis=0, keepdims=True)


PLANE = sorted(
    ((down, across) for down in range(NY) for across in range(4) if (down, across) != (0, 0)),
    key=lambda step: -(min(step[0], NY - step[0]) + min(step[1], 4 - step[1])),
)
PAIRS = 3 * CH // 2
HALF = CHUNK // 2
HEAD = 64
CHIPS = 16


BLOCK = 64
PANEL = 8


def forward_block(diag, tile_ref, column_ref, cross_ref):
    eye = lax.broadcasted_iota(jnp.int32, (BLOCK, BLOCK), 0) == lax.broadcasted_iota(
        jnp.int32, (BLOCK, BLOCK), 1
    )
    wide = jnp.concatenate([diag, jnp.where(eye, 1.0, 0.0)], axis=1)
    count = BLOCK // PANEL
    tiles = [wide[8 * q : 8 * q + 8] for q in range(count)]
    sub = lax.broadcasted_iota(jnp.int32, (8, 128), 0)

    def lanes(tile, col):
        return jnp.broadcast_to(tile[:, col : col + 1], (8, 128))

    def joined(parts):
        total = parts[0]
        for i in range(1, PANEL):
            total = jnp.where(sub == i, parts[i], total)
        return total

    def broadcast_row(ref, panel, j, i):
        return ref[panel, j, pl.ds(i, 8, stride=0), :]

    reduced, scaled = [], []
    columns = [lanes(tiles[0], j) for j in range(PANEL)]
    for panel in range(count):
        base = panel * PANEL
        last = panel == count - 1
        tile_ref[panel, 0] = tiles[panel]
        for j in range(PANEL):
            column_ref[panel, j] = columns[j]
        low = {
            (i, j): broadcast_row(column_ref, panel, j, i)
            for i in range(PANEL)
            for j in range(i + 1)
        }
        rows = [broadcast_row(tile_ref, panel, 0, i) for i in range(PANEL)]
        old_columns = {
            q: [lanes(tiles[q], base + i) for i in range(PANEL)] for q in range(panel + 1, count)
        }
        if not last:
            cross = list(old_columns[panel + 1])
            columns = [lanes(tiles[panel + 1], base + PANEL + j) for j in range(PANEL)]
        ups, downs, starts, cross_scaled = {}, {}, {}, {}
        for p in range(0, PANEL, 2):
            q = p + 1
            a, b, c = low[p, p], low[q, p], low[q, q]
            recip = pl.reciprocal(a * c - b * b, approx=True)
            for i in range(q + 1, PANEL):
                up = c * low[i, p] - b * low[i, q]
                down = a * low[i, q] - b * low[i, p]
                for m in range(q + 1, i + 1):
                    low[i, m] = low[i, m] - (up * low[m, p] + down * low[m, q]) * recip
                ups[i, p], downs[i, p] = up * recip, down * recip
            if not last:
                cross_scaled[p] = (c * cross[p] - b * cross[q]) * recip
                cross_scaled[q] = (a * cross[q] - b * cross[p]) * recip
                for i in range(q + 1, PANEL):
                    cross[i] = cross[i] - (ups[i, p] * cross[p] + downs[i, p] * cross[q])
            starts[p] = (c * rows[p] - b * rows[q]) * recip
            starts[q] = (a * rows[q] - b * rows[p]) * recip
            for i in range(q + 1, PANEL):
                rows[i] = rows[i] - (ups[i, p] * rows[p] + downs[i, p] * rows[q])
        if not last:
            for i in range(PANEL):
                cross_ref[panel, i] = cross[i]
            for j in range(PANEL):
                terms = [
                    cross_scaled[i] * broadcast_row(cross_ref, panel, i, j) for i in range(PANEL)
                ]
                while len(terms) > 1:
                    terms = [terms[a] + terms[a + 1] for a in range(0, len(terms), 2)]
                columns[j] = columns[j] - terms[0]
        reduced.append(joined(rows))
        scaled.append(joined([starts[i] for i in range(PANEL)]))
        if last:
            break
        solved = [None] * PANEL
        for p in reversed(range(0, PANEL, 2)):
            for total, factor, at in ((starts[p], ups, p), (starts[p + 1], downs, p + 1)):
                for i in reversed(range(p + 2, PANEL)):
                    total = total - factor[i, p] * solved[i]
                solved[at] = total
        for q in range(panel + 1, count):
            terms = [old_columns[q][i] * solved[i] for i in range(PANEL)]
            while len(terms) > 1:
                terms = [terms[a] + terms[a + 1] for a in range(0, len(terms), 2)]
            tiles[q] = tiles[q] - terms[0]
    lower = jnp.concatenate(reduced, axis=0)[:, BLOCK:]
    return lower, jnp.concatenate(scaled, axis=0)[:, BLOCK:]


def product(one, two, first_dim, second_dim):
    return lax.dot_general(
        one, two, (((first_dim,), (second_dim,)), ((), ())),
        precision=HIGHEST, preferred_element_type=jnp.float32,
    )


def main_kernel(
    act_hbm, cot_hbm, spin_ref, off_ref,
    update_ref, coeff_ref,
    act_ref, cot_ref, edges, lhs, rhs, stage, wide_rows, send_ref, recv_ref, cent_ref,
    energy_ref, energies_ref, part_ref, first, mine, second, gram_ref,
    work, held, tile_ref, column_ref, cross_ref,
    act_sem, cot_sem, send_sem, recv_sem, esem, sem1, sem2, sem3,
):
    samp = lax.axis_index("samp")
    par = lax.axis_index("par")
    z, y = samp // NY, samp % NY
    x, core = par // 2, par % 2
    slot_here = y * NZ + z
    sibling = (samp, x * 2 + 1 - core)
    zs = [wrap(z + hop, NZ) for hop in range(NZ)]
    ys = [wrap(y + down, NY) for down in range(NY)]
    xs = [wrap(x + across, 4) for across in range(4)]
    partners = [(down, zs[hop] * NY + ys[down]) for down, hop in STEPS]
    sorted_partners = [
        item for item, (_, hop) in sorted(zip(partners, STEPS), key=lambda pair: -min(pair[1][1], NZ - pair[1][1]))
    ]
    chip = y * 4 + x
    others = [
        (ys[down] * 4 + xs[across], z * NY + ys[down], xs[across] * 2)
        for down, across in PLANE
    ]
    around = [(other, (row, pair + side), side) for other, row, pair in others for side in range(2)]

    def by_core(body):
        @pl.when(core == 0)
        def _():
            body(0, 128)

        @pl.when(core == 1)
        def _():
            body(1, NS)

    def act_copy(n):
        return pltpu.make_async_copy(act_hbm.at[n], act_ref.at[n], act_sem.at[n])

    def cot_copy(n):
        return pltpu.make_async_copy(cot_hbm.at[n], cot_ref.at[n], cot_sem.at[n])

    for n in range(LOCAL):
        act_copy(n).start()
        cot_copy(n).start()

    def remote(source, target, send, recv, device):
        return pltpu.make_async_remote_copy(
            src_ref=source,
            dst_ref=target,
            send_sem=send,
            recv_sem=recv,
            device_id=device,
            device_id_type=MESH,
        )

    barrier = pltpu.get_barrier_semaphore()
    greeted = 0
    for _, other in partners:
        pl.semaphore_signal(barrier, inc=1, device_id=(other, par), device_id_type=MESH)
        greeted += 1
    for down in range(NY):
        for across in range(4):
            for side in (core, 1 - core):
                if across > 0 or side is not core:
                    device = (z * NY + ys[down], xs[across] * 2 + side)
                    pl.semaphore_signal(barrier, inc=1, device_id=device, device_id_type=MESH)
                    greeted += 1

    left = lax.broadcasted_iota(jnp.int32, (PAIRS, 128), 1) < CH
    lhs[:, :, PADK - 128 :] = jnp.zeros((2, 3 * CH, 128), jnp.bfloat16)
    rhs[:, :, PADK - 128 :] = jnp.zeros((2, 3 * CH, 128), jnp.bfloat16)
    stage[:, 1] = jnp.zeros((2, 3 * CH, 128), jnp.float32)
    for at, step in enumerate((-1, 1)):
        strip = jnp.where(edge_mask((8, SITES), step), 1.0, 0.0)
        edges[at] = jnp.concatenate([strip] * (CH // 8), axis=0).astype(jnp.bfloat16)

    def compute(sample, layer, slot):
        act = act_ref[sample, layer]
        cot = cot_ref[sample, layer]
        for step in (-1, 0, 1):
            low = (step + 1) * CH
            edge = edges[max(step, 0)] > 0
            lhs[slot, low : low + CH, :SITES] = column_shift(act, step, edge)
            rhs[slot, low : low + CH, :SITES] = rolled(cot, -LAT * step)
        out = lax.dot_general(
            lhs[slot], rhs[slot], (((1,), (1,)), ((), ())), preferred_element_type=jnp.float32
        )
        stage[slot, 0] = out[:, :128]
        stage[slot, 1, :, :CH] = out[:, 128:]
        even, odd, even_last, odd_last = [
            stage[slot, part, pl.ds(parity, PAIRS, stride=2), :]
            for part in (0, 1)
            for parity in (0, 1)
        ]
        blocks = (
            jnp.where(left, even, pltpu.roll(odd, CH, 1)),
            jnp.where(left, pltpu.roll(even, CH, 1), odd),
            jnp.where(left, even_last, pltpu.roll(odd_last, CH, 1)),
        )
        for down in range(3):
            wide_rows[layer, pl.ds(down * PAIRS * LOCAL + sample, PAIRS, stride=LOCAL), :] = blocks[down]

    def first_layer(pair, carry):
        for slot in range(2):
            sample = pair * 2 + slot
            act_copy(sample).wait()
            cot_copy(sample).wait()
            compute(sample, 0, slot)
        return carry

    def second_layer(pair, carry):
        for slot in range(2):
            compute(pair * 2 + slot, 1, slot)
        return carry

    def rounded(other, layer, low, rows):
        start = pl.multiple_of(other * HALF + low, 8)
        return wide_rows[layer, pl.ds(start, rows), :]

    def send_wave(low, rows):
        for down, other in sorted_partners:
            if low == 0:
                block = rounded(other, 0, 0, HEAD)
            else:
                block = jnp.concatenate(
                    [rounded(other, 0, HEAD, HALF - HEAD), rounded(other, 1, 0, HALF)], axis=0
                )
            send_ref[other, low : low + rows] = block.astype(jnp.bfloat16)
            remote(
                send_ref.at[other, pl.ds(low, rows)],
                recv_ref.at[slot_here, pl.ds(low, rows)],
                send_sem,
                recv_sem.at[down],
                (other, par),
            ).start()

    lax.fori_loop(0, LOCAL // 2, first_layer, 0)
    pl.semaphore_wait(barrier, greeted)
    send_wave(0, HEAD)
    lax.fori_loop(0, LOCAL // 2, second_layer, 0)
    send_wave(HEAD, CHUNK - HEAD)

    flat = diagonal_energy(spin_ref[...])
    energy_ref[...] = jnp.zeros_like(energy_ref)
    energy_ref[:, :LOCAL] = flat[:, :LOCAL] + off_ref[...]
    for _, other in partners:
        remote(energy_ref, energies_ref.at[samp], esem.at[0], esem.at[1], (other, par)).start()
    energies_ref[samp] = energy_ref[...]
    recv_ref[slot_here] = jnp.concatenate(
        [rounded(samp, layer, 0, HALF) for layer in range(LAYERS)], axis=0
    ).astype(jnp.bfloat16)
    for down in range(NY):
        low = wrap(y + NY - down, NY) * NZ
        taken = recv_ref.at[pl.ds(0, NZ - 1)] if down == 0 else recv_ref.at[pl.ds(low, NZ)]
        remote(taken, taken, send_sem, recv_sem.at[down], sibling).wait_recv()

    for pair in range(ROWS // 2):
        tile = jnp.stack(
            [
                recv_ref[(src % NY) * NZ + src // NY, 16 * pair : 16 * pair + 16, :].astype(jnp.float32)
                for src in range(NSAMP)
            ]
        ).reshape(NSAMP, 2, LOCAL, 128)
        halves = []
        for half in range(2):
            part = tile[:, half]
            mean = jnp.sum(jnp.sum(part, axis=0), axis=0, keepdims=True) / NS
            cent = ((part - mean) / math.sqrt(NS)).reshape(NS, 128)
            halves.append(cent.astype(jnp.bfloat16))
        cent = jnp.concatenate(halves, axis=1)
        cent_ref[:, 256 * pair : 256 * pair + 256] = cent
        light = lax.dot_general(
            cent[:128], cent[:128], (((1,), (1,)), ((), ())), preferred_element_type=jnp.float32
        )
        heavy = lax.dot_general(
            cent[128:], cent, (((1,), (1,)), ((), ())), preferred_element_type=jnp.float32
        )
        if pair == 0:
            part_ref[:128, :128] = light
            part_ref[128:, :] = heavy
        else:
            part_ref[:128, :128] += light
            part_ref[128:, :] += heavy
    eye = lax.broadcasted_iota(jnp.int32, (128, 128), 0) == lax.broadcasted_iota(
        jnp.int32, (128, 128), 1
    )
    trace = jnp.sum(
        jnp.where(eye, part_ref[:128, :128] + part_ref[128:, 128:], 0.0), keepdims=True
    )
    corner = jnp.logical_and(
        lax.broadcasted_iota(jnp.int32, (8, 128), 0) == 0,
        lax.broadcasted_iota(jnp.int32, (8, 128), 1) == 127,
    )
    part_ref[:8, :128] = jnp.where(corner, trace, part_ref[:8, :128])

    def rows_of(side, index):
        return pl.ds(pl.multiple_of(side * 128 + index * 8, 8), 8)

    slot = core * CHIPS + chip
    widths = (128, NS)

    def send_first(other, device, side):
        wide = pl.ds(0, widths[side])
        remote(
            part_ref.at[rows_of(side, other), wide],
            first.at[slot, :, wide],
            sem1.at[side],
            sem1.at[2],
            device,
        ).start()

    by_core(lambda side, width: send_first(chip, sibling, 0) if side == 1 else None)
    for kind in range(2):
        for other, device, side in around:
            if side == kind:
                send_first(other, device, side)
    by_core(lambda side, width: send_first(chip, sibling, 1) if side == 0 else None)

    def middle(side, width):
        wide = pl.ds(0, width)
        first[slot, :, wide] = part_ref[rows_of(side, chip), wide]
        landed = first.at[pl.ds(0, 2 * CHIPS - 1), :, wide]
        remote(landed, landed, sem1.at[0], sem1.at[2], sibling).wait_recv()
        own = jnp.sum(first[:, :, wide], axis=0)
        mine[:, wide] = own
        for hop in (4, 3, 5, 2, 6, 1, 7):
            device = (zs[hop] * NY + y, par)
            remote(
                mine.at[:, wide], second.at[z, :, wide], sem2.at[0], sem2.at[1], device
            ).start()
        second[z, :, wide] = own
        landed = second.at[pl.ds(0, NZ - 1), :, wide]
        remote(landed, landed, sem2.at[0], sem2.at[1], sibling).wait_recv()
        block = rows_of(side, chip)
        gram_ref[block, wide] = jnp.sum(second[:, :, wide], axis=0)
        done = gram_ref.at[block, wide]
        kind = 1 + y // 2 if side == 0 else 3
        for _, device, _ in around:
            remote(done, done, sem3.at[0], sem3.at[kind], device).start()
        remote(done, done, sem3.at[0], sem3.at[kind], sibling).start()

    by_core(middle)

    def await_rows(kind, count, width, own_kind):
        for less in range(2):

            @pl.when(own_kind if less else jnp.logical_not(own_kind))
            def _(less=less):
                landed = gram_ref.at[pl.ds(0, (count - less) * 8), pl.ds(0, width)]
                remote(landed, landed, sem3.at[0], sem3.at[kind], sibling).wait_recv()

    await_rows(1, 8, 128, jnp.logical_and(core == 0, y < 2))
    level = 1.0 / (gram_ref[0:1, 127:128] / NS)
    block_eye = lax.broadcasted_iota(jnp.int32, (BLOCK, BLOCK), 0) == lax.broadcasted_iota(
        jnp.int32, (BLOCK, BLOCK), 1
    )
    leading = gram_ref[:BLOCK, :BLOCK] * level + jnp.where(block_eye, 0.01, 0.0)
    factors = forward_block(leading, tile_ref, column_ref, cross_ref)
    energy_bytes = energies_ref.at[pl.ds(0, NSAMP - 1)]
    remote(energy_bytes, energy_bytes, esem.at[0], esem.at[1], sibling).wait()
    await_rows(2, 8, 128, jnp.logical_and(core == 0, y >= 2))
    await_rows(3, CHIPS, NS, core == 1)

    below = gram_ref[128:, :128]
    above = gram_ref[:128, :128]
    wide_corner = jnp.logical_and(
        lax.broadcasted_iota(jnp.int32, (128, 128), 0) == 0,
        lax.broadcasted_iota(jnp.int32, (128, 128), 1) == 127,
    )
    above = jnp.where(wide_corner, gram_ref[127:128, 0:1], above)
    gram = jnp.concatenate(
        [jnp.concatenate([above, below.T], axis=1), gram_ref[128:, :]], axis=0
    )
    diagonal = lax.broadcasted_iota(jnp.int32, (NS, NS), 0) == lax.broadcasted_iota(
        jnp.int32, (NS, NS), 1
    )
    pieces = jnp.broadcast_to(energies_ref[...], (NSAMP, LOCAL, 128)).reshape(NS, 128)
    lane = lax.broadcasted_iota(jnp.int32, (NS, 128), 1)
    row = lax.broadcasted_iota(jnp.int32, (NSAMP, LOCAL, 128), 1).reshape(NS, 128)
    energy = jnp.sum(jnp.where(lane == row, pieces, 0.0), axis=1, keepdims=True)
    mean = jnp.sum(energy, axis=0, keepdims=True) / NS
    residual = -(energy - mean) / math.sqrt(NS)
    work[:, :NS] = gram * level + jnp.where(diagonal, 0.01, 0.0)
    work[:, NS:] = jnp.broadcast_to(residual, (NS, 128))

    for index in range(NS // BLOCK):
        low = index * BLOCK
        own = slice(low, low + BLOCK)
        rest = slice(128 * ((index + 1) // 2), NS + 128)
        if index > 0:
            factors = forward_block(work[own, own], tile_ref, column_ref, cross_ref)
        lower, scaled = factors
        middle_rows = product(scaled, work[own, rest], 1, 0)
        outer = product(work[:, own], lower, 1, 1)
        work[:, rest] = work[:, rest] - product(outer, middle_rows, 1, 0)
        work[own, rest] = product(lower, middle_rows, 0, 0)

    coeff = work[:, NS:] * level
    held[...] = coeff
    own = held[pl.ds(pl.multiple_of(samp * LOCAL, LOCAL), LOCAL), :]
    here = lax.broadcasted_iota(jnp.int32, (LOCAL, 128), 0) == lax.broadcasted_iota(
        jnp.int32, (LOCAL, 128), 1
    )
    coeff_ref[...] = jnp.sum(jnp.where(here, own, 0.0), axis=0, keepdims=True)[:, :LOCAL]
    both = jnp.concatenate([coeff, coeff], axis=1)
    weighted = jnp.sum(gram * both, axis=0, keepdims=True)
    across = jnp.sum(jnp.where(diagonal, both, 0.0), axis=0, keepdims=True)
    square_total = jnp.sum(weighted * across, keepdims=True)
    scale = lax.rsqrt(square_total / ENTRIES + 1e-06)
    for index in range(ROWS):
        cent = cent_ref[:, 128 * index : 128 * index + 128].astype(jnp.float32)
        layer, column = index // (ROWS // 2), 128 * (index % (ROWS // 2))
        update_ref[layer : layer + 1, column : column + 128] = (
            jnp.sum(cent * coeff, axis=0, keepdims=True) * scale
        )

    sent = send_ref.at[pl.ds(0, NSAMP - 1)]
    remote(sent, sent, send_sem, recv_sem.at[0], sibling).wait_send()

    def finish(side, width):
        wide = pl.ds(0, width)
        for kind in range(2):
            count = CHIPS - 1 if kind == side else CHIPS
            bytes_ref = gram_ref.at[pl.ds(0, count * 8), pl.ds(0, widths[kind])]
            remote(bytes_ref, bytes_ref, sem1.at[kind], sem1.at[2], sibling).wait_send()
        landed = second.at[pl.ds(0, NZ - 1), :, wide]
        remote(landed, landed, sem2.at[0], sem2.at[1], sibling).wait_send()
        landed = first.at[pl.ds(0, 2 * CHIPS - 1), :, wide]
        remote(landed, landed, sem3.at[0], sem1.at[2], sibling).wait_send()

    by_core(finish)


def main_call(activations, cotangents, spin_bits, off_row):
    whole = pl.BlockSpec(memory_space=VMEM)
    anywhere = pl.BlockSpec(memory_space=pl.ANY)
    dma = pltpu.SemaphoreType.DMA
    return pl.pallas_call(
        main_kernel,
        in_specs=[anywhere, anywhere, whole, whole],
        out_specs=[whole, whole],
        out_shape=[
            jax.ShapeDtypeStruct((LAYERS, ROWS * CH), jnp.float32),
            jax.ShapeDtypeStruct((1, LOCAL), jnp.float32),
        ],
        scratch_shapes=[
            VMEM((LOCAL, LAYERS, CH, SITES), jnp.bfloat16),
            VMEM((LOCAL, LAYERS, CH, SITES), jnp.bfloat16),
            VMEM((2, CH, SITES), jnp.bfloat16),
            VMEM((2, 3 * CH, PADK), jnp.bfloat16),
            VMEM((2, 3 * CH, PADK), jnp.bfloat16),
            VMEM((2, 2, 3 * CH, 128), jnp.float32),
            VMEM((LAYERS, NSAMP * HALF, 128), jnp.float32),
            VMEM((NSAMP, CHUNK, 128), jnp.bfloat16),
            VMEM((NSAMP, CHUNK, 128), jnp.bfloat16),
            VMEM((NS, WIDTH), jnp.bfloat16),
            VMEM((1, 128), jnp.float32),
            VMEM((NSAMP, 1, 128), jnp.float32),
            VMEM((NS, NS), jnp.float32),
            VMEM((2 * CHIPS, 8, NS), jnp.float32),
            VMEM((8, NS), jnp.float32),
            VMEM((NZ, 8, NS), jnp.float32),
            VMEM((NS, NS), jnp.float32),
            VMEM((NS, NS + 128), jnp.float32),
            VMEM((NS, 128), jnp.float32),
            VMEM((BLOCK // PANEL, 1, 8, 128), jnp.float32),
            VMEM((BLOCK // PANEL, PANEL, 8, 128), jnp.float32),
            VMEM((BLOCK // PANEL, PANEL, 8, 128), jnp.float32),
            dma((LOCAL,)),
            dma((LOCAL,)),
            dma,
            dma((NY,)),
            dma((2,)),
            dma((3,)),
            dma((2,)),
            dma((4,)),
        ],
        compiler_params=pltpu.CompilerParams(
            collective_id=0, has_side_effects=True, vmem_limit_bytes=VMEM_LIMIT
        ),
    )(activations, cotangents, spin_bits, off_row)


def hand_on_kernel(update_in, coeff_in, update_ref, coeff_ref, sems):
    copies = [
        pltpu.make_async_copy(update_in, update_ref, sems.at[0]),
        pltpu.make_async_copy(coeff_in, coeff_ref, sems.at[1]),
    ]
    for copy in copies:
        copy.start()
    for copy in copies:
        copy.wait()


def hand_on(update, coeff):
    anywhere = pl.BlockSpec(memory_space=pl.ANY)
    return pl.pallas_call(
        hand_on_kernel,
        in_specs=[anywhere, anywhere],
        out_specs=[anywhere, anywhere],
        out_shape=[
            jax.ShapeDtypeStruct((LAYERS, ROWS * CH), jnp.float32),
            jax.ShapeDtypeStruct((1, LOCAL), jnp.float32),
        ],
        scratch_shapes=[pltpu.SemaphoreType.DMA((2,))],
        compiler_params=pltpu.CompilerParams(vmem_limit_bytes=VMEM_LIMIT),
    )(update, coeff)


def on_device(activations, cotangents, spin_bits, offdiag_energy):
    update, coeff = hand_on(
        *main_call(activations, cotangents, spin_bits, offdiag_energy.reshape(1, LOCAL))
    )
    return update, coeff.reshape(LOCAL)


def solution(mesh):
    in_specs = (
        P("samp", "par", None, None),
        P("samp", "par", None, None),
        P("samp", None),
        P("samp"),
    )
    out_specs = (P("par", "samp"), P("samp"))
    return jax.shard_map(
        on_device, mesh=mesh, in_specs=in_specs, out_specs=out_specs, check_vma=False
    )
```

```python
import math

import jax
import jax.numpy as jnp
from jax import lax
from jax.experimental import pallas as pl
from jax.experimental.pallas import tpu as pltpu
from jax.sharding import PartitionSpec as P

CH = 64
KK = 9
LAT = 24
SITES = LAT * LAT
NSAMP = 32
NPAR = 8
NZ = 8
NY = 4
LOCAL = 8
NS = NSAMP * LOCAL
ROWS = KK * CH // NSAMP
CHUNK = ROWS * LOCAL
WIDTH = ROWS * 128
PADK = 640
LAYERS = 2
ENTRIES = 16 * KK * CH * CH
MESH = pl.DeviceIdType.MESH
VMEM_LIMIT = 56 * 1024 * 1024
HIGHEST = lax.Precision.HIGHEST
VMEM = pltpu.VMEM


def rolled(value, amount):
    amount = amount % SITES
    if amount == 0:
        return value
    return jnp.concatenate([value[:, amount:], value[:, :amount]], axis=1)


def edge_mask(shape, col_step):
    column = lax.broadcasted_iota(jnp.int32, shape, 1) % LAT
    return column == (LAT - 1 if col_step > 0 else 0)


def column_shift(value, col_step, edge):
    if col_step == 0:
        return value
    return jnp.where(edge, rolled(value, col_step - LAT * col_step), rolled(value, col_step))


def wrap(value, size):
    return lax.select(value >= size, value - size, value)


STEPS = [(down, hop) for down in range(NY) for hop in (1, 7, 2, 6, 3, 5, 4, 0) if (down, hop) != (0, 0)]


def diagonal_energy(spin_bits):
    spin = (2 * spin_bits - 1).astype(jnp.float32)
    right = column_shift(spin, 1, edge_mask(spin.shape, 1))
    left = column_shift(spin, -1, edge_mask(spin.shape, -1))
    pairs = spin * rolled(spin, LAT) + spin * right
    corners = spin * rolled(right, LAT) + spin * rolled(left, LAT)
    diag = 0.25 * jnp.sum(pairs + 0.5 * corners, axis=1, keepdims=True)
    wide = jnp.broadcast_to(diag, (LOCAL, 128))
    here = lax.broadcasted_iota(jnp.int32, (LOCAL, 128), 0) == lax.broadcasted_iota(
        jnp.int32, (LOCAL, 128), 1
    )
    return jnp.sum(jnp.where(here, wide, 0.0), axis=0, keepdims=True)


PLANE = sorted(
    ((down, across) for down in range(NY) for across in range(4) if (down, across) != (0, 0)),
    key=lambda step: -(min(step[0], NY - step[0]) + min(step[1], 4 - step[1])),
)
PAIRS = 3 * CH // 2
HALF = CHUNK // 2
HEAD = 64
SLOTS = 4
CHIPS = 16


BLOCK = 64
PANEL = 8


def forward_block(diag, tile_ref, column_ref, cross_ref):
    eye = lax.broadcasted_iota(jnp.int32, (BLOCK, BLOCK), 0) == lax.broadcasted_iota(
        jnp.int32, (BLOCK, BLOCK), 1
    )
    wide = jnp.concatenate([diag, jnp.where(eye, 1.0, 0.0)], axis=1)
    count = BLOCK // PANEL
    tiles = [wide[8 * q : 8 * q + 8] for q in range(count)]
    sub = lax.broadcasted_iota(jnp.int32, (8, 128), 0)

    def lanes(tile, col):
        return jnp.broadcast_to(tile[:, col : col + 1], (8, 128))

    def joined(parts):
        total = parts[0]
        for i in range(1, PANEL):
            total = jnp.where(sub == i, parts[i], total)
        return total

    def broadcast_row(ref, panel, j, i):
        return ref[panel, j, pl.ds(i, 8, stride=0), :]

    reduced, scaled = [], []
    columns = [lanes(tiles[0], j) for j in range(PANEL)]
    for panel in range(count):
        base = panel * PANEL
        last = panel == count - 1
        tile_ref[panel, 0] = tiles[panel]
        for j in range(PANEL):
            column_ref[panel, j] = columns[j]
        low = {
            (i, j): broadcast_row(column_ref, panel, j, i)
            for i in range(PANEL)
            for j in range(i + 1)
        }
        rows = [broadcast_row(tile_ref, panel, 0, i) for i in range(PANEL)]
        old_columns = {
            q: [lanes(tiles[q], base + i) for i in range(PANEL)] for q in range(panel + 1, count)
        }
        if not last:
            cross = list(old_columns[panel + 1])
            columns = [lanes(tiles[panel + 1], base + PANEL + j) for j in range(PANEL)]
        ups, downs, starts, cross_scaled = {}, {}, {}, {}
        for p in range(0, PANEL, 2):
            q = p + 1
            a, b, c = low[p, p], low[q, p], low[q, q]
            recip = pl.reciprocal(a * c - b * b, approx=True)
            for i in range(q + 1, PANEL):
                up = c * low[i, p] - b * low[i, q]
                down = a * low[i, q] - b * low[i, p]
                for m in range(q + 1, i + 1):
                    low[i, m] = low[i, m] - (up * low[m, p] + down * low[m, q]) * recip
                ups[i, p], downs[i, p] = up * recip, down * recip
            if not last:
                cross_scaled[p] = (c * cross[p] - b * cross[q]) * recip
                cross_scaled[q] = (a * cross[q] - b * cross[p]) * recip
                for i in range(q + 1, PANEL):
                    cross[i] = cross[i] - (ups[i, p] * cross[p] + downs[i, p] * cross[q])
            starts[p] = (c * rows[p] - b * rows[q]) * recip
            starts[q] = (a * rows[q] - b * rows[p]) * recip
            for i in range(q + 1, PANEL):
                rows[i] = rows[i] - (ups[i, p] * rows[p] + downs[i, p] * rows[q])
        if not last:
            for i in range(PANEL):
                cross_ref[panel, i] = cross[i]
            for j in range(PANEL):
                terms = [
                    cross_scaled[i] * broadcast_row(cross_ref, panel, i, j) for i in range(PANEL)
                ]
                while len(terms) > 1:
                    terms = [terms[a] + terms[a + 1] for a in range(0, len(terms), 2)]
                columns[j] = columns[j] - terms[0]
        reduced.append(joined(rows))
        scaled.append(joined([starts[i] for i in range(PANEL)]))
        if last:
            break
        solved = [None] * PANEL
        for p in reversed(range(0, PANEL, 2)):
            for total, factor, at in ((starts[p], ups, p), (starts[p + 1], downs, p + 1)):
                for i in reversed(range(p + 2, PANEL)):
                    total = total - factor[i, p] * solved[i]
                solved[at] = total
        for q in range(panel + 1, count):
            terms = [old_columns[q][i] * solved[i] for i in range(PANEL)]
            while len(terms) > 1:
                terms = [terms[a] + terms[a + 1] for a in range(0, len(terms), 2)]
            tiles[q] = tiles[q] - terms[0]
    lower = jnp.concatenate(reduced, axis=0)[:, BLOCK:]
    return lower, jnp.concatenate(scaled, axis=0)[:, BLOCK:]


def product(one, two, first_dim, second_dim):
    return lax.dot_general(
        one, two, (((first_dim,), (second_dim,)), ((), ())),
        precision=HIGHEST, preferred_element_type=jnp.float32,
    )


def main_kernel(
    act_hbm, cot_hbm, spin_ref, off_ref,
    update_ref, coeff_ref,
    act_ref, cot_ref, edges, lhs, rhs, stage, wide_rows, send_ref, recv_ref, cent_ref,
    energy_ref, energies_ref, part_ref, first, mine, second, gram_ref,
    work, held, tile_ref, column_ref, cross_ref,
    act_sem, cot_sem, send_sem, recv_sem, esem, sem1, sem2, sem3,
):
    samp = lax.axis_index("samp")
    par = lax.axis_index("par")
    z, y = samp // NY, samp % NY
    x, core = par // 2, par % 2
    slot_here = y * NZ + z
    sibling = (samp, x * 2 + 1 - core)
    zs = [wrap(z + hop, NZ) for hop in range(NZ)]
    ys = [wrap(y + down, NY) for down in range(NY)]
    xs = [wrap(x + across, 4) for across in range(4)]
    partners = [(down, zs[hop] * NY + ys[down]) for down, hop in STEPS]
    sorted_partners = [
        item for item, (_, hop) in sorted(zip(partners, STEPS), key=lambda pair: -min(pair[1][1], NZ - pair[1][1]))
    ]
    chip = y * 4 + x
    others = [
        (ys[down] * 4 + xs[across], z * NY + ys[down], xs[across] * 2)
        for down, across in PLANE
    ]
    around = [(other, (row, pair + side), side) for other, row, pair in others for side in range(2)]

    def by_core(body):
        @pl.when(core == 0)
        def _():
            body(0, 128)

        @pl.when(core == 1)
        def _():
            body(1, NS)

    def act_copy(n, layer):
        return pltpu.make_async_copy(
            act_hbm.at[n, layer], act_ref.at[n, layer], act_sem.at[layer, n]
        )

    def cot_copy(n, layer):
        return pltpu.make_async_copy(
            cot_hbm.at[n, layer], cot_ref.at[n, layer], cot_sem.at[layer, n]
        )

    for layer in range(LAYERS):
        for n in range(LOCAL):
            act_copy(n, layer).start()
            cot_copy(n, layer).start()

    def remote(source, target, send, recv, device):
        return pltpu.make_async_remote_copy(
            src_ref=source,
            dst_ref=target,
            send_sem=send,
            recv_sem=recv,
            device_id=device,
            device_id_type=MESH,
        )

    barrier = pltpu.get_barrier_semaphore()
    greeted = 0
    for _, other in partners:
        pl.semaphore_signal(barrier, inc=1, device_id=(other, par), device_id_type=MESH)
        greeted += 1
    for down in range(NY):
        for across in range(4):
            for side in (core, 1 - core):
                if across > 0 or side is not core:
                    device = (z * NY + ys[down], xs[across] * 2 + side)
                    pl.semaphore_signal(barrier, inc=1, device_id=device, device_id_type=MESH)
                    greeted += 1

    left = lax.broadcasted_iota(jnp.int32, (PAIRS, 128), 1) < CH
    lhs[:, :, PADK - 128 :] = jnp.zeros((SLOTS, 3 * CH, 128), jnp.bfloat16)
    rhs[:, :, PADK - 128 :] = jnp.zeros((SLOTS, 3 * CH, 128), jnp.bfloat16)
    stage[:, 1] = jnp.zeros((SLOTS, 3 * CH, 128), jnp.float32)
    for at, step in enumerate((-1, 1)):
        strip = jnp.where(edge_mask((8, SITES), step), 1.0, 0.0)
        edges[at] = jnp.concatenate([strip] * (CH // 8), axis=0).astype(jnp.bfloat16)

    def compute(sample, layer, slot):
        act = act_ref[sample, layer]
        cot = cot_ref[sample, layer]
        for step in (-1, 0, 1):
            low = (step + 1) * CH
            edge = edges[max(step, 0)] > 0
            lhs[slot, low : low + CH, :SITES] = column_shift(act, step, edge)
            rhs[slot, low : low + CH, :SITES] = rolled(cot, -LAT * step)
        out = lax.dot_general(
            lhs[slot], rhs[slot], (((1,), (1,)), ((), ())), preferred_element_type=jnp.float32
        )
        stage[slot, 0] = out[:, :128]
        stage[slot, 1, :, :CH] = out[:, 128:]
        even, odd, even_last, odd_last = [
            stage[slot, part, pl.ds(parity, PAIRS, stride=2), :]
            for part in (0, 1)
            for parity in (0, 1)
        ]
        blocks = (
            jnp.where(left, even, pltpu.roll(odd, CH, 1)),
            jnp.where(left, pltpu.roll(even, CH, 1), odd),
            jnp.where(left, even_last, pltpu.roll(odd_last, CH, 1)),
        )
        for down in range(3):
            wide_rows[layer, pl.ds(down * PAIRS * LOCAL + sample, PAIRS, stride=LOCAL), :] = blocks[down]

    def products(layer):
        def body(group, carry):
            for slot in range(SLOTS):
                sample = group * SLOTS + slot
                act_copy(sample, layer).wait()
                cot_copy(sample, layer).wait()
            for slot in range(SLOTS):
                compute(group * SLOTS + slot, layer, slot)
            return carry

        lax.fori_loop(0, LOCAL // SLOTS, body, 0)

    def rounded(other, layer, low, rows):
        start = pl.multiple_of(other * HALF + low, 8)
        return wide_rows[layer, pl.ds(start, rows), :]

    def send_wave(wave, low, rows):
        for down, other in sorted_partners:
            if low == 0:
                block = rounded(other, 0, 0, HEAD)
            else:
                block = jnp.concatenate(
                    [rounded(other, 0, HEAD, HALF - HEAD), rounded(other, 1, 0, HALF)], axis=0
                )
            send_ref[other, low : low + rows] = block.astype(jnp.bfloat16)
            remote(
                send_ref.at[other, pl.ds(low, rows)],
                recv_ref.at[slot_here, pl.ds(low, rows)],
                send_sem,
                recv_sem.at[wave, down],
                (other, par),
            ).start()

    products(0)
    pl.semaphore_wait(barrier, greeted)
    send_wave(0, 0, HEAD)
    products(1)
    send_wave(1, HEAD, CHUNK - HEAD)

    flat = diagonal_energy(spin_ref[...])
    energy_ref[...] = jnp.zeros_like(energy_ref)
    energy_ref[:, :LOCAL] = flat[:, :LOCAL] + off_ref[...]
    for _, other in partners:
        remote(energy_ref, energies_ref.at[samp], esem.at[0], esem.at[1], (other, par)).start()
    energies_ref[samp] = energy_ref[...]
    recv_ref[slot_here] = jnp.concatenate(
        [rounded(samp, layer, 0, HALF) for layer in range(LAYERS)], axis=0
    ).astype(jnp.bfloat16)
    def await_wave(wave, low, rows):
        for down in range(NY):
            at = wrap(y + NY - down, NY) * NZ
            slots = pl.ds(0, NZ - 1) if down == 0 else pl.ds(at, NZ)
            landed = recv_ref.at[slots, pl.ds(low, rows)]
            remote(landed, landed, send_sem, recv_sem.at[wave, down], sibling).wait_recv()

    await_wave(0, 0, HEAD)
    for pair in range(ROWS // 2):
        if pair == HEAD // 16:
            await_wave(1, HEAD, CHUNK - HEAD)
        tile = jnp.stack(
            [
                recv_ref[(src % NY) * NZ + src // NY, 16 * pair : 16 * pair + 16, :].astype(jnp.float32)
                for src in range(NSAMP)
            ]
        ).reshape(NSAMP, 2, LOCAL, 128)
        halves = []
        for half in range(2):
            part = tile[:, half]
            mean = jnp.sum(jnp.sum(part, axis=0), axis=0, keepdims=True) / NS
            cent = ((part - mean) / math.sqrt(NS)).reshape(NS, 128)
            halves.append(cent.astype(jnp.bfloat16))
        cent = jnp.concatenate(halves, axis=1)
        cent_ref[:, 256 * pair : 256 * pair + 256] = cent
        light = lax.dot_general(
            cent[:128], cent[:128], (((1,), (1,)), ((), ())), preferred_element_type=jnp.float32
        )
        heavy = lax.dot_general(
            cent[128:], cent, (((1,), (1,)), ((), ())), preferred_element_type=jnp.float32
        )
        if pair == 0:
            part_ref[:128, :128] = light
            part_ref[128:, :] = heavy
        else:
            part_ref[:128, :128] += light
            part_ref[128:, :] += heavy
    eye = lax.broadcasted_iota(jnp.int32, (128, 128), 0) == lax.broadcasted_iota(
        jnp.int32, (128, 128), 1
    )
    trace = jnp.sum(
        jnp.where(eye, part_ref[:128, :128] + part_ref[128:, 128:], 0.0), keepdims=True
    )
    corner = jnp.logical_and(
        lax.broadcasted_iota(jnp.int32, (8, 128), 0) == 0,
        lax.broadcasted_iota(jnp.int32, (8, 128), 1) == 127,
    )
    part_ref[:8, :128] = jnp.where(corner, trace, part_ref[:8, :128])

    def rows_of(side, index):
        return pl.ds(pl.multiple_of(side * 128 + index * 8, 8), 8)

    slot = core * CHIPS + chip
    widths = (128, NS)

    def send_first(other, device, side):
        wide = pl.ds(0, widths[side])
        remote(
            part_ref.at[rows_of(side, other), wide],
            first.at[slot, :, wide],
            sem1.at[side],
            sem1.at[2],
            device,
        ).start()

    by_core(lambda side, width: send_first(chip, sibling, 0) if side == 1 else None)
    for kind in range(2):
        for other, device, side in around:
            if side == kind:
                send_first(other, device, side)
    by_core(lambda side, width: send_first(chip, sibling, 1) if side == 0 else None)

    def middle(side, width):
        wide = pl.ds(0, width)
        first[slot, :, wide] = part_ref[rows_of(side, chip), wide]
        landed = first.at[pl.ds(0, 2 * CHIPS - 1), :, wide]
        remote(landed, landed, sem1.at[0], sem1.at[2], sibling).wait_recv()
        own = jnp.sum(first[:, :, wide], axis=0)
        mine[:, wide] = own
        for hop in (4, 3, 5, 2, 6, 1, 7):
            device = (zs[hop] * NY + y, par)
            remote(
                mine.at[:, wide], second.at[z, :, wide], sem2.at[0], sem2.at[1], device
            ).start()
        second[z, :, wide] = own
        landed = second.at[pl.ds(0, NZ - 1), :, wide]
        remote(landed, landed, sem2.at[0], sem2.at[1], sibling).wait_recv()
        block = rows_of(side, chip)
        gram_ref[block, wide] = jnp.sum(second[:, :, wide], axis=0)
        done = gram_ref.at[block, wide]
        kind = 1 + y // 2 if side == 0 else 3
        for _, device, _ in around:
            remote(done, done, sem3.at[0], sem3.at[kind], device).start()
        remote(done, done, sem3.at[0], sem3.at[kind], sibling).start()

    by_core(middle)

    def await_rows(kind, count, width, own_kind):
        for less in range(2):

            @pl.when(own_kind if less else jnp.logical_not(own_kind))
            def _(less=less):
                landed = gram_ref.at[pl.ds(0, (count - less) * 8), pl.ds(0, width)]
                remote(landed, landed, sem3.at[0], sem3.at[kind], sibling).wait_recv()

    energy_bytes = energies_ref.at[pl.ds(0, NSAMP - 1)]
    remote(energy_bytes, energy_bytes, esem.at[0], esem.at[1], sibling).wait()
    pieces = jnp.broadcast_to(energies_ref[...], (NSAMP, LOCAL, 128)).reshape(NS, 128)
    lane = lax.broadcasted_iota(jnp.int32, (NS, 128), 1)
    row = lax.broadcasted_iota(jnp.int32, (NSAMP, LOCAL, 128), 1).reshape(NS, 128)
    energy = jnp.sum(jnp.where(lane == row, pieces, 0.0), axis=1, keepdims=True)
    mean = jnp.sum(energy, axis=0, keepdims=True) / NS
    residual = -(energy - mean) / math.sqrt(NS)
    work[:, NS:] = jnp.broadcast_to(residual, (NS, 128))

    await_rows(1, 8, 128, jnp.logical_and(core == 0, y < 2))
    level = 1.0 / (gram_ref[0:1, 127:128] / NS)
    block_eye = lax.broadcasted_iota(jnp.int32, (BLOCK, BLOCK), 0) == lax.broadcasted_iota(
        jnp.int32, (BLOCK, BLOCK), 1
    )
    leading = gram_ref[:BLOCK, :BLOCK] * level + jnp.where(block_eye, 0.01, 0.0)
    factors = forward_block(leading, tile_ref, column_ref, cross_ref)
    await_rows(2, 8, 128, jnp.logical_and(core == 0, y >= 2))
    await_rows(3, CHIPS, NS, core == 1)

    below = gram_ref[128:, :128]
    above = gram_ref[:128, :128]
    wide_corner = jnp.logical_and(
        lax.broadcasted_iota(jnp.int32, (128, 128), 0) == 0,
        lax.broadcasted_iota(jnp.int32, (128, 128), 1) == 127,
    )
    above = jnp.where(wide_corner, gram_ref[127:128, 0:1], above)
    gram = jnp.concatenate(
        [jnp.concatenate([above, below.T], axis=1), gram_ref[128:, :]], axis=0
    )
    diagonal = lax.broadcasted_iota(jnp.int32, (NS, NS), 0) == lax.broadcasted_iota(
        jnp.int32, (NS, NS), 1
    )
    work[:, :NS] = gram * level + jnp.where(diagonal, 0.01, 0.0)

    for index in range(NS // BLOCK):
        low = index * BLOCK
        own = slice(low, low + BLOCK)
        rest = slice(128 * ((index + 1) // 2), NS + 128)
        if index > 0:
            factors = forward_block(work[own, own], tile_ref, column_ref, cross_ref)
        lower, scaled = factors
        middle_rows = product(scaled, work[own, rest], 1, 0)
        outer = product(work[:, own], lower, 1, 1)
        work[:, rest] = work[:, rest] - product(outer, middle_rows, 1, 0)
        work[own, rest] = product(lower, middle_rows, 0, 0)

    coeff = work[:, NS:] * level
    held[...] = coeff
    own = held[pl.ds(pl.multiple_of(samp * LOCAL, LOCAL), LOCAL), :]
    here = lax.broadcasted_iota(jnp.int32, (LOCAL, 128), 0) == lax.broadcasted_iota(
        jnp.int32, (LOCAL, 128), 1
    )
    coeff_ref[...] = jnp.sum(jnp.where(here, own, 0.0), axis=0, keepdims=True)[:, :LOCAL]
    both = jnp.concatenate([coeff, coeff], axis=1)
    weighted = jnp.sum(gram * both, axis=0, keepdims=True)
    across = jnp.sum(jnp.where(diagonal, both, 0.0), axis=0, keepdims=True)
    square_total = jnp.sum(weighted * across, keepdims=True)
    scale = lax.rsqrt(square_total / ENTRIES + 1e-06)
    for index in range(ROWS):
        cent = cent_ref[:, 128 * index : 128 * index + 128].astype(jnp.float32)
        layer, column = index // (ROWS // 2), 128 * (index % (ROWS // 2))
        update_ref[layer : layer + 1, column : column + 128] = (
            jnp.sum(cent * coeff, axis=0, keepdims=True) * scale
        )

    sent = send_ref.at[pl.ds(0, NSAMP - 1)]
    remote(sent, sent, send_sem, recv_sem.at[0, 0], sibling).wait_send()

    def finish(side, width):
        wide = pl.ds(0, width)
        for kind in range(2):
            count = CHIPS - 1 if kind == side else CHIPS
            bytes_ref = gram_ref.at[pl.ds(0, count * 8), pl.ds(0, widths[kind])]
            remote(bytes_ref, bytes_ref, sem1.at[kind], sem1.at[2], sibling).wait_send()
        landed = second.at[pl.ds(0, NZ - 1), :, wide]
        remote(landed, landed, sem2.at[0], sem2.at[1], sibling).wait_send()
        landed = first.at[pl.ds(0, 2 * CHIPS - 1), :, wide]
        remote(landed, landed, sem3.at[0], sem1.at[2], sibling).wait_send()

    by_core(finish)


def main_call(activations, cotangents, spin_bits, off_row):
    whole = pl.BlockSpec(memory_space=VMEM)
    anywhere = pl.BlockSpec(memory_space=pl.ANY)
    dma = pltpu.SemaphoreType.DMA
    return pl.pallas_call(
        main_kernel,
        in_specs=[anywhere, anywhere, whole, whole],
        out_specs=[whole, whole],
        out_shape=[
            jax.ShapeDtypeStruct((LAYERS, ROWS * CH), jnp.float32),
            jax.ShapeDtypeStruct((1, LOCAL), jnp.float32),
        ],
        scratch_shapes=[
            VMEM((LOCAL, LAYERS, CH, SITES), jnp.bfloat16),
            VMEM((LOCAL, LAYERS, CH, SITES), jnp.bfloat16),
            VMEM((2, CH, SITES), jnp.bfloat16),
            VMEM((SLOTS, 3 * CH, PADK), jnp.bfloat16),
            VMEM((SLOTS, 3 * CH, PADK), jnp.bfloat16),
            VMEM((SLOTS, 2, 3 * CH, 128), jnp.float32),
            VMEM((LAYERS, NSAMP * HALF, 128), jnp.float32),
            VMEM((NSAMP, CHUNK, 128), jnp.bfloat16),
            VMEM((NSAMP, CHUNK, 128), jnp.bfloat16),
            VMEM((NS, WIDTH), jnp.bfloat16),
            VMEM((1, 128), jnp.float32),
            VMEM((NSAMP, 1, 128), jnp.float32),
            VMEM((NS, NS), jnp.float32),
            VMEM((2 * CHIPS, 8, NS), jnp.float32),
            VMEM((8, NS), jnp.float32),
            VMEM((NZ, 8, NS), jnp.float32),
            VMEM((NS, NS), jnp.float32),
            VMEM((NS, NS + 128), jnp.float32),
            VMEM((NS, 128), jnp.float32),
            VMEM((BLOCK // PANEL, 1, 8, 128), jnp.float32),
            VMEM((BLOCK // PANEL, PANEL, 8, 128), jnp.float32),
            VMEM((BLOCK // PANEL, PANEL, 8, 128), jnp.float32),
            dma((LAYERS, LOCAL)),
            dma((LAYERS, LOCAL)),
            dma,
            dma((2, NY)),
            dma((2,)),
            dma((3,)),
            dma((2,)),
            dma((4,)),
        ],
        compiler_params=pltpu.CompilerParams(
            collective_id=0, has_side_effects=True, vmem_limit_bytes=VMEM_LIMIT
        ),
    )(activations, cotangents, spin_bits, off_row)


def hand_on_kernel(update_in, coeff_in, update_ref, coeff_ref, sems):
    copies = [
        pltpu.make_async_copy(update_in, update_ref, sems.at[0]),
        pltpu.make_async_copy(coeff_in, coeff_ref, sems.at[1]),
    ]
    for copy in copies:
        copy.start()
    for copy in copies:
        copy.wait()


def hand_on(update, coeff):
    anywhere = pl.BlockSpec(memory_space=pl.ANY)
    return pl.pallas_call(
        hand_on_kernel,
        in_specs=[anywhere, anywhere],
        out_specs=[anywhere, anywhere],
        out_shape=[
            jax.ShapeDtypeStruct((LAYERS, ROWS * CH), jnp.float32),
            jax.ShapeDtypeStruct((1, LOCAL), jnp.float32),
        ],
        scratch_shapes=[pltpu.SemaphoreType.DMA((2,))],
        compiler_params=pltpu.CompilerParams(vmem_limit_bytes=VMEM_LIMIT),
    )(update, coeff)


def on_device(activations, cotangents, spin_bits, offdiag_energy):
    update, coeff = hand_on(
        *main_call(activations, cotangents, spin_bits, offdiag_energy.reshape(1, LOCAL))
    )
    return update, coeff.reshape(LOCAL)


def solution(mesh):
    in_specs = (
        P("samp", "par", None, None),
        P("samp", "par", None, None),
        P("samp", None),
        P("samp"),
    )
    out_specs = (P("par", "samp"), P("samp"))
    return jax.shard_map(
        on_device, mesh=mesh, in_specs=in_specs, out_specs=out_specs, check_vma=False
    )
```

```python
import math

import jax
import jax.numpy as jnp
from jax import lax
from jax.experimental import pallas as pl
from jax.experimental.pallas import tpu as pltpu
from jax.sharding import PartitionSpec as P

CH = 64
KK = 9
LAT = 24
SITES = LAT * LAT
NSAMP = 32
NPAR = 8
NZ = 8
NY = 4
LOCAL = 8
NS = NSAMP * LOCAL
ROWS = KK * CH // NSAMP
CHUNK = ROWS * LOCAL
WIDTH = ROWS * 128
PADK = 640
LAYERS = 2
ENTRIES = 16 * KK * CH * CH
MESH = pl.DeviceIdType.MESH
VMEM_LIMIT = 56 * 1024 * 1024
HIGHEST = lax.Precision.HIGHEST
VMEM = pltpu.VMEM


def rolled(value, amount):
    amount = amount % SITES
    if amount == 0:
        return value
    return jnp.concatenate([value[:, amount:], value[:, :amount]], axis=1)


def edge_mask(shape, col_step):
    column = lax.broadcasted_iota(jnp.int32, shape, 1) % LAT
    return column == (LAT - 1 if col_step > 0 else 0)


def column_shift(value, col_step, edge):
    if col_step == 0:
        return value
    return jnp.where(edge, rolled(value, col_step - LAT * col_step), rolled(value, col_step))


def wrap(value, size):
    return lax.select(value >= size, value - size, value)


STEPS = [(down, hop) for down in range(NY) for hop in (1, 7, 2, 6, 3, 5, 4, 0) if (down, hop) != (0, 0)]


def diagonal_energy(spin_bits):
    spin = (2 * spin_bits - 1).astype(jnp.float32)
    right = column_shift(spin, 1, edge_mask(spin.shape, 1))
    left = column_shift(spin, -1, edge_mask(spin.shape, -1))
    pairs = spin * rolled(spin, LAT) + spin * right
    corners = spin * rolled(right, LAT) + spin * rolled(left, LAT)
    diag = 0.25 * jnp.sum(pairs + 0.5 * corners, axis=1, keepdims=True)
    wide = jnp.broadcast_to(diag, (LOCAL, 128))
    here = lax.broadcasted_iota(jnp.int32, (LOCAL, 128), 0) == lax.broadcasted_iota(
        jnp.int32, (LOCAL, 128), 1
    )
    return jnp.sum(jnp.where(here, wide, 0.0), axis=0, keepdims=True)


PLANE = sorted(
    ((down, across) for down in range(NY) for across in range(4) if (down, across) != (0, 0)),
    key=lambda step: -(min(step[0], NY - step[0]) + min(step[1], 4 - step[1])),
)
PAIRS = 3 * CH // 2
HALF = CHUNK // 2
HEAD = 64
SLOTS = 4
CHIPS = 16


BLOCK = 64
PANEL = 8


def forward_block(diag, tile_ref, column_ref, cross_ref):
    eye = lax.broadcasted_iota(jnp.int32, (BLOCK, BLOCK), 0) == lax.broadcasted_iota(
        jnp.int32, (BLOCK, BLOCK), 1
    )
    wide = jnp.concatenate([diag, jnp.where(eye, 1.0, 0.0)], axis=1)
    count = BLOCK // PANEL
    tiles = [wide[8 * q : 8 * q + 8] for q in range(count)]
    sub = lax.broadcasted_iota(jnp.int32, (8, 128), 0)

    def lanes(tile, col):
        return jnp.broadcast_to(tile[:, col : col + 1], (8, 128))

    def joined(parts):
        total = parts[0]
        for i in range(1, PANEL):
            total = jnp.where(sub == i, parts[i], total)
        return total

    def broadcast_row(ref, panel, j, i):
        return ref[panel, j, pl.ds(i, 8, stride=0), :]

    reduced, scaled = [], []
    columns = [lanes(tiles[0], j) for j in range(PANEL)]
    for panel in range(count):
        base = panel * PANEL
        last = panel == count - 1
        tile_ref[panel, 0] = tiles[panel]
        for j in range(PANEL):
            column_ref[panel, j] = columns[j]
        low = {
            (i, j): broadcast_row(column_ref, panel, j, i)
            for i in range(PANEL)
            for j in range(i + 1)
        }
        rows = [broadcast_row(tile_ref, panel, 0, i) for i in range(PANEL)]
        old_columns = {
            q: [lanes(tiles[q], base + i) for i in range(PANEL)] for q in range(panel + 1, count)
        }
        if not last:
            cross = list(old_columns[panel + 1])
            columns = [lanes(tiles[panel + 1], base + PANEL + j) for j in range(PANEL)]
        ups, downs, starts, cross_scaled = {}, {}, {}, {}
        for p in range(0, PANEL, 2):
            q = p + 1
            a, b, c = low[p, p], low[q, p], low[q, q]
            recip = pl.reciprocal(a * c - b * b, approx=True)
            for i in range(q + 1, PANEL):
                up = c * low[i, p] - b * low[i, q]
                down = a * low[i, q] - b * low[i, p]
                for m in range(q + 1, i + 1):
                    low[i, m] = low[i, m] - (up * low[m, p] + down * low[m, q]) * recip
                ups[i, p], downs[i, p] = up * recip, down * recip
            if not last:
                cross_scaled[p] = (c * cross[p] - b * cross[q]) * recip
                cross_scaled[q] = (a * cross[q] - b * cross[p]) * recip
                for i in range(q + 1, PANEL):
                    cross[i] = cross[i] - (ups[i, p] * cross[p] + downs[i, p] * cross[q])
            starts[p] = (c * rows[p] - b * rows[q]) * recip
            starts[q] = (a * rows[q] - b * rows[p]) * recip
            for i in range(q + 1, PANEL):
                rows[i] = rows[i] - (ups[i, p] * rows[p] + downs[i, p] * rows[q])
        if not last:
            for i in range(PANEL):
                cross_ref[panel, i] = cross[i]
            for j in range(PANEL):
                terms = [
                    cross_scaled[i] * broadcast_row(cross_ref, panel, i, j) for i in range(PANEL)
                ]
                while len(terms) > 1:
                    terms = [terms[a] + terms[a + 1] for a in range(0, len(terms), 2)]
                columns[j] = columns[j] - terms[0]
        reduced.append(joined(rows))
        scaled.append(joined([starts[i] for i in range(PANEL)]))
        if last:
            break
        solved = [None] * PANEL
        for p in reversed(range(0, PANEL, 2)):
            for total, factor, at in ((starts[p], ups, p), (starts[p + 1], downs, p + 1)):
                for i in reversed(range(p + 2, PANEL)):
                    total = total - factor[i, p] * solved[i]
                solved[at] = total
        for q in range(panel + 1, count):
            terms = [old_columns[q][i] * solved[i] for i in range(PANEL)]
            while len(terms) > 1:
                terms = [terms[a] + terms[a + 1] for a in range(0, len(terms), 2)]
            tiles[q] = tiles[q] - terms[0]
    lower = jnp.concatenate(reduced, axis=0)[:, BLOCK:]
    return lower, jnp.concatenate(scaled, axis=0)[:, BLOCK:]


def product(one, two, first_dim, second_dim):
    return lax.dot_general(
        one, two, (((first_dim,), (second_dim,)), ((), ())),
        precision=HIGHEST, preferred_element_type=jnp.float32,
    )


def main_kernel(
    act_hbm, cot_hbm, spin_ref, off_ref,
    update_ref, coeff_ref,
    act_ref, cot_ref, edges, lhs, rhs, stage, wide_rows, send_ref, recv_ref, cent_ref,
    energy_ref, energies_ref, part_ref, first, mine, second, gram_ref,
    work, held, tile_ref, column_ref, cross_ref,
    act_sem, cot_sem, send_sem, recv_sem, esem, sem1, sem2, sem3,
):
    samp = lax.axis_index("samp")
    par = lax.axis_index("par")
    z, y = samp // NY, samp % NY
    x, core = par // 2, par % 2
    slot_here = y * NZ + z
    sibling = (samp, x * 2 + 1 - core)
    zs = [wrap(z + hop, NZ) for hop in range(NZ)]
    ys = [wrap(y + down, NY) for down in range(NY)]
    xs = [wrap(x + across, 4) for across in range(4)]
    partners = [(down, zs[hop] * NY + ys[down]) for down, hop in STEPS]
    sorted_partners = [
        item for item, (_, hop) in sorted(zip(partners, STEPS), key=lambda pair: -min(pair[1][1], NZ - pair[1][1]))
    ]
    chip = y * 4 + x
    others = [
        (ys[down] * 4 + xs[across], z * NY + ys[down], xs[across] * 2)
        for down, across in PLANE
    ]
    around = [(other, (row, pair + side), side) for other, row, pair in others for side in range(2)]

    def by_core(body):
        @pl.when(core == 0)
        def _():
            body(0, 128)

        @pl.when(core == 1)
        def _():
            body(1, NS)

    def act_copy(n, layer):
        return pltpu.make_async_copy(
            act_hbm.at[n, layer], act_ref.at[n, layer], act_sem.at[layer, n]
        )

    def cot_copy(n, layer):
        return pltpu.make_async_copy(
            cot_hbm.at[n, layer], cot_ref.at[n, layer], cot_sem.at[layer, n]
        )

    for layer in range(LAYERS):
        for n in range(LOCAL):
            act_copy(n, layer).start()
            cot_copy(n, layer).start()

    def remote(source, target, send, recv, device):
        return pltpu.make_async_remote_copy(
            src_ref=source,
            dst_ref=target,
            send_sem=send,
            recv_sem=recv,
            device_id=device,
            device_id_type=MESH,
        )

    barrier = pltpu.get_barrier_semaphore()
    greeted = 0
    for _, other in partners:
        pl.semaphore_signal(barrier, inc=1, device_id=(other, par), device_id_type=MESH)
        greeted += 1
    for down in range(NY):
        for across in range(4):
            for side in (core, 1 - core):
                if across > 0 or side is not core:
                    device = (z * NY + ys[down], xs[across] * 2 + side)
                    pl.semaphore_signal(barrier, inc=1, device_id=device, device_id_type=MESH)
                    greeted += 1

    left = lax.broadcasted_iota(jnp.int32, (PAIRS, 128), 1) < CH
    lhs[:, :, PADK - 128 :] = jnp.zeros((SLOTS, 3 * CH, 128), jnp.bfloat16)
    rhs[:, :, PADK - 128 :] = jnp.zeros((SLOTS, 3 * CH, 128), jnp.bfloat16)
    stage[:, 1] = jnp.zeros((SLOTS, 3 * CH, 128), jnp.float32)
    for at, step in enumerate((-1, 1)):
        strip = jnp.where(edge_mask((8, SITES), step), 1.0, 0.0)
        edges[at] = jnp.concatenate([strip] * (CH // 8), axis=0).astype(jnp.bfloat16)

    def compute(sample, layer, slot):
        act = act_ref[sample, layer]
        cot = cot_ref[sample, layer]
        for step in (-1, 0, 1):
            low = (step + 1) * CH
            edge = edges[max(step, 0)] > 0
            lhs[slot, low : low + CH, :SITES] = column_shift(act, step, edge)
            rhs[slot, low : low + CH, :SITES] = rolled(cot, -LAT * step)
        out = lax.dot_general(
            lhs[slot], rhs[slot], (((1,), (1,)), ((), ())), preferred_element_type=jnp.float32
        )
        stage[slot, 0] = out[:, :128]
        stage[slot, 1, :, :CH] = out[:, 128:]
        even, odd, even_last, odd_last = [
            stage[slot, part, pl.ds(parity, PAIRS, stride=2), :]
            for part in (0, 1)
            for parity in (0, 1)
        ]
        blocks = (
            jnp.where(left, even, pltpu.roll(odd, CH, 1)),
            jnp.where(left, pltpu.roll(even, CH, 1), odd),
            jnp.where(left, even_last, pltpu.roll(odd_last, CH, 1)),
        )
        for down in range(3):
            wide_rows[layer, pl.ds(down * PAIRS * LOCAL + sample, PAIRS, stride=LOCAL), :] = blocks[down]

    def products(layer):
        def body(group, carry):
            for slot in range(SLOTS):
                sample = group * SLOTS + slot
                act_copy(sample, layer).wait()
                cot_copy(sample, layer).wait()
            for slot in range(SLOTS):
                compute(group * SLOTS + slot, layer, slot)
            return carry

        lax.fori_loop(0, LOCAL // SLOTS, body, 0)

    def rounded(other, layer, low, rows):
        start = pl.multiple_of(other * HALF + low, 8)
        return wide_rows[layer, pl.ds(start, rows), :]

    def send_wave(wave, low, rows):
        for down, other in sorted_partners:
            if low == 0:
                block = rounded(other, 0, 0, HEAD)
            else:
                block = jnp.concatenate(
                    [rounded(other, 0, HEAD, HALF - HEAD), rounded(other, 1, 0, HALF)], axis=0
                )
            send_ref[other, low : low + rows] = block.astype(jnp.bfloat16)
            remote(
                send_ref.at[other, pl.ds(low, rows)],
                recv_ref.at[slot_here, pl.ds(low, rows)],
                send_sem,
                recv_sem.at[wave, down],
                (other, par),
            ).start()

    products(0)
    pl.semaphore_wait(barrier, greeted)
    send_wave(0, 0, HEAD)
    products(1)
    send_wave(1, HEAD, CHUNK - HEAD)

    flat = diagonal_energy(spin_ref[...])
    energy_ref[...] = jnp.zeros_like(energy_ref)
    energy_ref[:, :LOCAL] = flat[:, :LOCAL] + off_ref[...]
    for _, other in partners:
        remote(energy_ref, energies_ref.at[samp], esem.at[0], esem.at[1], (other, par)).start()
    energies_ref[samp] = energy_ref[...]
    recv_ref[slot_here] = jnp.concatenate(
        [rounded(samp, layer, 0, HALF) for layer in range(LAYERS)], axis=0
    ).astype(jnp.bfloat16)
    def await_wave(wave, low, rows):
        for down in range(NY):
            at = wrap(y + NY - down, NY) * NZ
            slots = pl.ds(0, NZ - 1) if down == 0 else pl.ds(at, NZ)
            landed = recv_ref.at[slots, pl.ds(low, rows)]
            remote(landed, landed, send_sem, recv_sem.at[wave, down], sibling).wait_recv()

    await_wave(0, 0, HEAD)
    for pair in range(ROWS // 2):
        if pair == HEAD // 16:
            await_wave(1, HEAD, CHUNK - HEAD)
        tile = jnp.stack(
            [
                recv_ref[(src % NY) * NZ + src // NY, 16 * pair : 16 * pair + 16, :].astype(jnp.float32)
                for src in range(NSAMP)
            ]
        ).reshape(NSAMP, 2, LOCAL, 128)
        halves = []
        for half in range(2):
            part = tile[:, half]
            mean = jnp.sum(jnp.sum(part, axis=0), axis=0, keepdims=True) / NS
            cent = ((part - mean) / math.sqrt(NS)).reshape(NS, 128)
            halves.append(cent.astype(jnp.bfloat16))
        cent = jnp.concatenate(halves, axis=1)
        cent_ref[:, 256 * pair : 256 * pair + 256] = cent
        light = lax.dot_general(
            cent[:128], cent[:128], (((1,), (1,)), ((), ())), preferred_element_type=jnp.float32
        )
        heavy = lax.dot_general(
            cent[128:], cent, (((1,), (1,)), ((), ())), preferred_element_type=jnp.float32
        )
        if pair == 0:
            part_ref[:128, :128] = light
            part_ref[128:, :] = heavy
        else:
            part_ref[:128, :128] += light
            part_ref[128:, :] += heavy
    eye = lax.broadcasted_iota(jnp.int32, (128, 128), 0) == lax.broadcasted_iota(
        jnp.int32, (128, 128), 1
    )
    trace = jnp.sum(
        jnp.where(eye, part_ref[:128, :128] + part_ref[128:, 128:], 0.0), keepdims=True
    )
    corner = jnp.logical_and(
        lax.broadcasted_iota(jnp.int32, (8, 128), 0) == 0,
        lax.broadcasted_iota(jnp.int32, (8, 128), 1) == 127,
    )
    part_ref[:8, :128] = jnp.where(corner, trace, part_ref[:8, :128])

    def rows_of(side, index):
        return pl.ds(pl.multiple_of(side * 128 + index * 8, 8), 8)

    slot = core * CHIPS + chip
    widths = (128, NS)

    def send_first(other, device, side):
        wide = pl.ds(0, widths[side])
        remote(
            part_ref.at[rows_of(side, other), wide],
            first.at[slot, :, wide],
            sem1.at[side],
            sem1.at[2],
            device,
        ).start()

    by_core(lambda side, width: send_first(chip, sibling, 0) if side == 1 else None)
    for kind in range(2):
        for other, device, side in around:
            if side == kind:
                send_first(other, device, side)
    by_core(lambda side, width: send_first(chip, sibling, 1) if side == 0 else None)

    def middle(side, width):
        wide = pl.ds(0, width)
        first[slot, :, wide] = part_ref[rows_of(side, chip), wide]
        landed = first.at[pl.ds(0, 2 * CHIPS - 1), :, wide]
        remote(landed, landed, sem1.at[0], sem1.at[2], sibling).wait_recv()
        own = jnp.sum(first[:, :, wide], axis=0)
        mine[:, wide] = own
        for hop in (4, 3, 5, 2, 6, 1, 7):
            device = (zs[hop] * NY + y, par)
            remote(
                mine.at[:, wide], second.at[z, :, wide], sem2.at[0], sem2.at[1], device
            ).start()
        second[z, :, wide] = own
        landed = second.at[pl.ds(0, NZ - 1), :, wide]
        remote(landed, landed, sem2.at[0], sem2.at[1], sibling).wait_recv()
        block = rows_of(side, chip)
        gram_ref[block, wide] = jnp.sum(second[:, :, wide], axis=0)
        done = gram_ref.at[block, wide]
        for _, device, _ in around:
            remote(done, done, sem3.at[0], sem3.at[1 + side], device).start()
        remote(done, done, sem3.at[0], sem3.at[1 + side], sibling).start()

    by_core(middle)

    def await_rows(kind):
        def body(side, width):
            count = CHIPS - 1 if side == kind else CHIPS
            landed = gram_ref.at[pl.ds(0, count * 8), pl.ds(0, widths[kind])]
            remote(landed, landed, sem3.at[0], sem3.at[1 + kind], sibling).wait_recv()

        by_core(body)

    energy_bytes = energies_ref.at[pl.ds(0, NSAMP - 1)]
    remote(energy_bytes, energy_bytes, esem.at[0], esem.at[1], sibling).wait()
    pieces = jnp.broadcast_to(energies_ref[...], (NSAMP, LOCAL, 128)).reshape(NS, 128)
    lane = lax.broadcasted_iota(jnp.int32, (NS, 128), 1)
    row = lax.broadcasted_iota(jnp.int32, (NSAMP, LOCAL, 128), 1).reshape(NS, 128)
    energy = jnp.sum(jnp.where(lane == row, pieces, 0.0), axis=1, keepdims=True)
    mean = jnp.sum(energy, axis=0, keepdims=True) / NS
    residual = -(energy - mean) / math.sqrt(NS)
    work[:, NS:] = jnp.broadcast_to(residual, (NS, 128))

    await_rows(0)
    level = 1.0 / (gram_ref[0:1, 127:128] / NS)
    wide_corner = jnp.logical_and(
        lax.broadcasted_iota(jnp.int32, (128, 128), 0) == 0,
        lax.broadcasted_iota(jnp.int32, (128, 128), 1) == 127,
    )
    light = jnp.where(wide_corner, gram_ref[127:128, 0:1], gram_ref[:128, :128])
    ridge = jnp.where(eye, 0.01, 0.0)
    work[:128, :128] = light * level + ridge
    one, two = slice(0, BLOCK), slice(BLOCK, 2 * BLOCK)
    lower_one, scaled_one = forward_block(work[one, one], tile_ref, column_ref, cross_ref)
    left = product(work[two, one], lower_one, 1, 1)
    right = product(scaled_one, work[one, two], 1, 0)
    lower_two, scaled_two = forward_block(
        work[two, two] - product(left, right, 1, 0), tile_ref, column_ref, cross_ref
    )
    cross_part = product(left, scaled_one, 1, 0)
    blank = jnp.zeros((BLOCK, BLOCK), jnp.float32)

    def joined_factor(first_part, second_part):
        return jnp.concatenate(
            [
                jnp.concatenate([first_part, blank], axis=1),
                jnp.concatenate([-product(second_part, cross_part, 1, 0), second_part], axis=1),
            ],
            axis=0,
        )

    lower = joined_factor(lower_one, lower_two)
    scaled = joined_factor(scaled_one, scaled_two)

    await_rows(1)
    below = gram_ref[128:, :128]
    corner_block = gram_ref[128:, 128:]
    scaled_below = below * level
    work[:128, 128:NS] = scaled_below.T
    work[128:, 128:NS] = corner_block * level + ridge
    middle_rows = product(scaled, work[:128, 128:], 1, 0)
    outer = product(scaled_below, lower, 1, 1)
    work[128:, 128:] = work[128:, 128:] - product(outer, middle_rows, 1, 0)
    work[:128, 128:] = product(lower, middle_rows, 0, 0)

    for index in range(2, NS // BLOCK):
        low = index * BLOCK
        own = slice(low, low + BLOCK)
        rest = slice(128 * ((index + 1) // 2), NS + 128)
        lower, scaled = forward_block(work[own, own], tile_ref, column_ref, cross_ref)
        middle_rows = product(scaled, work[own, rest], 1, 0)
        outer = product(work[:, own], lower, 1, 1)
        work[:, rest] = work[:, rest] - product(outer, middle_rows, 1, 0)
        work[own, rest] = product(lower, middle_rows, 0, 0)

    coeff = work[:, NS:] * level
    held[...] = coeff
    own = held[pl.ds(pl.multiple_of(samp * LOCAL, LOCAL), LOCAL), :]
    here = lax.broadcasted_iota(jnp.int32, (LOCAL, 128), 0) == lax.broadcasted_iota(
        jnp.int32, (LOCAL, 128), 1
    )
    coeff_ref[...] = jnp.sum(jnp.where(here, own, 0.0), axis=0, keepdims=True)[:, :LOCAL]
    upper, under = coeff[:128], coeff[128:]
    weighted = jnp.sum(light * upper + 2.0 * (below * under), axis=0, keepdims=True) * jnp.sum(
        jnp.where(eye, upper, 0.0), axis=0, keepdims=True
    ) + jnp.sum(corner_block * under, axis=0, keepdims=True) * jnp.sum(
        jnp.where(eye, under, 0.0), axis=0, keepdims=True
    )
    square_total = jnp.sum(weighted, keepdims=True)
    scale = lax.rsqrt(square_total / ENTRIES + 1e-06)
    for index in range(ROWS):
        cent = cent_ref[:, 128 * index : 128 * index + 128].astype(jnp.float32)
        layer, column = index // (ROWS // 2), 128 * (index % (ROWS // 2))
        update_ref[layer : layer + 1, column : column + 128] = (
            jnp.sum(cent * coeff, axis=0, keepdims=True) * scale
        )

    sent = send_ref.at[pl.ds(0, NSAMP - 1)]
    remote(sent, sent, send_sem, recv_sem.at[0, 0], sibling).wait_send()

    def finish(side, width):
        wide = pl.ds(0, width)
        for kind in range(2):
            count = CHIPS - 1 if kind == side else CHIPS
            bytes_ref = gram_ref.at[pl.ds(0, count * 8), pl.ds(0, widths[kind])]
            remote(bytes_ref, bytes_ref, sem1.at[kind], sem1.at[2], sibling).wait_send()
        landed = second.at[pl.ds(0, NZ - 1), :, wide]
        remote(landed, landed, sem2.at[0], sem2.at[1], sibling).wait_send()
        landed = first.at[pl.ds(0, 2 * CHIPS - 1), :, wide]
        remote(landed, landed, sem3.at[0], sem1.at[2], sibling).wait_send()

    by_core(finish)


def main_call(activations, cotangents, spin_bits, off_row):
    whole = pl.BlockSpec(memory_space=VMEM)
    anywhere = pl.BlockSpec(memory_space=pl.ANY)
    dma = pltpu.SemaphoreType.DMA
    return pl.pallas_call(
        main_kernel,
        in_specs=[anywhere, anywhere, whole, whole],
        out_specs=[whole, whole],
        out_shape=[
            jax.ShapeDtypeStruct((LAYERS, ROWS * CH), jnp.float32),
            jax.ShapeDtypeStruct((1, LOCAL), jnp.float32),
        ],
        scratch_shapes=[
            VMEM((LOCAL, LAYERS, CH, SITES), jnp.bfloat16),
            VMEM((LOCAL, LAYERS, CH, SITES), jnp.bfloat16),
            VMEM((2, CH, SITES), jnp.bfloat16),
            VMEM((SLOTS, 3 * CH, PADK), jnp.bfloat16),
            VMEM((SLOTS, 3 * CH, PADK), jnp.bfloat16),
            VMEM((SLOTS, 2, 3 * CH, 128), jnp.float32),
            VMEM((LAYERS, NSAMP * HALF, 128), jnp.float32),
            VMEM((NSAMP, CHUNK, 128), jnp.bfloat16),
            VMEM((NSAMP, CHUNK, 128), jnp.bfloat16),
            VMEM((NS, WIDTH), jnp.bfloat16),
            VMEM((1, 128), jnp.float32),
            VMEM((NSAMP, 1, 128), jnp.float32),
            VMEM((NS, NS), jnp.float32),
            VMEM((2 * CHIPS, 8, NS), jnp.float32),
            VMEM((8, NS), jnp.float32),
            VMEM((NZ, 8, NS), jnp.float32),
            VMEM((NS, NS), jnp.float32),
            VMEM((NS, NS + 128), jnp.float32),
            VMEM((NS, 128), jnp.float32),
            VMEM((BLOCK // PANEL, 1, 8, 128), jnp.float32),
            VMEM((BLOCK // PANEL, PANEL, 8, 128), jnp.float32),
            VMEM((BLOCK // PANEL, PANEL, 8, 128), jnp.float32),
            dma((LAYERS, LOCAL)),
            dma((LAYERS, LOCAL)),
            dma,
            dma((2, NY)),
            dma((2,)),
            dma((3,)),
            dma((2,)),
            dma((3,)),
        ],
        compiler_params=pltpu.CompilerParams(
            collective_id=0, has_side_effects=True, vmem_limit_bytes=VMEM_LIMIT
        ),
    )(activations, cotangents, spin_bits, off_row)


def hand_on_kernel(update_in, coeff_in, update_ref, coeff_ref, sems):
    copies = [
        pltpu.make_async_copy(update_in, update_ref, sems.at[0]),
        pltpu.make_async_copy(coeff_in, coeff_ref, sems.at[1]),
    ]
    for copy in copies:
        copy.start()
    for copy in copies:
        copy.wait()


def hand_on(update, coeff):
    anywhere = pl.BlockSpec(memory_space=pl.ANY)
    return pl.pallas_call(
        hand_on_kernel,
        in_specs=[anywhere, anywhere],
        out_specs=[anywhere, anywhere],
        out_shape=[
            jax.ShapeDtypeStruct((LAYERS, ROWS * CH), jnp.float32),
            jax.ShapeDtypeStruct((1, LOCAL), jnp.float32),
        ],
        scratch_shapes=[pltpu.SemaphoreType.DMA((2,))],
        compiler_params=pltpu.CompilerParams(vmem_limit_bytes=VMEM_LIMIT),
    )(update, coeff)


def on_device(activations, cotangents, spin_bits, offdiag_energy):
    update, coeff = hand_on(
        *main_call(activations, cotangents, spin_bits, offdiag_energy.reshape(1, LOCAL))
    )
    return update, coeff.reshape(LOCAL)


def solution(mesh):
    in_specs = (
        P("samp", "par", None, None),
        P("samp", "par", None, None),
        P("samp", None),
        P("samp"),
    )
    out_specs = (P("par", "samp"), P("samp"))
    return jax.shard_map(
        on_device, mesh=mesh, in_specs=in_specs, out_specs=out_specs, check_vma=False
    )
```

```python
import math

import jax
import jax.numpy as jnp
from jax import lax
from jax.experimental import pallas as pl
from jax.experimental.pallas import tpu as pltpu
from jax.sharding import PartitionSpec as P

CH = 64
KK = 9
LAT = 24
SITES = LAT * LAT
NSAMP = 32
NPAR = 8
NZ = 8
NY = 4
LOCAL = 8
NS = NSAMP * LOCAL
ROWS = KK * CH // NSAMP
CHUNK = ROWS * LOCAL
WIDTH = ROWS * 128
PADK = 640
LAYERS = 2
ENTRIES = 16 * KK * CH * CH
MESH = pl.DeviceIdType.MESH
VMEM_LIMIT = 56 * 1024 * 1024
HIGHEST = lax.Precision.HIGHEST
VMEM = pltpu.VMEM


def rolled(value, amount):
    amount = amount % SITES
    if amount == 0:
        return value
    return jnp.concatenate([value[:, amount:], value[:, :amount]], axis=1)


def edge_mask(shape, col_step):
    column = lax.broadcasted_iota(jnp.int32, shape, 1) % LAT
    return column == (LAT - 1 if col_step > 0 else 0)


def column_shift(value, col_step, edge):
    if col_step == 0:
        return value
    return jnp.where(edge, rolled(value, col_step - LAT * col_step), rolled(value, col_step))


def wrap(value, size):
    return lax.select(value >= size, value - size, value)


STEPS = [(down, hop) for down in range(NY) for hop in (1, 7, 2, 6, 3, 5, 4, 0) if (down, hop) != (0, 0)]


def diagonal_energy(spin_bits):
    spin = (2 * spin_bits - 1).astype(jnp.float32)
    right = column_shift(spin, 1, edge_mask(spin.shape, 1))
    left = column_shift(spin, -1, edge_mask(spin.shape, -1))
    pairs = spin * rolled(spin, LAT) + spin * right
    corners = spin * rolled(right, LAT) + spin * rolled(left, LAT)
    diag = 0.25 * jnp.sum(pairs + 0.5 * corners, axis=1, keepdims=True)
    wide = jnp.broadcast_to(diag, (LOCAL, 128))
    here = lax.broadcasted_iota(jnp.int32, (LOCAL, 128), 0) == lax.broadcasted_iota(
        jnp.int32, (LOCAL, 128), 1
    )
    return jnp.sum(jnp.where(here, wide, 0.0), axis=0, keepdims=True)


PLANE = sorted(
    ((down, across) for down in range(NY) for across in range(4) if (down, across) != (0, 0)),
    key=lambda step: -(min(step[0], NY - step[0]) + min(step[1], 4 - step[1])),
)
PAIRS = 3 * CH // 2
HALF = CHUNK // 2
HEAD = 64
TAIL = 112
SLOTS = 4
CHIPS = 16


BLOCK = 64
PANEL = 8


def forward_block(diag, tile_ref, column_ref, cross_ref):
    eye = lax.broadcasted_iota(jnp.int32, (BLOCK, BLOCK), 0) == lax.broadcasted_iota(
        jnp.int32, (BLOCK, BLOCK), 1
    )
    wide = jnp.concatenate([diag, jnp.where(eye, 1.0, 0.0)], axis=1)
    count = BLOCK // PANEL
    tiles = [wide[8 * q : 8 * q + 8] for q in range(count)]
    sub = lax.broadcasted_iota(jnp.int32, (8, 128), 0)

    def lanes(tile, col):
        return jnp.broadcast_to(tile[:, col : col + 1], (8, 128))

    def joined(parts):
        total = parts[0]
        for i in range(1, PANEL):
            total = jnp.where(sub == i, parts[i], total)
        return total

    def broadcast_row(ref, panel, j, i):
        return ref[panel, j, pl.ds(i, 8, stride=0), :]

    reduced, scaled = [], []
    columns = [lanes(tiles[0], j) for j in range(PANEL)]
    for panel in range(count):
        base = panel * PANEL
        last = panel == count - 1
        tile_ref[panel, 0] = tiles[panel]
        for j in range(PANEL):
            column_ref[panel, j] = columns[j]
        low = {
            (i, j): broadcast_row(column_ref, panel, j, i)
            for i in range(PANEL)
            for j in range(i + 1)
        }
        rows = [broadcast_row(tile_ref, panel, 0, i) for i in range(PANEL)]
        old_columns = {
            q: [lanes(tiles[q], base + i) for i in range(PANEL)] for q in range(panel + 1, count)
        }
        if not last:
            cross = list(old_columns[panel + 1])
            columns = [lanes(tiles[panel + 1], base + PANEL + j) for j in range(PANEL)]
        ups, downs, starts, cross_scaled = {}, {}, {}, {}
        for p in range(0, PANEL, 2):
            q = p + 1
            a, b, c = low[p, p], low[q, p], low[q, q]
            recip = pl.reciprocal(a * c - b * b, approx=True)
            for i in range(q + 1, PANEL):
                up = c * low[i, p] - b * low[i, q]
                down = a * low[i, q] - b * low[i, p]
                ups[i, p], downs[i, p] = up * recip, down * recip
                for m in range(q + 1, i + 1):
                    if i <= q + 2:
                        step = (up * low[m, p] + down * low[m, q]) * recip
                    else:
                        step = ups[i, p] * low[m, p] + downs[i, p] * low[m, q]
                    low[i, m] = low[i, m] - step
            if not last:
                cross_scaled[p] = (c * cross[p] - b * cross[q]) * recip
                cross_scaled[q] = (a * cross[q] - b * cross[p]) * recip
                for i in range(q + 1, PANEL):
                    cross[i] = cross[i] - (ups[i, p] * cross[p] + downs[i, p] * cross[q])
            starts[p] = (c * rows[p] - b * rows[q]) * recip
            starts[q] = (a * rows[q] - b * rows[p]) * recip
            for i in range(q + 1, PANEL):
                rows[i] = rows[i] - (ups[i, p] * rows[p] + downs[i, p] * rows[q])
        if not last:
            for i in range(PANEL):
                cross_ref[panel, i] = cross[i]
            for j in range(PANEL):
                terms = [
                    cross_scaled[i] * broadcast_row(cross_ref, panel, i, j) for i in range(PANEL)
                ]
                while len(terms) > 1:
                    terms = [terms[a] + terms[a + 1] for a in range(0, len(terms), 2)]
                columns[j] = columns[j] - terms[0]
        reduced.append(joined(rows))
        scaled.append(joined([starts[i] for i in range(PANEL)]))
        if last:
            break
        solved = [None] * PANEL
        for p in reversed(range(0, PANEL, 2)):
            for total, factor, at in ((starts[p], ups, p), (starts[p + 1], downs, p + 1)):
                for i in reversed(range(p + 2, PANEL)):
                    total = total - factor[i, p] * solved[i]
                solved[at] = total
        for q in range(panel + 1, count):
            terms = [old_columns[q][i] * solved[i] for i in range(PANEL)]
            while len(terms) > 1:
                terms = [terms[a] + terms[a + 1] for a in range(0, len(terms), 2)]
            tiles[q] = tiles[q] - terms[0]
    lower = jnp.concatenate(reduced, axis=0)[:, BLOCK:]
    return lower, jnp.concatenate(scaled, axis=0)[:, BLOCK:]


def product(one, two, first_dim, second_dim):
    return lax.dot_general(
        one, two, (((first_dim,), (second_dim,)), ((), ())),
        precision=HIGHEST, preferred_element_type=jnp.float32,
    )


def main_kernel(
    act_hbm, cot_hbm, spin_ref, off_ref,
    update_ref, coeff_ref,
    act_ref, cot_ref, edges, lhs, rhs, stage, wide_rows, send_ref, recv_ref, cent_ref,
    energy_ref, energies_ref, part_ref, first, mine, second, gram_ref,
    work, held, tile_ref, column_ref, cross_ref,
    act_sem, cot_sem, send_sem, recv_sem, esem, sem1, sem2, sem3,
):
    samp = lax.axis_index("samp")
    par = lax.axis_index("par")
    z, y = samp // NY, samp % NY
    x, core = par // 2, par % 2
    slot_here = y * NZ + z
    sibling = (samp, x * 2 + 1 - core)
    zs = [wrap(z + hop, NZ) for hop in range(NZ)]
    ys = [wrap(y + down, NY) for down in range(NY)]
    xs = [wrap(x + across, 4) for across in range(4)]
    partners = [(down, zs[hop] * NY + ys[down]) for down, hop in STEPS]
    sorted_partners = [
        item for item, (_, hop) in sorted(zip(partners, STEPS), key=lambda pair: -min(pair[1][1], NZ - pair[1][1]))
    ]
    chip = y * 4 + x
    others = [
        (ys[down] * 4 + xs[across], z * NY + ys[down], xs[across] * 2)
        for down, across in PLANE
    ]
    around = [(other, (row, pair + side), side) for other, row, pair in others for side in range(2)]

    def by_core(body):
        @pl.when(core == 0)
        def _():
            body(0, 128)

        @pl.when(core == 1)
        def _():
            body(1, NS)

    def act_copy(n, layer):
        return pltpu.make_async_copy(
            act_hbm.at[n, layer], act_ref.at[n, layer], act_sem.at[layer, n]
        )

    def cot_copy(n, layer):
        return pltpu.make_async_copy(
            cot_hbm.at[n, layer], cot_ref.at[n, layer], cot_sem.at[layer, n]
        )

    for layer in range(LAYERS):
        for n in range(LOCAL):
            act_copy(n, layer).start()
            cot_copy(n, layer).start()

    def remote(source, target, send, recv, device):
        return pltpu.make_async_remote_copy(
            src_ref=source,
            dst_ref=target,
            send_sem=send,
            recv_sem=recv,
            device_id=device,
            device_id_type=MESH,
        )

    barrier = pltpu.get_barrier_semaphore()
    greeted = 0
    for _, other in partners:
        pl.semaphore_signal(barrier, inc=1, device_id=(other, par), device_id_type=MESH)
        greeted += 1
    for down in range(NY):
        for across in range(4):
            for side in (core, 1 - core):
                if across > 0 or side is not core:
                    device = (z * NY + ys[down], xs[across] * 2 + side)
                    pl.semaphore_signal(barrier, inc=1, device_id=device, device_id_type=MESH)
                    greeted += 1

    left = lax.broadcasted_iota(jnp.int32, (PAIRS, 128), 1) < CH
    lhs[:, :, PADK - 128 :] = jnp.zeros((SLOTS, 3 * CH, 128), jnp.bfloat16)
    rhs[:, :, PADK - 128 :] = jnp.zeros((SLOTS, 3 * CH, 128), jnp.bfloat16)
    stage[:, 1] = jnp.zeros((SLOTS, 3 * CH, 128), jnp.float32)
    for at, step in enumerate((-1, 1)):
        strip = jnp.where(edge_mask((8, SITES), step), 1.0, 0.0)
        edges[at] = jnp.concatenate([strip] * (CH // 8), axis=0).astype(jnp.bfloat16)

    def compute(sample, layer, slot):
        act = act_ref[sample, layer]
        cot = cot_ref[sample, layer]
        for step in (-1, 0, 1):
            low = (step + 1) * CH
            edge = edges[max(step, 0)] > 0
            lhs[slot, low : low + CH, :SITES] = column_shift(act, step, edge)
            rhs[slot, low : low + CH, :SITES] = rolled(cot, -LAT * step)
        out = lax.dot_general(
            lhs[slot], rhs[slot], (((1,), (1,)), ((), ())), preferred_element_type=jnp.float32
        )
        stage[slot, 0] = out[:, :128]
        stage[slot, 1, :, :CH] = out[:, 128:]
        even, odd, even_last, odd_last = [
            stage[slot, part, pl.ds(parity, PAIRS, stride=2), :]
            for part in (0, 1)
            for parity in (0, 1)
        ]
        blocks = (
            jnp.where(left, even, pltpu.roll(odd, CH, 1)),
            jnp.where(left, pltpu.roll(even, CH, 1), odd),
            jnp.where(left, even_last, pltpu.roll(odd_last, CH, 1)),
        )
        for down in range(3):
            wide_rows[layer, pl.ds(down * PAIRS * LOCAL + sample, PAIRS, stride=LOCAL), :] = blocks[down]

    def products(layer):
        def body(group, carry):
            for slot in range(SLOTS):
                sample = group * SLOTS + slot
                act_copy(sample, layer).wait()
                cot_copy(sample, layer).wait()
            for slot in range(SLOTS):
                compute(group * SLOTS + slot, layer, slot)
            return carry

        lax.fori_loop(0, LOCAL // SLOTS, body, 0)

    def rounded(other, layer, low, rows):
        start = pl.multiple_of(other * HALF + low, 8)
        return wide_rows[layer, pl.ds(start, rows), :]

    def send_wave(wave, low, rows):
        for down, other in sorted_partners:
            if wave == 0:
                block = rounded(other, 0, 0, HEAD)
            elif wave == 1:
                block = jnp.concatenate(
                    [rounded(other, 0, HEAD, HALF - HEAD), rounded(other, 1, 0, TAIL - HALF)], axis=0
                )
            else:
                block = rounded(other, 1, TAIL - HALF, CHUNK - TAIL)
            send_ref[other, low : low + rows] = block.astype(jnp.bfloat16)
            remote(
                send_ref.at[other, pl.ds(low, rows)],
                recv_ref.at[slot_here, pl.ds(low, rows)],
                send_sem,
                recv_sem.at[wave, down],
                (other, par),
            ).start()

    products(0)
    pl.semaphore_wait(barrier, greeted)
    send_wave(0, 0, HEAD)
    products(1)
    send_wave(1, HEAD, TAIL - HEAD)
    send_wave(2, TAIL, CHUNK - TAIL)

    flat = diagonal_energy(spin_ref[...])
    energy_ref[...] = jnp.zeros_like(energy_ref)
    energy_ref[:, :LOCAL] = flat[:, :LOCAL] + off_ref[...]
    for _, other in partners:
        remote(energy_ref, energies_ref.at[samp], esem.at[0], esem.at[1], (other, par)).start()
    energies_ref[samp] = energy_ref[...]
    recv_ref[slot_here] = jnp.concatenate(
        [rounded(samp, layer, 0, HALF) for layer in range(LAYERS)], axis=0
    ).astype(jnp.bfloat16)
    def await_wave(wave, low, rows):
        for down in range(NY):
            at = wrap(y + NY - down, NY) * NZ
            slots = pl.ds(0, NZ - 1) if down == 0 else pl.ds(at, NZ)
            landed = recv_ref.at[slots, pl.ds(low, rows)]
            remote(landed, landed, send_sem, recv_sem.at[wave, down], sibling).wait_recv()

    def heavy_part(pair):
        columns = pl.ds(256 * pair, 256)
        heavy = lax.dot_general(
            cent_ref[128:, columns], cent_ref[:, columns], (((1,), (1,)), ((), ())),
            preferred_element_type=jnp.float32,
        )
        part_ref[128:, :] = heavy if pair == 0 else part_ref[128:, :] + heavy

    squares = jnp.zeros((8, 256), jnp.float32)
    await_wave(0, 0, HEAD)
    for pair in range(ROWS // 2):
        if pair == HEAD // 16:
            await_wave(1, HEAD, TAIL - HEAD)
        if pair == TAIL // 16:
            await_wave(2, TAIL, CHUNK - TAIL)
        tile = jnp.stack(
            [
                recv_ref[(src % NY) * NZ + src // NY, 16 * pair : 16 * pair + 16, :].astype(jnp.float32)
                for src in range(NSAMP)
            ]
        ).reshape(NSAMP, 2, LOCAL, 128)
        halves = []
        for half in range(2):
            part = tile[:, half]
            mean = jnp.sum(jnp.sum(part, axis=0), axis=0, keepdims=True) / NS
            cent = ((part - mean) / math.sqrt(NS)).reshape(NS, 128)
            halves.append(cent.astype(jnp.bfloat16))
        cent = jnp.concatenate(halves, axis=1)
        cent_ref[:, 256 * pair : 256 * pair + 256] = cent
        light = lax.dot_general(
            cent[:128], cent[:128], (((1,), (1,)), ((), ())), preferred_element_type=jnp.float32
        )
        part_ref[:128, :128] = light if pair == 0 else part_ref[:128, :128] + light
        wide = cent[128:].astype(jnp.float32)
        squares = squares + jnp.sum((wide * wide).reshape(16, 8, 256), axis=0)
        if pair < TAIL // 16:
            heavy_part(pair)

    eye = lax.broadcasted_iota(jnp.int32, (128, 128), 0) == lax.broadcasted_iota(
        jnp.int32, (128, 128), 1
    )
    trace = jnp.sum(jnp.where(eye, part_ref[:128, :128], 0.0), keepdims=True) + jnp.sum(
        squares, keepdims=True
    )
    corner = jnp.logical_and(
        lax.broadcasted_iota(jnp.int32, (8, 128), 0) == 0,
        lax.broadcasted_iota(jnp.int32, (8, 128), 1) == 127,
    )
    part_ref[:8, :128] = jnp.where(corner, trace, part_ref[:8, :128])

    def rows_of(side, index):
        return pl.ds(pl.multiple_of(side * 128 + index * 8, 8), 8)

    slot = core * CHIPS + chip
    widths = (128, NS)

    def send_first(other, device, side):
        wide = pl.ds(0, widths[side])
        remote(
            part_ref.at[rows_of(side, other), wide],
            first.at[slot, :, wide],
            sem1.at[side],
            sem1.at[2],
            device,
        ).start()

    by_core(lambda side, width: send_first(chip, sibling, 0) if side == 1 else None)
    for kind in range(2):
        if kind == 1:
            for pair in range(TAIL // 16, ROWS // 2):
                heavy_part(pair)
        for other, device, side in around:
            if side == kind:
                send_first(other, device, side)
    by_core(lambda side, width: send_first(chip, sibling, 1) if side == 0 else None)

    def middle(side, width):
        wide = pl.ds(0, width)
        first[slot, :, wide] = part_ref[rows_of(side, chip), wide]
        landed = first.at[pl.ds(0, 2 * CHIPS - 1), :, wide]
        remote(landed, landed, sem1.at[0], sem1.at[2], sibling).wait_recv()
        own = jnp.sum(first[:, :, wide], axis=0)
        mine[:, wide] = own
        for hop in (4, 3, 5, 2, 6, 1, 7):
            device = (zs[hop] * NY + y, par)
            remote(
                mine.at[:, wide], second.at[z, :, wide], sem2.at[0], sem2.at[1], device
            ).start()
        second[z, :, wide] = own
        landed = second.at[pl.ds(0, NZ - 1), :, wide]
        remote(landed, landed, sem2.at[0], sem2.at[1], sibling).wait_recv()
        block = rows_of(side, chip)
        gram_ref[block, wide] = jnp.sum(second[:, :, wide], axis=0)
        done = gram_ref.at[block, wide]
        for _, device, _ in around:
            remote(done, done, sem3.at[0], sem3.at[1 + side], device).start()
        remote(done, done, sem3.at[0], sem3.at[1 + side], sibling).start()

    by_core(middle)

    def await_rows(kind):
        def body(side, width):
            count = CHIPS - 1 if side == kind else CHIPS
            landed = gram_ref.at[pl.ds(0, count * 8), pl.ds(0, widths[kind])]
            remote(landed, landed, sem3.at[0], sem3.at[1 + kind], sibling).wait_recv()

        by_core(body)

    energy_bytes = energies_ref.at[pl.ds(0, NSAMP - 1)]
    remote(energy_bytes, energy_bytes, esem.at[0], esem.at[1], sibling).wait()
    pieces = jnp.broadcast_to(energies_ref[...], (NSAMP, LOCAL, 128)).reshape(NS, 128)
    lane = lax.broadcasted_iota(jnp.int32, (NS, 128), 1)
    row = lax.broadcasted_iota(jnp.int32, (NSAMP, LOCAL, 128), 1).reshape(NS, 128)
    energy = jnp.sum(jnp.where(lane == row, pieces, 0.0), axis=1, keepdims=True)
    mean = jnp.sum(energy, axis=0, keepdims=True) / NS
    residual = -(energy - mean) / math.sqrt(NS)
    work[:, NS:] = jnp.broadcast_to(residual, (NS, 128))

    await_rows(0)
    level = 1.0 / (gram_ref[0:1, 127:128] / NS)
    wide_corner = jnp.logical_and(
        lax.broadcasted_iota(jnp.int32, (128, 128), 0) == 0,
        lax.broadcasted_iota(jnp.int32, (128, 128), 1) == 127,
    )
    light = jnp.where(wide_corner, gram_ref[127:128, 0:1], gram_ref[:128, :128])
    ridge = jnp.where(eye, 0.01, 0.0)
    work[:128, :128] = light * level + ridge
    one, two = slice(0, BLOCK), slice(BLOCK, 2 * BLOCK)
    lower_one, scaled_one = forward_block(work[one, one], tile_ref, column_ref, cross_ref)
    left = product(work[two, one], lower_one, 1, 1)
    right = product(scaled_one, work[one, two], 1, 0)
    lower_two, scaled_two = forward_block(
        work[two, two] - product(left, right, 1, 0), tile_ref, column_ref, cross_ref
    )
    cross_part = product(left, scaled_one, 1, 0)
    blank = jnp.zeros((BLOCK, BLOCK), jnp.float32)

    def joined_factor(first_part, second_part):
        return jnp.concatenate(
            [
                jnp.concatenate([first_part, blank], axis=1),
                jnp.concatenate([-product(second_part, cross_part, 1, 0), second_part], axis=1),
            ],
            axis=0,
        )

    lower = joined_factor(lower_one, lower_two)
    scaled = joined_factor(scaled_one, scaled_two)

    await_rows(1)
    below = gram_ref[128:, :128]
    corner_block = gram_ref[128:, 128:]
    scaled_below = below * level
    work[:128, 128:NS] = scaled_below.T
    work[128:, 128:NS] = corner_block * level + ridge
    middle_rows = product(scaled, work[:128, 128:], 1, 0)
    outer = product(scaled_below, lower, 1, 1)
    work[128:, 128:] = work[128:, 128:] - product(outer, middle_rows, 1, 0)
    work[:128, 128:] = product(lower, middle_rows, 0, 0)

    for index in range(2, NS // BLOCK):
        low = index * BLOCK
        own = slice(low, low + BLOCK)
        rest = slice(128 * ((index + 1) // 2), NS + 128)
        lower, scaled = forward_block(work[own, own], tile_ref, column_ref, cross_ref)
        middle_rows = product(scaled, work[own, rest], 1, 0)
        outer = product(work[:, own], lower, 1, 1)
        work[:, rest] = work[:, rest] - product(outer, middle_rows, 1, 0)
        work[own, rest] = product(lower, middle_rows, 0, 0)

    coeff = work[:, NS:] * level
    held[...] = coeff
    own = held[pl.ds(pl.multiple_of(samp * LOCAL, LOCAL), LOCAL), :]
    here = lax.broadcasted_iota(jnp.int32, (LOCAL, 128), 0) == lax.broadcasted_iota(
        jnp.int32, (LOCAL, 128), 1
    )
    coeff_ref[...] = jnp.sum(jnp.where(here, own, 0.0), axis=0, keepdims=True)[:, :LOCAL]
    upper, under = coeff[:128], coeff[128:]
    weighted = jnp.sum(light * upper + 2.0 * (below * under), axis=0, keepdims=True) * jnp.sum(
        jnp.where(eye, upper, 0.0), axis=0, keepdims=True
    ) + jnp.sum(corner_block * under, axis=0, keepdims=True) * jnp.sum(
        jnp.where(eye, under, 0.0), axis=0, keepdims=True
    )
    square_total = jnp.sum(weighted, keepdims=True)
    scale = lax.rsqrt(square_total / ENTRIES + 1e-06)
    for index in range(ROWS):
        cent = cent_ref[:, 128 * index : 128 * index + 128].astype(jnp.float32)
        layer, column = index // (ROWS // 2), 128 * (index % (ROWS // 2))
        update_ref[layer : layer + 1, column : column + 128] = (
            jnp.sum(cent * coeff, axis=0, keepdims=True) * scale
        )

    sent = send_ref.at[pl.ds(0, NSAMP - 1)]
    remote(sent, sent, send_sem, recv_sem.at[0, 0], sibling).wait_send()

    def finish(side, width):
        wide = pl.ds(0, width)
        for kind in range(2):
            count = CHIPS - 1 if kind == side else CHIPS
            bytes_ref = gram_ref.at[pl.ds(0, count * 8), pl.ds(0, widths[kind])]
            remote(bytes_ref, bytes_ref, sem1.at[kind], sem1.at[2], sibling).wait_send()
        landed = second.at[pl.ds(0, NZ - 1), :, wide]
        remote(landed, landed, sem2.at[0], sem2.at[1], sibling).wait_send()
        landed = first.at[pl.ds(0, 2 * CHIPS - 1), :, wide]
        remote(landed, landed, sem3.at[0], sem1.at[2], sibling).wait_send()

    by_core(finish)


def main_call(activations, cotangents, spin_bits, off_row):
    whole = pl.BlockSpec(memory_space=VMEM)
    anywhere = pl.BlockSpec(memory_space=pl.ANY)
    dma = pltpu.SemaphoreType.DMA
    return pl.pallas_call(
        main_kernel,
        in_specs=[anywhere, anywhere, whole, whole],
        out_specs=[whole, whole],
        out_shape=[
            jax.ShapeDtypeStruct((LAYERS, ROWS * CH), jnp.float32),
            jax.ShapeDtypeStruct((1, LOCAL), jnp.float32),
        ],
        scratch_shapes=[
            VMEM((LOCAL, LAYERS, CH, SITES), jnp.bfloat16),
            VMEM((LOCAL, LAYERS, CH, SITES), jnp.bfloat16),
            VMEM((2, CH, SITES), jnp.bfloat16),
            VMEM((SLOTS, 3 * CH, PADK), jnp.bfloat16),
            VMEM((SLOTS, 3 * CH, PADK), jnp.bfloat16),
            VMEM((SLOTS, 2, 3 * CH, 128), jnp.float32),
            VMEM((LAYERS, NSAMP * HALF, 128), jnp.float32),
            VMEM((NSAMP, CHUNK, 128), jnp.bfloat16),
            VMEM((NSAMP, CHUNK, 128), jnp.bfloat16),
            VMEM((NS, WIDTH), jnp.bfloat16),
            VMEM((1, 128), jnp.float32),
            VMEM((NSAMP, 1, 128), jnp.float32),
            VMEM((NS, NS), jnp.float32),
            VMEM((2 * CHIPS, 8, NS), jnp.float32),
            VMEM((8, NS), jnp.float32),
            VMEM((NZ, 8, NS), jnp.float32),
            VMEM((NS, NS), jnp.float32),
            VMEM((NS, NS + 128), jnp.float32),
            VMEM((NS, 128), jnp.float32),
            VMEM((BLOCK // PANEL, 1, 8, 128), jnp.float32),
            VMEM((BLOCK // PANEL, PANEL, 8, 128), jnp.float32),
            VMEM((BLOCK // PANEL, PANEL, 8, 128), jnp.float32),
            dma((LAYERS, LOCAL)),
            dma((LAYERS, LOCAL)),
            dma,
            dma((3, NY)),
            dma((2,)),
            dma((3,)),
            dma((2,)),
            dma((3,)),
        ],
        compiler_params=pltpu.CompilerParams(
            collective_id=0, has_side_effects=True, vmem_limit_bytes=VMEM_LIMIT
        ),
    )(activations, cotangents, spin_bits, off_row)


def hand_on_kernel(update_in, coeff_in, update_ref, coeff_ref, sems):
    copies = [
        pltpu.make_async_copy(update_in, update_ref, sems.at[0]),
        pltpu.make_async_copy(coeff_in, coeff_ref, sems.at[1]),
    ]
    for copy in copies:
        copy.start()
    for copy in copies:
        copy.wait()


def hand_on(update, coeff):
    anywhere = pl.BlockSpec(memory_space=pl.ANY)
    return pl.pallas_call(
        hand_on_kernel,
        in_specs=[anywhere, anywhere],
        out_specs=[anywhere, anywhere],
        out_shape=[
            jax.ShapeDtypeStruct((LAYERS, ROWS * CH), jnp.float32),
            jax.ShapeDtypeStruct((1, LOCAL), jnp.float32),
        ],
        scratch_shapes=[pltpu.SemaphoreType.DMA((2,))],
        compiler_params=pltpu.CompilerParams(vmem_limit_bytes=VMEM_LIMIT),
    )(update, coeff)


def on_device(activations, cotangents, spin_bits, offdiag_energy):
    update, coeff = hand_on(
        *main_call(activations, cotangents, spin_bits, offdiag_energy.reshape(1, LOCAL))
    )
    return update, coeff.reshape(LOCAL)


def solution(mesh):
    in_specs = (
        P("samp", "par", None, None),
        P("samp", "par", None, None),
        P("samp", None),
        P("samp"),
    )
    out_specs = (P("par", "samp"), P("samp"))
    return jax.shard_map(
        on_device, mesh=mesh, in_specs=in_specs, out_specs=out_specs, check_vma=False
    )
```

```python
import math

import jax
import jax.numpy as jnp
from jax import lax
from jax.experimental import pallas as pl
from jax.experimental.pallas import tpu as pltpu
from jax.sharding import PartitionSpec as P

CH = 64
KK = 9
LAT = 24
SITES = LAT * LAT
NSAMP = 32
NPAR = 8
NZ = 8
NY = 4
LOCAL = 8
NS = NSAMP * LOCAL
ROWS = KK * CH // NSAMP
CHUNK = ROWS * LOCAL
WIDTH = ROWS * 128
PADK = 640
LAYERS = 2
ENTRIES = 16 * KK * CH * CH
MESH = pl.DeviceIdType.MESH
VMEM_LIMIT = 56 * 1024 * 1024
HIGHEST = lax.Precision.HIGHEST
VMEM = pltpu.VMEM


def rolled(value, amount):
    amount = amount % SITES
    if amount == 0:
        return value
    return jnp.concatenate([value[:, amount:], value[:, :amount]], axis=1)


def edge_mask(shape, col_step):
    column = lax.broadcasted_iota(jnp.int32, shape, 1) % LAT
    return column == (LAT - 1 if col_step > 0 else 0)


def column_shift(value, col_step, edge):
    if col_step == 0:
        return value
    return jnp.where(edge, rolled(value, col_step - LAT * col_step), rolled(value, col_step))


def wrap(value, size):
    return lax.select(value >= size, value - size, value)


STEPS = [(down, hop) for down in range(NY) for hop in (1, 7, 2, 6, 3, 5, 4, 0) if (down, hop) != (0, 0)]


def diagonal_energy(spin_bits):
    spin = (2 * spin_bits - 1).astype(jnp.float32)
    right = column_shift(spin, 1, edge_mask(spin.shape, 1))
    left = column_shift(spin, -1, edge_mask(spin.shape, -1))
    pairs = spin * rolled(spin, LAT) + spin * right
    corners = spin * rolled(right, LAT) + spin * rolled(left, LAT)
    diag = 0.25 * jnp.sum(pairs + 0.5 * corners, axis=1, keepdims=True)
    wide = jnp.broadcast_to(diag, (LOCAL, 128))
    here = lax.broadcasted_iota(jnp.int32, (LOCAL, 128), 0) == lax.broadcasted_iota(
        jnp.int32, (LOCAL, 128), 1
    )
    return jnp.sum(jnp.where(here, wide, 0.0), axis=0, keepdims=True)


PLANE = sorted(
    ((down, across) for down in range(NY) for across in range(4) if (down, across) != (0, 0)),
    key=lambda step: -(min(step[0], NY - step[0]) + min(step[1], 4 - step[1])),
)
PAIRS = 3 * CH // 2
HALF = CHUNK // 2
HEAD = 64
TAIL = 112
SLOTS = 8
CHIPS = 16


BLOCK = 64
PANEL = 8


def forward_block(diag, tile_ref, column_ref, cross_ref):
    eye = lax.broadcasted_iota(jnp.int32, (BLOCK, BLOCK), 0) == lax.broadcasted_iota(
        jnp.int32, (BLOCK, BLOCK), 1
    )
    wide = jnp.concatenate([diag, jnp.where(eye, 1.0, 0.0)], axis=1)
    count = BLOCK // PANEL
    tiles = [wide[8 * q : 8 * q + 8] for q in range(count)]
    sub = lax.broadcasted_iota(jnp.int32, (8, 128), 0)

    def lanes(tile, col):
        return jnp.broadcast_to(tile[:, col : col + 1], (8, 128))

    def joined(parts):
        total = parts[0]
        for i in range(1, PANEL):
            total = jnp.where(sub == i, parts[i], total)
        return total

    def broadcast_row(ref, panel, j, i):
        return ref[panel, j, pl.ds(i, 8, stride=0), :]

    reduced, scaled = [], []
    columns = [lanes(tiles[0], j) for j in range(PANEL)]
    for panel in range(count):
        base = panel * PANEL
        last = panel == count - 1
        tile_ref[panel, 0] = tiles[panel]
        for j in range(PANEL):
            column_ref[panel, j] = columns[j]
        low = {
            (i, j): broadcast_row(column_ref, panel, j, i)
            for i in range(PANEL)
            for j in range(i + 1)
        }
        rows = [broadcast_row(tile_ref, panel, 0, i) for i in range(PANEL)]
        old_columns = {
            q: [lanes(tiles[q], base + i) for i in range(PANEL)] for q in range(panel + 1, count)
        }
        if not last:
            cross = list(old_columns[panel + 1])
            columns = [lanes(tiles[panel + 1], base + PANEL + j) for j in range(PANEL)]
        ups, downs, starts, cross_scaled = {}, {}, {}, {}
        for p in range(0, PANEL, 2):
            q = p + 1
            a, b, c = low[p, p], low[q, p], low[q, q]
            recip = pl.reciprocal(a * c - b * b, approx=True)
            for i in range(q + 1, PANEL):
                up = c * low[i, p] - b * low[i, q]
                down = a * low[i, q] - b * low[i, p]
                ups[i, p], downs[i, p] = up * recip, down * recip
                for m in range(q + 1, i + 1):
                    if i <= q + 2:
                        step = (up * low[m, p] + down * low[m, q]) * recip
                    else:
                        step = ups[i, p] * low[m, p] + downs[i, p] * low[m, q]
                    low[i, m] = low[i, m] - step
            if not last:
                cross_scaled[p] = (c * cross[p] - b * cross[q]) * recip
                cross_scaled[q] = (a * cross[q] - b * cross[p]) * recip
                for i in range(q + 1, PANEL):
                    cross[i] = cross[i] - (ups[i, p] * cross[p] + downs[i, p] * cross[q])
            starts[p] = (c * rows[p] - b * rows[q]) * recip
            starts[q] = (a * rows[q] - b * rows[p]) * recip
            for i in range(q + 1, PANEL):
                rows[i] = rows[i] - (ups[i, p] * rows[p] + downs[i, p] * rows[q])
        if not last:
            for i in range(PANEL):
                cross_ref[panel, i] = cross[i]
            for j in range(PANEL):
                terms = [
                    cross_scaled[i] * broadcast_row(cross_ref, panel, i, j) for i in range(PANEL)
                ]
                while len(terms) > 1:
                    terms = [terms[a] + terms[a + 1] for a in range(0, len(terms), 2)]
                columns[j] = columns[j] - terms[0]
        reduced.append(joined(rows))
        scaled.append(joined([starts[i] for i in range(PANEL)]))
        if last:
            break
        solved = [None] * PANEL
        for p in reversed(range(0, PANEL, 2)):
            for total, factor, at in ((starts[p], ups, p), (starts[p + 1], downs, p + 1)):
                for i in reversed(range(p + 2, PANEL)):
                    total = total - factor[i, p] * solved[i]
                solved[at] = total
        for q in range(panel + 1, count):
            terms = [old_columns[q][i] * solved[i] for i in range(PANEL)]
            while len(terms) > 1:
                terms = [terms[a] + terms[a + 1] for a in range(0, len(terms), 2)]
            tiles[q] = tiles[q] - terms[0]
    lower = jnp.concatenate(reduced, axis=0)[:, BLOCK:]
    return lower, jnp.concatenate(scaled, axis=0)[:, BLOCK:]


def product(one, two, first_dim, second_dim):
    return lax.dot_general(
        one, two, (((first_dim,), (second_dim,)), ((), ())),
        precision=HIGHEST, preferred_element_type=jnp.float32,
    )


def main_kernel(
    act_hbm, cot_hbm, spin_ref, off_ref,
    update_ref, coeff_ref,
    act_ref, cot_ref, edges, lhs, rhs, stage, wide_rows, send_ref, recv_ref, cent_ref,
    energy_ref, energies_ref, part_ref, first, mine, second, gram_ref,
    work, held, tile_ref, column_ref, cross_ref,
    act_sem, cot_sem, send_sem, recv_sem, esem, sem1, sem2, sem3,
):
    samp = lax.axis_index("samp")
    par = lax.axis_index("par")
    z, y = samp // NY, samp % NY
    x, core = par // 2, par % 2
    slot_here = y * NZ + z
    sibling = (samp, x * 2 + 1 - core)
    zs = [wrap(z + hop, NZ) for hop in range(NZ)]
    ys = [wrap(y + down, NY) for down in range(NY)]
    xs = [wrap(x + across, 4) for across in range(4)]
    partners = [(down, zs[hop] * NY + ys[down]) for down, hop in STEPS]
    sorted_partners = [
        item for item, (_, hop) in sorted(zip(partners, STEPS), key=lambda pair: -min(pair[1][1], NZ - pair[1][1]))
    ]
    chip = y * 4 + x
    others = [
        (ys[down] * 4 + xs[across], z * NY + ys[down], xs[across] * 2)
        for down, across in PLANE
    ]
    around = [(other, (row, pair + side), side) for other, row, pair in others for side in range(2)]

    def by_core(body):
        @pl.when(core == 0)
        def _():
            body(0, 128)

        @pl.when(core == 1)
        def _():
            body(1, NS)

    def act_copy(n, layer):
        return pltpu.make_async_copy(
            act_hbm.at[n, layer], act_ref.at[n, layer], act_sem.at[layer, n]
        )

    def cot_copy(n, layer):
        return pltpu.make_async_copy(
            cot_hbm.at[n, layer], cot_ref.at[n, layer], cot_sem.at[layer, n]
        )

    for layer in range(LAYERS):
        for n in range(LOCAL):
            act_copy(n, layer).start()
            cot_copy(n, layer).start()

    def remote(source, target, send, recv, device):
        return pltpu.make_async_remote_copy(
            src_ref=source,
            dst_ref=target,
            send_sem=send,
            recv_sem=recv,
            device_id=device,
            device_id_type=MESH,
        )

    barrier = pltpu.get_barrier_semaphore()
    greeted = 0
    for _, other in partners:
        pl.semaphore_signal(barrier, inc=1, device_id=(other, par), device_id_type=MESH)
        greeted += 1
    for down in range(NY):
        for across in range(4):
            for side in (core, 1 - core):
                if across > 0 or side is not core:
                    device = (z * NY + ys[down], xs[across] * 2 + side)
                    pl.semaphore_signal(barrier, inc=1, device_id=device, device_id_type=MESH)
                    greeted += 1

    left = lax.broadcasted_iota(jnp.int32, (PAIRS, 128), 1) < CH
    lhs[:, :, PADK - 128 :] = jnp.zeros((SLOTS, 3 * CH, 128), jnp.bfloat16)
    rhs[:, :, PADK - 128 :] = jnp.zeros((SLOTS, 3 * CH, 128), jnp.bfloat16)
    stage[:, 1] = jnp.zeros((SLOTS, 3 * CH, 128), jnp.float32)
    for at, step in enumerate((-1, 1)):
        strip = jnp.where(edge_mask((8, SITES), step), 1.0, 0.0)
        edges[at] = jnp.concatenate([strip] * (CH // 8), axis=0).astype(jnp.bfloat16)

    def compute(sample, layer, slot):
        act = act_ref[sample, layer]
        cot = cot_ref[sample, layer]
        for step in (-1, 0, 1):
            low = (step + 1) * CH
            edge = edges[max(step, 0)] > 0
            lhs[slot, low : low + CH, :SITES] = column_shift(act, step, edge)
            rhs[slot, low : low + CH, :SITES] = rolled(cot, -LAT * step)
        out = lax.dot_general(
            lhs[slot], rhs[slot], (((1,), (1,)), ((), ())), preferred_element_type=jnp.float32
        )
        stage[slot, 0] = out[:, :128]
        stage[slot, 1, :, :CH] = out[:, 128:]
        even, odd, even_last, odd_last = [
            stage[slot, part, pl.ds(parity, PAIRS, stride=2), :]
            for part in (0, 1)
            for parity in (0, 1)
        ]
        blocks = (
            jnp.where(left, even, pltpu.roll(odd, CH, 1)),
            jnp.where(left, pltpu.roll(even, CH, 1), odd),
            jnp.where(left, even_last, pltpu.roll(odd_last, CH, 1)),
        )
        for down in range(3):
            wide_rows[layer, pl.ds(down * PAIRS * LOCAL + sample, PAIRS, stride=LOCAL), :] = blocks[down]

    def products(layer):
        def body(group, carry):
            for slot in range(SLOTS):
                sample = group * SLOTS + slot
                act_copy(sample, layer).wait()
                cot_copy(sample, layer).wait()
            for slot in range(SLOTS):
                compute(group * SLOTS + slot, layer, slot)
            return carry

        lax.fori_loop(0, LOCAL // SLOTS, body, 0)

    def rounded(other, layer, low, rows):
        start = pl.multiple_of(other * HALF + low, 8)
        return wide_rows[layer, pl.ds(start, rows), :]

    def send_wave(wave, low, rows):
        for down, other in sorted_partners:
            if wave == 0:
                block = rounded(other, 0, 0, HEAD)
            elif wave == 1:
                block = jnp.concatenate(
                    [rounded(other, 0, HEAD, HALF - HEAD), rounded(other, 1, 0, TAIL - HALF)], axis=0
                )
            else:
                block = rounded(other, 1, TAIL - HALF, CHUNK - TAIL)
            send_ref[other, low : low + rows] = block.astype(jnp.bfloat16)
            remote(
                send_ref.at[other, pl.ds(low, rows)],
                recv_ref.at[slot_here, pl.ds(low, rows)],
                send_sem,
                recv_sem.at[wave, down],
                (other, par),
            ).start()

    products(0)
    pl.semaphore_wait(barrier, greeted)
    send_wave(0, 0, HEAD)
    products(1)
    send_wave(1, HEAD, TAIL - HEAD)
    send_wave(2, TAIL, CHUNK - TAIL)

    flat = diagonal_energy(spin_ref[...])
    energy_ref[...] = jnp.zeros_like(energy_ref)
    energy_ref[:, :LOCAL] = flat[:, :LOCAL] + off_ref[...]
    for _, other in partners:
        remote(energy_ref, energies_ref.at[samp], esem.at[0], esem.at[1], (other, par)).start()
    energies_ref[samp] = energy_ref[...]
    recv_ref[slot_here] = jnp.concatenate(
        [rounded(samp, layer, 0, HALF) for layer in range(LAYERS)], axis=0
    ).astype(jnp.bfloat16)
    def await_wave(wave, low, rows):
        for down in range(NY):
            at = wrap(y + NY - down, NY) * NZ
            slots = pl.ds(0, NZ - 1) if down == 0 else pl.ds(at, NZ)
            landed = recv_ref.at[slots, pl.ds(low, rows)]
            remote(landed, landed, send_sem, recv_sem.at[wave, down], sibling).wait_recv()

    def heavy_part(pair):
        columns = pl.ds(256 * pair, 256)
        heavy = lax.dot_general(
            cent_ref[128:, columns], cent_ref[:, columns], (((1,), (1,)), ((), ())),
            preferred_element_type=jnp.float32,
        )
        part_ref[128:, :] = heavy if pair == 0 else part_ref[128:, :] + heavy

    squares = jnp.zeros((8, 256), jnp.float32)
    await_wave(0, 0, HEAD)
    for pair in range(ROWS // 2):
        if pair == HEAD // 16:
            await_wave(1, HEAD, TAIL - HEAD)
        if pair == TAIL // 16:
            await_wave(2, TAIL, CHUNK - TAIL)
        tile = jnp.stack(
            [
                recv_ref[(src % NY) * NZ + src // NY, 16 * pair : 16 * pair + 16, :].astype(jnp.float32)
                for src in range(NSAMP)
            ]
        ).reshape(NSAMP, 2, LOCAL, 128)
        halves = []
        for half in range(2):
            part = tile[:, half]
            mean = jnp.sum(jnp.sum(part, axis=0), axis=0, keepdims=True) / NS
            cent = ((part - mean) / math.sqrt(NS)).reshape(NS, 128)
            halves.append(cent.astype(jnp.bfloat16))
        cent = jnp.concatenate(halves, axis=1)
        cent_ref[:, 256 * pair : 256 * pair + 256] = cent
        light = lax.dot_general(
            cent[:128], cent[:128], (((1,), (1,)), ((), ())), preferred_element_type=jnp.float32
        )
        part_ref[:128, :128] = light if pair == 0 else part_ref[:128, :128] + light
        wide = cent[128:].astype(jnp.float32)
        squares = squares + jnp.sum((wide * wide).reshape(16, 8, 256), axis=0)
        if pair < TAIL // 16:
            heavy_part(pair)

    eye = lax.broadcasted_iota(jnp.int32, (128, 128), 0) == lax.broadcasted_iota(
        jnp.int32, (128, 128), 1
    )
    trace = jnp.sum(jnp.where(eye, part_ref[:128, :128], 0.0), keepdims=True) + jnp.sum(
        squares, keepdims=True
    )
    corner = jnp.logical_and(
        lax.broadcasted_iota(jnp.int32, (8, 128), 0) == 0,
        lax.broadcasted_iota(jnp.int32, (8, 128), 1) == 127,
    )
    part_ref[:8, :128] = jnp.where(corner, trace, part_ref[:8, :128])

    def rows_of(side, index):
        return pl.ds(pl.multiple_of(side * 128 + index * 8, 8), 8)

    slot = core * CHIPS + chip
    widths = (128, NS)

    def send_first(other, device, side):
        wide = pl.ds(0, widths[side])
        remote(
            part_ref.at[rows_of(side, other), wide],
            first.at[slot, :, wide],
            sem1.at[side],
            sem1.at[2],
            device,
        ).start()

    by_core(lambda side, width: send_first(chip, sibling, 0) if side == 1 else None)
    for kind in range(2):
        if kind == 1:
            for pair in range(TAIL // 16, ROWS // 2):
                heavy_part(pair)
        for other, device, side in around:
            if side == kind:
                send_first(other, device, side)
    by_core(lambda side, width: send_first(chip, sibling, 1) if side == 0 else None)

    def middle(side, width):
        wide = pl.ds(0, width)
        first[slot, :, wide] = part_ref[rows_of(side, chip), wide]
        landed = first.at[pl.ds(0, 2 * CHIPS - 1), :, wide]
        remote(landed, landed, sem1.at[0], sem1.at[2], sibling).wait_recv()
        own = jnp.sum(first[:, :, wide], axis=0)
        mine[:, wide] = own
        for hop in (4, 3, 5, 2, 6, 1, 7):
            device = (zs[hop] * NY + y, par)
            remote(
                mine.at[:, wide], second.at[z, :, wide], sem2.at[0], sem2.at[1], device
            ).start()
        second[z, :, wide] = own
        landed = second.at[pl.ds(0, NZ - 1), :, wide]
        remote(landed, landed, sem2.at[0], sem2.at[1], sibling).wait_recv()
        block = rows_of(side, chip)
        gram_ref[block, wide] = jnp.sum(second[:, :, wide], axis=0)
        done = gram_ref.at[block, wide]
        for _, device, _ in around:
            remote(done, done, sem3.at[0], sem3.at[1 + side], device).start()
        remote(done, done, sem3.at[0], sem3.at[1 + side], sibling).start()

    by_core(middle)

    def await_rows(kind):
        def body(side, width):
            count = CHIPS - 1 if side == kind else CHIPS
            landed = gram_ref.at[pl.ds(0, count * 8), pl.ds(0, widths[kind])]
            remote(landed, landed, sem3.at[0], sem3.at[1 + kind], sibling).wait_recv()

        by_core(body)

    energy_bytes = energies_ref.at[pl.ds(0, NSAMP - 1)]
    remote(energy_bytes, energy_bytes, esem.at[0], esem.at[1], sibling).wait()
    pieces = jnp.broadcast_to(energies_ref[...], (NSAMP, LOCAL, 128)).reshape(NS, 128)
    lane = lax.broadcasted_iota(jnp.int32, (NS, 128), 1)
    row = lax.broadcasted_iota(jnp.int32, (NSAMP, LOCAL, 128), 1).reshape(NS, 128)
    energy = jnp.sum(jnp.where(lane == row, pieces, 0.0), axis=1, keepdims=True)
    mean = jnp.sum(energy, axis=0, keepdims=True) / NS
    residual = -(energy - mean) / math.sqrt(NS)
    work[:, NS:] = jnp.broadcast_to(residual, (NS, 128))

    await_rows(0)
    level = 1.0 / (gram_ref[0:1, 127:128] / NS)
    wide_corner = jnp.logical_and(
        lax.broadcasted_iota(jnp.int32, (128, 128), 0) == 0,
        lax.broadcasted_iota(jnp.int32, (128, 128), 1) == 127,
    )
    light = jnp.where(wide_corner, gram_ref[127:128, 0:1], gram_ref[:128, :128])
    ridge = jnp.where(eye, 0.01, 0.0)
    work[:128, :128] = light * level + ridge
    one, two = slice(0, BLOCK), slice(BLOCK, 2 * BLOCK)
    lower_one, scaled_one = forward_block(work[one, one], tile_ref, column_ref, cross_ref)
    left = product(work[two, one], lower_one, 1, 1)
    right = product(scaled_one, work[one, two], 1, 0)
    lower_two, scaled_two = forward_block(
        work[two, two] - product(left, right, 1, 0), tile_ref, column_ref, cross_ref
    )
    cross_part = product(left, scaled_one, 1, 0)
    blank = jnp.zeros((BLOCK, BLOCK), jnp.float32)

    def joined_factor(first_part, second_part):
        return jnp.concatenate(
            [
                jnp.concatenate([first_part, blank], axis=1),
                jnp.concatenate([-product(second_part, cross_part, 1, 0), second_part], axis=1),
            ],
            axis=0,
        )

    lower = joined_factor(lower_one, lower_two)
    scaled = joined_factor(scaled_one, scaled_two)

    await_rows(1)
    below = gram_ref[128:, :128]
    corner_block = gram_ref[128:, 128:]
    scaled_below = below * level
    above = scaled_below.T
    last = corner_block * level + ridge
    near_middle = product(scaled, above[:, :BLOCK], 1, 0)
    near_outer = product(scaled_below[:BLOCK], lower, 1, 1)
    lower_three, scaled_three = forward_block(
        last[:BLOCK, :BLOCK] - product(near_outer, near_middle, 1, 0), tile_ref, column_ref, cross_ref
    )
    work[:128, 128:NS] = above
    work[128:, 128:NS] = last
    middle_rows = product(scaled, work[:128, 128:], 1, 0)
    outer = product(scaled_below, lower, 1, 1)
    work[128:, 128:] = work[128:, 128:] - product(outer, middle_rows, 1, 0)
    work[:128, 128:] = product(lower, middle_rows, 0, 0)

    three, four = slice(128, 128 + BLOCK), slice(128 + BLOCK, NS)
    near_middle = product(scaled_three, work[three, four], 1, 0)
    near_outer = product(work[four, three], lower_three, 1, 1)
    lower_four, scaled_four = forward_block(
        work[four, four] - product(near_outer, near_middle, 1, 0), tile_ref, column_ref, cross_ref
    )
    middle_rows = product(scaled_three, work[three, 128:], 1, 0)
    outer = product(work[:, three], lower_three, 1, 1)
    work[:, 128:] = work[:, 128:] - product(outer, middle_rows, 1, 0)
    work[three, 128:] = product(lower_three, middle_rows, 0, 0)

    middle_rows = product(scaled_four, work[four, NS:], 1, 0)
    outer = product(work[:, four], lower_four, 1, 1)
    work[:, NS:] = work[:, NS:] - product(outer, middle_rows, 1, 0)
    work[four, NS:] = product(lower_four, middle_rows, 0, 0)

    coeff = work[:, NS:] * level
    held[...] = coeff
    own = held[pl.ds(pl.multiple_of(samp * LOCAL, LOCAL), LOCAL), :]
    here = lax.broadcasted_iota(jnp.int32, (LOCAL, 128), 0) == lax.broadcasted_iota(
        jnp.int32, (LOCAL, 128), 1
    )
    coeff_ref[...] = jnp.sum(jnp.where(here, own, 0.0), axis=0, keepdims=True)[:, :LOCAL]
    upper, under = coeff[:128], coeff[128:]
    weighted = jnp.sum(light * upper + 2.0 * (below * under), axis=0, keepdims=True) * jnp.sum(
        jnp.where(eye, upper, 0.0), axis=0, keepdims=True
    ) + jnp.sum(corner_block * under, axis=0, keepdims=True) * jnp.sum(
        jnp.where(eye, under, 0.0), axis=0, keepdims=True
    )
    square_total = jnp.sum(weighted, keepdims=True)
    scale = lax.rsqrt(square_total / ENTRIES + 1e-06)
    for index in range(ROWS):
        cent = cent_ref[:, 128 * index : 128 * index + 128].astype(jnp.float32)
        layer, column = index // (ROWS // 2), 128 * (index % (ROWS // 2))
        update_ref[layer : layer + 1, column : column + 128] = (
            jnp.sum(cent * coeff, axis=0, keepdims=True) * scale
        )

    sent = send_ref.at[pl.ds(0, NSAMP - 1)]
    remote(sent, sent, send_sem, recv_sem.at[0, 0], sibling).wait_send()

    def finish(side, width):
        wide = pl.ds(0, width)
        for kind in range(2):
            count = CHIPS - 1 if kind == side else CHIPS
            bytes_ref = gram_ref.at[pl.ds(0, count * 8), pl.ds(0, widths[kind])]
            remote(bytes_ref, bytes_ref, sem1.at[kind], sem1.at[2], sibling).wait_send()
        landed = second.at[pl.ds(0, NZ - 1), :, wide]
        remote(landed, landed, sem2.at[0], sem2.at[1], sibling).wait_send()
        landed = first.at[pl.ds(0, 2 * CHIPS - 1), :, wide]
        remote(landed, landed, sem3.at[0], sem1.at[2], sibling).wait_send()

    by_core(finish)


def main_call(activations, cotangents, spin_bits, off_row):
    whole = pl.BlockSpec(memory_space=VMEM)
    anywhere = pl.BlockSpec(memory_space=pl.ANY)
    dma = pltpu.SemaphoreType.DMA
    return pl.pallas_call(
        main_kernel,
        in_specs=[anywhere, anywhere, whole, whole],
        out_specs=[whole, whole],
        out_shape=[
            jax.ShapeDtypeStruct((LAYERS, ROWS * CH), jnp.float32),
            jax.ShapeDtypeStruct((1, LOCAL), jnp.float32),
        ],
        scratch_shapes=[
            VMEM((LOCAL, LAYERS, CH, SITES), jnp.bfloat16),
            VMEM((LOCAL, LAYERS, CH, SITES), jnp.bfloat16),
            VMEM((2, CH, SITES), jnp.bfloat16),
            VMEM((SLOTS, 3 * CH, PADK), jnp.bfloat16),
            VMEM((SLOTS, 3 * CH, PADK), jnp.bfloat16),
            VMEM((SLOTS, 2, 3 * CH, 128), jnp.float32),
            VMEM((LAYERS, NSAMP * HALF, 128), jnp.float32),
            VMEM((NSAMP, CHUNK, 128), jnp.bfloat16),
            VMEM((NSAMP, CHUNK, 128), jnp.bfloat16),
            VMEM((NS, WIDTH), jnp.bfloat16),
            VMEM((1, 128), jnp.float32),
            VMEM((NSAMP, 1, 128), jnp.float32),
            VMEM((NS, NS), jnp.float32),
            VMEM((2 * CHIPS, 8, NS), jnp.float32),
            VMEM((8, NS), jnp.float32),
            VMEM((NZ, 8, NS), jnp.float32),
            VMEM((NS, NS), jnp.float32),
            VMEM((NS, NS + 128), jnp.float32),
            VMEM((NS, 128), jnp.float32),
            VMEM((BLOCK // PANEL, 1, 8, 128), jnp.float32),
            VMEM((BLOCK // PANEL, PANEL, 8, 128), jnp.float32),
            VMEM((BLOCK // PANEL, PANEL, 8, 128), jnp.float32),
            dma((LAYERS, LOCAL)),
            dma((LAYERS, LOCAL)),
            dma,
            dma((3, NY)),
            dma((2,)),
            dma((3,)),
            dma((2,)),
            dma((3,)),
        ],
        compiler_params=pltpu.CompilerParams(
            collective_id=0, has_side_effects=True, vmem_limit_bytes=VMEM_LIMIT
        ),
    )(activations, cotangents, spin_bits, off_row)


def hand_on_kernel(update_in, coeff_in, update_ref, coeff_ref, sems):
    copies = [
        pltpu.make_async_copy(update_in, update_ref, sems.at[0]),
        pltpu.make_async_copy(coeff_in, coeff_ref, sems.at[1]),
    ]
    for copy in copies:
        copy.start()
    for copy in copies:
        copy.wait()


def hand_on(update, coeff):
    anywhere = pl.BlockSpec(memory_space=pl.ANY)
    return pl.pallas_call(
        hand_on_kernel,
        in_specs=[anywhere, anywhere],
        out_specs=[anywhere, anywhere],
        out_shape=[
            jax.ShapeDtypeStruct((LAYERS, ROWS * CH), jnp.float32),
            jax.ShapeDtypeStruct((1, LOCAL), jnp.float32),
        ],
        scratch_shapes=[pltpu.SemaphoreType.DMA((2,))],
        compiler_params=pltpu.CompilerParams(vmem_limit_bytes=VMEM_LIMIT),
    )(update, coeff)


def on_device(activations, cotangents, spin_bits, offdiag_energy):
    update, coeff = hand_on(
        *main_call(activations, cotangents, spin_bits, offdiag_energy.reshape(1, LOCAL))
    )
    return update, coeff.reshape(LOCAL)


def solution(mesh):
    in_specs = (
        P("samp", "par", None, None),
        P("samp", "par", None, None),
        P("samp", None),
        P("samp"),
    )
    out_specs = (P("par", "samp"), P("samp"))
    return jax.shard_map(
        on_device, mesh=mesh, in_specs=in_specs, out_specs=out_specs, check_vma=False
    )
```

```python
import math

import jax
import jax.numpy as jnp
from jax import lax
from jax.experimental import pallas as pl
from jax.experimental.pallas import tpu as pltpu
from jax.sharding import PartitionSpec as P

CH = 64
KK = 9
LAT = 24
SITES = LAT * LAT
NSAMP = 32
NPAR = 8
NZ = 8
NY = 4
LOCAL = 8
NS = NSAMP * LOCAL
ROWS = KK * CH // NSAMP
CHUNK = ROWS * LOCAL
WIDTH = ROWS * 128
PADK = 640
LAYERS = 2
ENTRIES = 16 * KK * CH * CH
MESH = pl.DeviceIdType.MESH
VMEM_LIMIT = 56 * 1024 * 1024
HIGHEST = lax.Precision.HIGHEST
VMEM = pltpu.VMEM


def rolled(value, amount):
    amount = amount % SITES
    if amount == 0:
        return value
    return jnp.concatenate([value[:, amount:], value[:, :amount]], axis=1)


def edge_mask(shape, col_step):
    column = lax.broadcasted_iota(jnp.int32, shape, 1) % LAT
    return column == (LAT - 1 if col_step > 0 else 0)


def column_shift(value, col_step, edge):
    if col_step == 0:
        return value
    return jnp.where(edge, rolled(value, col_step - LAT * col_step), rolled(value, col_step))


def wrap(value, size):
    return lax.select(value >= size, value - size, value)


STEPS = [(down, hop) for down in range(NY) for hop in (1, 7, 2, 6, 3, 5, 4, 0) if (down, hop) != (0, 0)]


def diagonal_energy(spin_bits):
    spin = (2 * spin_bits - 1).astype(jnp.float32)
    right = column_shift(spin, 1, edge_mask(spin.shape, 1))
    left = column_shift(spin, -1, edge_mask(spin.shape, -1))
    pairs = spin * rolled(spin, LAT) + spin * right
    corners = spin * rolled(right, LAT) + spin * rolled(left, LAT)
    diag = 0.25 * jnp.sum(pairs + 0.5 * corners, axis=1, keepdims=True)
    wide = jnp.broadcast_to(diag, (LOCAL, 128))
    here = lax.broadcasted_iota(jnp.int32, (LOCAL, 128), 0) == lax.broadcasted_iota(
        jnp.int32, (LOCAL, 128), 1
    )
    return jnp.sum(jnp.where(here, wide, 0.0), axis=0, keepdims=True)


PLANE = sorted(
    ((down, across) for down in range(NY) for across in range(4) if (down, across) != (0, 0)),
    key=lambda step: -(min(step[0], NY - step[0]) + min(step[1], 4 - step[1])),
)
PAIRS = 3 * CH // 2
HALF = CHUNK // 2
HEAD = 64
TAIL = 112
SLOTS = 2
CHIPS = 16


BLOCK = 64
PANEL = 8


def forward_block(diag, tile_ref, column_ref, cross_ref):
    eye = lax.broadcasted_iota(jnp.int32, (BLOCK, BLOCK), 0) == lax.broadcasted_iota(
        jnp.int32, (BLOCK, BLOCK), 1
    )
    wide = jnp.concatenate([diag, jnp.where(eye, 1.0, 0.0)], axis=1)
    count = BLOCK // PANEL
    tiles = [wide[8 * q : 8 * q + 8] for q in range(count)]
    sub = lax.broadcasted_iota(jnp.int32, (8, 128), 0)

    def lanes(tile, col):
        return jnp.broadcast_to(tile[:, col : col + 1], (8, 128))

    def joined(parts):
        total = parts[0]
        for i in range(1, PANEL):
            total = jnp.where(sub == i, parts[i], total)
        return total

    def broadcast_row(ref, panel, j, i):
        return ref[panel, j, pl.ds(i, 8, stride=0), :]

    reduced, scaled = [], []
    columns = [lanes(tiles[0], j) for j in range(PANEL)]
    for panel in range(count):
        base = panel * PANEL
        last = panel == count - 1
        tile_ref[panel, 0] = tiles[panel]
        for j in range(PANEL):
            column_ref[panel, j] = columns[j]
        low = {
            (i, j): broadcast_row(column_ref, panel, j, i)
            for i in range(PANEL)
            for j in range(i + 1)
        }
        rows = [broadcast_row(tile_ref, panel, 0, i) for i in range(PANEL)]
        old_columns = {
            q: [lanes(tiles[q], base + i) for i in range(PANEL)] for q in range(panel + 1, count)
        }
        if not last:
            cross = list(old_columns[panel + 1])
            columns = [lanes(tiles[panel + 1], base + PANEL + j) for j in range(PANEL)]
        ups, downs, starts, cross_scaled = {}, {}, {}, {}
        for p in range(0, PANEL, 2):
            q = p + 1
            a, b, c = low[p, p], low[q, p], low[q, q]
            recip = pl.reciprocal(a * c - b * b, approx=True)
            for i in range(q + 1, PANEL):
                up = c * low[i, p] - b * low[i, q]
                down = a * low[i, q] - b * low[i, p]
                ups[i, p], downs[i, p] = up * recip, down * recip
                for m in range(q + 1, i + 1):
                    if i <= q + 2:
                        step = (up * low[m, p] + down * low[m, q]) * recip
                    else:
                        step = ups[i, p] * low[m, p] + downs[i, p] * low[m, q]
                    low[i, m] = low[i, m] - step
            if not last:
                cross_scaled[p] = (c * cross[p] - b * cross[q]) * recip
                cross_scaled[q] = (a * cross[q] - b * cross[p]) * recip
                for i in range(q + 1, PANEL):
                    cross[i] = cross[i] - (ups[i, p] * cross[p] + downs[i, p] * cross[q])
            starts[p] = (c * rows[p] - b * rows[q]) * recip
            starts[q] = (a * rows[q] - b * rows[p]) * recip
            for i in range(q + 1, PANEL):
                rows[i] = rows[i] - (ups[i, p] * rows[p] + downs[i, p] * rows[q])
        if not last:
            for i in range(PANEL):
                cross_ref[panel, i] = cross[i]
            for j in range(PANEL):
                terms = [
                    cross_scaled[i] * broadcast_row(cross_ref, panel, i, j) for i in range(PANEL)
                ]
                while len(terms) > 1:
                    terms = [terms[a] + terms[a + 1] for a in range(0, len(terms), 2)]
                columns[j] = columns[j] - terms[0]
        reduced.append(joined(rows))
        scaled.append(joined([starts[i] for i in range(PANEL)]))
        if last:
            break
        solved = [None] * PANEL
        for p in reversed(range(0, PANEL, 2)):
            for total, factor, at in ((starts[p], ups, p), (starts[p + 1], downs, p + 1)):
                for i in reversed(range(p + 2, PANEL)):
                    total = total - factor[i, p] * solved[i]
                solved[at] = total
        for q in range(panel + 1, count):
            terms = [old_columns[q][i] * solved[i] for i in range(PANEL)]
            while len(terms) > 1:
                terms = [terms[a] + terms[a + 1] for a in range(0, len(terms), 2)]
            tiles[q] = tiles[q] - terms[0]
    lower = jnp.concatenate(reduced, axis=0)[:, BLOCK:]
    return lower, jnp.concatenate(scaled, axis=0)[:, BLOCK:]


def product(one, two, first_dim, second_dim):
    return lax.dot_general(
        one, two, (((first_dim,), (second_dim,)), ((), ())),
        precision=HIGHEST, preferred_element_type=jnp.float32,
    )


def main_kernel(
    act_hbm, cot_hbm, spin_ref, off_ref,
    update_ref, coeff_ref,
    act_ref, cot_ref, edges, lhs, rhs, stage, wide_rows, send_ref, recv_ref, cent_ref,
    energy_ref, energies_ref, part_ref, first, mine, second, gram_ref,
    work, held, tile_ref, column_ref, cross_ref,
    act_sem, cot_sem, send_sem, recv_sem, esem, sem1, sem2, sem3,
):
    samp = lax.axis_index("samp")
    par = lax.axis_index("par")
    z, y = samp // NY, samp % NY
    x, core = par // 2, par % 2
    slot_here = y * NZ + z
    sibling = (samp, x * 2 + 1 - core)
    zs = [wrap(z + hop, NZ) for hop in range(NZ)]
    ys = [wrap(y + down, NY) for down in range(NY)]
    xs = [wrap(x + across, 4) for across in range(4)]
    partners = [(down, zs[hop] * NY + ys[down]) for down, hop in STEPS]
    sorted_partners = [
        item for item, (_, hop) in sorted(zip(partners, STEPS), key=lambda pair: -min(pair[1][1], NZ - pair[1][1]))
    ]
    chip = y * 4 + x
    others = [
        (ys[down] * 4 + xs[across], z * NY + ys[down], xs[across] * 2)
        for down, across in PLANE
    ]
    around = [(other, (row, pair + side), side) for other, row, pair in others for side in range(2)]

    def by_core(body):
        @pl.when(core == 0)
        def _():
            body(0, 128)

        @pl.when(core == 1)
        def _():
            body(1, NS)

    def act_copy(n, layer):
        return pltpu.make_async_copy(
            act_hbm.at[n, layer], act_ref.at[n, layer], act_sem.at[layer, n]
        )

    def cot_copy(n, layer):
        return pltpu.make_async_copy(
            cot_hbm.at[n, layer], cot_ref.at[n, layer], cot_sem.at[layer, n]
        )

    for layer in range(LAYERS):
        for n in range(LOCAL):
            act_copy(n, layer).start()
            cot_copy(n, layer).start()

    def remote(source, target, send, recv, device):
        return pltpu.make_async_remote_copy(
            src_ref=source,
            dst_ref=target,
            send_sem=send,
            recv_sem=recv,
            device_id=device,
            device_id_type=MESH,
        )

    barrier = pltpu.get_barrier_semaphore()
    greeted = 0
    for _, other in partners:
        pl.semaphore_signal(barrier, inc=1, device_id=(other, par), device_id_type=MESH)
        greeted += 1
    for down in range(NY):
        for across in range(4):
            for side in (core, 1 - core):
                if across > 0 or side is not core:
                    device = (z * NY + ys[down], xs[across] * 2 + side)
                    pl.semaphore_signal(barrier, inc=1, device_id=device, device_id_type=MESH)
                    greeted += 1

    left = lax.broadcasted_iota(jnp.int32, (PAIRS, 128), 1) < CH
    lhs[:, :, PADK - 128 :] = jnp.zeros((SLOTS, 3 * CH, 128), jnp.bfloat16)
    rhs[:, :, PADK - 128 :] = jnp.zeros((SLOTS, 3 * CH, 128), jnp.bfloat16)
    stage[:, 1] = jnp.zeros((SLOTS, 3 * CH, 128), jnp.float32)
    for at, step in enumerate((-1, 1)):
        strip = jnp.where(edge_mask((8, SITES), step), 1.0, 0.0)
        edges[at] = jnp.concatenate([strip] * (CH // 8), axis=0).astype(jnp.bfloat16)

    def compute(sample, layer, slot):
        act = act_ref[sample, layer]
        cot = cot_ref[sample, layer]
        for step in (-1, 0, 1):
            low = (step + 1) * CH
            edge = edges[max(step, 0)] > 0
            lhs[slot, low : low + CH, :SITES] = column_shift(act, step, edge)
            rhs[slot, low : low + CH, :SITES] = rolled(cot, -LAT * step)
        out = lax.dot_general(
            lhs[slot], rhs[slot], (((1,), (1,)), ((), ())), preferred_element_type=jnp.float32
        )
        stage[slot, 0] = out[:, :128]
        stage[slot, 1, :, :CH] = out[:, 128:]
        even, odd, even_last, odd_last = [
            stage[slot, part, pl.ds(parity, PAIRS, stride=2), :]
            for part in (0, 1)
            for parity in (0, 1)
        ]
        blocks = (
            jnp.where(left, even, pltpu.roll(odd, CH, 1)),
            jnp.where(left, pltpu.roll(even, CH, 1), odd),
            jnp.where(left, even_last, pltpu.roll(odd_last, CH, 1)),
        )
        for down in range(3):
            wide_rows[layer, pl.ds(down * PAIRS * LOCAL + sample, PAIRS, stride=LOCAL), :] = blocks[down]

    def products(layer):
        def body(group, carry):
            for slot in range(SLOTS):
                sample = group * SLOTS + slot
                act_copy(sample, layer).wait()
                cot_copy(sample, layer).wait()
            for slot in range(SLOTS):
                compute(group * SLOTS + slot, layer, slot)
            return carry

        lax.fori_loop(0, LOCAL // SLOTS, body, 0)

    def rounded(other, layer, low, rows):
        start = pl.multiple_of(other * HALF + low, 8)
        return wide_rows[layer, pl.ds(start, rows), :]

    def send_wave(wave, low, rows):
        for down, other in sorted_partners:
            if wave == 0:
                block = rounded(other, 0, 0, HEAD)
            elif wave == 1:
                block = jnp.concatenate(
                    [rounded(other, 0, HEAD, HALF - HEAD), rounded(other, 1, 0, TAIL - HALF)], axis=0
                )
            else:
                block = rounded(other, 1, TAIL - HALF, CHUNK - TAIL)
            send_ref[other, low : low + rows] = block.astype(jnp.bfloat16)
            remote(
                send_ref.at[other, pl.ds(low, rows)],
                recv_ref.at[slot_here, pl.ds(low, rows)],
                send_sem,
                recv_sem.at[wave, down],
                (other, par),
            ).start()

    products(0)
    pl.semaphore_wait(barrier, greeted)
    send_wave(0, 0, HEAD)
    products(1)
    send_wave(1, HEAD, TAIL - HEAD)
    send_wave(2, TAIL, CHUNK - TAIL)

    flat = diagonal_energy(spin_ref[...])
    energy_ref[...] = jnp.zeros_like(energy_ref)
    energy_ref[:, :LOCAL] = flat[:, :LOCAL] + off_ref[...]
    for _, other in partners:
        remote(energy_ref, energies_ref.at[samp], esem.at[0], esem.at[1], (other, par)).start()
    energies_ref[samp] = energy_ref[...]
    recv_ref[slot_here] = jnp.concatenate(
        [rounded(samp, layer, 0, HALF) for layer in range(LAYERS)], axis=0
    ).astype(jnp.bfloat16)
    def await_wave(wave, low, rows):
        for down in range(NY):
            at = wrap(y + NY - down, NY) * NZ
            slots = pl.ds(0, NZ - 1) if down == 0 else pl.ds(at, NZ)
            landed = recv_ref.at[slots, pl.ds(low, rows)]
            remote(landed, landed, send_sem, recv_sem.at[wave, down], sibling).wait_recv()

    def heavy_part(pair):
        columns = pl.ds(256 * pair, 256)
        heavy = lax.dot_general(
            cent_ref[128:, columns], cent_ref[:, columns], (((1,), (1,)), ((), ())),
            preferred_element_type=jnp.float32,
        )
        part_ref[128:, :] = heavy if pair == 0 else part_ref[128:, :] + heavy

    squares = jnp.zeros((8, 256), jnp.float32)
    await_wave(0, 0, HEAD)
    for pair in range(ROWS // 2):
        if pair == HEAD // 16:
            await_wave(1, HEAD, TAIL - HEAD)
        if pair == TAIL // 16:
            await_wave(2, TAIL, CHUNK - TAIL)
        tile = jnp.stack(
            [
                recv_ref[(src % NY) * NZ + src // NY, 16 * pair : 16 * pair + 16, :].astype(jnp.float32)
                for src in range(NSAMP)
            ]
        ).reshape(NSAMP, 2, LOCAL, 128)
        halves = []
        for half in range(2):
            part = tile[:, half]
            mean = jnp.sum(jnp.sum(part, axis=0), axis=0, keepdims=True) / NS
            cent = ((part - mean) / math.sqrt(NS)).reshape(NS, 128)
            halves.append(cent.astype(jnp.bfloat16))
        cent = jnp.concatenate(halves, axis=1)
        cent_ref[:, 256 * pair : 256 * pair + 256] = cent
        light = lax.dot_general(
            cent[:128], cent[:128], (((1,), (1,)), ((), ())), preferred_element_type=jnp.float32
        )
        part_ref[:128, :128] = light if pair == 0 else part_ref[:128, :128] + light
        wide = cent[128:].astype(jnp.float32)
        squares = squares + jnp.sum((wide * wide).reshape(16, 8, 256), axis=0)
        if pair < TAIL // 16:
            heavy_part(pair)

    eye = lax.broadcasted_iota(jnp.int32, (128, 128), 0) == lax.broadcasted_iota(
        jnp.int32, (128, 128), 1
    )
    trace = jnp.sum(jnp.where(eye, part_ref[:128, :128], 0.0), keepdims=True) + jnp.sum(
        squares, keepdims=True
    )
    corner = jnp.logical_and(
        lax.broadcasted_iota(jnp.int32, (8, 128), 0) == 0,
        lax.broadcasted_iota(jnp.int32, (8, 128), 1) == 127,
    )
    part_ref[:8, :128] = jnp.where(corner, trace, part_ref[:8, :128])

    def rows_of(side, index):
        return pl.ds(pl.multiple_of(side * 128 + index * 8, 8), 8)

    slot = core * CHIPS + chip
    widths = (128, NS)

    def send_first(other, device, side):
        wide = pl.ds(0, widths[side])
        remote(
            part_ref.at[rows_of(side, other), wide],
            first.at[slot, :, wide],
            sem1.at[side],
            sem1.at[2],
            device,
        ).start()

    by_core(lambda side, width: send_first(chip, sibling, 0) if side == 1 else None)
    for kind in range(2):
        if kind == 1:
            for pair in range(TAIL // 16, ROWS // 2):
                heavy_part(pair)
        for other, device, side in around:
            if side == kind:
                send_first(other, device, side)
    by_core(lambda side, width: send_first(chip, sibling, 1) if side == 0 else None)

    def middle(side, width):
        wide = pl.ds(0, width)
        first[slot, :, wide] = part_ref[rows_of(side, chip), wide]
        landed = first.at[pl.ds(0, 2 * CHIPS - 1), :, wide]
        remote(landed, landed, sem1.at[0], sem1.at[2], sibling).wait_recv()
        own = jnp.sum(first[:, :, wide], axis=0)
        mine[:, wide] = own
        for hop in (4, 3, 5, 2, 6, 1, 7):
            device = (zs[hop] * NY + y, par)
            remote(
                mine.at[:, wide], second.at[z, :, wide], sem2.at[0], sem2.at[1], device
            ).start()
        second[z, :, wide] = own
        landed = second.at[pl.ds(0, NZ - 1), :, wide]
        remote(landed, landed, sem2.at[0], sem2.at[1], sibling).wait_recv()
        block = rows_of(side, chip)
        gram_ref[block, wide] = jnp.sum(second[:, :, wide], axis=0)
        done = gram_ref.at[block, wide]
        for _, device, _ in around:
            remote(done, done, sem3.at[0], sem3.at[1 + side], device).start()
        remote(done, done, sem3.at[0], sem3.at[1 + side], sibling).start()

    by_core(middle)

    def await_rows(kind):
        def body(side, width):
            count = CHIPS - 1 if side == kind else CHIPS
            landed = gram_ref.at[pl.ds(0, count * 8), pl.ds(0, widths[kind])]
            remote(landed, landed, sem3.at[0], sem3.at[1 + kind], sibling).wait_recv()

        by_core(body)

    energy_bytes = energies_ref.at[pl.ds(0, NSAMP - 1)]
    remote(energy_bytes, energy_bytes, esem.at[0], esem.at[1], sibling).wait()
    pieces = jnp.broadcast_to(energies_ref[...], (NSAMP, LOCAL, 128)).reshape(NS, 128)
    lane = lax.broadcasted_iota(jnp.int32, (NS, 128), 1)
    row = lax.broadcasted_iota(jnp.int32, (NSAMP, LOCAL, 128), 1).reshape(NS, 128)
    energy = jnp.sum(jnp.where(lane == row, pieces, 0.0), axis=1, keepdims=True)
    mean = jnp.sum(energy, axis=0, keepdims=True) / NS
    residual = -(energy - mean) / math.sqrt(NS)
    work[:, NS:] = jnp.broadcast_to(residual, (NS, 128))

    await_rows(0)
    level = 1.0 / (gram_ref[0:1, 127:128] / NS)
    wide_corner = jnp.logical_and(
        lax.broadcasted_iota(jnp.int32, (128, 128), 0) == 0,
        lax.broadcasted_iota(jnp.int32, (128, 128), 1) == 127,
    )
    light = jnp.where(wide_corner, gram_ref[127:128, 0:1], gram_ref[:128, :128])
    ridge = jnp.where(eye, 0.01, 0.0)
    work[:128, :128] = light * level + ridge
    one, two = slice(0, BLOCK), slice(BLOCK, 2 * BLOCK)
    lower_one, scaled_one = forward_block(work[one, one], tile_ref, column_ref, cross_ref)
    left = product(work[two, one], lower_one, 1, 1)
    right = product(scaled_one, work[one, two], 1, 0)
    lower_two, scaled_two = forward_block(
        work[two, two] - product(left, right, 1, 0), tile_ref, column_ref, cross_ref
    )
    cross_part = product(left, scaled_one, 1, 0)
    blank = jnp.zeros((BLOCK, BLOCK), jnp.float32)

    def joined_factor(first_part, second_part):
        return jnp.concatenate(
            [
                jnp.concatenate([first_part, blank], axis=1),
                jnp.concatenate([-product(second_part, cross_part, 1, 0), second_part], axis=1),
            ],
            axis=0,
        )

    lower = joined_factor(lower_one, lower_two)
    scaled = joined_factor(scaled_one, scaled_two)

    await_rows(1)
    below = gram_ref[128:, :128]
    corner_block = gram_ref[128:, 128:]
    scaled_below = below * level
    above = scaled_below.T
    last = corner_block * level + ridge
    near_middle = product(scaled, above[:, :BLOCK], 1, 0)
    near_outer = product(scaled_below[:BLOCK], lower, 1, 1)
    lower_three, scaled_three = forward_block(
        last[:BLOCK, :BLOCK] - product(near_outer, near_middle, 1, 0), tile_ref, column_ref, cross_ref
    )
    work[:128, 128:NS] = above
    work[128:, 128:NS] = last
    middle_rows = product(scaled, work[:128, 128:], 1, 0)
    outer = product(scaled_below, lower, 1, 1)
    work[128:, 128:] = work[128:, 128:] - product(outer, middle_rows, 1, 0)
    work[:128, 128:] = product(lower, middle_rows, 0, 0)

    three, four = slice(128, 128 + BLOCK), slice(128 + BLOCK, NS)
    near_middle = product(scaled_three, work[three, four], 1, 0)
    near_outer = product(work[four, three], lower_three, 1, 1)
    lower_four, scaled_four = forward_block(
        work[four, four] - product(near_outer, near_middle, 1, 0), tile_ref, column_ref, cross_ref
    )
    middle_rows = product(scaled_three, work[three, 128:], 1, 0)
    outer = product(work[:, three], lower_three, 1, 1)
    work[:, 128:] = work[:, 128:] - product(outer, middle_rows, 1, 0)
    work[three, 128:] = product(lower_three, middle_rows, 0, 0)

    middle_rows = product(scaled_four, work[four, NS:], 1, 0)
    outer = product(work[:, four], lower_four, 1, 1)
    work[:, NS:] = work[:, NS:] - product(outer, middle_rows, 1, 0)
    work[four, NS:] = product(lower_four, middle_rows, 0, 0)

    coeff = work[:, NS:] * level
    held[...] = coeff
    own = held[pl.ds(pl.multiple_of(samp * LOCAL, LOCAL), LOCAL), :]
    here = lax.broadcasted_iota(jnp.int32, (LOCAL, 128), 0) == lax.broadcasted_iota(
        jnp.int32, (LOCAL, 128), 1
    )
    coeff_ref[...] = jnp.sum(jnp.where(here, own, 0.0), axis=0, keepdims=True)[:, :LOCAL]
    upper, under = coeff[:128], coeff[128:]
    weighted = jnp.sum(light * upper + 2.0 * (below * under), axis=0, keepdims=True) * jnp.sum(
        jnp.where(eye, upper, 0.0), axis=0, keepdims=True
    ) + jnp.sum(corner_block * under, axis=0, keepdims=True) * jnp.sum(
        jnp.where(eye, under, 0.0), axis=0, keepdims=True
    )
    square_total = jnp.sum(weighted, keepdims=True)
    scale = lax.rsqrt(square_total / ENTRIES + 1e-06)
    for index in range(ROWS):
        cent = cent_ref[:, 128 * index : 128 * index + 128].astype(jnp.float32)
        layer, column = index // (ROWS // 2), 128 * (index % (ROWS // 2))
        update_ref[layer : layer + 1, column : column + 128] = (
            jnp.sum(cent * coeff, axis=0, keepdims=True) * scale
        )

    sent = send_ref.at[pl.ds(0, NSAMP - 1)]
    remote(sent, sent, send_sem, recv_sem.at[0, 0], sibling).wait_send()

    def finish(side, width):
        wide = pl.ds(0, width)
        for kind in range(2):
            count = CHIPS - 1 if kind == side else CHIPS
            bytes_ref = gram_ref.at[pl.ds(0, count * 8), pl.ds(0, widths[kind])]
            remote(bytes_ref, bytes_ref, sem1.at[kind], sem1.at[2], sibling).wait_send()
        landed = second.at[pl.ds(0, NZ - 1), :, wide]
        remote(landed, landed, sem2.at[0], sem2.at[1], sibling).wait_send()
        landed = first.at[pl.ds(0, 2 * CHIPS - 1), :, wide]
        remote(landed, landed, sem3.at[0], sem1.at[2], sibling).wait_send()

    by_core(finish)


def main_call(activations, cotangents, spin_bits, off_row):
    whole = pl.BlockSpec(memory_space=VMEM)
    anywhere = pl.BlockSpec(memory_space=pl.ANY)
    dma = pltpu.SemaphoreType.DMA
    return pl.pallas_call(
        main_kernel,
        in_specs=[anywhere, anywhere, whole, whole],
        out_specs=[whole, whole],
        out_shape=[
            jax.ShapeDtypeStruct((LAYERS, ROWS * CH), jnp.float32),
            jax.ShapeDtypeStruct((1, LOCAL), jnp.float32),
        ],
        scratch_shapes=[
            VMEM((LOCAL, LAYERS, CH, SITES), jnp.bfloat16),
            VMEM((LOCAL, LAYERS, CH, SITES), jnp.bfloat16),
            VMEM((2, CH, SITES), jnp.bfloat16),
            VMEM((SLOTS, 3 * CH, PADK), jnp.bfloat16),
            VMEM((SLOTS, 3 * CH, PADK), jnp.bfloat16),
            VMEM((SLOTS, 2, 3 * CH, 128), jnp.float32),
            VMEM((LAYERS, NSAMP * HALF, 128), jnp.float32),
            VMEM((NSAMP, CHUNK, 128), jnp.bfloat16),
            VMEM((NSAMP, CHUNK, 128), jnp.bfloat16),
            VMEM((NS, WIDTH), jnp.bfloat16),
            VMEM((1, 128), jnp.float32),
            VMEM((NSAMP, 1, 128), jnp.float32),
            VMEM((NS, NS), jnp.float32),
            VMEM((2 * CHIPS, 8, NS), jnp.float32),
            VMEM((8, NS), jnp.float32),
            VMEM((NZ, 8, NS), jnp.float32),
            VMEM((NS, NS), jnp.float32),
            VMEM((NS, NS + 128), jnp.float32),
            VMEM((NS, 128), jnp.float32),
            VMEM((BLOCK // PANEL, 1, 8, 128), jnp.float32),
            VMEM((BLOCK // PANEL, PANEL, 8, 128), jnp.float32),
            VMEM((BLOCK // PANEL, PANEL, 8, 128), jnp.float32),
            dma((LAYERS, LOCAL)),
            dma((LAYERS, LOCAL)),
            dma,
            dma((3, NY)),
            dma((2,)),
            dma((3,)),
            dma((2,)),
            dma((3,)),
        ],
        compiler_params=pltpu.CompilerParams(
            collective_id=0, has_side_effects=True, vmem_limit_bytes=VMEM_LIMIT
        ),
    )(activations, cotangents, spin_bits, off_row)


def hand_on_kernel(update_in, coeff_in, update_ref, coeff_ref, sems):
    copies = [
        pltpu.make_async_copy(update_in, update_ref, sems.at[0]),
        pltpu.make_async_copy(coeff_in, coeff_ref, sems.at[1]),
    ]
    for copy in copies:
        copy.start()
    for copy in copies:
        copy.wait()


def hand_on(update, coeff):
    anywhere = pl.BlockSpec(memory_space=pl.ANY)
    return pl.pallas_call(
        hand_on_kernel,
        in_specs=[anywhere, anywhere],
        out_specs=[anywhere, anywhere],
        out_shape=[
            jax.ShapeDtypeStruct((LAYERS, ROWS * CH), jnp.float32),
            jax.ShapeDtypeStruct((1, LOCAL), jnp.float32),
        ],
        scratch_shapes=[pltpu.SemaphoreType.DMA((2,))],
        compiler_params=pltpu.CompilerParams(vmem_limit_bytes=VMEM_LIMIT),
    )(update, coeff)


def on_device(activations, cotangents, spin_bits, offdiag_energy):
    update, coeff = hand_on(
        *main_call(activations, cotangents, spin_bits, offdiag_energy.reshape(1, LOCAL))
    )
    return update, coeff.reshape(LOCAL)


def solution(mesh):
    in_specs = (
        P("samp", "par", None, None),
        P("samp", "par", None, None),
        P("samp", None),
        P("samp"),
    )
    out_specs = (P("par", "samp"), P("samp"))
    return jax.shard_map(
        on_device, mesh=mesh, in_specs=in_specs, out_specs=out_specs, check_vma=False
    )
```

```python
import math

import jax
import jax.numpy as jnp
from jax import lax
from jax.experimental import pallas as pl
from jax.experimental.pallas import tpu as pltpu
from jax.sharding import PartitionSpec as P

CH = 64
KK = 9
LAT = 24
SITES = LAT * LAT
NSAMP = 32
NPAR = 8
NZ = 8
NY = 4
LOCAL = 8
NS = NSAMP * LOCAL
ROWS = KK * CH // NSAMP
CHUNK = ROWS * LOCAL
WIDTH = ROWS * 128
PADK = 640
LAYERS = 2
ENTRIES = 16 * KK * CH * CH
MESH = pl.DeviceIdType.MESH
VMEM_LIMIT = 56 * 1024 * 1024
HIGHEST = lax.Precision.HIGHEST
VMEM = pltpu.VMEM


def rolled(value, amount):
    amount = amount % SITES
    if amount == 0:
        return value
    return jnp.concatenate([value[:, amount:], value[:, :amount]], axis=1)


def edge_mask(shape, col_step):
    column = lax.broadcasted_iota(jnp.int32, shape, 1) % LAT
    return column == (LAT - 1 if col_step > 0 else 0)


def column_shift(value, col_step, edge):
    if col_step == 0:
        return value
    return jnp.where(edge, rolled(value, col_step - LAT * col_step), rolled(value, col_step))


def wrap(value, size):
    return lax.select(value >= size, value - size, value)


STEPS = [(down, hop) for down in range(NY) for hop in (1, 7, 2, 6, 3, 5, 4, 0) if (down, hop) != (0, 0)]


def diagonal_energy(spin_bits):
    spin = (2 * spin_bits - 1).astype(jnp.float32)
    right = column_shift(spin, 1, edge_mask(spin.shape, 1))
    left = column_shift(spin, -1, edge_mask(spin.shape, -1))
    pairs = spin * rolled(spin, LAT) + spin * right
    corners = spin * rolled(right, LAT) + spin * rolled(left, LAT)
    diag = 0.25 * jnp.sum(pairs + 0.5 * corners, axis=1, keepdims=True)
    wide = jnp.broadcast_to(diag, (LOCAL, 128))
    here = lax.broadcasted_iota(jnp.int32, (LOCAL, 128), 0) == lax.broadcasted_iota(
        jnp.int32, (LOCAL, 128), 1
    )
    return jnp.sum(jnp.where(here, wide, 0.0), axis=0, keepdims=True)


PLANE = sorted(
    ((down, across) for down in range(NY) for across in range(4) if (down, across) != (0, 0)),
    key=lambda step: -(min(step[0], NY - step[0]) + min(step[1], 4 - step[1])),
)
PAIRS = 3 * CH // 2
HALF = CHUNK // 2
HEAD = 64
TAIL = 112
SLOTS = 2
CHIPS = 16


BLOCK = 64
PANEL = 8


def forward_block(diag, tile_ref, column_ref, cross_ref):
    eye = lax.broadcasted_iota(jnp.int32, (BLOCK, BLOCK), 0) == lax.broadcasted_iota(
        jnp.int32, (BLOCK, BLOCK), 1
    )
    wide = jnp.concatenate([diag, jnp.where(eye, 1.0, 0.0)], axis=1)
    count = BLOCK // PANEL
    tiles = [wide[8 * q : 8 * q + 8] for q in range(count)]
    sub = lax.broadcasted_iota(jnp.int32, (8, 128), 0)

    def lanes(tile, col):
        return jnp.broadcast_to(tile[:, col : col + 1], (8, 128))

    def joined(parts):
        total = parts[0]
        for i in range(1, PANEL):
            total = jnp.where(sub == i, parts[i], total)
        return total

    def broadcast_row(ref, panel, j, i):
        return ref[panel, j, pl.ds(i, 8, stride=0), :]

    reduced, scaled = [], []
    columns = [lanes(tiles[0], j) for j in range(PANEL)]
    for panel in range(count):
        base = panel * PANEL
        last = panel == count - 1
        tile_ref[panel, 0] = tiles[panel]
        for j in range(PANEL):
            column_ref[panel, j] = columns[j]
        low = {
            (i, j): broadcast_row(column_ref, panel, j, i)
            for i in range(PANEL)
            for j in range(i + 1)
        }
        rows = [broadcast_row(tile_ref, panel, 0, i) for i in range(PANEL)]
        old_columns = {
            q: [lanes(tiles[q], base + i) for i in range(PANEL)] for q in range(panel + 1, count)
        }
        if not last:
            cross = list(old_columns[panel + 1])
            columns = [lanes(tiles[panel + 1], base + PANEL + j) for j in range(PANEL)]
        ups, downs, starts, cross_scaled = {}, {}, {}, {}
        for p in range(0, PANEL, 2):
            q = p + 1
            a, b, c = low[p, p], low[q, p], low[q, q]
            recip = pl.reciprocal(a * c - b * b, approx=True)
            for i in range(q + 1, PANEL):
                up = c * low[i, p] - b * low[i, q]
                down = a * low[i, q] - b * low[i, p]
                ups[i, p], downs[i, p] = up * recip, down * recip
                for m in range(q + 1, i + 1):
                    if i <= q + 2:
                        step = (up * low[m, p] + down * low[m, q]) * recip
                    else:
                        step = ups[i, p] * low[m, p] + downs[i, p] * low[m, q]
                    low[i, m] = low[i, m] - step
            if not last:
                cross_scaled[p] = (c * cross[p] - b * cross[q]) * recip
                cross_scaled[q] = (a * cross[q] - b * cross[p]) * recip
                for i in range(q + 1, PANEL):
                    cross[i] = cross[i] - (ups[i, p] * cross[p] + downs[i, p] * cross[q])
            starts[p] = (c * rows[p] - b * rows[q]) * recip
            starts[q] = (a * rows[q] - b * rows[p]) * recip
            for i in range(q + 1, PANEL):
                rows[i] = rows[i] - (ups[i, p] * rows[p] + downs[i, p] * rows[q])
        if not last:
            for i in range(PANEL):
                cross_ref[panel, i] = cross[i]
            for j in range(PANEL):
                terms = [
                    cross_scaled[i] * broadcast_row(cross_ref, panel, i, j) for i in range(PANEL)
                ]
                while len(terms) > 1:
                    terms = [terms[a] + terms[a + 1] for a in range(0, len(terms), 2)]
                columns[j] = columns[j] - terms[0]
        reduced.append(joined(rows))
        scaled.append(joined([starts[i] for i in range(PANEL)]))
        if last:
            break
        solved = [None] * PANEL
        for p in reversed(range(0, PANEL, 2)):
            for total, factor, at in ((starts[p], ups, p), (starts[p + 1], downs, p + 1)):
                for i in reversed(range(p + 2, PANEL)):
                    total = total - factor[i, p] * solved[i]
                solved[at] = total
        for q in range(panel + 1, count):
            terms = [old_columns[q][i] * solved[i] for i in range(PANEL)]
            while len(terms) > 1:
                terms = [terms[a] + terms[a + 1] for a in range(0, len(terms), 2)]
            tiles[q] = tiles[q] - terms[0]
    lower = jnp.concatenate(reduced, axis=0)[:, BLOCK:]
    return lower, jnp.concatenate(scaled, axis=0)[:, BLOCK:]


def product(one, two, first_dim, second_dim):
    return lax.dot_general(
        one, two, (((first_dim,), (second_dim,)), ((), ())),
        precision=HIGHEST, preferred_element_type=jnp.float32,
    )


def main_kernel(
    act_hbm, cot_hbm, spin_ref, off_ref,
    update_ref, coeff_ref,
    act_ref, cot_ref, edges, lhs, rhs, stage, wide_rows, send_ref, recv_ref, cent_ref,
    energy_ref, energies_ref, part_ref, first, mine, second, gram_ref,
    work, held, tile_ref, column_ref, cross_ref,
    act_sem, cot_sem, send_sem, recv_sem, esem, sem1, sem2, sem3,
):
    samp = lax.axis_index("samp")
    par = lax.axis_index("par")
    z, y = samp // NY, samp % NY
    x, core = par // 2, par % 2
    slot_here = y * NZ + z
    sibling = (samp, x * 2 + 1 - core)
    zs = [wrap(z + hop, NZ) for hop in range(NZ)]
    ys = [wrap(y + down, NY) for down in range(NY)]
    xs = [wrap(x + across, 4) for across in range(4)]
    partners = [(down, zs[hop] * NY + ys[down]) for down, hop in STEPS]
    sorted_partners = [
        item for item, (_, hop) in sorted(zip(partners, STEPS), key=lambda pair: -min(pair[1][1], NZ - pair[1][1]))
    ]
    chip = y * 4 + x
    others = [
        (ys[down] * 4 + xs[across], z * NY + ys[down], xs[across] * 2)
        for down, across in PLANE
    ]
    around = [(other, (row, pair + side), side) for other, row, pair in others for side in range(2)]

    def by_core(body):
        @pl.when(core == 0)
        def _():
            body(0, 128)

        @pl.when(core == 1)
        def _():
            body(1, NS)

    def fetches(group, layer):
        samples = pl.ds(group * SLOTS, SLOTS) if layer == 0 else pl.ds(0, LOCAL)
        return [
            pltpu.make_async_copy(
                hbm.at[samples, layer], local.at[samples, layer], sems.at[group]
            )
            for hbm, local, sems in ((act_hbm, act_ref, act_sem), (cot_hbm, cot_ref, cot_sem))
        ]

    groups = LOCAL // SLOTS
    for group in range(groups):
        for fetch in fetches(group, 0):
            fetch.start()

    def remote(source, target, send, recv, device):
        return pltpu.make_async_remote_copy(
            src_ref=source,
            dst_ref=target,
            send_sem=send,
            recv_sem=recv,
            device_id=device,
            device_id_type=MESH,
        )

    barrier = pltpu.get_barrier_semaphore()
    greeted = 0
    for _, other in partners:
        pl.semaphore_signal(barrier, inc=1, device_id=(other, par), device_id_type=MESH)
        greeted += 1
    for down in range(NY):
        for across in range(4):
            for side in (core, 1 - core):
                if across > 0 or side is not core:
                    device = (z * NY + ys[down], xs[across] * 2 + side)
                    pl.semaphore_signal(barrier, inc=1, device_id=device, device_id_type=MESH)
                    greeted += 1

    left = lax.broadcasted_iota(jnp.int32, (PAIRS, 128), 1) < CH
    lhs[:, :, PADK - 128 :] = jnp.zeros((SLOTS, 3 * CH, 128), jnp.bfloat16)
    rhs[:, :, PADK - 128 :] = jnp.zeros((SLOTS, 3 * CH, 128), jnp.bfloat16)
    stage[:, 1] = jnp.zeros((SLOTS, 3 * CH, 128), jnp.float32)
    for at, step in enumerate((-1, 1)):
        strip = jnp.where(edge_mask((8, SITES), step), 1.0, 0.0)
        edges[at] = jnp.concatenate([strip] * (CH // 8), axis=0).astype(jnp.bfloat16)

    def compute(sample, layer, slot):
        act = act_ref[sample, layer]
        cot = cot_ref[sample, layer]
        for step in (-1, 0, 1):
            low = (step + 1) * CH
            edge = edges[max(step, 0)] > 0
            lhs[slot, low : low + CH, :SITES] = column_shift(act, step, edge)
            rhs[slot, low : low + CH, :SITES] = rolled(cot, -LAT * step)
        out = lax.dot_general(
            lhs[slot], rhs[slot], (((1,), (1,)), ((), ())), preferred_element_type=jnp.float32
        )
        stage[slot, 0] = out[:, :128]
        stage[slot, 1, :, :CH] = out[:, 128:]
        even, odd, even_last, odd_last = [
            stage[slot, part, pl.ds(parity, PAIRS, stride=2), :]
            for part in (0, 1)
            for parity in (0, 1)
        ]
        blocks = (
            jnp.where(left, even, pltpu.roll(odd, CH, 1)),
            jnp.where(left, pltpu.roll(even, CH, 1), odd),
            jnp.where(left, even_last, pltpu.roll(odd_last, CH, 1)),
        )
        for down in range(3):
            wide_rows[layer, pl.ds(down * PAIRS * LOCAL + sample, PAIRS, stride=LOCAL), :] = blocks[down]

    def products(layer):
        def body(group, carry):
            if layer == 0:
                for fetch in fetches(group, 0):
                    fetch.wait()
            for slot in range(SLOTS):
                compute(group * SLOTS + slot, layer, slot)
            return carry

        lax.fori_loop(0, groups, body, 0)

    def rounded(other, layer, low, rows):
        start = pl.multiple_of(other * HALF + low, 8)
        return wide_rows[layer, pl.ds(start, rows), :]

    def send_wave(wave, low, rows):
        for down, other in sorted_partners:
            if wave == 0:
                block = rounded(other, 0, 0, HEAD)
            elif wave == 1:
                block = jnp.concatenate(
                    [rounded(other, 0, HEAD, HALF - HEAD), rounded(other, 1, 0, TAIL - HALF)], axis=0
                )
            else:
                block = rounded(other, 1, TAIL - HALF, CHUNK - TAIL)
            send_ref[other, low : low + rows] = block.astype(jnp.bfloat16)
            remote(
                send_ref.at[other, pl.ds(low, rows)],
                recv_ref.at[slot_here, pl.ds(low, rows)],
                send_sem,
                recv_sem.at[wave, down],
                (other, par),
            ).start()

    products(0)
    pl.semaphore_wait(barrier, greeted)
    send_wave(0, 0, HEAD)
    for fetch in fetches(groups, 1):
        fetch.start()
    for fetch in fetches(groups, 1):
        fetch.wait()
    products(1)
    send_wave(1, HEAD, TAIL - HEAD)
    send_wave(2, TAIL, CHUNK - TAIL)

    flat = diagonal_energy(spin_ref[...])
    energy_ref[...] = jnp.zeros_like(energy_ref)
    energy_ref[:, :LOCAL] = flat[:, :LOCAL] + off_ref[...]
    for _, other in partners:
        remote(energy_ref, energies_ref.at[samp], esem.at[0], esem.at[1], (other, par)).start()
    energies_ref[samp] = energy_ref[...]
    recv_ref[slot_here] = jnp.concatenate(
        [rounded(samp, layer, 0, HALF) for layer in range(LAYERS)], axis=0
    ).astype(jnp.bfloat16)
    def await_wave(wave, low, rows):
        for down in range(NY):
            at = wrap(y + NY - down, NY) * NZ
            slots = pl.ds(0, NZ - 1) if down == 0 else pl.ds(at, NZ)
            landed = recv_ref.at[slots, pl.ds(low, rows)]
            remote(landed, landed, send_sem, recv_sem.at[wave, down], sibling).wait_recv()

    def heavy_part(pair):
        columns = pl.ds(256 * pair, 256)
        heavy = lax.dot_general(
            cent_ref[128:, columns], cent_ref[:, columns], (((1,), (1,)), ((), ())),
            preferred_element_type=jnp.float32,
        )
        part_ref[128:, :] = heavy if pair == 0 else part_ref[128:, :] + heavy

    squares = jnp.zeros((8, 256), jnp.float32)
    await_wave(0, 0, HEAD)
    for pair in range(ROWS // 2):
        if pair == HEAD // 16:
            await_wave(1, HEAD, TAIL - HEAD)
        if pair == TAIL // 16:
            await_wave(2, TAIL, CHUNK - TAIL)
        tile = jnp.stack(
            [
                recv_ref[(src % NY) * NZ + src // NY, 16 * pair : 16 * pair + 16, :].astype(jnp.float32)
                for src in range(NSAMP)
            ]
        ).reshape(NSAMP, 2, LOCAL, 128)
        halves = []
        for half in range(2):
            part = tile[:, half]
            mean = jnp.sum(jnp.sum(part, axis=0), axis=0, keepdims=True) / NS
            cent = ((part - mean) / math.sqrt(NS)).reshape(NS, 128)
            halves.append(cent.astype(jnp.bfloat16))
        cent = jnp.concatenate(halves, axis=1)
        cent_ref[:, 256 * pair : 256 * pair + 256] = cent
        light = lax.dot_general(
            cent[:128], cent[:128], (((1,), (1,)), ((), ())), preferred_element_type=jnp.float32
        )
        part_ref[:128, :128] = light if pair == 0 else part_ref[:128, :128] + light
        wide = cent[128:].astype(jnp.float32)
        squares = squares + jnp.sum((wide * wide).reshape(16, 8, 256), axis=0)
        if pair < TAIL // 16:
            heavy_part(pair)

    eye = lax.broadcasted_iota(jnp.int32, (128, 128), 0) == lax.broadcasted_iota(
        jnp.int32, (128, 128), 1
    )
    trace = jnp.sum(jnp.where(eye, part_ref[:128, :128], 0.0), keepdims=True) + jnp.sum(
        squares, keepdims=True
    )
    corner = jnp.logical_and(
        lax.broadcasted_iota(jnp.int32, (8, 128), 0) == 0,
        lax.broadcasted_iota(jnp.int32, (8, 128), 1) == 127,
    )
    part_ref[:8, :128] = jnp.where(corner, trace, part_ref[:8, :128])

    def rows_of(side, index):
        return pl.ds(pl.multiple_of(side * 128 + index * 8, 8), 8)

    slot = core * CHIPS + chip
    widths = (128, NS)

    def send_first(other, device, side):
        wide = pl.ds(0, widths[side])
        remote(
            part_ref.at[rows_of(side, other), wide],
            first.at[slot, :, wide],
            sem1.at[side],
            sem1.at[2],
            device,
        ).start()

    by_core(lambda side, width: send_first(chip, sibling, 0) if side == 1 else None)
    for kind in range(2):
        if kind == 1:
            for pair in range(TAIL // 16, ROWS // 2):
                heavy_part(pair)
        for other, device, side in around:
            if side == kind:
                send_first(other, device, side)
    by_core(lambda side, width: send_first(chip, sibling, 1) if side == 0 else None)

    def middle(side, width):
        wide = pl.ds(0, width)
        first[slot, :, wide] = part_ref[rows_of(side, chip), wide]
        landed = first.at[pl.ds(0, 2 * CHIPS - 1), :, wide]
        remote(landed, landed, sem1.at[0], sem1.at[2], sibling).wait_recv()
        own = jnp.sum(first[:, :, wide], axis=0)
        mine[:, wide] = own
        for hop in (4, 3, 5, 2, 6, 1, 7):
            device = (zs[hop] * NY + y, par)
            remote(
                mine.at[:, wide], second.at[z, :, wide], sem2.at[0], sem2.at[1], device
            ).start()
        second[z, :, wide] = own
        landed = second.at[pl.ds(0, NZ - 1), :, wide]
        remote(landed, landed, sem2.at[0], sem2.at[1], sibling).wait_recv()
        block = rows_of(side, chip)
        gram_ref[block, wide] = jnp.sum(second[:, :, wide], axis=0)
        done = gram_ref.at[block, wide]
        for _, device, _ in around:
            remote(done, done, sem3.at[0], sem3.at[1 + side], device).start()
        remote(done, done, sem3.at[0], sem3.at[1 + side], sibling).start()

    by_core(middle)

    def await_rows(kind):
        def body(side, width):
            count = CHIPS - 1 if side == kind else CHIPS
            landed = gram_ref.at[pl.ds(0, count * 8), pl.ds(0, widths[kind])]
            remote(landed, landed, sem3.at[0], sem3.at[1 + kind], sibling).wait_recv()

        by_core(body)

    energy_bytes = energies_ref.at[pl.ds(0, NSAMP - 1)]
    remote(energy_bytes, energy_bytes, esem.at[0], esem.at[1], sibling).wait()
    pieces = jnp.broadcast_to(energies_ref[...], (NSAMP, LOCAL, 128)).reshape(NS, 128)
    lane = lax.broadcasted_iota(jnp.int32, (NS, 128), 1)
    row = lax.broadcasted_iota(jnp.int32, (NSAMP, LOCAL, 128), 1).reshape(NS, 128)
    energy = jnp.sum(jnp.where(lane == row, pieces, 0.0), axis=1, keepdims=True)
    mean = jnp.sum(energy, axis=0, keepdims=True) / NS
    residual = -(energy - mean) / math.sqrt(NS)
    work[:, NS:] = jnp.broadcast_to(residual, (NS, 128))

    await_rows(0)
    level = 1.0 / (gram_ref[0:1, 127:128] / NS)
    wide_corner = jnp.logical_and(
        lax.broadcasted_iota(jnp.int32, (128, 128), 0) == 0,
        lax.broadcasted_iota(jnp.int32, (128, 128), 1) == 127,
    )
    light = jnp.where(wide_corner, gram_ref[127:128, 0:1], gram_ref[:128, :128])
    ridge = jnp.where(eye, 0.01, 0.0)
    work[:128, :128] = light * level + ridge
    one, two = slice(0, BLOCK), slice(BLOCK, 2 * BLOCK)
    lower_one, scaled_one = forward_block(work[one, one], tile_ref, column_ref, cross_ref)
    left = product(work[two, one], lower_one, 1, 1)
    right = product(scaled_one, work[one, two], 1, 0)
    lower_two, scaled_two = forward_block(
        work[two, two] - product(left, right, 1, 0), tile_ref, column_ref, cross_ref
    )
    cross_part = product(left, scaled_one, 1, 0)
    blank = jnp.zeros((BLOCK, BLOCK), jnp.float32)

    def joined_factor(first_part, second_part):
        return jnp.concatenate(
            [
                jnp.concatenate([first_part, blank], axis=1),
                jnp.concatenate([-product(second_part, cross_part, 1, 0), second_part], axis=1),
            ],
            axis=0,
        )

    lower = joined_factor(lower_one, lower_two)
    scaled = joined_factor(scaled_one, scaled_two)

    await_rows(1)
    below = gram_ref[128:, :128]
    corner_block = gram_ref[128:, 128:]
    scaled_below = below * level
    above = scaled_below.T
    last = corner_block * level + ridge
    near_middle = product(scaled, above[:, :BLOCK], 1, 0)
    near_outer = product(scaled_below[:BLOCK], lower, 1, 1)
    lower_three, scaled_three = forward_block(
        last[:BLOCK, :BLOCK] - product(near_outer, near_middle, 1, 0), tile_ref, column_ref, cross_ref
    )
    work[:128, 128:NS] = above
    work[128:, 128:NS] = last
    middle_rows = product(scaled, work[:128, 128:], 1, 0)
    outer = product(scaled_below, lower, 1, 1)
    work[128:, 128:] = work[128:, 128:] - product(outer, middle_rows, 1, 0)
    work[:128, 128:] = product(lower, middle_rows, 0, 0)

    three, four = slice(128, 128 + BLOCK), slice(128 + BLOCK, NS)
    near_middle = product(scaled_three, work[three, four], 1, 0)
    near_outer = product(work[four, three], lower_three, 1, 1)
    lower_four, scaled_four = forward_block(
        work[four, four] - product(near_outer, near_middle, 1, 0), tile_ref, column_ref, cross_ref
    )
    middle_rows = product(scaled_three, work[three, 128:], 1, 0)
    outer = product(work[:, three], lower_three, 1, 1)
    work[:, 128:] = work[:, 128:] - product(outer, middle_rows, 1, 0)
    work[three, 128:] = product(lower_three, middle_rows, 0, 0)

    middle_rows = product(scaled_four, work[four, NS:], 1, 0)
    outer = product(work[:, four], lower_four, 1, 1)
    work[:, NS:] = work[:, NS:] - product(outer, middle_rows, 1, 0)
    work[four, NS:] = product(lower_four, middle_rows, 0, 0)

    coeff = work[:, NS:] * level
    held[...] = coeff
    own = held[pl.ds(pl.multiple_of(samp * LOCAL, LOCAL), LOCAL), :]
    here = lax.broadcasted_iota(jnp.int32, (LOCAL, 128), 0) == lax.broadcasted_iota(
        jnp.int32, (LOCAL, 128), 1
    )
    coeff_ref[...] = jnp.sum(jnp.where(here, own, 0.0), axis=0, keepdims=True)[:, :LOCAL]
    upper, under = coeff[:128], coeff[128:]
    weighted = jnp.sum(light * upper + 2.0 * (below * under), axis=0, keepdims=True) * jnp.sum(
        jnp.where(eye, upper, 0.0), axis=0, keepdims=True
    ) + jnp.sum(corner_block * under, axis=0, keepdims=True) * jnp.sum(
        jnp.where(eye, under, 0.0), axis=0, keepdims=True
    )
    square_total = jnp.sum(weighted, keepdims=True)
    scale = lax.rsqrt(square_total / ENTRIES + 1e-06)
    for index in range(ROWS):
        cent = cent_ref[:, 128 * index : 128 * index + 128].astype(jnp.float32)
        layer, column = index // (ROWS // 2), 128 * (index % (ROWS // 2))
        update_ref[layer : layer + 1, column : column + 128] = (
            jnp.sum(cent * coeff, axis=0, keepdims=True) * scale
        )

    sent = send_ref.at[pl.ds(0, NSAMP - 1)]
    remote(sent, sent, send_sem, recv_sem.at[0, 0], sibling).wait_send()

    def finish(side, width):
        wide = pl.ds(0, width)
        for kind in range(2):
            count = CHIPS - 1 if kind == side else CHIPS
            bytes_ref = gram_ref.at[pl.ds(0, count * 8), pl.ds(0, widths[kind])]
            remote(bytes_ref, bytes_ref, sem1.at[kind], sem1.at[2], sibling).wait_send()
        landed = second.at[pl.ds(0, NZ - 1), :, wide]
        remote(landed, landed, sem2.at[0], sem2.at[1], sibling).wait_send()
        landed = first.at[pl.ds(0, 2 * CHIPS - 1), :, wide]
        remote(landed, landed, sem3.at[0], sem1.at[2], sibling).wait_send()

    by_core(finish)


def main_call(activations, cotangents, spin_bits, off_row):
    whole = pl.BlockSpec(memory_space=VMEM)
    anywhere = pl.BlockSpec(memory_space=pl.ANY)
    dma = pltpu.SemaphoreType.DMA
    return pl.pallas_call(
        main_kernel,
        in_specs=[anywhere, anywhere, whole, whole],
        out_specs=[whole, whole],
        out_shape=[
            jax.ShapeDtypeStruct((LAYERS, ROWS * CH), jnp.float32),
            jax.ShapeDtypeStruct((1, LOCAL), jnp.float32),
        ],
        scratch_shapes=[
            VMEM((LOCAL, LAYERS, CH, SITES), jnp.bfloat16),
            VMEM((LOCAL, LAYERS, CH, SITES), jnp.bfloat16),
            VMEM((2, CH, SITES), jnp.bfloat16),
            VMEM((SLOTS, 3 * CH, PADK), jnp.bfloat16),
            VMEM((SLOTS, 3 * CH, PADK), jnp.bfloat16),
            VMEM((SLOTS, 2, 3 * CH, 128), jnp.float32),
            VMEM((LAYERS, NSAMP * HALF, 128), jnp.float32),
            VMEM((NSAMP, CHUNK, 128), jnp.bfloat16),
            VMEM((NSAMP, CHUNK, 128), jnp.bfloat16),
            VMEM((NS, WIDTH), jnp.bfloat16),
            VMEM((1, 128), jnp.float32),
            VMEM((NSAMP, 1, 128), jnp.float32),
            VMEM((NS, NS), jnp.float32),
            VMEM((2 * CHIPS, 8, NS), jnp.float32),
            VMEM((8, NS), jnp.float32),
            VMEM((NZ, 8, NS), jnp.float32),
            VMEM((NS, NS), jnp.float32),
            VMEM((NS, NS + 128), jnp.float32),
            VMEM((NS, 128), jnp.float32),
            VMEM((BLOCK // PANEL, 1, 8, 128), jnp.float32),
            VMEM((BLOCK // PANEL, PANEL, 8, 128), jnp.float32),
            VMEM((BLOCK // PANEL, PANEL, 8, 128), jnp.float32),
            dma((LOCAL // SLOTS + 1,)),
            dma((LOCAL // SLOTS + 1,)),
            dma,
            dma((3, NY)),
            dma((2,)),
            dma((3,)),
            dma((2,)),
            dma((3,)),
        ],
        compiler_params=pltpu.CompilerParams(
            collective_id=0, has_side_effects=True, vmem_limit_bytes=VMEM_LIMIT
        ),
    )(activations, cotangents, spin_bits, off_row)


def hand_on_kernel(update_in, coeff_in, update_ref, coeff_ref, sems):
    copies = [
        pltpu.make_async_copy(update_in, update_ref, sems.at[0]),
        pltpu.make_async_copy(coeff_in, coeff_ref, sems.at[1]),
    ]
    for copy in copies:
        copy.start()
    for copy in copies:
        copy.wait()


def hand_on(update, coeff):
    anywhere = pl.BlockSpec(memory_space=pl.ANY)
    return pl.pallas_call(
        hand_on_kernel,
        in_specs=[anywhere, anywhere],
        out_specs=[anywhere, anywhere],
        out_shape=[
            jax.ShapeDtypeStruct((LAYERS, ROWS * CH), jnp.float32),
            jax.ShapeDtypeStruct((1, LOCAL), jnp.float32),
        ],
        scratch_shapes=[pltpu.SemaphoreType.DMA((2,))],
        compiler_params=pltpu.CompilerParams(vmem_limit_bytes=VMEM_LIMIT),
    )(update, coeff)


def on_device(activations, cotangents, spin_bits, offdiag_energy):
    update, coeff = hand_on(
        *main_call(activations, cotangents, spin_bits, offdiag_energy.reshape(1, LOCAL))
    )
    return update, coeff.reshape(LOCAL)


def solution(mesh):
    in_specs = (
        P("samp", "par", None, None),
        P("samp", "par", None, None),
        P("samp", None),
        P("samp"),
    )
    out_specs = (P("par", "samp"), P("samp"))
    return jax.shard_map(
        on_device, mesh=mesh, in_specs=in_specs, out_specs=out_specs, check_vma=False
    )
```

```python
import math

import jax
import jax.numpy as jnp
from jax import lax
from jax.experimental import pallas as pl
from jax.experimental.pallas import tpu as pltpu
from jax.sharding import PartitionSpec as P

CH = 64
KK = 9
LAT = 24
SITES = LAT * LAT
NSAMP = 32
NPAR = 8
NZ = 8
NY = 4
LOCAL = 8
NS = NSAMP * LOCAL
ROWS = KK * CH // NSAMP
CHUNK = ROWS * LOCAL
WIDTH = ROWS * 128
PADK = 640
LAYERS = 2
ENTRIES = 16 * KK * CH * CH
MESH = pl.DeviceIdType.MESH
VMEM_LIMIT = 56 * 1024 * 1024
HIGHEST = lax.Precision.HIGHEST
VMEM = pltpu.VMEM


def rolled(value, amount):
    amount = amount % SITES
    if amount == 0:
        return value
    return jnp.concatenate([value[:, amount:], value[:, :amount]], axis=1)


def edge_mask(shape, col_step):
    column = lax.broadcasted_iota(jnp.int32, shape, 1) % LAT
    return column == (LAT - 1 if col_step > 0 else 0)


def column_shift(value, col_step, edge):
    if col_step == 0:
        return value
    return jnp.where(edge, rolled(value, col_step - LAT * col_step), rolled(value, col_step))


def wrap(value, size):
    return lax.select(value >= size, value - size, value)


STEPS = [(down, hop) for down in range(NY) for hop in (1, 7, 2, 6, 3, 5, 4, 0) if (down, hop) != (0, 0)]


def diagonal_energy(spin_bits):
    spin = (2 * spin_bits - 1).astype(jnp.float32)
    right = column_shift(spin, 1, edge_mask(spin.shape, 1))
    left = column_shift(spin, -1, edge_mask(spin.shape, -1))
    pairs = spin * rolled(spin, LAT) + spin * right
    corners = spin * rolled(right, LAT) + spin * rolled(left, LAT)
    diag = 0.25 * jnp.sum(pairs + 0.5 * corners, axis=1, keepdims=True)
    wide = jnp.broadcast_to(diag, (LOCAL, 128))
    here = lax.broadcasted_iota(jnp.int32, (LOCAL, 128), 0) == lax.broadcasted_iota(
        jnp.int32, (LOCAL, 128), 1
    )
    return jnp.sum(jnp.where(here, wide, 0.0), axis=0, keepdims=True)


PLANE = sorted(
    ((down, across) for down in range(NY) for across in range(4) if (down, across) != (0, 0)),
    key=lambda step: -(min(step[0], NY - step[0]) + min(step[1], 4 - step[1])),
)
PAIRS = 3 * CH // 2
HALF = CHUNK // 2
HEAD = 64
TAIL = 128
SLOTS = 2
CHIPS = 16


BLOCK = 64
PANEL = 8


def forward_block(diag, tile_ref, column_ref, cross_ref):
    eye = lax.broadcasted_iota(jnp.int32, (BLOCK, BLOCK), 0) == lax.broadcasted_iota(
        jnp.int32, (BLOCK, BLOCK), 1
    )
    wide = jnp.concatenate([diag, jnp.where(eye, 1.0, 0.0)], axis=1)
    count = BLOCK // PANEL
    tiles = [wide[8 * q : 8 * q + 8] for q in range(count)]
    sub = lax.broadcasted_iota(jnp.int32, (8, 128), 0)

    def lanes(tile, col):
        return jnp.broadcast_to(tile[:, col : col + 1], (8, 128))

    def joined(parts):
        total = parts[0]
        for i in range(1, PANEL):
            total = jnp.where(sub == i, parts[i], total)
        return total

    def broadcast_row(ref, panel, j, i):
        return ref[panel, j, pl.ds(i, 8, stride=0), :]

    reduced, scaled = [], []
    columns = [lanes(tiles[0], j) for j in range(PANEL)]
    for panel in range(count):
        base = panel * PANEL
        last = panel == count - 1
        tile_ref[panel, 0] = tiles[panel]
        low = {
            (i, j): jnp.broadcast_to(columns[j][i : i + 1], (8, 128))
            for i in range(PANEL)
            for j in range(i + 1)
        }
        rows = [broadcast_row(tile_ref, panel, 0, i) for i in range(PANEL)]
        old_columns = {
            q: [lanes(tiles[q], base + i) for i in range(PANEL)] for q in range(panel + 1, count)
        }
        if not last:
            cross = list(old_columns[panel + 1])
            columns = [lanes(tiles[panel + 1], base + PANEL + j) for j in range(PANEL)]
        ups, downs, starts, cross_scaled = {}, {}, {}, {}
        for p in range(0, PANEL, 2):
            q = p + 1
            a, b, c = low[p, p], low[q, p], low[q, q]
            recip = pl.reciprocal(a * c - b * b, approx=True)
            for i in range(q + 1, PANEL):
                up = c * low[i, p] - b * low[i, q]
                down = a * low[i, q] - b * low[i, p]
                ups[i, p], downs[i, p] = up * recip, down * recip
                for m in range(q + 1, i + 1):
                    if i <= q + 2:
                        step = (up * low[m, p] + down * low[m, q]) * recip
                    else:
                        step = ups[i, p] * low[m, p] + downs[i, p] * low[m, q]
                    low[i, m] = low[i, m] - step
            if not last:
                cross_scaled[p] = (c * cross[p] - b * cross[q]) * recip
                cross_scaled[q] = (a * cross[q] - b * cross[p]) * recip
                for i in range(q + 1, PANEL):
                    cross[i] = cross[i] - (ups[i, p] * cross[p] + downs[i, p] * cross[q])
            starts[p] = (c * rows[p] - b * rows[q]) * recip
            starts[q] = (a * rows[q] - b * rows[p]) * recip
            for i in range(q + 1, PANEL):
                rows[i] = rows[i] - (ups[i, p] * rows[p] + downs[i, p] * rows[q])
        if not last:
            for i in range(PANEL):
                cross_ref[panel, i] = cross[i]
            for j in range(PANEL):
                terms = [
                    cross_scaled[i] * broadcast_row(cross_ref, panel, i, j) for i in range(PANEL)
                ]
                while len(terms) > 1:
                    terms = [terms[a] + terms[a + 1] for a in range(0, len(terms), 2)]
                columns[j] = columns[j] - terms[0]
        reduced.append(joined(rows))
        scaled.append(joined([starts[i] for i in range(PANEL)]))
        if last:
            break
        solved = [None] * PANEL
        for p in reversed(range(0, PANEL, 2)):
            for total, factor, at in ((starts[p], ups, p), (starts[p + 1], downs, p + 1)):
                for i in reversed(range(p + 2, PANEL)):
                    total = total - factor[i, p] * solved[i]
                solved[at] = total
        for q in range(panel + 1, count):
            terms = [old_columns[q][i] * solved[i] for i in range(PANEL)]
            while len(terms) > 1:
                terms = [terms[a] + terms[a + 1] for a in range(0, len(terms), 2)]
            tiles[q] = tiles[q] - terms[0]
    lower = jnp.concatenate(reduced, axis=0)[:, BLOCK:]
    return lower, jnp.concatenate(scaled, axis=0)[:, BLOCK:]


def product(one, two, first_dim, second_dim):
    return lax.dot_general(
        one, two, (((first_dim,), (second_dim,)), ((), ())),
        precision=HIGHEST, preferred_element_type=jnp.float32,
    )


def main_kernel(
    act_hbm, cot_hbm, spin_ref, off_ref,
    update_ref, coeff_ref,
    act_ref, cot_ref, edges, lhs, rhs, stage, wide_rows, send_ref, recv_ref, cent_ref,
    energy_ref, energies_ref, part_ref, first, mine, second, gram_ref,
    work, held, tile_ref, column_ref, cross_ref,
    act_sem, cot_sem, send_sem, recv_sem, esem, sem1, sem2, sem3,
):
    samp = lax.axis_index("samp")
    par = lax.axis_index("par")
    z, y = samp // NY, samp % NY
    x, core = par // 2, par % 2
    slot_here = y * NZ + z
    sibling = (samp, x * 2 + 1 - core)
    zs = [wrap(z + hop, NZ) for hop in range(NZ)]
    ys = [wrap(y + down, NY) for down in range(NY)]
    xs = [wrap(x + across, 4) for across in range(4)]
    partners = [(down, zs[hop] * NY + ys[down]) for down, hop in STEPS]
    sorted_partners = [
        item for item, (_, hop) in sorted(zip(partners, STEPS), key=lambda pair: -min(pair[1][1], NZ - pair[1][1]))
    ]
    chip = y * 4 + x
    others = [
        (ys[down] * 4 + xs[across], z * NY + ys[down], xs[across] * 2)
        for down, across in PLANE
    ]
    around = [(other, (row, pair + side), side) for other, row, pair in others for side in range(2)]

    def by_core(body):
        @pl.when(core == 0)
        def _():
            body(0, 128)

        @pl.when(core == 1)
        def _():
            body(1, NS)

    def fetches(group, layer):
        samples = pl.ds(group * SLOTS, SLOTS) if layer == 0 else pl.ds(0, LOCAL)
        return [
            pltpu.make_async_copy(
                hbm.at[samples, layer], local.at[samples, layer], sems.at[group]
            )
            for hbm, local, sems in ((act_hbm, act_ref, act_sem), (cot_hbm, cot_ref, cot_sem))
        ]

    groups = LOCAL // SLOTS
    for group in range(groups):
        for fetch in fetches(group, 0):
            fetch.start()

    def remote(source, target, send, recv, device):
        return pltpu.make_async_remote_copy(
            src_ref=source,
            dst_ref=target,
            send_sem=send,
            recv_sem=recv,
            device_id=device,
            device_id_type=MESH,
        )

    barrier = pltpu.get_barrier_semaphore()
    greeted = 0
    for _, other in partners:
        pl.semaphore_signal(barrier, inc=1, device_id=(other, par), device_id_type=MESH)
        greeted += 1
    for down in range(NY):
        for across in range(4):
            for side in (core, 1 - core):
                if across > 0 or side is not core:
                    device = (z * NY + ys[down], xs[across] * 2 + side)
                    pl.semaphore_signal(barrier, inc=1, device_id=device, device_id_type=MESH)
                    greeted += 1

    left = lax.broadcasted_iota(jnp.int32, (PAIRS, 128), 1) < CH
    lhs[:, :, PADK - 128 :] = jnp.zeros((SLOTS, 3 * CH, 128), jnp.bfloat16)
    rhs[:, :, PADK - 128 :] = jnp.zeros((SLOTS, 3 * CH, 128), jnp.bfloat16)
    stage[:, 1] = jnp.zeros((SLOTS, 3 * CH, 128), jnp.float32)
    for at, step in enumerate((-1, 1)):
        strip = jnp.where(edge_mask((8, SITES), step), 1.0, 0.0)
        edges[at] = jnp.concatenate([strip] * (CH // 8), axis=0).astype(jnp.bfloat16)

    def compute(sample, layer, slot):
        act = act_ref[sample, layer]
        cot = cot_ref[sample, layer]
        for step in (-1, 0, 1):
            low = (step + 1) * CH
            edge = edges[max(step, 0)] > 0
            lhs[slot, low : low + CH, :SITES] = column_shift(act, step, edge)
            rhs[slot, low : low + CH, :SITES] = rolled(cot, -LAT * step)
        out = lax.dot_general(
            lhs[slot], rhs[slot], (((1,), (1,)), ((), ())), preferred_element_type=jnp.float32
        )
        stage[slot, 0] = out[:, :128]
        stage[slot, 1, :, :CH] = out[:, 128:]
        even, odd, even_last, odd_last = [
            stage[slot, part, pl.ds(parity, PAIRS, stride=2), :]
            for part in (0, 1)
            for parity in (0, 1)
        ]
        blocks = (
            jnp.where(left, even, pltpu.roll(odd, CH, 1)),
            jnp.where(left, pltpu.roll(even, CH, 1), odd),
            jnp.where(left, even_last, pltpu.roll(odd_last, CH, 1)),
        )
        for down in range(3):
            wide_rows[layer, pl.ds(down * PAIRS * LOCAL + sample, PAIRS, stride=LOCAL), :] = blocks[down]

    def products(layer):
        def body(group, carry):
            if layer == 0:
                for fetch in fetches(group, 0):
                    fetch.wait()
            for slot in range(SLOTS):
                compute(group * SLOTS + slot, layer, slot)
            return carry

        lax.fori_loop(0, groups, body, 0)

    def rounded(other, layer, low, rows):
        start = pl.multiple_of(other * HALF + low, 8)
        return wide_rows[layer, pl.ds(start, rows), :]

    def send_wave(wave, low, rows):
        for down, other in sorted_partners:
            if wave == 0:
                block = rounded(other, 0, 0, HEAD)
            elif wave == 1:
                block = jnp.concatenate(
                    [rounded(other, 0, HEAD, HALF - HEAD), rounded(other, 1, 0, TAIL - HALF)], axis=0
                )
            else:
                block = rounded(other, 1, TAIL - HALF, CHUNK - TAIL)
            send_ref[other, low : low + rows] = block.astype(jnp.bfloat16)
            remote(
                send_ref.at[other, pl.ds(low, rows)],
                recv_ref.at[slot_here, pl.ds(low, rows)],
                send_sem,
                recv_sem.at[wave, down],
                (other, par),
            ).start()

    products(0)
    pl.semaphore_wait(barrier, greeted)
    send_wave(0, 0, HEAD)
    for fetch in fetches(groups, 1):
        fetch.start()
    for fetch in fetches(groups, 1):
        fetch.wait()
    products(1)
    send_wave(1, HEAD, TAIL - HEAD)
    send_wave(2, TAIL, CHUNK - TAIL)

    flat = diagonal_energy(spin_ref[...])
    energy_ref[...] = jnp.zeros_like(energy_ref)
    energy_ref[:, :LOCAL] = flat[:, :LOCAL] + off_ref[...]
    for _, other in partners:
        remote(energy_ref, energies_ref.at[samp], esem.at[0], esem.at[1], (other, par)).start()
    energies_ref[samp] = energy_ref[...]
    recv_ref[slot_here] = jnp.concatenate(
        [rounded(samp, layer, 0, HALF) for layer in range(LAYERS)], axis=0
    ).astype(jnp.bfloat16)
    def await_wave(wave, low, rows):
        for down in range(NY):
            at = wrap(y + NY - down, NY) * NZ
            slots = pl.ds(0, NZ - 1) if down == 0 else pl.ds(at, NZ)
            landed = recv_ref.at[slots, pl.ds(low, rows)]
            remote(landed, landed, send_sem, recv_sem.at[wave, down], sibling).wait_recv()

    def heavy_part(pair):
        columns = pl.ds(256 * pair, 256)
        heavy = lax.dot_general(
            cent_ref[128:, columns], cent_ref[:, columns], (((1,), (1,)), ((), ())),
            preferred_element_type=jnp.float32,
        )
        part_ref[128:, :] = heavy if pair == 0 else part_ref[128:, :] + heavy

    squares = jnp.zeros((8, 256), jnp.float32)
    await_wave(0, 0, HEAD)
    for pair in range(ROWS // 2):
        if pair == HEAD // 16:
            await_wave(1, HEAD, TAIL - HEAD)
        if pair == TAIL // 16:
            await_wave(2, TAIL, CHUNK - TAIL)
        tile = jnp.stack(
            [
                recv_ref[(src % NY) * NZ + src // NY, 16 * pair : 16 * pair + 16, :].astype(jnp.float32)
                for src in range(NSAMP)
            ]
        ).reshape(NSAMP, 2, LOCAL, 128)
        halves = []
        for half in range(2):
            part = tile[:, half]
            mean = jnp.sum(jnp.sum(part, axis=0), axis=0, keepdims=True) / NS
            cent = ((part - mean) / math.sqrt(NS)).reshape(NS, 128)
            halves.append(cent.astype(jnp.bfloat16))
        cent = jnp.concatenate(halves, axis=1)
        cent_ref[:, 256 * pair : 256 * pair + 256] = cent
        light = lax.dot_general(
            cent[:128], cent[:128], (((1,), (1,)), ((), ())), preferred_element_type=jnp.float32
        )
        part_ref[:128, :128] = light if pair == 0 else part_ref[:128, :128] + light
        wide = cent[128:].astype(jnp.float32)
        squares = squares + jnp.sum((wide * wide).reshape(16, 8, 256), axis=0)
        if pair < TAIL // 16:
            heavy_part(pair)

    eye = lax.broadcasted_iota(jnp.int32, (128, 128), 0) == lax.broadcasted_iota(
        jnp.int32, (128, 128), 1
    )
    trace = jnp.sum(jnp.where(eye, part_ref[:128, :128], 0.0), keepdims=True) + jnp.sum(
        squares, keepdims=True
    )
    corner = jnp.logical_and(
        lax.broadcasted_iota(jnp.int32, (8, 128), 0) == 0,
        lax.broadcasted_iota(jnp.int32, (8, 128), 1) == 127,
    )
    part_ref[:8, :128] = jnp.where(corner, trace, part_ref[:8, :128])

    def rows_of(side, index):
        return pl.ds(pl.multiple_of(side * 128 + index * 8, 8), 8)

    slot = core * CHIPS + chip
    widths = (128, NS)

    def send_first(other, device, side):
        wide = pl.ds(0, widths[side])
        remote(
            part_ref.at[rows_of(side, other), wide],
            first.at[slot, :, wide],
            sem1.at[side],
            sem1.at[2],
            device,
        ).start()

    by_core(lambda side, width: send_first(chip, sibling, 0) if side == 1 else None)
    for kind in range(2):
        if kind == 1:
            for pair in range(TAIL // 16, ROWS // 2):
                heavy_part(pair)
        for other, device, side in around:
            if side == kind:
                send_first(other, device, side)
    by_core(lambda side, width: send_first(chip, sibling, 1) if side == 0 else None)

    def middle(side, width):
        wide = pl.ds(0, width)
        first[slot, :, wide] = part_ref[rows_of(side, chip), wide]
        landed = first.at[pl.ds(0, 2 * CHIPS - 1), :, wide]
        remote(landed, landed, sem1.at[0], sem1.at[2], sibling).wait_recv()
        own = jnp.sum(first[:, :, wide], axis=0)
        mine[:, wide] = own
        for hop in (4, 3, 5, 2, 6, 1, 7):
            device = (zs[hop] * NY + y, par)
            remote(
                mine.at[:, wide], second.at[z, :, wide], sem2.at[0], sem2.at[1], device
            ).start()
        second[z, :, wide] = own
        landed = second.at[pl.ds(0, NZ - 1), :, wide]
        remote(landed, landed, sem2.at[0], sem2.at[1], sibling).wait_recv()
        block = rows_of(side, chip)
        gram_ref[block, wide] = jnp.sum(second[:, :, wide], axis=0)
        done = gram_ref.at[block, wide]
        for _, device, _ in around:
            remote(done, done, sem3.at[0], sem3.at[1 + side], device).start()
        remote(done, done, sem3.at[0], sem3.at[1 + side], sibling).start()

    by_core(middle)

    def await_rows(kind):
        def body(side, width):
            count = CHIPS - 1 if side == kind else CHIPS
            landed = gram_ref.at[pl.ds(0, count * 8), pl.ds(0, widths[kind])]
            remote(landed, landed, sem3.at[0], sem3.at[1 + kind], sibling).wait_recv()

        by_core(body)

    energy_bytes = energies_ref.at[pl.ds(0, NSAMP - 1)]
    remote(energy_bytes, energy_bytes, esem.at[0], esem.at[1], sibling).wait()
    pieces = jnp.broadcast_to(energies_ref[...], (NSAMP, LOCAL, 128)).reshape(NS, 128)
    lane = lax.broadcasted_iota(jnp.int32, (NS, 128), 1)
    row = lax.broadcasted_iota(jnp.int32, (NSAMP, LOCAL, 128), 1).reshape(NS, 128)
    energy = jnp.sum(jnp.where(lane == row, pieces, 0.0), axis=1, keepdims=True)
    mean = jnp.sum(energy, axis=0, keepdims=True) / NS
    residual = -(energy - mean) / math.sqrt(NS)
    work[:, NS:] = jnp.broadcast_to(residual, (NS, 128))

    await_rows(0)
    level = 1.0 / (gram_ref[0:1, 127:128] / NS)
    wide_corner = jnp.logical_and(
        lax.broadcasted_iota(jnp.int32, (128, 128), 0) == 0,
        lax.broadcasted_iota(jnp.int32, (128, 128), 1) == 127,
    )
    light = jnp.where(wide_corner, gram_ref[127:128, 0:1], gram_ref[:128, :128])
    ridge = jnp.where(eye, 0.01, 0.0)
    work[:128, :128] = light * level + ridge
    one, two = slice(0, BLOCK), slice(BLOCK, 2 * BLOCK)
    lower_one, scaled_one = forward_block(work[one, one], tile_ref, column_ref, cross_ref)
    left = product(work[two, one], lower_one, 1, 1)
    right = product(scaled_one, work[one, two], 1, 0)
    lower_two, scaled_two = forward_block(
        work[two, two] - product(left, right, 1, 0), tile_ref, column_ref, cross_ref
    )
    cross_part = product(left, scaled_one, 1, 0)
    blank = jnp.zeros((BLOCK, BLOCK), jnp.float32)

    def joined_factor(first_part, second_part):
        return jnp.concatenate(
            [
                jnp.concatenate([first_part, blank], axis=1),
                jnp.concatenate([-product(second_part, cross_part, 1, 0), second_part], axis=1),
            ],
            axis=0,
        )

    lower = joined_factor(lower_one, lower_two)
    scaled = joined_factor(scaled_one, scaled_two)

    await_rows(1)
    below = gram_ref[128:, :128]
    corner_block = gram_ref[128:, 128:]
    scaled_below = below * level
    above = scaled_below.T
    last = corner_block * level + ridge
    near_middle = product(scaled, above[:, :BLOCK], 1, 0)
    near_outer = product(scaled_below[:BLOCK], lower, 1, 1)
    lower_three, scaled_three = forward_block(
        last[:BLOCK, :BLOCK] - product(near_outer, near_middle, 1, 0), tile_ref, column_ref, cross_ref
    )
    work[:128, 128:NS] = above
    work[128:, 128:NS] = last
    middle_rows = product(scaled, work[:128, 128:], 1, 0)
    outer = product(scaled_below, lower, 1, 1)
    work[128:, 128:] = work[128:, 128:] - product(outer, middle_rows, 1, 0)
    work[:128, 128:] = product(lower, middle_rows, 0, 0)

    three, four = slice(128, 128 + BLOCK), slice(128 + BLOCK, NS)
    near_middle = product(scaled_three, work[three, four], 1, 0)
    near_outer = product(work[four, three], lower_three, 1, 1)
    lower_four, scaled_four = forward_block(
        work[four, four] - product(near_outer, near_middle, 1, 0), tile_ref, column_ref, cross_ref
    )
    middle_rows = product(scaled_three, work[three, 128:], 1, 0)
    outer = product(work[:, three], lower_three, 1, 1)
    work[:, 128:] = work[:, 128:] - product(outer, middle_rows, 1, 0)
    work[three, 128:] = product(lower_three, middle_rows, 0, 0)

    middle_rows = product(scaled_four, work[four, NS:], 1, 0)
    outer = product(work[:, four], lower_four, 1, 1)
    work[:, NS:] = work[:, NS:] - product(outer, middle_rows, 1, 0)
    work[four, NS:] = product(lower_four, middle_rows, 0, 0)

    coeff = work[:, NS:] * level
    held[...] = coeff
    own = held[pl.ds(pl.multiple_of(samp * LOCAL, LOCAL), LOCAL), :]
    here = lax.broadcasted_iota(jnp.int32, (LOCAL, 128), 0) == lax.broadcasted_iota(
        jnp.int32, (LOCAL, 128), 1
    )
    coeff_ref[...] = jnp.sum(jnp.where(here, own, 0.0), axis=0, keepdims=True)[:, :LOCAL]
    upper, under = coeff[:128], coeff[128:]
    weighted = jnp.sum(light * upper + 2.0 * (below * under), axis=0, keepdims=True) * jnp.sum(
        jnp.where(eye, upper, 0.0), axis=0, keepdims=True
    ) + jnp.sum(corner_block * under, axis=0, keepdims=True) * jnp.sum(
        jnp.where(eye, under, 0.0), axis=0, keepdims=True
    )
    square_total = jnp.sum(weighted, keepdims=True)
    scale = lax.rsqrt(square_total / ENTRIES + 1e-06)
    for index in range(ROWS):
        cent = cent_ref[:, 128 * index : 128 * index + 128].astype(jnp.float32)
        layer, column = index // (ROWS // 2), 128 * (index % (ROWS // 2))
        update_ref[layer : layer + 1, column : column + 128] = (
            jnp.sum(cent * coeff, axis=0, keepdims=True) * scale
        )

    sent = send_ref.at[pl.ds(0, NSAMP - 1)]
    remote(sent, sent, send_sem, recv_sem.at[0, 0], sibling).wait_send()

    def finish(side, width):
        wide = pl.ds(0, width)
        for kind in range(2):
            count = CHIPS - 1 if kind == side else CHIPS
            bytes_ref = gram_ref.at[pl.ds(0, count * 8), pl.ds(0, widths[kind])]
            remote(bytes_ref, bytes_ref, sem1.at[kind], sem1.at[2], sibling).wait_send()
        landed = second.at[pl.ds(0, NZ - 1), :, wide]
        remote(landed, landed, sem2.at[0], sem2.at[1], sibling).wait_send()
        landed = first.at[pl.ds(0, 2 * CHIPS - 1), :, wide]
        remote(landed, landed, sem3.at[0], sem1.at[2], sibling).wait_send()

    by_core(finish)


def main_call(activations, cotangents, spin_bits, off_row):
    whole = pl.BlockSpec(memory_space=VMEM)
    anywhere = pl.BlockSpec(memory_space=pl.ANY)
    dma = pltpu.SemaphoreType.DMA
    return pl.pallas_call(
        main_kernel,
        in_specs=[anywhere, anywhere, whole, whole],
        out_specs=[whole, whole],
        out_shape=[
            jax.ShapeDtypeStruct((LAYERS, ROWS * CH), jnp.float32),
            jax.ShapeDtypeStruct((1, LOCAL), jnp.float32),
        ],
        scratch_shapes=[
            VMEM((LOCAL, LAYERS, CH, SITES), jnp.bfloat16),
            VMEM((LOCAL, LAYERS, CH, SITES), jnp.bfloat16),
            VMEM((2, CH, SITES), jnp.bfloat16),
            VMEM((SLOTS, 3 * CH, PADK), jnp.bfloat16),
            VMEM((SLOTS, 3 * CH, PADK), jnp.bfloat16),
            VMEM((SLOTS, 2, 3 * CH, 128), jnp.float32),
            VMEM((LAYERS, NSAMP * HALF, 128), jnp.float32),
            VMEM((NSAMP, CHUNK, 128), jnp.bfloat16),
            VMEM((NSAMP, CHUNK, 128), jnp.bfloat16),
            VMEM((NS, WIDTH), jnp.bfloat16),
            VMEM((1, 128), jnp.float32),
            VMEM((NSAMP, 1, 128), jnp.float32),
            VMEM((NS, NS), jnp.float32),
            VMEM((2 * CHIPS, 8, NS), jnp.float32),
            VMEM((8, NS), jnp.float32),
            VMEM((NZ, 8, NS), jnp.float32),
            VMEM((NS, NS), jnp.float32),
            VMEM((NS, NS + 128), jnp.float32),
            VMEM((NS, 128), jnp.float32),
            VMEM((BLOCK // PANEL, 1, 8, 128), jnp.float32),
            VMEM((BLOCK // PANEL, PANEL, 8, 128), jnp.float32),
            VMEM((BLOCK // PANEL, PANEL, 8, 128), jnp.float32),
            dma((LOCAL // SLOTS + 1,)),
            dma((LOCAL // SLOTS + 1,)),
            dma,
            dma((3, NY)),
            dma((2,)),
            dma((3,)),
            dma((2,)),
            dma((3,)),
        ],
        compiler_params=pltpu.CompilerParams(
            collective_id=0, has_side_effects=True, vmem_limit_bytes=VMEM_LIMIT
        ),
    )(activations, cotangents, spin_bits, off_row)


def hand_on_kernel(update_in, coeff_in, update_ref, coeff_ref, sems):
    copies = [
        pltpu.make_async_copy(update_in, update_ref, sems.at[0]),
        pltpu.make_async_copy(coeff_in, coeff_ref, sems.at[1]),
    ]
    for copy in copies:
        copy.start()
    for copy in copies:
        copy.wait()


def hand_on(update, coeff):
    anywhere = pl.BlockSpec(memory_space=pl.ANY)
    return pl.pallas_call(
        hand_on_kernel,
        in_specs=[anywhere, anywhere],
        out_specs=[anywhere, anywhere],
        out_shape=[
            jax.ShapeDtypeStruct((LAYERS, ROWS * CH), jnp.float32),
            jax.ShapeDtypeStruct((1, LOCAL), jnp.float32),
        ],
        scratch_shapes=[pltpu.SemaphoreType.DMA((2,))],
        compiler_params=pltpu.CompilerParams(vmem_limit_bytes=VMEM_LIMIT),
    )(update, coeff)


def on_device(activations, cotangents, spin_bits, offdiag_energy):
    update, coeff = hand_on(
        *main_call(activations, cotangents, spin_bits, offdiag_energy.reshape(1, LOCAL))
    )
    return update, coeff.reshape(LOCAL)


def solution(mesh):
    in_specs = (
        P("samp", "par", None, None),
        P("samp", "par", None, None),
        P("samp", None),
        P("samp"),
    )
    out_specs = (P("par", "samp"), P("samp"))
    return jax.shard_map(
        on_device, mesh=mesh, in_specs=in_specs, out_specs=out_specs, check_vma=False
    )
```

```python
import math

import jax
import jax.numpy as jnp
from jax import lax
from jax.experimental import pallas as pl
from jax.experimental.pallas import tpu as pltpu
from jax.sharding import PartitionSpec as P

CH = 64
KK = 9
LAT = 24
SITES = LAT * LAT
NSAMP = 32
NPAR = 8
NZ = 8
NY = 4
LOCAL = 8
NS = NSAMP * LOCAL
ROWS = KK * CH // NSAMP
CHUNK = ROWS * LOCAL
WIDTH = ROWS * 128
PADK = 640
LAYERS = 2
ENTRIES = 16 * KK * CH * CH
MESH = pl.DeviceIdType.MESH
VMEM_LIMIT = 56 * 1024 * 1024
HIGHEST = lax.Precision.HIGHEST
VMEM = pltpu.VMEM


def rolled(value, amount):
    amount = amount % SITES
    if amount == 0:
        return value
    return jnp.concatenate([value[:, amount:], value[:, :amount]], axis=1)


def edge_mask(shape, col_step):
    column = lax.broadcasted_iota(jnp.int32, shape, 1) % LAT
    return column == (LAT - 1 if col_step > 0 else 0)


def column_shift(value, col_step, edge):
    if col_step == 0:
        return value
    return jnp.where(edge, rolled(value, col_step - LAT * col_step), rolled(value, col_step))


def wrap(value, size):
    return lax.select(value >= size, value - size, value)


STEPS = [(down, hop) for down in range(NY) for hop in (1, 7, 2, 6, 3, 5, 4, 0) if (down, hop) != (0, 0)]


def diagonal_energy(spin_bits):
    spin = (2 * spin_bits - 1).astype(jnp.float32)
    right = column_shift(spin, 1, edge_mask(spin.shape, 1))
    left = column_shift(spin, -1, edge_mask(spin.shape, -1))
    pairs = spin * rolled(spin, LAT) + spin * right
    corners = spin * rolled(right, LAT) + spin * rolled(left, LAT)
    diag = 0.25 * jnp.sum(pairs + 0.5 * corners, axis=1, keepdims=True)
    wide = jnp.broadcast_to(diag, (LOCAL, 128))
    here = lax.broadcasted_iota(jnp.int32, (LOCAL, 128), 0) == lax.broadcasted_iota(
        jnp.int32, (LOCAL, 128), 1
    )
    return jnp.sum(jnp.where(here, wide, 0.0), axis=0, keepdims=True)


PLANE = sorted(
    ((down, across) for down in range(NY) for across in range(4) if (down, across) != (0, 0)),
    key=lambda step: -(min(step[0], NY - step[0]) + min(step[1], 4 - step[1])),
)
PAIRS = 3 * CH // 2
HALF = CHUNK // 2
HEAD = 64
TAIL = 128
SLOTS = 4
PAIR = 2
CHIPS = 16


BLOCK = 64
PANEL = 8


def forward_block(diag, tile_ref, column_ref, cross_ref):
    eye = lax.broadcasted_iota(jnp.int32, (BLOCK, BLOCK), 0) == lax.broadcasted_iota(
        jnp.int32, (BLOCK, BLOCK), 1
    )
    wide = jnp.concatenate([diag, jnp.where(eye, 1.0, 0.0)], axis=1)
    count = BLOCK // PANEL
    tiles = [wide[8 * q : 8 * q + 8] for q in range(count)]
    sub = lax.broadcasted_iota(jnp.int32, (8, 128), 0)

    def lanes(tile, col):
        return jnp.broadcast_to(tile[:, col : col + 1], (8, 128))

    def joined(parts):
        total = parts[0]
        for i in range(1, PANEL):
            total = jnp.where(sub == i, parts[i], total)
        return total

    def broadcast_row(ref, panel, j, i):
        return ref[panel, j, pl.ds(i, 8, stride=0), :]

    reduced, scaled = [], []
    columns = [lanes(tiles[0], j) for j in range(PANEL)]
    for panel in range(count):
        base = panel * PANEL
        last = panel == count - 1
        tile_ref[panel, 0] = tiles[panel]
        for j in range(PANEL):
            column_ref[panel, j] = columns[j]
        low = {
            (i, j): broadcast_row(column_ref, panel, j, i)
            for i in range(PANEL)
            for j in range(i + 1)
        }
        rows = [broadcast_row(tile_ref, panel, 0, i) for i in range(PANEL)]
        old_columns = {
            q: [lanes(tiles[q], base + i) for i in range(PANEL)] for q in range(panel + 1, count)
        }
        if not last:
            cross = list(old_columns[panel + 1])
            columns = [lanes(tiles[panel + 1], base + PANEL + j) for j in range(PANEL)]
        ups, downs, starts, cross_scaled = {}, {}, {}, {}
        for p in range(0, PANEL, 2):
            q = p + 1
            a, b, c = low[p, p], low[q, p], low[q, q]
            recip = pl.reciprocal(a * c - b * b, approx=True)
            for i in range(q + 1, PANEL):
                up = c * low[i, p] - b * low[i, q]
                down = a * low[i, q] - b * low[i, p]
                ups[i, p], downs[i, p] = up * recip, down * recip
                for m in range(q + 1, i + 1):
                    if i <= q + 2:
                        step = (up * low[m, p] + down * low[m, q]) * recip
                    else:
                        step = ups[i, p] * low[m, p] + downs[i, p] * low[m, q]
                    low[i, m] = low[i, m] - step
            if not last:
                cross_scaled[p] = (c * cross[p] - b * cross[q]) * recip
                cross_scaled[q] = (a * cross[q] - b * cross[p]) * recip
                for i in range(q + 1, PANEL):
                    cross[i] = cross[i] - (ups[i, p] * cross[p] + downs[i, p] * cross[q])
            starts[p] = (c * rows[p] - b * rows[q]) * recip
            starts[q] = (a * rows[q] - b * rows[p]) * recip
            for i in range(q + 1, PANEL):
                rows[i] = rows[i] - (ups[i, p] * rows[p] + downs[i, p] * rows[q])
        if not last:
            for i in range(PANEL):
                cross_ref[panel, i] = cross[i]
            for j in range(PANEL):
                terms = [
                    cross_scaled[i] * broadcast_row(cross_ref, panel, i, j) for i in range(PANEL)
                ]
                while len(terms) > 1:
                    terms = [terms[a] + terms[a + 1] for a in range(0, len(terms), 2)]
                columns[j] = columns[j] - terms[0]
        reduced.append(joined(rows))
        scaled.append(joined([starts[i] for i in range(PANEL)]))
        if last:
            break
        solved = [None] * PANEL
        for p in reversed(range(0, PANEL, 2)):
            for total, factor, at in ((starts[p], ups, p), (starts[p + 1], downs, p + 1)):
                for i in reversed(range(p + 2, PANEL)):
                    total = total - factor[i, p] * solved[i]
                solved[at] = total
        for q in range(panel + 1, count):
            terms = [old_columns[q][i] * solved[i] for i in range(PANEL)]
            while len(terms) > 1:
                terms = [terms[a] + terms[a + 1] for a in range(0, len(terms), 2)]
            tiles[q] = tiles[q] - terms[0]
    lower = jnp.concatenate(reduced, axis=0)[:, BLOCK:]
    return lower, jnp.concatenate(scaled, axis=0)[:, BLOCK:]


def product(one, two, first_dim, second_dim):
    return lax.dot_general(
        one, two, (((first_dim,), (second_dim,)), ((), ())),
        precision=HIGHEST, preferred_element_type=jnp.float32,
    )


def main_kernel(
    act_hbm, cot_hbm, spin_ref, off_ref,
    update_ref, coeff_ref,
    act_ref, cot_ref, edges, lhs, rhs, stage, wide_rows, send_ref, recv_ref, cent_ref,
    energy_ref, energies_ref, part_ref, first, mine, second, gram_ref,
    work, held, tile_ref, column_ref, cross_ref,
    act_sem, cot_sem, send_sem, recv_sem, esem, sem1, sem2, sem3,
):
    samp = lax.axis_index("samp")
    par = lax.axis_index("par")
    z, y = samp // NY, samp % NY
    x, core = par // 2, par % 2
    slot_here = y * NZ + z
    sibling = (samp, x * 2 + 1 - core)
    zs = [wrap(z + hop, NZ) for hop in range(NZ)]
    ys = [wrap(y + down, NY) for down in range(NY)]
    xs = [wrap(x + across, 4) for across in range(4)]
    partners = [(down, zs[hop] * NY + ys[down]) for down, hop in STEPS]
    sorted_partners = [
        item for item, (_, hop) in sorted(zip(partners, STEPS), key=lambda pair: -min(pair[1][1], NZ - pair[1][1]))
    ]
    chip = y * 4 + x
    others = [
        (ys[down] * 4 + xs[across], z * NY + ys[down], xs[across] * 2)
        for down, across in PLANE
    ]
    around = [(other, (row, pair + side), side) for other, row, pair in others for side in range(2)]

    def by_core(body):
        @pl.when(core == 0)
        def _():
            body(0, 128)

        @pl.when(core == 1)
        def _():
            body(1, NS)

    def fetches(group, layer):
        samples = pl.ds(group * PAIR, PAIR) if layer == 0 else pl.ds(0, LOCAL)
        return [
            pltpu.make_async_copy(
                hbm.at[samples, layer], local.at[samples, layer], sems.at[group]
            )
            for hbm, local, sems in ((act_hbm, act_ref, act_sem), (cot_hbm, cot_ref, cot_sem))
        ]

    groups = LOCAL // PAIR
    for group in range(groups):
        for fetch in fetches(group, 0):
            fetch.start()

    def remote(source, target, send, recv, device):
        return pltpu.make_async_remote_copy(
            src_ref=source,
            dst_ref=target,
            send_sem=send,
            recv_sem=recv,
            device_id=device,
            device_id_type=MESH,
        )

    barrier = pltpu.get_barrier_semaphore()
    greeted = 0
    for _, other in partners:
        pl.semaphore_signal(barrier, inc=1, device_id=(other, par), device_id_type=MESH)
        greeted += 1
    for down in range(NY):
        for across in range(4):
            for side in (core, 1 - core):
                if across > 0 or side is not core:
                    device = (z * NY + ys[down], xs[across] * 2 + side)
                    pl.semaphore_signal(barrier, inc=1, device_id=device, device_id_type=MESH)
                    greeted += 1

    left = lax.broadcasted_iota(jnp.int32, (PAIRS, 128), 1) < CH
    lhs[:, :, PADK - 128 :] = jnp.zeros((SLOTS, 3 * CH, 128), jnp.bfloat16)
    rhs[:, :, PADK - 128 :] = jnp.zeros((SLOTS, 3 * CH, 128), jnp.bfloat16)
    stage[:, 1] = jnp.zeros((SLOTS, 3 * CH, 128), jnp.float32)
    for at, step in enumerate((-1, 1)):
        strip = jnp.where(edge_mask((8, SITES), step), 1.0, 0.0)
        edges[at] = jnp.concatenate([strip] * (CH // 8), axis=0).astype(jnp.bfloat16)

    def compute(sample, layer, slot):
        act = act_ref[sample, layer]
        cot = cot_ref[sample, layer]
        for step in (-1, 0, 1):
            low = (step + 1) * CH
            edge = edges[max(step, 0)] > 0
            lhs[slot, low : low + CH, :SITES] = column_shift(act, step, edge)
            rhs[slot, low : low + CH, :SITES] = rolled(cot, -LAT * step)
        out = lax.dot_general(
            lhs[slot], rhs[slot], (((1,), (1,)), ((), ())), preferred_element_type=jnp.float32
        )
        stage[slot, 0] = out[:, :128]
        stage[slot, 1, :, :CH] = out[:, 128:]
        even, odd, even_last, odd_last = [
            stage[slot, part, pl.ds(parity, PAIRS, stride=2), :]
            for part in (0, 1)
            for parity in (0, 1)
        ]
        blocks = (
            jnp.where(left, even, pltpu.roll(odd, CH, 1)),
            jnp.where(left, pltpu.roll(even, CH, 1), odd),
            jnp.where(left, even_last, pltpu.roll(odd_last, CH, 1)),
        )
        for down in range(3):
            wide_rows[layer, pl.ds(down * PAIRS * LOCAL + sample, PAIRS, stride=LOCAL), :] = blocks[down]

    def products(layer):
        def body(step, carry):
            for slot in range(SLOTS):
                if layer == 0 and slot % PAIR == 0:
                    for fetch in fetches(step * (SLOTS // PAIR) + slot // PAIR, 0):
                        fetch.wait()
                compute(step * SLOTS + slot, layer, slot)
            return carry

        lax.fori_loop(0, LOCAL // SLOTS, body, 0)

    def rounded(other, layer, low, rows):
        start = pl.multiple_of(other * HALF + low, 8)
        return wide_rows[layer, pl.ds(start, rows), :]

    def send_wave(wave, low, rows):
        for down, other in sorted_partners:
            if wave == 0:
                block = rounded(other, 0, 0, HEAD)
            elif wave == 1:
                block = jnp.concatenate(
                    [rounded(other, 0, HEAD, HALF - HEAD), rounded(other, 1, 0, TAIL - HALF)], axis=0
                )
            else:
                block = rounded(other, 1, TAIL - HALF, CHUNK - TAIL)
            send_ref[other, low : low + rows] = block.astype(jnp.bfloat16)
            remote(
                send_ref.at[other, pl.ds(low, rows)],
                recv_ref.at[slot_here, pl.ds(low, rows)],
                send_sem,
                recv_sem.at[wave, down],
                (other, par),
            ).start()

    products(0)
    pl.semaphore_wait(barrier, greeted)
    send_wave(0, 0, HEAD)
    for fetch in fetches(groups, 1):
        fetch.start()
    for fetch in fetches(groups, 1):
        fetch.wait()
    products(1)
    send_wave(1, HEAD, TAIL - HEAD)
    send_wave(2, TAIL, CHUNK - TAIL)

    flat = diagonal_energy(spin_ref[...])
    energy_ref[...] = jnp.zeros_like(energy_ref)
    energy_ref[:, :LOCAL] = flat[:, :LOCAL] + off_ref[...]
    for _, other in partners:
        remote(energy_ref, energies_ref.at[samp], esem.at[0], esem.at[1], (other, par)).start()
    energies_ref[samp] = energy_ref[...]
    recv_ref[slot_here] = jnp.concatenate(
        [rounded(samp, layer, 0, HALF) for layer in range(LAYERS)], axis=0
    ).astype(jnp.bfloat16)
    def await_wave(wave, low, rows):
        for down in range(NY):
            at = wrap(y + NY - down, NY) * NZ
            slots = pl.ds(0, NZ - 1) if down == 0 else pl.ds(at, NZ)
            landed = recv_ref.at[slots, pl.ds(low, rows)]
            remote(landed, landed, send_sem, recv_sem.at[wave, down], sibling).wait_recv()

    def heavy_part(pair):
        columns = pl.ds(256 * pair, 256)
        heavy = lax.dot_general(
            cent_ref[128:, columns], cent_ref[:, columns], (((1,), (1,)), ((), ())),
            preferred_element_type=jnp.float32,
        )
        part_ref[128:, :] = heavy if pair == 0 else part_ref[128:, :] + heavy

    squares = jnp.zeros((8, 256), jnp.float32)
    await_wave(0, 0, HEAD)
    for pair in range(ROWS // 2):
        if pair == HEAD // 16:
            await_wave(1, HEAD, TAIL - HEAD)
        if pair == TAIL // 16:
            await_wave(2, TAIL, CHUNK - TAIL)
        tile = jnp.stack(
            [
                recv_ref[(src % NY) * NZ + src // NY, 16 * pair : 16 * pair + 16, :].astype(jnp.float32)
                for src in range(NSAMP)
            ]
        ).reshape(NSAMP, 2, LOCAL, 128)
        halves = []
        for half in range(2):
            part = tile[:, half]
            mean = jnp.sum(jnp.sum(part, axis=0), axis=0, keepdims=True) / NS
            cent = ((part - mean) / math.sqrt(NS)).reshape(NS, 128)
            halves.append(cent.astype(jnp.bfloat16))
        cent = jnp.concatenate(halves, axis=1)
        cent_ref[:, 256 * pair : 256 * pair + 256] = cent
        light = lax.dot_general(
            cent[:128], cent[:128], (((1,), (1,)), ((), ())), preferred_element_type=jnp.float32
        )
        part_ref[:128, :128] = light if pair == 0 else part_ref[:128, :128] + light
        wide = cent[128:].astype(jnp.float32)
        squares = squares + jnp.sum((wide * wide).reshape(16, 8, 256), axis=0)
        if pair < TAIL // 16:
            heavy_part(pair)

    eye = lax.broadcasted_iota(jnp.int32, (128, 128), 0) == lax.broadcasted_iota(
        jnp.int32, (128, 128), 1
    )
    trace = jnp.sum(jnp.where(eye, part_ref[:128, :128], 0.0), keepdims=True) + jnp.sum(
        squares, keepdims=True
    )
    corner = jnp.logical_and(
        lax.broadcasted_iota(jnp.int32, (8, 128), 0) == 0,
        lax.broadcasted_iota(jnp.int32, (8, 128), 1) == 127,
    )
    part_ref[:8, :128] = jnp.where(corner, trace, part_ref[:8, :128])

    def rows_of(side, index):
        return pl.ds(pl.multiple_of(side * 128 + index * 8, 8), 8)

    slot = core * CHIPS + chip
    widths = (128, NS)

    def send_first(other, device, side):
        wide = pl.ds(0, widths[side])
        remote(
            part_ref.at[rows_of(side, other), wide],
            first.at[slot, :, wide],
            sem1.at[side],
            sem1.at[2],
            device,
        ).start()

    by_core(lambda side, width: send_first(chip, sibling, 0) if side == 1 else None)
    for kind in range(2):
        if kind == 1:
            for pair in range(TAIL // 16, ROWS // 2):
                heavy_part(pair)
        for other, device, side in around:
            if side == kind:
                send_first(other, device, side)
    by_core(lambda side, width: send_first(chip, sibling, 1) if side == 0 else None)

    def middle(side, width):
        wide = pl.ds(0, width)
        first[slot, :, wide] = part_ref[rows_of(side, chip), wide]
        landed = first.at[pl.ds(0, 2 * CHIPS - 1), :, wide]
        remote(landed, landed, sem1.at[0], sem1.at[2], sibling).wait_recv()
        own = jnp.sum(first[:, :, wide], axis=0)
        mine[:, wide] = own
        for hop in (4, 3, 5, 2, 6, 1, 7):
            device = (zs[hop] * NY + y, par)
            remote(
                mine.at[:, wide], second.at[z, :, wide], sem2.at[0], sem2.at[1], device
            ).start()
        second[z, :, wide] = own
        landed = second.at[pl.ds(0, NZ - 1), :, wide]
        remote(landed, landed, sem2.at[0], sem2.at[1], sibling).wait_recv()
        block = rows_of(side, chip)
        gram_ref[block, wide] = jnp.sum(second[:, :, wide], axis=0)
        done = gram_ref.at[block, wide]
        for _, device, _ in around:
            remote(done, done, sem3.at[0], sem3.at[1 + side], device).start()
        remote(done, done, sem3.at[0], sem3.at[1 + side], sibling).start()

    by_core(middle)

    def await_rows(kind):
        def body(side, width):
            count = CHIPS - 1 if side == kind else CHIPS
            landed = gram_ref.at[pl.ds(0, count * 8), pl.ds(0, widths[kind])]
            remote(landed, landed, sem3.at[0], sem3.at[1 + kind], sibling).wait_recv()

        by_core(body)

    energy_bytes = energies_ref.at[pl.ds(0, NSAMP - 1)]
    remote(energy_bytes, energy_bytes, esem.at[0], esem.at[1], sibling).wait()
    pieces = jnp.broadcast_to(energies_ref[...], (NSAMP, LOCAL, 128)).reshape(NS, 128)
    lane = lax.broadcasted_iota(jnp.int32, (NS, 128), 1)
    row = lax.broadcasted_iota(jnp.int32, (NSAMP, LOCAL, 128), 1).reshape(NS, 128)
    energy = jnp.sum(jnp.where(lane == row, pieces, 0.0), axis=1, keepdims=True)
    mean = jnp.sum(energy, axis=0, keepdims=True) / NS
    residual = -(energy - mean) / math.sqrt(NS)
    work[:, NS:] = jnp.broadcast_to(residual, (NS, 128))

    await_rows(0)
    level = 1.0 / (gram_ref[0:1, 127:128] / NS)
    wide_corner = jnp.logical_and(
        lax.broadcasted_iota(jnp.int32, (128, 128), 0) == 0,
        lax.broadcasted_iota(jnp.int32, (128, 128), 1) == 127,
    )
    light = jnp.where(wide_corner, gram_ref[127:128, 0:1], gram_ref[:128, :128])
    ridge = jnp.where(eye, 0.01, 0.0)
    work[:128, :128] = light * level + ridge
    one, two = slice(0, BLOCK), slice(BLOCK, 2 * BLOCK)
    lower_one, scaled_one = forward_block(work[one, one], tile_ref, column_ref, cross_ref)
    left = product(work[two, one], lower_one, 1, 1)
    right = product(scaled_one, work[one, two], 1, 0)
    lower_two, scaled_two = forward_block(
        work[two, two] - product(left, right, 1, 0), tile_ref, column_ref, cross_ref
    )
    cross_part = product(left, scaled_one, 1, 0)
    blank = jnp.zeros((BLOCK, BLOCK), jnp.float32)

    def joined_factor(first_part, second_part):
        return jnp.concatenate(
            [
                jnp.concatenate([first_part, blank], axis=1),
                jnp.concatenate([-product(second_part, cross_part, 1, 0), second_part], axis=1),
            ],
            axis=0,
        )

    lower = joined_factor(lower_one, lower_two)
    scaled = joined_factor(scaled_one, scaled_two)

    await_rows(1)
    below = gram_ref[128:, :128]
    corner_block = gram_ref[128:, 128:]
    scaled_below = below * level
    above = scaled_below.T
    last = corner_block * level + ridge
    near_middle = product(scaled, above[:, :BLOCK], 1, 0)
    near_outer = product(scaled_below[:BLOCK], lower, 1, 1)
    lower_three, scaled_three = forward_block(
        last[:BLOCK, :BLOCK] - product(near_outer, near_middle, 1, 0), tile_ref, column_ref, cross_ref
    )
    work[:128, 128:NS] = above
    work[128:, 128:NS] = last
    middle_rows = product(scaled, work[:128, 128:], 1, 0)
    outer = product(scaled_below, lower, 1, 1)
    work[128:, 128:] = work[128:, 128:] - product(outer, middle_rows, 1, 0)
    work[:128, 128:] = product(lower, middle_rows, 0, 0)

    three, four = slice(128, 128 + BLOCK), slice(128 + BLOCK, NS)
    near_middle = product(scaled_three, work[three, four], 1, 0)
    near_outer = product(work[four, three], lower_three, 1, 1)
    lower_four, scaled_four = forward_block(
        work[four, four] - product(near_outer, near_middle, 1, 0), tile_ref, column_ref, cross_ref
    )
    middle_rows = product(scaled_three, work[three, 128:], 1, 0)
    outer = product(work[:, three], lower_three, 1, 1)
    work[:, 128:] = work[:, 128:] - product(outer, middle_rows, 1, 0)
    work[three, 128:] = product(lower_three, middle_rows, 0, 0)

    middle_rows = product(scaled_four, work[four, NS:], 1, 0)
    outer = product(work[:, four], lower_four, 1, 1)
    work[:, NS:] = work[:, NS:] - product(outer, middle_rows, 1, 0)
    work[four, NS:] = product(lower_four, middle_rows, 0, 0)

    coeff = work[:, NS:] * level
    held[...] = coeff
    own = held[pl.ds(pl.multiple_of(samp * LOCAL, LOCAL), LOCAL), :]
    here = lax.broadcasted_iota(jnp.int32, (LOCAL, 128), 0) == lax.broadcasted_iota(
        jnp.int32, (LOCAL, 128), 1
    )
    coeff_ref[...] = jnp.sum(jnp.where(here, own, 0.0), axis=0, keepdims=True)[:, :LOCAL]
    upper, under = coeff[:128], coeff[128:]
    weighted = jnp.sum(light * upper + 2.0 * (below * under), axis=0, keepdims=True) * jnp.sum(
        jnp.where(eye, upper, 0.0), axis=0, keepdims=True
    ) + jnp.sum(corner_block * under, axis=0, keepdims=True) * jnp.sum(
        jnp.where(eye, under, 0.0), axis=0, keepdims=True
    )
    square_total = jnp.sum(weighted, keepdims=True)
    scale = lax.rsqrt(square_total / ENTRIES + 1e-06)
    for index in range(ROWS):
        cent = cent_ref[:, 128 * index : 128 * index + 128].astype(jnp.float32)
        layer, column = index // (ROWS // 2), 128 * (index % (ROWS // 2))
        update_ref[layer : layer + 1, column : column + 128] = (
            jnp.sum(cent * coeff, axis=0, keepdims=True) * scale
        )

    sent = send_ref.at[pl.ds(0, NSAMP - 1)]
    remote(sent, sent, send_sem, recv_sem.at[0, 0], sibling).wait_send()

    def finish(side, width):
        wide = pl.ds(0, width)
        for kind in range(2):
            count = CHIPS - 1 if kind == side else CHIPS
            bytes_ref = gram_ref.at[pl.ds(0, count * 8), pl.ds(0, widths[kind])]
            remote(bytes_ref, bytes_ref, sem1.at[kind], sem1.at[2], sibling).wait_send()
        landed = second.at[pl.ds(0, NZ - 1), :, wide]
        remote(landed, landed, sem2.at[0], sem2.at[1], sibling).wait_send()
        landed = first.at[pl.ds(0, 2 * CHIPS - 1), :, wide]
        remote(landed, landed, sem3.at[0], sem1.at[2], sibling).wait_send()

    by_core(finish)


def main_call(activations, cotangents, spin_bits, off_row):
    whole = pl.BlockSpec(memory_space=VMEM)
    anywhere = pl.BlockSpec(memory_space=pl.ANY)
    dma = pltpu.SemaphoreType.DMA
    return pl.pallas_call(
        main_kernel,
        in_specs=[anywhere, anywhere, whole, whole],
        out_specs=[whole, whole],
        out_shape=[
            jax.ShapeDtypeStruct((LAYERS, ROWS * CH), jnp.float32),
            jax.ShapeDtypeStruct((1, LOCAL), jnp.float32),
        ],
        scratch_shapes=[
            VMEM((LOCAL, LAYERS, CH, SITES), jnp.bfloat16),
            VMEM((LOCAL, LAYERS, CH, SITES), jnp.bfloat16),
            VMEM((2, CH, SITES), jnp.bfloat16),
            VMEM((SLOTS, 3 * CH, PADK), jnp.bfloat16),
            VMEM((SLOTS, 3 * CH, PADK), jnp.bfloat16),
            VMEM((SLOTS, 2, 3 * CH, 128), jnp.float32),
            VMEM((LAYERS, NSAMP * HALF, 128), jnp.float32),
            VMEM((NSAMP, CHUNK, 128), jnp.bfloat16),
            VMEM((NSAMP, CHUNK, 128), jnp.bfloat16),
            VMEM((NS, WIDTH), jnp.bfloat16),
            VMEM((1, 128), jnp.float32),
            VMEM((NSAMP, 1, 128), jnp.float32),
            VMEM((NS, NS), jnp.float32),
            VMEM((2 * CHIPS, 8, NS), jnp.float32),
            VMEM((8, NS), jnp.float32),
            VMEM((NZ, 8, NS), jnp.float32),
            VMEM((NS, NS), jnp.float32),
            VMEM((NS, NS + 128), jnp.float32),
            VMEM((NS, 128), jnp.float32),
            VMEM((BLOCK // PANEL, 1, 8, 128), jnp.float32),
            VMEM((BLOCK // PANEL, PANEL, 8, 128), jnp.float32),
            VMEM((BLOCK // PANEL, PANEL, 8, 128), jnp.float32),
            dma((LOCAL // PAIR + 1,)),
            dma((LOCAL // PAIR + 1,)),
            dma,
            dma((3, NY)),
            dma((2,)),
            dma((3,)),
            dma((2,)),
            dma((3,)),
        ],
        compiler_params=pltpu.CompilerParams(
            collective_id=0, has_side_effects=True, vmem_limit_bytes=VMEM_LIMIT
        ),
    )(activations, cotangents, spin_bits, off_row)


def hand_on_kernel(update_in, coeff_in, update_ref, coeff_ref, sems):
    copies = [
        pltpu.make_async_copy(update_in, update_ref, sems.at[0]),
        pltpu.make_async_copy(coeff_in, coeff_ref, sems.at[1]),
    ]
    for copy in copies:
        copy.start()
    for copy in copies:
        copy.wait()


def hand_on(update, coeff):
    anywhere = pl.BlockSpec(memory_space=pl.ANY)
    return pl.pallas_call(
        hand_on_kernel,
        in_specs=[anywhere, anywhere],
        out_specs=[anywhere, anywhere],
        out_shape=[
            jax.ShapeDtypeStruct((LAYERS, ROWS * CH), jnp.float32),
            jax.ShapeDtypeStruct((1, LOCAL), jnp.float32),
        ],
        scratch_shapes=[pltpu.SemaphoreType.DMA((2,))],
        compiler_params=pltpu.CompilerParams(vmem_limit_bytes=VMEM_LIMIT),
    )(update, coeff)


def on_device(activations, cotangents, spin_bits, offdiag_energy):
    update, coeff = hand_on(
        *main_call(activations, cotangents, spin_bits, offdiag_energy.reshape(1, LOCAL))
    )
    return update, coeff.reshape(LOCAL)


def solution(mesh):
    in_specs = (
        P("samp", "par", None, None),
        P("samp", "par", None, None),
        P("samp", None),
        P("samp"),
    )
    out_specs = (P("par", "samp"), P("samp"))
    return jax.shard_map(
        on_device, mesh=mesh, in_specs=in_specs, out_specs=out_specs, check_vma=False
    )
```
